32 devices in a mesh: dp: 4 (over y, x), space: 8 (over z, core).
Axes of the slice: x: 2, y: 2, z: 4, core: 2. Of those that a mesh axis runs over, the one named last changes fastest.
Arguments:
- node_scalar: bfloat16 [4096, 1024], P(('dp', 'space')), may hold values from -6 to 6
- node_vector: bfloat16 [3, 4096, 256], P(None, ('dp', 'space')), may hold values from -6 to 6
- edge_scalar: bfloat16 [4096, 960], P(('dp', 'space')), may hold values from -6 to 6
- edge_vector: bfloat16 [3, 122880], P(None, ('dp', 'space')), may hold values from -6 to 6
- neighbours: int32 [4096, 30], P(('dp', 'space')), may hold values from 0 to 255, as said below
- send_rows: int32 [32, 8, 16], P(('dp', 'space')), may hold values from -1 to 127, as said below
- complex_id: int32 [4096], P('dp'), may hold values 0 or 1
- cotangent: bfloat16 [4096, 512], P(('dp', 'space')), may hold values from -6 to 6
- w_node: bfloat16 [1024, 2048], replicated, may hold values from -0.1875 to 0.1875
- w_edge: bfloat16 [32, 1024], replicated, may hold values from -1 to 1
- w_norms: bfloat16 [513, 1024], replicated, may hold values from -0.25 to 0.25
- vec_node: bfloat16 [256, 1026], replicated, may hold values from -0.375 to 0.375
- vec_edge: bfloat16 [1, 513], replicated, may hold values from -6 to 6
- vec_out: bfloat16 [513, 256], replicated, may hold values from -0.25 to 0.25
- norm_gain: bfloat16 [1024], replicated, may hold values from 0.5 to 1.5
- ff_vec: bfloat16 [256, 256], replicated, may hold values from -0.375 to 0.375
- ff_scalar: bfloat16 [1280, 1024], replicated, may hold values from -0.15625 to 0.15625
- ff_up: bfloat16 [256, 256], replicated, may hold values from -0.375 to 0.375
- w_embed: bfloat16 [1280, 512], replicated, may hold values from -0.15625 to 0.15625
- attn_gain: bfloat16 [512], replicated, may hold values from 0.5 to 1.5
- w_qkv: bfloat16 [512, 1536], replicated, may hold values from -0.25 to 0.25
- w_out: bfloat16 [512, 512], replicated, may hold values from -6 to 6
- ffn_gain: bfloat16 [512], replicated, may hold values from 0.5 to 1.5
- w_up: bfloat16 [512, 2048], replicated, may hold values from -0.25 to 0.25
- w_down: bfloat16 [2048, 512], replicated, may hold values from -0.125 to 0.125
Outputs:
- stream_out: bfloat16 [4096, 512], P(('dp', 'space'))
- grad_scalar: bfloat16 [4096, 1024], P(('dp', 'space'))
- grad_vector: bfloat16 [3, 4096, 256], P(None, ('dp', 'space'))
- grad_w_node: float32 [1024, 2048], P('space')
- grad_w_edge: float32 [32, 1024], P(None, 'space')
- grad_w_norms: float32 [513, 1024], P(None, 'space')
- grad_vec_node: float32 [256, 1026], P('space')
- grad_vec_edge: float32 [1, 513], replicated
- grad_vec_out: float32 [513, 256], P(None, 'space')
- grad_norm_gain: float32 [1024], P('space')
- grad_ff_vec: float32 [256, 256], P('space')
- grad_ff_scalar: float32 [1280, 1024], P('space')
- grad_ff_up: float32 [256, 256], P('space')
- grad_w_embed: float32 [1280, 512], P('space')
- grad_attn_gain: float32 [512], P('space')
- grad_w_qkv: float32 [512, 1536], P('space')
- grad_w_out: float32 [512, 512], P('space')
- grad_ffn_gain: float32 [512], P('space')
- grad_w_up: float32 [512, 2048], P('space')
- grad_w_down: float32 [2048, 512], P('space')
The draws below stay inside these ranges and needn't reach their ends.
Inputs may be any that keep to these rules, and one draw needn't show every extreme that they name: `neighbours`: an entry below 128 is a row of the residue's own device; any other entry is 128 + d * 16 + c with send_rows[d, p, c] not -1 (a live slot sent to this device p by device d of the same batch). For device q of a space group, send_rows[q, d] holds the rows sent to device d: the live ones first, then -1. Rows may repeat. Blocks form a periodic cube grid of 8 blocks; live rows go only to the up to 26 adjacent blocks, between 8 and 16 to each, and some pair has 16 in every draw.
All inputs are finite; a program needn't handle non-finite values. No bound on the sum of `complex_id` on one device may be relied on, other than what follows from the above.
Results may differ from the reference program's by a relative error of at most 0.018.
Values may be sent and summed in bfloat16 or wider, within the bound.
A program may use at most 320 MiB of HBM per device.

```python
import jax
import jax.numpy as jnp
from jax import lax

D_S = 1024
D_V = 256
H_V = 513
D_E = 32
NEIGH = 30
D_MODEL = 512
HEADS = 8
HEAD_DIM = 64
FFN = 2048
NODES_DEV = 128
CAP = 16
NODES = 1024
ROWS = 4096
N_DP = 4
N_SPACE = 8


def cube_length():
    return [length for length in range(1, 64) if length * length * length == N_SPACE][0]


def pair_counts(key):
    length = cube_length()
    places = jnp.arange(N_SPACE, dtype=jnp.int32)
    coords = jnp.stack([places // (length * length), places // length % length, places % length], 0)
    coord_gap = (coords[:, :, None] - coords[:, None, :]) % length
    adjacent = jnp.all((coord_gap == 0) | (coord_gap == 1) | (coord_gap == length - 1), axis=0)
    adjacent = adjacent & (places[:, None] != places[None, :])
    count_draw = jax.random.randint(key, (N_DP, N_SPACE, N_SPACE), CAP // 2, CAP + 1)
    partner = places - places % length + (places % length + 1) % length
    forced = places[None, :] == partner[:, None]
    count_draw = jnp.where(forced[None], CAP, count_draw)
    return jnp.where(adjacent[None], count_draw, 0).astype(jnp.int32)


def draw_send_rows(key, part):
    counts = pair_counts(key)
    key = jax.random.fold_in(key, 11)
    row_draw = jax.random.randint(key, (N_DP, N_SPACE, N_SPACE, CAP), 0, NODES_DEV)
    slot_ids = jnp.arange(CAP, dtype=jnp.int32)
    is_live = slot_ids[None, None, None, :] < counts[..., None]
    return jnp.where(is_live, row_draw, -1).reshape(N_DP * N_SPACE, N_SPACE, CAP).astype(jnp.int32)


def find_slot(running, wanted):
    return jnp.searchsorted(running, wanted + 1, side='left')


def draw_neighbours(key, part):
    counts = pair_counts(key)
    key = jax.random.fold_in(key, 23)
    self_key, pick_key, local_key = jax.random.split(key, 3)
    slot_ids = jnp.arange(CAP, dtype=jnp.int32)
    incoming = jnp.swapaxes(counts, 1, 2)
    is_live = (slot_ids[None, None, None, :] < incoming[..., None]).astype(jnp.int32)
    is_live = is_live.reshape(N_DP, N_SPACE, N_SPACE * CAP)
    running = jnp.cumsum(is_live, axis=-1)
    live_total = running[..., -1]
    edge_shape = (N_DP, N_SPACE, NODES_DEV * NEIGH)
    pick_draw = jax.random.randint(pick_key, edge_shape, 0, 1 << 20) % live_total[..., None]
    slot_pick = jax.vmap(jax.vmap(find_slot))(running, pick_draw).astype(jnp.int32)
    local_pick = jax.random.randint(local_key, edge_shape, 0, NODES_DEV)
    choose_self = jax.random.randint(self_key, edge_shape, 0, 2) == 0
    chosen = jnp.where(choose_self, local_pick, NODES_DEV + slot_pick)
    return chosen.reshape(N_DP * N_SPACE * NODES_DEV, NEIGH).astype(jnp.int32)


def plant(array, own_key, smallest, high):
    longest = array.shape.index(max(array.shape))
    spots = []
    for shift in (0, 1):
        where = [jax.random.randint(jax.random.fold_in(own_key, axis), (), 0, length) for axis, length in enumerate(array.shape)]
        where[longest] = (where[longest] + shift) % array.shape[longest]
        spots.append(tuple(where))
    return array.at[spots[0]].set(smallest).at[spots[1]].set(high)


def block_scale(stream_key, shape, shards, least, largest):
    def one(axis_at, parts):
        draws = jax.random.uniform(jax.random.fold_in(jax.random.fold_in(stream_key, 6), axis_at), (parts,), jnp.float32, least / len(shards), largest / len(shards))
        return jnp.repeat(jnp.exp(draws), shape[axis_at] // parts).reshape((-1,) + (1,) * (len(shape) - axis_at - 1))

    loudness = one(*shards[0])
    for cut in shards[1:]:
        loudness = loudness * one(*cut)
    return loudness


def bell_draw(stream_key, extent, scale, bound, cuts=(), kind=jnp.bfloat16):
    array = scale * jax.random.normal(stream_key, extent, jnp.float32)
    if cuts:
        array = array * block_scale(stream_key, extent, cuts, -0.22, 0.18)
    return jnp.clip(array, -bound, bound).astype(kind)


def setup_inputs(seed: int = 0) -> dict:
    streams_of = jax.random.split(jax.random.key(seed), 26)
    node_scalar = bell_draw(streams_of[0], (ROWS, D_S), 1.0, 6.0, ((0, 32),))
    node_vector = bell_draw(streams_of[1], (3, ROWS, D_V), 1.0, 6.0, ((1, 32),))
    edge_scalar = bell_draw(streams_of[2], (ROWS, NEIGH * D_E), 1.0, 6.0, ((0, 32),))
    edge_vector = bell_draw(streams_of[3], (3, ROWS * NEIGH), 1.0, 6.0, ((1, 32),))
    neighbours = draw_neighbours(jax.random.fold_in(streams_of[25], 71), 0)
    send_rows = draw_send_rows(jax.random.fold_in(streams_of[25], 71), 0)
    complex_id = plant((jax.random.randint(streams_of[6], (N_DP * NODES,), 0, 8) < 1).astype(jnp.int32), jax.random.fold_in(streams_of[6], 1), 0, 1)
    cotangent = bell_draw(streams_of[7], (ROWS, D_MODEL), 1.0, 6.0, ((0, 32),))
    w_node = bell_draw(streams_of[8], (D_S, 2 * D_S), D_S ** -0.5, 0.1875)
    w_edge = bell_draw(streams_of[9], (D_E, D_S), D_E ** -0.5, 1.0)
    w_norms = bell_draw(streams_of[10], (H_V, D_S), H_V ** -0.5, 0.25)
    vec_node = bell_draw(streams_of[11], (D_V, 2 * H_V), D_V ** -0.5, 0.375)
    vec_edge = bell_draw(streams_of[12], (1, H_V), 1.0, 6.0)
    vec_out = bell_draw(streams_of[13], (H_V, D_V), H_V ** -0.5, 0.25)
    norm_gain = jnp.clip(1.0 + 0.1 * jax.random.normal(streams_of[14], (D_S,), jnp.float32), 0.5, 1.5).astype(jnp.bfloat16)
    ff_vec = bell_draw(streams_of[15], (D_V, D_V), D_V ** -0.5, 0.375)
    ff_scalar = bell_draw(streams_of[16], (D_S + D_V, D_S), (D_S + D_V) ** -0.5, 0.15625)
    ff_up = bell_draw(streams_of[17], (D_V, D_V), D_V ** -0.5, 0.375)
    w_embed = bell_draw(streams_of[18], (D_S + D_V, D_MODEL), (D_S + D_V) ** -0.5, 0.15625)
    attn_gain = jnp.clip(1.0 + 0.1 * jax.random.normal(streams_of[19], (D_MODEL,), jnp.float32), 0.5, 1.5).astype(jnp.bfloat16)
    w_qkv = bell_draw(streams_of[20], (D_MODEL, 3 * D_MODEL), D_MODEL ** -0.5, 0.25)
    w_out = bell_draw(streams_of[21], (D_MODEL, D_MODEL), ((NODES // 2) ** 0.5 * D_MODEL ** -0.5), 6.0)
    ffn_gain = jnp.clip(1.0 + 0.1 * jax.random.normal(streams_of[22], (D_MODEL,), jnp.float32), 0.5, 1.5).astype(jnp.bfloat16)
    w_up = bell_draw(streams_of[23], (D_MODEL, FFN), D_MODEL ** -0.5, 0.25)
    w_down = bell_draw(streams_of[24], (FFN, D_MODEL), FFN ** -0.5, 0.125)
    return {"node_scalar": node_scalar, "node_vector": node_vector, "edge_scalar": edge_scalar, "edge_vector": edge_vector, "neighbours": neighbours, "send_rows": send_rows, "complex_id": complex_id, "cotangent": cotangent, "w_node": w_node, "w_edge": w_edge, "w_norms": w_norms, "vec_node": vec_node, "vec_edge": vec_edge, "vec_out": vec_out, "norm_gain": norm_gain, "ff_vec": ff_vec, "ff_scalar": ff_scalar, "ff_up": ff_up, "w_embed": w_embed, "attn_gain": attn_gain, "w_qkv": w_qkv, "w_out": w_out, "ffn_gain": ffn_gain, "w_up": w_up, "w_down": w_down}


@jax.custom_vjp
def low(v):
    return lax.optimization_barrier(v.astype(jnp.bfloat16)).astype(jnp.float32)

@jax.custom_vjp
def low_back(v):
    return v

def low_keep(v):
    return (low(v), None)

def low_pass(kept, grad):
    return (grad,)

def back_keep(v):
    return (v, None)

def back_low(kept, grad):
    return (low(grad),)
low.defvjp(low_keep, low_pass)
low_back.defvjp(back_keep, back_low)
HIGHEST = lax.Precision.HIGHEST

def product(former, latter):
    return jnp.dot(former, latter, precision=HIGHEST, preferred_element_type=jnp.float32)

def layer_norm(values, gain_row):
    centred = values - lax.optimization_barrier(jnp.mean(values, axis=-1, keepdims=True))
    spread = lax.optimization_barrier(jnp.mean(centred * centred, axis=-1, keepdims=True))
    return centred * lax.rsqrt(spread + 1e-05) * gain_row

def vector_norm(vectors):
    mean_power = lax.optimization_barrier(jnp.mean(lax.optimization_barrier(jnp.sum(vectors * vectors, axis=0)), axis=-1, keepdims=True))
    return vectors * lax.rsqrt(mean_power + 1e-05)[None]

def length_plus(vectors):
    return jnp.sqrt(lax.optimization_barrier(jnp.sum(vectors * vectors, axis=0)) + 1.0)

def vector_gate(vectors):
    return vectors * jax.nn.sigmoid(length_plus(vectors))[None]

def table_rows(send_block):
    owners = jnp.arange(N_SPACE, dtype=jnp.int32)
    remote = owners[:, None, None] * NODES_DEV + jnp.maximum(send_block, 0)
    remote = jnp.transpose(remote, (1, 0, 2)).reshape(N_SPACE, N_SPACE * CAP)
    own_rows = owners[:, None] * NODES_DEV + jnp.arange(NODES_DEV, dtype=jnp.int32)[None, :]
    return jnp.concatenate([own_rows, remote], axis=1).astype(jnp.int32)

def forward_batch(scalar_in, vector_in, weights, edge_scalar, edge_vector, neighbours, tables, complex_id):
    w_node, w_edge, w_norms, vec_node, vec_edge, vec_out, norm_gain, ff_vec, ff_scalar, ff_up, w_embed, attn_gain, w_qkv, w_out, ffn_gain, w_up, w_down = weights

    def device_messages(inputs):
        table, nearby, scalars_in, vectors_in, own_scalar, own_vector = inputs
        table_s = scalar_in[table]
        table_v = vector_in[:, table]
        a_source = low_back(product(table_s, w_node[:, :D_S]))
        b_target = low_back(product(own_scalar, w_node[:, D_S:]))
        p_source = low_back(product(table_v, vec_node[:, :H_V]))
        q_target = low_back(product(own_vector, vec_node[:, H_V:]))
        hidden_v = p_source[:, nearby] + q_target[:, :, None] + vectors_in[..., None] * vec_edge[0]
        lengths = length_plus(hidden_v)
        preact = low_back(a_source[nearby] + b_target[:, None] + product(scalars_in, w_edge) + product(low(lengths), w_norms))
        update = low_back(product(low(hidden_v), vec_out))
        return (lax.optimization_barrier(jnp.mean(jax.nn.silu(preact), axis=1)), lax.optimization_barrier(jnp.mean(vector_gate(update), axis=2)))
    inputs = (tables, neighbours.reshape(N_SPACE, NODES_DEV, NEIGH), edge_scalar.reshape(N_SPACE, NODES_DEV, NEIGH, D_E), jnp.moveaxis(edge_vector.reshape(3, N_SPACE, NODES_DEV, NEIGH), 1, 0), scalar_in.reshape(N_SPACE, NODES_DEV, D_S), jnp.moveaxis(vector_in.reshape(3, N_SPACE, NODES_DEV, D_V), 1, 0))
    agg_s, agg_v = lax.map(jax.checkpoint(device_messages), inputs)
    agg_s = agg_s.reshape(NODES, D_S)
    agg_v = jnp.moveaxis(agg_v, 0, 1).reshape(3, NODES, D_V)
    scalar_one = scalar_in + agg_s
    vector_one = vector_in + agg_v
    normed_s = layer_norm(scalar_one, norm_gain)
    normed_v = vector_norm(vector_one)
    ff_hidden = low_back(product(low(normed_v), ff_vec))
    ff_length = length_plus(ff_hidden)
    ff_preact = low_back(product(jnp.concatenate([low(normed_s), low(ff_length)], -1), ff_scalar))
    ff_update = low_back(product(low(ff_hidden), ff_up))
    scalar_two = normed_s + jax.nn.silu(ff_preact)
    vector_two = normed_v + vector_gate(ff_update)
    embed_input = jnp.concatenate([low(scalar_two), low(length_plus(vector_two))], -1)
    stream_zero = low_back(product(embed_input, w_embed))
    attn_in = low(layer_norm(stream_zero, attn_gain))
    qkv = low(low_back(product(attn_in, w_qkv)))
    queries = qkv[:, :D_MODEL].reshape(NODES, HEADS, HEAD_DIM)
    key_heads = qkv[:, D_MODEL:2 * D_MODEL].reshape(NODES, HEADS, HEAD_DIM)
    value_heads = qkv[:, 2 * D_MODEL:].reshape(NODES, HEADS, HEAD_DIM)
    score_scale = HEAD_DIM ** (-0.5)
    query_block = NODES_DEV * 8
    block_count = NODES // query_block

    def attend(inputs):
        block_q, block_ids = inputs
        scores = low_back(jnp.einsum('qhd,khd->hqk', block_q, key_heads, precision=HIGHEST) * score_scale)
        scores = jnp.where((block_ids[:, None] == complex_id[None, :])[None], scores, -1000000000.0)
        shifted = jnp.exp(scores - lax.optimization_barrier(jnp.max(scores, axis=-1, keepdims=True)))
        probs = shifted / lax.optimization_barrier(jnp.sum(shifted, axis=-1, keepdims=True))
        return jnp.einsum('hqk,khd->qhd', low(probs), value_heads, precision=HIGHEST)
    attended = lax.map(jax.checkpoint(attend), (queries.reshape(block_count, query_block, HEADS, HEAD_DIM), complex_id.reshape(block_count, query_block)))
    attended = low(low_back(attended.reshape(NODES, D_MODEL)))
    stream_one = stream_zero + low_back(product(attended, w_out))
    ffn_in = low(layer_norm(stream_one, ffn_gain))
    hidden_up = low_back(product(ffn_in, w_up))
    return stream_one + product(low(jax.nn.gelu(hidden_up, approximate=False)), w_down)

def reference(node_scalar, node_vector, edge_scalar, edge_vector, neighbours, send_rows, complex_id, cotangent, w_node, w_edge, w_norms, vec_node, vec_edge, vec_out, norm_gain, ff_vec, ff_scalar, ff_up, w_embed, attn_gain, w_qkv, w_out, ffn_gain, w_up, w_down):
    weight_list = (w_node, w_edge, w_norms, vec_node, vec_edge, vec_out, norm_gain, ff_vec, ff_scalar, ff_up, w_embed, attn_gain, w_qkv, w_out, ffn_gain, w_up, w_down)
    weights = tuple((weight.astype(jnp.float32) for weight in weight_list))
    stream_parts = []
    scalar_parts = []
    vector_parts = []
    weight_grads = None
    for group_index in range(N_DP):
        first_row = group_index * NODES
        scalar_in = node_scalar[first_row:first_row + NODES].astype(jnp.float32)
        vector_in = node_vector[:, first_row:first_row + NODES].astype(jnp.float32)
        edges_s = edge_scalar[first_row:first_row + NODES].astype(jnp.float32)
        edges_v = edge_vector[:, first_row * NEIGH:(first_row + NODES) * NEIGH].astype(jnp.float32)
        nearby = neighbours[first_row:first_row + NODES]
        tables = table_rows(send_rows[group_index * N_SPACE:(group_index + 1) * N_SPACE])
        group_ids = complex_id[first_row:first_row + NODES]

        def whole(scalar_arg, vector_arg, *weight_args):
            return forward_batch(scalar_arg, vector_arg, weight_args, edges_s, edges_v, nearby, tables, group_ids)
        stream_out, puller = jax.vjp(whole, scalar_in, vector_in, *weights)
        grads = puller(cotangent[first_row:first_row + NODES].astype(jnp.float32))
        stream_parts.append(stream_out.astype(jnp.bfloat16))
        scalar_parts.append(grads[0].astype(jnp.bfloat16))
        vector_parts.append(grads[1].astype(jnp.bfloat16))
        if weight_grads is None:
            weight_grads = list(grads[2:])
        else:
            weight_grads = [total + extra for total, extra in zip(weight_grads, grads[2:])]
    return (jnp.concatenate(stream_parts, 0), jnp.concatenate(scalar_parts, 0), jnp.concatenate(vector_parts, 1), weight_grads[0], weight_grads[1], weight_grads[2], weight_grads[3], weight_grads[4], weight_grads[5], weight_grads[6], weight_grads[7], weight_grads[8], weight_grads[9], weight_grads[10], weight_grads[11], weight_grads[12], weight_grads[13], weight_grads[14], weight_grads[15], weight_grads[16])
```

```python
import functools
import math

import jax
import jax.numpy as jnp
from jax import lax
from jax.experimental import pallas as pl
from jax.experimental.pallas import tpu as pltpu
from jax.sharding import PartitionSpec as P

D_S = 1024
D_V = 256
H_V = 513
H_P = 640
D_E = 32
NEIGH = 30
D_MODEL = 512
HEADS = 8
HEAD_DIM = 64
CAP = 16
GROUP = 5
VMEM_LIMIT = 60 * 1024 * 1024

BF = jnp.bfloat16
F32 = jnp.float32


def layer_norm(values, gain_row):
    centred = values - jnp.mean(values, axis=-1, keepdims=True)
    spread = jnp.mean(centred * centred, axis=-1, keepdims=True)
    return centred * lax.rsqrt(spread + 1e-05) * gain_row


def vector_norm(vectors):
    mean_power = jnp.mean(jnp.sum(vectors * vectors, axis=0), axis=-1, keepdims=True)
    return vectors * lax.rsqrt(mean_power + 1e-05)[None]


def length_plus(vectors):
    return jnp.sqrt(jnp.sum(vectors * vectors, axis=0) + 1.0)


def vector_gate(vectors):
    return vectors * jax.nn.sigmoid(length_plus(vectors))[None]


def gelu_exact(values):
    return jax.nn.gelu(values, approximate=False)


def product(former, latter):
    return jnp.dot(former, latter, preferred_element_type=F32)


def product_lead(former, latter):
    leading = tuple(range(former.ndim - 1))
    return lax.dot_general(
        former, latter, ((leading, leading), ((), ())), preferred_element_type=F32
    )


def product_back(former, latter):
    return lax.dot_general(
        former, latter, (((former.ndim - 1,), (1,)), ((), ())), preferred_element_type=F32
    )


def pullback(function, at_point, cotangent_in):
    unused, puller = jax.vjp(function, at_point)
    return puller(cotangent_in)[0]


def sigmoid(values):
    return 0.5 * jnp.tanh(0.5 * values) + 0.5


LANE_BLOCKS = ((0, 256), (256, 256), (512, 128))
ROW_TILE = 64


def edge_forward_kernel(
    near_ref, es_ref, ev_ref, a_ref, b_ref, p_ref, q_ref, ve_ref, vo_ref,
    aggs_ref, aggv_ref, h_ref, lx_ref, ds_ref, z_ref, x_scr,
):
    nodes = b_ref.shape[0]
    table = p_ref.shape[1]
    rows = GROUP * nodes
    idx = near_ref[...].reshape(rows, 1)
    x_scr[:, :table] = (idx == lax.broadcasted_iota(jnp.int32, (rows, table), 1)).astype(BF)
    one_hot = x_scr[:, :table]
    for start, width in LANE_BLOCKS:
        cols = pl.ds(start, width)
        gathered = [product(one_hot, p_ref[c, :, cols]) for c in range(3)]
        for k in range(GROUP):
            for first in range(0, nodes, ROW_TILE):
                at = k * nodes + first
                evk = ev_ref[k, pl.ds(first, ROW_TILE), :]
                total = None
                for c in range(3):
                    h = (
                        gathered[c][at : at + ROW_TILE]
                        + q_ref[c, pl.ds(first, ROW_TILE), cols]
                        + evk[:, c : c + 1] * ve_ref[:, cols]
                    )
                    h_ref[k, c, pl.ds(first, ROW_TILE), cols] = h.astype(BF)
                    total = h * h + 1.0 if total is None else total + h * h
                length = total * lax.rsqrt(total)
                if start == 512:
                    lane = lax.broadcasted_iota(jnp.int32, (ROW_TILE, width), 1)
                    length = jnp.where(
                        lane == 0, length, es_ref[k, pl.ds(first, ROW_TILE), :].astype(F32)
                    )
                length = length.astype(BF)
                x_scr[pl.ds(at, ROW_TILE), pl.ds(table + start, width)] = length
                lx_ref[k, pl.ds(first, ROW_TILE), cols] = length

    @pl.when(pl.program_id(0) == 0)
    def _():
        aggs_ref[...] = jnp.zeros_like(aggs_ref)
        aggv_ref[...] = jnp.zeros_like(aggv_ref)

    full = x_scr[...]
    for start in range(0, D_S, 256):
        cols = pl.ds(start, 256)
        pre = product(full, a_ref[:, cols])
        for first in range(0, nodes, ROW_TILE):
            part = pl.ds(first, ROW_TILE)
            acc = None
            for k in range(GROUP):
                at = k * nodes + first
                x = pre[at : at + ROW_TILE] + b_ref[part, cols]
                s = sigmoid(x)
                y = x * s
                ds_ref[k, part, cols] = (s + y * (1.0 - s)).astype(BF)
                acc = y if acc is None else acc + y
            aggs_ref[part, cols] += acc * (1.0 / NEIGH)
    ups = [
        product(h_ref[:, c, :, :].reshape(rows, H_P), vo_ref[...]) for c in range(3)
    ]
    for first in range(0, nodes, ROW_TILE):
        part = pl.ds(first, ROW_TILE)
        acc = [None] * 3
        for k in range(GROUP):
            at = k * nodes + first
            z = [ups[c][at : at + ROW_TILE] for c in range(3)]
            power = z[0] * z[0] + z[1] * z[1] + z[2] * z[2] + 1.0
            s = sigmoid(power * lax.rsqrt(power))
            for c in range(3):
                z_ref[k, c, part, :] = z[c].astype(BF)
                gated = z[c] * s
                acc[c] = gated if acc[c] is None else acc[c] + gated
        for c in range(3):
            aggv_ref[c, part, :] += acc[c] * (1.0 / NEIGH)


def edge_forward(near_col, es_pad, ev_col, mix, b_target, p_source, q_target, ve_row, vout):
    nodes = b_target.shape[0]
    table = p_source.shape[1]
    whole = lambda shape: pl.BlockSpec(shape, lambda g: (0,) * len(shape))
    slots = lambda *shape: pl.BlockSpec((GROUP,) + shape, lambda g: (g,) + (0,) * len(shape))
    return pl.pallas_call(
        edge_forward_kernel,
        grid=(NEIGH // GROUP,),
        in_specs=[
            slots(nodes, 1),
            slots(nodes, 128),
            slots(nodes, 3),
            whole((table + H_P, D_S)),
            whole((nodes, D_S)),
            whole((3, table, H_P)),
            whole((3, nodes, H_P)),
            whole((1, H_P)),
            whole((H_P, D_V)),
        ],
        out_specs=[
            whole((nodes, D_S)),
            whole((3, nodes, D_V)),
            slots(3, nodes, H_P),
            slots(nodes, H_P),
            slots(nodes, D_S),
            slots(3, nodes, D_V),
        ],
        out_shape=[
            jax.ShapeDtypeStruct((nodes, D_S), F32),
            jax.ShapeDtypeStruct((3, nodes, D_V), F32),
            jax.ShapeDtypeStruct((NEIGH, 3, nodes, H_P), BF),
            jax.ShapeDtypeStruct((NEIGH, nodes, H_P), BF),
            jax.ShapeDtypeStruct((NEIGH, nodes, D_S), BF),
            jax.ShapeDtypeStruct((NEIGH, 3, nodes, D_V), BF),
        ],
        scratch_shapes=[pltpu.VMEM((GROUP * nodes, table + H_P), BF)],
        compiler_params=pltpu.CompilerParams(vmem_limit_bytes=VMEM_LIMIT),
        name="edge_forward",
    )(near_col, es_pad, ev_col, mix, b_target, p_source, q_target, ve_row, vout)


def edge_backward_kernel(
    near_ref, ev_ref, evr_ref, h_ref, lx_ref, ds_ref, z_ref, gs_ref, gv_ref, wn_ref, vo_ref,
    ga_ref, gw_ref, gb_ref, gp_ref, gq_ref, gvo_ref, pre_scr, up_scr, gh_scr,
):
    nodes = gs_ref.shape[0]
    table = ga_ref.shape[0]
    rows = GROUP * nodes

    @pl.when(pl.program_id(0) == 0)
    def _():
        for ref in (ga_ref, gw_ref, gb_ref, gp_ref, gq_ref, gvo_ref):
            ref[...] = jnp.zeros_like(ref)

    for start in range(0, D_S, 256):
        cols = pl.ds(start, 256)
        for first in range(0, nodes, ROW_TILE):
            part = pl.ds(first, ROW_TILE)
            share = gs_ref[part, cols]
            acc = None
            for k in range(GROUP):
                g = (ds_ref[k, part, cols].astype(F32) * share).astype(BF)
                pre_scr[pl.ds(k * nodes + first, ROW_TILE), cols] = g
                g = g.astype(F32)
                acc = g if acc is None else acc + g
            gb_ref[part, cols] += acc
    for first in range(0, nodes, ROW_TILE):
        part = pl.ds(first, ROW_TILE)
        share = [gv_ref[c, part, :] for c in range(3)]
        for k in range(GROUP):
            z = [z_ref[k, c, part, :].astype(F32) for c in range(3)]
            power = z[0] * z[0] + z[1] * z[1] + z[2] * z[2] + 1.0
            inverse = lax.rsqrt(power)
            s = sigmoid(power * inverse)
            dot = z[0] * share[0] + z[1] * share[1] + z[2] * share[2]
            factor = dot * inverse * (s * (1.0 - s))
            for c in range(3):
                up_scr[c, pl.ds(k * nodes + first, ROW_TILE), :] = (
                    share[c] * s + z[c] * factor
                ).astype(BF)

    near = near_ref[0]
    one_hot = (lax.broadcasted_iota(jnp.int32, (table, rows), 0) == near).astype(BF)
    grad_pre = pre_scr[...]
    ga_ref[...] += product(one_hot, grad_pre)
    lx = lx_ref[...].reshape(rows, H_P)
    gw_ref[...] += lax.dot_general(
        lx, grad_pre, (((0,), (0,)), ((), ())), preferred_element_type=F32
    )
    for start, width in LANE_BLOCKS:
        cols = pl.ds(start, width)
        grad_length = product_back(grad_pre, wn_ref[cols, :])
        grad_direct = [product_back(up_scr[c], vo_ref[cols, :]) for c in range(3)]
        for first in range(0, nodes, ROW_TILE):
            part = pl.ds(first, ROW_TILE)
            acc = [None] * 3
            for k in range(GROUP):
                at = k * nodes + first
                ratio = grad_length[at : at + ROW_TILE] * pl.reciprocal(
                    lx_ref[k, part, cols].astype(F32), approx=True
                )
                if start == 512:
                    lane = lax.broadcasted_iota(jnp.int32, (ROW_TILE, width), 1)
                    ratio = jnp.where(lane == 0, ratio, 0.0)
                for c in range(3):
                    g = grad_direct[c][at : at + ROW_TILE] + ratio * h_ref[
                        k, c, part, cols
                    ].astype(F32)
                    gh_scr[c, pl.ds(at, ROW_TILE), cols] = g.astype(BF)
                    acc[c] = g if acc[c] is None else acc[c] + g
            for c in range(3):
                gq_ref[c, part, cols] += acc[c]
    for c in range(3):
        evr = jnp.broadcast_to(evr_ref[0, c : c + 1, :], (16, rows))
        lead = jnp.concatenate([one_hot, evr.astype(BF)], axis=0)
        gp_ref[c] += product(lead, gh_scr[c])
        gvo_ref[...] += lax.dot_general(
            up_scr[c],
            h_ref[:, c, :, :].reshape(rows, H_P),
            (((0,), (0,)), ((), ())),
            preferred_element_type=F32,
        )


def edge_backward(near_row, ev_col, ev_row, hidden, lx, dsilu, update, gs, gv, wn, vout, table):
    nodes = gs.shape[0]
    rows = GROUP * nodes
    whole = lambda shape: pl.BlockSpec(shape, lambda g: (0,) * len(shape))
    slots = lambda *shape: pl.BlockSpec((GROUP,) + shape, lambda g: (g,) + (0,) * len(shape))
    steps = lambda *shape: pl.BlockSpec((1,) + shape, lambda g: (g,) + (0,) * len(shape))
    outs = [
        (table, D_S),
        (H_P, D_S),
        (nodes, D_S),
        (3, table + 16, H_P),
        (3, nodes, H_P),
        (D_V, H_P),
    ]
    return pl.pallas_call(
        edge_backward_kernel,
        grid=(NEIGH // GROUP,),
        in_specs=[
            steps(1, rows),
            slots(nodes, 3),
            steps(3, rows),
            slots(3, nodes, H_P),
            slots(nodes, H_P),
            slots(nodes, D_S),
            slots(3, nodes, D_V),
            whole((nodes, D_S)),
            whole((3, nodes, D_V)),
            whole((H_P, D_S)),
            whole((H_P, D_V)),
        ],
        out_specs=[whole(shape) for shape in outs],
        out_shape=[jax.ShapeDtypeStruct(shape, F32) for shape in outs],
        scratch_shapes=[
            pltpu.VMEM((rows, D_S), BF),
            pltpu.VMEM((3, rows, D_V), BF),
            pltpu.VMEM((3, rows, H_P), BF),
        ],
        compiler_params=pltpu.CompilerParams(vmem_limit_bytes=VMEM_LIMIT),
        name="edge_backward",
    )(near_row, ev_col, ev_row, hidden, lx, dsilu, update, gs, gv, wn, vout)


def pad_to(values, size, axis):
    pads = [(0, 0)] * values.ndim
    pads[axis] = (0, size - values.shape[axis])
    return jnp.pad(values, pads)


def fold(blocks, width=512):
    shards, rows, columns = blocks.shape
    parts = columns // width
    return jnp.moveaxis(blocks.reshape(shards, rows, parts, width), 2, 1).reshape(
        shards, parts * rows, width
    )


def unfold(rows_in, rows, columns, width=512):
    parts = columns // width
    return jnp.moveaxis(rows_in.reshape(parts, rows, width), 0, 1).reshape(rows, columns)


def body(
    node_scalar, node_vector, edge_scalar, edge_vector, neighbours, send_rows, complex_id, cotangent,
    w_node, w_edge, w_norms, vec_node, vec_edge, vec_out, norm_gain, ff_vec, ff_scalar, ff_up,
    w_embed, attn_gain, w_qkv, w_out, ffn_gain, w_up, w_down,
):
    local_rows = node_scalar.shape[0]
    spaces = lax.axis_size("space")
    extra_rows = spaces * CAP
    table_count = local_rows + extra_rows
    all_nodes = complex_id.shape[0]
    steps = NEIGH // GROUP

    sent_index = send_rows[0].reshape(-1)
    sent_live = sent_index >= 0
    pick = sent_index[:, None] == jnp.arange(local_rows, dtype=jnp.int32)[None, :]
    pick = pick.astype(BF)
    flat_nodes = jnp.concatenate([node_scalar] + [node_vector[c] for c in range(3)], 1)
    outgoing = product(pick, flat_nodes).astype(BF).reshape(spaces, CAP, D_S + 3 * D_V)
    incoming = lax.all_to_all(outgoing, "space", split_axis=0, concat_axis=0, tiled=True)
    incoming = incoming.reshape(extra_rows, D_S + 3 * D_V)
    table_s = jnp.concatenate([node_scalar, incoming[:, :D_S]], 0)
    table_v = jnp.stack(
        [
            jnp.concatenate(
                [node_vector[c], incoming[:, D_S + c * D_V : D_S + (c + 1) * D_V]], 0
            )
            for c in range(3)
        ]
    )
    vec_source = pad_to(vec_node[:, :H_V], H_P, 1)
    vec_target = pad_to(vec_node[:, H_V:], H_P, 1)
    a_source = product(table_s, w_node[:, :D_S]).astype(BF)
    b_target = product(node_scalar, w_node[:, D_S:])
    p_source = product(table_v, vec_source).astype(BF)
    q_target = product(node_vector, vec_target)
    ve_row = pad_to(vec_edge.astype(F32), H_P, 1)
    vout = pad_to(vec_out, H_P, 0)
    wn_mix = pad_to(jnp.concatenate([w_norms, w_edge], 0), H_P, 0)
    mix = jnp.concatenate([a_source, wn_mix], 0)

    near = neighbours.T
    near_col = near[:, :, None]
    near_row = near.reshape(steps, 1, GROUP * local_rows)
    es_k = edge_scalar.reshape(local_rows, NEIGH, D_E).transpose(1, 0, 2)
    es_pad = jnp.pad(es_k, ((0, 0), (0, 0), (1, 128 - 1 - D_E)))
    ev_k = edge_vector.reshape(3, local_rows, NEIGH)
    ev_col = ev_k.transpose(2, 1, 0).astype(F32)
    ev_row = ev_k.transpose(2, 0, 1).reshape(steps, GROUP, 3, local_rows)
    ev_row = ev_row.transpose(0, 2, 1, 3).reshape(steps, 3, GROUP * local_rows)

    agg_s, agg_v, hidden, lx, dsilu, update = edge_forward(
        near_col, es_pad, ev_col, mix, b_target, p_source, q_target, ve_row, vout
    )

    scalar_one = node_scalar.astype(F32) + agg_s
    vector_one = node_vector.astype(F32) + agg_v
    gain_norm = norm_gain.astype(F32)
    normed_s = layer_norm(scalar_one, gain_norm)
    normed_v = vector_norm(vector_one)
    normed_vr = normed_v.astype(BF)
    ff_hidden = product(normed_vr, ff_vec)
    ff_hidden_r = ff_hidden.astype(BF)
    ff_length = length_plus(ff_hidden)
    ff_input = jnp.concatenate([normed_s.astype(BF), ff_length.astype(BF)], -1)
    ff_preact = product(ff_input, ff_scalar)
    ff_update = product(ff_hidden_r, ff_up)
    scalar_two = normed_s + jax.nn.silu(ff_preact)
    vector_two = normed_v + vector_gate(ff_update)
    embed_input = jnp.concatenate([scalar_two.astype(BF), length_plus(vector_two).astype(BF)], -1)
    stream_zero = product(embed_input, w_embed)
    gain_attn = attn_gain.astype(F32)
    attn_in = layer_norm(stream_zero, gain_attn).astype(BF)
    qkv = product(attn_in, w_qkv).astype(BF)
    queries = qkv[:, :D_MODEL]
    keys_own = qkv[:, D_MODEL : 2 * D_MODEL]
    values_own = qkv[:, 2 * D_MODEL :]
    full_qkv = lax.all_gather(qkv, "space", axis=0, tiled=True)
    heads = lambda values: values.reshape(values.shape[0], HEADS, HEAD_DIM)
    full_queries = heads(full_qkv[:, :D_MODEL])
    full_keys = heads(full_qkv[:, D_MODEL : 2 * D_MODEL])
    full_values = heads(full_qkv[:, 2 * D_MODEL :])
    position = lax.axis_index("space")
    own_ids = lax.dynamic_slice_in_dim(complex_id, position * local_rows, local_rows, 0)
    same = own_ids[:, None] == complex_id[None, :]
    score_scale = HEAD_DIM ** (-0.5)
    scores = jnp.einsum("qhd,khd->hqk", heads(queries), full_keys, preferred_element_type=F32)
    scores = jnp.where(same[None], scores * score_scale, -1000000000.0)
    row_peak = jnp.max(scores, axis=-1, keepdims=True)
    shifted = jnp.exp(scores - row_peak)
    totals = jnp.sum(shifted, axis=-1, keepdims=True)
    probs = shifted / totals
    log_total = row_peak + jnp.log(totals)
    attended = jnp.einsum(
        "hqk,khd->qhd", probs.astype(BF), full_values, preferred_element_type=F32
    ).reshape(local_rows, D_MODEL)
    attended_r = attended.astype(BF)
    stream_one = stream_zero + product(attended_r, w_out)
    gain_ffn = ffn_gain.astype(F32)
    ffn_in = layer_norm(stream_one, gain_ffn).astype(BF)
    hidden_up = product(ffn_in, w_up)
    gelu_r = gelu_exact(hidden_up).astype(BF)
    stream_out = (stream_one + product(gelu_r, w_down)).astype(BF)
    grad_w_down = product_lead(gelu_r, cotangent)
    grad_gelu = product_back(cotangent, w_down)
    grad_up_r = pullback(gelu_exact, hidden_up, grad_gelu).astype(BF)
    grad_w_up = product_lead(ffn_in, grad_up_r)
    grad_ffn_in = product_back(grad_up_r, w_up)
    unused, ffn_pull = jax.vjp(layer_norm, stream_one, gain_ffn)
    grad_stream_ln, grad_ffn_gain = ffn_pull(grad_ffn_in)
    grad_stream_one = cotangent.astype(F32) + grad_stream_ln
    grad_branch = grad_stream_one.astype(BF)
    grad_w_out = product_lead(attended_r, grad_branch)
    grad_attended = product_back(grad_branch, w_out).astype(BF)
    row_dots = jnp.sum(heads(grad_attended).astype(F32) * heads(attended), axis=-1).T

    def halves(values):
        high = lax.reduce_precision(values, exponent_bits=8, mantissa_bits=7)
        return [high.astype(BF), (values - high).astype(BF)]

    numbers = jnp.concatenate(halves(log_total[:, :, 0]) + halves(row_dots), 0)
    packed = jnp.concatenate([grad_attended, pad_to(numbers.T, 128, 1)], 1)
    full_packed = lax.all_gather(packed, "space", axis=0, tiled=True)
    full_grad = heads(full_packed[:, :D_MODEL])
    numbers = full_packed[:, D_MODEL : D_MODEL + 4 * HEADS].astype(F32).T
    full_log = numbers[:HEADS] + numbers[HEADS : 2 * HEADS]
    full_dots = numbers[2 * HEADS : 3 * HEADS] + numbers[3 * HEADS :]

    grad_probs = jnp.einsum(
        "qhd,khd->hqk", heads(grad_attended), full_values, preferred_element_type=F32
    )
    grad_scores = (probs * (grad_probs - row_dots[:, :, None])).astype(BF)
    grad_query = jnp.einsum("hqk,khd->qhd", grad_scores, full_keys, preferred_element_type=F32)
    own_scores = jnp.einsum(
        "khd,qhd->hkq", heads(keys_own), full_queries, preferred_element_type=F32
    )
    own_scores = jnp.where(same[None], own_scores * score_scale, -1000000000.0)
    own_probs = jnp.exp(own_scores - full_log[:, None, :])
    own_grad_probs = jnp.einsum(
        "khd,qhd->hkq", heads(values_own), full_grad, preferred_element_type=F32
    )
    own_grad_scores = (own_probs * (own_grad_probs - full_dots[:, None, :])).astype(BF)
    grad_keys = jnp.einsum(
        "hkq,qhd->khd", own_grad_scores, full_queries, preferred_element_type=F32
    )
    grad_values = jnp.einsum(
        "hkq,qhd->khd", own_probs.astype(BF), full_grad, preferred_element_type=F32
    )
    flat = lambda values: values.reshape(local_rows, D_MODEL)
    grad_qkv = jnp.concatenate(
        [flat(grad_query) * score_scale, flat(grad_keys) * score_scale, flat(grad_values)], -1
    ).astype(BF)
    grad_w_qkv = product_lead(attn_in, grad_qkv)
    grad_attn_in = product_back(grad_qkv, w_qkv)
    unused, attn_pull = jax.vjp(layer_norm, stream_zero, gain_attn)
    grad_zero_ln, grad_attn_gain = attn_pull(grad_attn_in)
    grad_stream_r = (grad_stream_one + grad_zero_ln).astype(BF)
    grad_w_embed = product_lead(embed_input, grad_stream_r)
    grad_embed_in = product_back(grad_stream_r, w_embed)
    grad_vector_two = pullback(length_plus, vector_two, grad_embed_in[:, D_S:])
    grad_ff_pre = pullback(jax.nn.silu, ff_preact, grad_embed_in[:, :D_S]).astype(BF)
    grad_ff_scalar = product_lead(ff_input, grad_ff_pre)
    grad_ff_input = product_back(grad_ff_pre, ff_scalar)
    grad_ff_update = pullback(vector_gate, ff_update, grad_vector_two).astype(BF)
    grad_ff_up = product_lead(ff_hidden_r, grad_ff_update)
    grad_ff_hidden = (
        product_back(grad_ff_update, ff_up)
        + pullback(length_plus, ff_hidden, grad_ff_input[:, D_S:])
    ).astype(BF)
    grad_ff_vec = product_lead(normed_vr, grad_ff_hidden)
    grad_normed_v = grad_vector_two + product_back(grad_ff_hidden, ff_vec)
    grad_normed_s = grad_embed_in[:, :D_S] + grad_ff_input[:, :D_S]
    unused, norm_pull = jax.vjp(layer_norm, scalar_one, gain_norm)
    grad_scalar_one, grad_norm_gain = norm_pull(grad_normed_s)
    grad_vector_one = pullback(vector_norm, vector_one, grad_normed_v)

    shard = lambda grad: grad.astype(BF).reshape((spaces, grad.shape[0] // spaces) + grad.shape[1:])
    gains = jnp.concatenate(
        [shard(grad_norm_gain), shard(grad_attn_gain), shard(grad_ffn_gain)], 1
    )
    gains = pad_to(pad_to(gains, 512, 1)[:, None, :], 16, 1)
    first_share = jnp.concatenate(
        [
            shard(grad_w_down),
            fold(shard(grad_w_up)),
            fold(shard(grad_w_qkv)),
            shard(grad_w_out),
            shard(grad_w_embed),
            fold(shard(grad_ff_scalar)),
            jnp.concatenate([shard(grad_ff_vec), shard(grad_ff_up)], 2),
            gains,
        ],
        1,
    )
    first_sum = lax.psum_scatter(first_share, "space", scatter_dimension=0, tiled=False)
    first_sum = lax.psum(first_sum, "dp").astype(F32)

    grad_a, grad_mix, grad_b, grad_p, grad_q, grad_vout = edge_backward(
        near_row, ev_col, ev_row, hidden, lx, dsilu, update,
        grad_scalar_one * (1.0 / NEIGH), grad_vector_one * (1.0 / NEIGH), wn_mix, vout, table_count,
    )
    grad_vedge = jnp.sum(grad_p[:, table_count], 0)[:H_V]
    grad_vec_edge = lax.psum(grad_vedge[None, :], ("dp", "space"))
    grad_a_r = grad_a.astype(BF)
    grad_p_r = grad_p[:, :table_count].astype(BF)
    grad_b_r = grad_b.astype(BF)
    grad_q_r = grad_q.astype(BF)
    grad_node_a = product_lead(table_s, grad_a_r)
    grad_node_b = product_lead(node_scalar, grad_b_r)
    grad_vec_a = product_lead(table_v, grad_p_r)
    grad_vec_b = product_lead(node_vector, grad_q_r)
    grad_table_scalar = product_back(grad_a_r, w_node[:, :D_S])
    grad_table_vector = product_back(grad_p_r, vec_source)
    grad_scalar = (
        grad_scalar_one + product_back(grad_b_r, w_node[:, D_S:]) + grad_table_scalar[:local_rows]
    )
    grad_vector = (
        grad_vector_one + product_back(grad_q_r, vec_target) + grad_table_vector[:, :local_rows]
    )
    back = jnp.concatenate(
        [grad_table_scalar[local_rows:]] + [grad_table_vector[c, local_rows:] for c in range(3)], 1
    )
    back = back.astype(BF).reshape(spaces, CAP, D_S + 3 * D_V)
    got = lax.all_to_all(back, "space", split_axis=0, concat_axis=0, tiled=True)
    got = got.reshape(extra_rows, D_S + 3 * D_V)
    got = jnp.where(sent_live[:, None], got, 0)
    added = lax.dot_general(pick, got, (((0,), (0,)), ((), ())), preferred_element_type=F32)
    grad_scalar = grad_scalar + added[:, :D_S]
    grad_vector = grad_vector + jnp.moveaxis(
        added[:, D_S:].reshape(local_rows, 3, D_V), 1, 0
    )

    columns = lambda grad: jnp.moveaxis(
        grad.reshape(grad.shape[0], spaces, grad.shape[1] // spaces), 1, 0
    )
    mix_block = columns(grad_mix.astype(BF))
    mix_width = D_S // spaces
    mix_rows = H_P * mix_width // 512
    second_share = jnp.concatenate(
        [
            fold(shard(grad_node_a)),
            fold(shard(grad_node_b)),
            mix_block.reshape(spaces, mix_rows, 512),
            shard(grad_vec_a)[:, :, :512],
            shard(grad_vec_b)[:, :, :512],
            shard(grad_vout)[:, :, :512],
            jnp.concatenate(
                [
                    shard(grad_vec_a)[:, :, 512:],
                    shard(grad_vec_b)[:, :, 512:],
                    shard(grad_vout)[:, :, 512:],
                    jnp.zeros((spaces, D_V // spaces, 128), BF),
                ],
                2,
            ),
        ],
        1,
    )
    second_sum = lax.psum_scatter(second_share, "space", scatter_dimension=0, tiled=False)
    second_sum = lax.psum(second_sum, "dp").astype(F32)

    def taker(rows_in):
        at = [0]

        def take(rows, cols, blocks=1):
            part = rows_in[at[0] : at[0] + rows * blocks]
            at[0] += rows * blocks
            return unfold(part, rows, cols) if blocks > 1 else part

        return take

    take = taker(first_sum)
    out_down = take(grad_w_down.shape[0] // spaces, 512)
    out_up = take(D_MODEL // spaces, 2048, 4)
    out_qkv = take(D_MODEL // spaces, 1536, 3)
    out_out = take(D_MODEL // spaces, 512)
    out_embed = take((D_S + D_V) // spaces, 512)
    out_ffs = take((D_S + D_V) // spaces, 1024, 2)
    both = take(D_V // spaces, 512)
    out_ffv, out_ffu = both[:, :D_V], both[:, D_V:]
    gain_row = take(16, 512)[0]
    cuts = [D_S // spaces, D_MODEL // spaces, D_MODEL // spaces]
    out_gn = gain_row[: cuts[0]]
    out_ga = gain_row[cuts[0] : cuts[0] + cuts[1]]
    out_gf = gain_row[cuts[0] + cuts[1] : sum(cuts)]
    take = taker(second_sum)
    node_a = take(D_S // spaces, 1024, 2)
    node_b = take(D_S // spaces, 1024, 2)
    mixed = take(mix_rows, 512).reshape(H_P, mix_width)
    vec_a = take(D_V // spaces, 512)
    vec_b = take(D_V // spaces, 512)
    vout_t = take(D_V // spaces, 512)
    tails = take(D_V // spaces, 512)
    out_vec_node = jnp.concatenate([vec_a, tails[:, :1], vec_b, tails[:, 128:129]], 1)
    out_vec_out = jnp.concatenate([vout_t, tails[:, 256:257]], 1).T
    return (
        stream_out,
        grad_scalar.astype(BF),
        grad_vector.astype(BF),
        jnp.concatenate([node_a, node_b], 1),
        mixed[H_V : H_V + D_E],
        mixed[:H_V],
        out_vec_node,
        grad_vec_edge,
        out_vec_out,
        out_gn,
        out_ffv,
        out_ffs,
        out_ffu,
        out_embed,
        out_ga,
        out_qkv,
        out_out,
        out_gf,
        out_up,
        out_down,
    )


def solution(mesh):
    rows = P(("dp", "space"), None)
    component = P(None, ("dp", "space"), None)
    return jax.shard_map(
        body,
        mesh=mesh,
        in_specs=(
            rows, component, rows, P(None, ("dp", "space")), rows,
            P(("dp", "space"), None, None), P("dp"), rows,
        ) + (P(),) * 17,
        out_specs=(
            rows, rows, component, P("space", None), P(None, "space"), P(None, "space"),
            P("space", None), P(), P(None, "space"), P("space"), P("space", None),
            P("space", None), P("space", None), P("space", None), P("space"), P("space", None),
            P("space", None), P("space"), P("space", None), P("space", None),
        ),
        check_vma=False,
    )
```

```python
import functools
import math

import jax
import jax.numpy as jnp
from jax import lax
from jax.experimental import pallas as pl
from jax.experimental.pallas import tpu as pltpu
from jax.sharding import PartitionSpec as P

D_S = 1024
D_V = 256
H_V = 513
H_P = 640
D_E = 32
NEIGH = 30
D_MODEL = 512
HEADS = 8
HEAD_DIM = 64
CAP = 16
GROUP = 5
VMEM_LIMIT = 60 * 1024 * 1024

MESH = pl.DeviceIdType.MESH
BF = jnp.bfloat16
F32 = jnp.float32


def layer_norm(values, gain_row):
    centred = values - jnp.mean(values, axis=-1, keepdims=True)
    spread = jnp.mean(centred * centred, axis=-1, keepdims=True)
    return centred * lax.rsqrt(spread + 1e-05) * gain_row


def vector_norm(vectors):
    mean_power = jnp.mean(jnp.sum(vectors * vectors, axis=0), axis=-1, keepdims=True)
    return vectors * lax.rsqrt(mean_power + 1e-05)[None]


def length_plus(vectors):
    return jnp.sqrt(jnp.sum(vectors * vectors, axis=0) + 1.0)


def vector_gate(vectors):
    return vectors * jax.nn.sigmoid(length_plus(vectors))[None]


def gelu_exact(values):
    return jax.nn.gelu(values, approximate=False)


def product(former, latter):
    return jnp.dot(former, latter, preferred_element_type=F32)


def product_lead(former, latter):
    leading = tuple(range(former.ndim - 1))
    return lax.dot_general(
        former, latter, ((leading, leading), ((), ())), preferred_element_type=F32
    )


def product_back(former, latter):
    return lax.dot_general(
        former, latter, (((former.ndim - 1,), (1,)), ((), ())), preferred_element_type=F32
    )


def pullback(function, at_point, cotangent_in):
    unused, puller = jax.vjp(function, at_point)
    return puller(cotangent_in)[0]


def sigmoid(values):
    return 0.5 * jnp.tanh(0.5 * values) + 0.5


LANE_BLOCKS = ((0, 256), (256, 256), (512, 128))
ROW_TILE = 64


def edge_forward_kernel(
    near_ref, es_ref, ev_ref, a_ref, b_ref, p_ref, q_ref, ve_ref, vo_ref,
    aggs_ref, aggv_ref, h_ref, lx_ref, ds_ref, z_ref, x_scr,
):
    nodes = b_ref.shape[0]
    table = p_ref.shape[1]
    rows = GROUP * nodes
    idx = near_ref[...].reshape(rows, 1)
    x_scr[:, :table] = (idx == lax.broadcasted_iota(jnp.int32, (rows, table), 1)).astype(BF)
    one_hot = x_scr[:, :table]
    for start, width in LANE_BLOCKS:
        cols = pl.ds(start, width)
        gathered = [product(one_hot, p_ref[c, :, cols]) for c in range(3)]
        for k in range(GROUP):
            for first in range(0, nodes, ROW_TILE):
                at = k * nodes + first
                evk = ev_ref[k, pl.ds(first, ROW_TILE), :]
                total = None
                for c in range(3):
                    h = (
                        gathered[c][at : at + ROW_TILE]
                        + q_ref[c, pl.ds(first, ROW_TILE), cols]
                        + evk[:, c : c + 1] * ve_ref[:, cols]
                    )
                    h_ref[k, c, pl.ds(first, ROW_TILE), cols] = h.astype(BF)
                    total = h * h + 1.0 if total is None else total + h * h
                length = total * lax.rsqrt(total)
                if start == 512:
                    lane = lax.broadcasted_iota(jnp.int32, (ROW_TILE, width), 1)
                    length = jnp.where(
                        lane == 0, length, es_ref[k, pl.ds(first, ROW_TILE), :].astype(F32)
                    )
                length = length.astype(BF)
                x_scr[pl.ds(at, ROW_TILE), pl.ds(table + start, width)] = length
                lx_ref[k, pl.ds(first, ROW_TILE), cols] = length

    @pl.when(pl.program_id(0) == 0)
    def _():
        aggs_ref[...] = jnp.zeros_like(aggs_ref)
        aggv_ref[...] = jnp.zeros_like(aggv_ref)

    full = x_scr[...]
    for start in range(0, D_S, 256):
        cols = pl.ds(start, 256)
        pre = product(full, a_ref[:, cols])
        for first in range(0, nodes, ROW_TILE):
            part = pl.ds(first, ROW_TILE)
            acc = None
            for k in range(GROUP):
                at = k * nodes + first
                x = pre[at : at + ROW_TILE] + b_ref[part, cols]
                s = sigmoid(x)
                y = x * s
                ds_ref[k, part, cols] = (s + y * (1.0 - s)).astype(BF)
                acc = y if acc is None else acc + y
            aggs_ref[part, cols] += acc * (1.0 / NEIGH)
    ups = [
        product(h_ref[:, c, :, :].reshape(rows, H_P), vo_ref[...]) for c in range(3)
    ]
    for first in range(0, nodes, ROW_TILE):
        part = pl.ds(first, ROW_TILE)
        acc = [None] * 3
        for k in range(GROUP):
            at = k * nodes + first
            z = [ups[c][at : at + ROW_TILE] for c in range(3)]
            power = z[0] * z[0] + z[1] * z[1] + z[2] * z[2] + 1.0
            s = sigmoid(power * lax.rsqrt(power))
            for c in range(3):
                z_ref[k, c, part, :] = z[c].astype(BF)
                gated = z[c] * s
                acc[c] = gated if acc[c] is None else acc[c] + gated
        for c in range(3):
            aggv_ref[c, part, :] += acc[c] * (1.0 / NEIGH)


def edge_forward(near_col, es_pad, ev_col, mix, b_target, p_source, q_target, ve_row, vout):
    nodes = b_target.shape[0]
    table = p_source.shape[1]
    whole = lambda shape: pl.BlockSpec(shape, lambda g: (0,) * len(shape))
    slots = lambda *shape: pl.BlockSpec((GROUP,) + shape, lambda g: (g,) + (0,) * len(shape))
    return pl.pallas_call(
        edge_forward_kernel,
        grid=(NEIGH // GROUP,),
        in_specs=[
            slots(nodes, 1),
            slots(nodes, 128),
            slots(nodes, 3),
            whole((table + H_P, D_S)),
            whole((nodes, D_S)),
            whole((3, table, H_P)),
            whole((3, nodes, H_P)),
            whole((1, H_P)),
            whole((H_P, D_V)),
        ],
        out_specs=[
            whole((nodes, D_S)),
            whole((3, nodes, D_V)),
            slots(3, nodes, H_P),
            slots(nodes, H_P),
            slots(nodes, D_S),
            slots(3, nodes, D_V),
        ],
        out_shape=[
            jax.ShapeDtypeStruct((nodes, D_S), F32),
            jax.ShapeDtypeStruct((3, nodes, D_V), F32),
            jax.ShapeDtypeStruct((NEIGH, 3, nodes, H_P), BF),
            jax.ShapeDtypeStruct((NEIGH, nodes, H_P), BF),
            jax.ShapeDtypeStruct((NEIGH, nodes, D_S), BF),
            jax.ShapeDtypeStruct((NEIGH, 3, nodes, D_V), BF),
        ],
        scratch_shapes=[pltpu.VMEM((GROUP * nodes, table + H_P), BF)],
        compiler_params=pltpu.CompilerParams(vmem_limit_bytes=VMEM_LIMIT),
        name="edge_forward",
    )(near_col, es_pad, ev_col, mix, b_target, p_source, q_target, ve_row, vout)


def edge_backward_kernel(
    near_ref, ev_ref, evr_ref, h_ref, lx_ref, ds_ref, z_ref, gs_ref, gv_ref, wn_ref, vo_ref,
    ga_ref, gw_ref, gb_ref, gp_ref, gq_ref, gvo_ref, pre_scr, up_scr, gh_scr,
):
    nodes = gs_ref.shape[0]
    table = ga_ref.shape[0]
    rows = GROUP * nodes

    @pl.when(pl.program_id(0) == 0)
    def _():
        for ref in (ga_ref, gw_ref, gb_ref, gp_ref, gq_ref, gvo_ref):
            ref[...] = jnp.zeros_like(ref)

    for start in range(0, D_S, 256):
        cols = pl.ds(start, 256)
        for first in range(0, nodes, ROW_TILE):
            part = pl.ds(first, ROW_TILE)
            share = gs_ref[part, cols]
            acc = None
            for k in range(GROUP):
                g = (ds_ref[k, part, cols].astype(F32) * share).astype(BF)
                pre_scr[pl.ds(k * nodes + first, ROW_TILE), cols] = g
                g = g.astype(F32)
                acc = g if acc is None else acc + g
            gb_ref[part, cols] += acc
    for first in range(0, nodes, ROW_TILE):
        part = pl.ds(first, ROW_TILE)
        share = [gv_ref[c, part, :] for c in range(3)]
        for k in range(GROUP):
            z = [z_ref[k, c, part, :].astype(F32) for c in range(3)]
            power = z[0] * z[0] + z[1] * z[1] + z[2] * z[2] + 1.0
            inverse = lax.rsqrt(power)
            s = sigmoid(power * inverse)
            dot = z[0] * share[0] + z[1] * share[1] + z[2] * share[2]
            factor = dot * inverse * (s * (1.0 - s))
            for c in range(3):
                up_scr[c, pl.ds(k * nodes + first, ROW_TILE), :] = (
                    share[c] * s + z[c] * factor
                ).astype(BF)

    near = near_ref[0]
    one_hot = (lax.broadcasted_iota(jnp.int32, (table, rows), 0) == near).astype(BF)
    grad_pre = pre_scr[...]
    ga_ref[...] += product(one_hot, grad_pre)
    lx = lx_ref[...].reshape(rows, H_P)
    gw_ref[...] += lax.dot_general(
        lx, grad_pre, (((0,), (0,)), ((), ())), preferred_element_type=F32
    )
    for start, width in LANE_BLOCKS:
        cols = pl.ds(start, width)
        grad_length = product_back(grad_pre, wn_ref[cols, :])
        grad_direct = [product_back(up_scr[c], vo_ref[cols, :]) for c in range(3)]
        for first in range(0, nodes, ROW_TILE):
            part = pl.ds(first, ROW_TILE)
            acc = [None] * 3
            for k in range(GROUP):
                at = k * nodes + first
                ratio = grad_length[at : at + ROW_TILE] * pl.reciprocal(
                    lx_ref[k, part, cols].astype(F32), approx=True
                )
                if start == 512:
                    lane = lax.broadcasted_iota(jnp.int32, (ROW_TILE, width), 1)
                    ratio = jnp.where(lane == 0, ratio, 0.0)
                for c in range(3):
                    g = grad_direct[c][at : at + ROW_TILE] + ratio * h_ref[
                        k, c, part, cols
                    ].astype(F32)
                    gh_scr[c, pl.ds(at, ROW_TILE), cols] = g.astype(BF)
                    acc[c] = g if acc[c] is None else acc[c] + g
            for c in range(3):
                gq_ref[c, part, cols] += acc[c]
    for c in range(3):
        evr = jnp.broadcast_to(evr_ref[0, c : c + 1, :], (16, rows))
        lead = jnp.concatenate([one_hot, evr.astype(BF)], axis=0)
        gp_ref[c] += product(lead, gh_scr[c])
        gvo_ref[...] += lax.dot_general(
            up_scr[c],
            h_ref[:, c, :, :].reshape(rows, H_P),
            (((0,), (0,)), ((), ())),
            preferred_element_type=F32,
        )


def edge_backward(near_row, ev_col, ev_row, hidden, lx, dsilu, update, gs, gv, wn, vout, table):
    nodes = gs.shape[0]
    rows = GROUP * nodes
    whole = lambda shape: pl.BlockSpec(shape, lambda g: (0,) * len(shape))
    slots = lambda *shape: pl.BlockSpec((GROUP,) + shape, lambda g: (g,) + (0,) * len(shape))
    steps = lambda *shape: pl.BlockSpec((1,) + shape, lambda g: (g,) + (0,) * len(shape))
    outs = [
        (table, D_S),
        (H_P, D_S),
        (nodes, D_S),
        (3, table + 16, H_P),
        (3, nodes, H_P),
        (D_V, H_P),
    ]
    return pl.pallas_call(
        edge_backward_kernel,
        grid=(NEIGH // GROUP,),
        in_specs=[
            steps(1, rows),
            slots(nodes, 3),
            steps(3, rows),
            slots(3, nodes, H_P),
            slots(nodes, H_P),
            slots(nodes, D_S),
            slots(3, nodes, D_V),
            whole((nodes, D_S)),
            whole((3, nodes, D_V)),
            whole((H_P, D_S)),
            whole((H_P, D_V)),
        ],
        out_specs=[whole(shape) for shape in outs],
        out_shape=[jax.ShapeDtypeStruct(shape, F32) for shape in outs],
        scratch_shapes=[
            pltpu.VMEM((rows, D_S), BF),
            pltpu.VMEM((3, rows, D_V), BF),
            pltpu.VMEM((3, rows, H_P), BF),
        ],
        compiler_params=pltpu.CompilerParams(vmem_limit_bytes=VMEM_LIMIT),
        name="edge_backward",
    )(near_row, ev_col, ev_row, hidden, lx, dsilu, update, gs, gv, wn, vout)


def skip_refs(kernel, first, count):
    def wrapped(*refs):
        return kernel(*refs[:first], *refs[first + count :])

    return wrapped


def scalar_backward_kernel(
    shards, near_ref, lx_ref, ds_ref, gsone_ref, wn_ref, ts_ref, ns_ref, wnode_ref,
    ratio_ref, pack_ref, rest_ref, gscal_ref, back_ref, ga_ref, gw_ref, gb_ref, pre_scr,
):
    nodes = gsone_ref.shape[0]
    table = ts_ref.shape[0]
    rows = GROUP * nodes

    @pl.when(pl.program_id(0) == 0)
    def _():
        for ref in (ga_ref, gw_ref, gb_ref):
            ref[...] = jnp.zeros_like(ref)

    for start in range(0, D_S, 256):
        cols = pl.ds(start, 256)
        for first in range(0, nodes, ROW_TILE):
            part = pl.ds(first, ROW_TILE)
            share = gsone_ref[part, cols] * (1.0 / NEIGH)
            acc = None
            for k in range(GROUP):
                g = (ds_ref[k, part, cols].astype(F32) * share).astype(BF)
                pre_scr[pl.ds(k * nodes + first, ROW_TILE), cols] = g
                g = g.astype(F32)
                acc = g if acc is None else acc + g
            gb_ref[part, cols] += acc
    one_hot = (lax.broadcasted_iota(jnp.int32, (table, rows), 0) == near_ref[0]).astype(BF)
    grad_pre = pre_scr[...]
    ga_ref[...] += product(one_hot, grad_pre)
    lx = lx_ref[...].reshape(rows, H_P)
    gw_ref[...] += lax.dot_general(
        lx, grad_pre, (((0,), (0,)), ((), ())), preferred_element_type=F32
    )
    for start, width in LANE_BLOCKS:
        cols = pl.ds(start, width)
        grad_length = product_back(grad_pre, wn_ref[cols, :])
        for first in range(0, nodes, ROW_TILE):
            part = pl.ds(first, ROW_TILE)
            for k in range(GROUP):
                at = k * nodes + first
                ratio = grad_length[at : at + ROW_TILE] * pl.reciprocal(
                    lx_ref[k, part, cols].astype(F32), approx=True
                )
                if start == 512:
                    lane = lax.broadcasted_iota(jnp.int32, (ROW_TILE, width), 1)
                    ratio = jnp.where(lane == 0, ratio, 0.0)
                ratio_ref[k, part, cols] = ratio.astype(BF)

    @pl.when(pl.program_id(0) == pl.num_programs(0) - 1)
    def _():
        ga = ga_ref[...].astype(BF)
        gb = gb_ref[...].astype(BF)
        tall = D_S // shards
        for half, (left, right) in enumerate(((ts_ref, ga), (ns_ref, gb))):
            for start in range(0, D_S, 512):
                block = lax.dot_general(
                    left[...], right[:, start : start + 512], (((0,), (0,)), ((), ())),
                    preferred_element_type=F32,
                ).astype(BF)
                at = (half * (D_S // 512) + start // 512) * tall
                for p in range(shards):
                    pack_ref[p, pl.ds(at, tall), :] = block[p * tall : (p + 1) * tall]
        base = 2 * (D_S // 512) * tall
        for p in range(shards):
            own = pl.ds(p * tall, tall)
            for r in range(4):
                pack_ref[p, pl.ds(base, 128), pl.ds(r * 128, 128)] = gw_ref[
                    pl.ds(r * 128, 128), own
                ].astype(BF)
            rest_ref[p] = gw_ref[pl.ds(512, 64), own].astype(BF)
        own_part = gsone_ref[...] + product_back(gb, wnode_ref[:, pl.ds(D_S, D_S)])
        projected = product_back(ga, wnode_ref[:, pl.ds(0, D_S)])
        gscal_ref[...] = own_part + projected[:nodes]
        back_ref[...] = projected[nodes:].astype(BF)


def scalar_backward(shards, near_row, lx, dsilu, gsone, wn, table_s, node_scalar, w_node, *before):
    nodes = gsone.shape[0]
    table = table_s.shape[0]
    rows = GROUP * nodes
    whole = lambda shape: pl.BlockSpec(shape, lambda g: (0,) * len(shape))
    slots = lambda *shape: pl.BlockSpec((GROUP,) + shape, lambda g: (g,) + (0,) * len(shape))
    steps = lambda *shape: pl.BlockSpec((1,) + shape, lambda g: (g,) + (0,) * len(shape))
    pack_rows = 2 * (D_S // 512) * (D_S // shards) + 128
    outs = [
        ((shards, pack_rows, 512), BF),
        ((shards, 64, D_S // shards), BF),
        ((nodes, D_S), F32),
        ((table - nodes, D_S), BF),
    ]
    return pl.pallas_call(
        skip_refs(functools.partial(scalar_backward_kernel, shards), 8, len(before)),
        grid=(NEIGH // GROUP,),
        in_specs=[
            steps(1, rows),
            slots(nodes, H_P),
            slots(nodes, D_S),
            whole((nodes, D_S)),
            whole((H_P, D_S)),
            whole((table, D_S)),
            whole((nodes, D_S)),
            whole((D_S, 2 * D_S)),
        ]
        + [pl.BlockSpec(memory_space=pl.ANY)] * len(before),
        out_specs=[slots(nodes, H_P)] + [whole(shape) for shape, kind in outs],
        out_shape=[jax.ShapeDtypeStruct((NEIGH, nodes, H_P), BF)]
        + [jax.ShapeDtypeStruct(shape, kind) for shape, kind in outs],
        scratch_shapes=[
            pltpu.VMEM((table, D_S), F32),
            pltpu.VMEM((H_P, D_S), F32),
            pltpu.VMEM((nodes, D_S), F32),
            pltpu.VMEM((rows, D_S), BF),
        ],
        compiler_params=pltpu.CompilerParams(vmem_limit_bytes=VMEM_LIMIT),
        cost_estimate=pl.CostEstimate(
            flops=2 * NEIGH * nodes * D_S * (table + 2 * H_P), bytes_accessed=30 << 20,
            transcendentals=NEIGH * nodes * H_P,
        ),
        name="scalar_backward",
    )(near_row, lx, dsilu, gsone, wn, table_s, node_scalar, w_node, *before)


def vector_backward_kernel(
    shards, near_ref, ev_ref, evr_ref, h_ref, ratio_ref, z_ref, gvone_ref, vo_ref, tv_ref,
    nv_ref, vs_ref, vt_ref, rest_ref, gains_ref,
    pack_ref, gvec_ref, back_ref, gp_ref, gq_ref, gvo_ref, up_scr, gh_scr,
):
    nodes = gvone_ref.shape[1]
    table = tv_ref.shape[1]
    rows = GROUP * nodes

    @pl.when(pl.program_id(0) == 0)
    def _():
        for ref in (gp_ref, gq_ref, gvo_ref):
            ref[...] = jnp.zeros_like(ref)

    for first in range(0, nodes, ROW_TILE):
        part = pl.ds(first, ROW_TILE)
        share = [gvone_ref[c, part, :] * (1.0 / NEIGH) for c in range(3)]
        for k in range(GROUP):
            z = [z_ref[k, c, part, :].astype(F32) for c in range(3)]
            power = z[0] * z[0] + z[1] * z[1] + z[2] * z[2] + 1.0
            inverse = lax.rsqrt(power)
            s = sigmoid(power * inverse)
            dot = z[0] * share[0] + z[1] * share[1] + z[2] * share[2]
            factor = dot * inverse * (s * (1.0 - s))
            for c in range(3):
                up_scr[c, pl.ds(k * nodes + first, ROW_TILE), :] = (
                    share[c] * s + z[c] * factor
                ).astype(BF)
    for start, width in LANE_BLOCKS:
        cols = pl.ds(start, width)
        grad_direct = [product_back(up_scr[c], vo_ref[cols, :]) for c in range(3)]
        for first in range(0, nodes, ROW_TILE):
            part = pl.ds(first, ROW_TILE)
            acc = [None] * 3
            for k in range(GROUP):
                at = k * nodes + first
                ratio = ratio_ref[k, part, cols].astype(F32)
                for c in range(3):
                    g = grad_direct[c][at : at + ROW_TILE] + ratio * h_ref[
                        k, c, part, cols
                    ].astype(F32)
                    gh_scr[c, pl.ds(at, ROW_TILE), cols] = g.astype(BF)
                    acc[c] = g if acc[c] is None else acc[c] + g
            for c in range(3):
                gq_ref[c, part, cols] += acc[c]
    one_hot = (lax.broadcasted_iota(jnp.int32, (table, rows), 0) == near_ref[0]).astype(BF)
    for c in range(3):
        evr = jnp.broadcast_to(evr_ref[0, c : c + 1, :], (16, rows))
        lead = jnp.concatenate([one_hot, evr.astype(BF)], axis=0)
        gp_ref[c] += product(lead, gh_scr[c])
        gvo_ref[...] += lax.dot_general(
            up_scr[c],
            h_ref[:, c, :, :].reshape(rows, H_P),
            (((0,), (0,)), ((), ())),
            preferred_element_type=F32,
        )

    @pl.when(pl.program_id(0) == pl.num_programs(0) - 1)
    def _():
        tall = D_V // shards
        grads = []
        gp = [gp_ref[c, pl.ds(0, table), :].astype(BF) for c in range(3)]
        gq = [gq_ref[c].astype(BF) for c in range(3)]
        for lead_ref, right in ((tv_ref, gp), (nv_ref, gq)):
            total = None
            for c in range(3):
                one = lax.dot_general(
                    lead_ref[c], right[c], (((0,), (0,)), ((), ())), preferred_element_type=F32
                )
                total = one if total is None else total + one
            grads.append(total)
        grads.append(gvo_ref[...])
        lane = lax.broadcasted_iota(jnp.int32, (D_V, 128), 1)
        tails = jnp.zeros((D_V, 128), F32)
        for n, grad in enumerate(grads):
            for p in range(shards):
                pack_ref[p, pl.ds(n * tall, tall), :] = grad[
                    p * tall : (p + 1) * tall, :512
                ].astype(BF)
            tails = tails + jnp.where(
                lane == n, jnp.broadcast_to(grad[:, 512:513], (D_V, 128)), 0.0
            )
        tails = tails.astype(BF)
        vedge = gp_ref[0, pl.ds(table, 8), :] + gp_ref[1, pl.ds(table, 8), :]
        vedge = vedge + gp_ref[2, pl.ds(table, 8), :]
        row = lax.broadcasted_iota(jnp.int32, (tall, 128), 0)
        for p in range(shards):
            at = pl.ds(3 * tall, tall)
            rest = rest_ref[p].astype(F32)
            pack_ref[p, at, pl.ds(0, 128)] = tails[p * tall : (p + 1) * tall]
            pack_ref[p, at, pl.ds(128, 128)] = rest[1 : 1 + tall].astype(BF)
            extra = jnp.where(row == 0, jnp.broadcast_to(rest[0:1], (tall, 128)), 0.0)
            for n in range(5):
                piece = jnp.broadcast_to(vedge[0:1, n * 128 : (n + 1) * 128], (tall, 128))
                extra = jnp.where(row == 1 + n, piece, extra)
            for n in range(2):
                piece = jnp.broadcast_to(gains_ref[n : n + 1, p * 128 : (p + 1) * 128], (tall, 128))
                extra = jnp.where(row == 6 + n, piece, extra)
            pack_ref[p, at, pl.ds(256, 128)] = extra.astype(BF)
            pack_ref[p, at, pl.ds(384, 128)] = jnp.zeros((tall, 128), BF)
        for c in range(3):
            projected = product_back(gp[c], vs_ref[...])
            gvec_ref[c] = (
                gvone_ref[c] + product_back(gq[c], vt_ref[...]) + projected[:nodes]
            )
            back_ref[:, pl.ds(c * D_V, D_V)] = projected[nodes:].astype(BF)


def vector_backward(
    shards, near_row, ev_col, ev_row, hidden, ratio, update, gvone, vout, table_v, node_vector,
    vec_source, vec_target, rest, gains, *before,
):
    nodes = gvone.shape[1]
    table = table_v.shape[1]
    rows = GROUP * nodes
    whole = lambda shape: pl.BlockSpec(shape, lambda g: (0,) * len(shape))
    slots = lambda *shape: pl.BlockSpec((GROUP,) + shape, lambda g: (g,) + (0,) * len(shape))
    steps = lambda *shape: pl.BlockSpec((1,) + shape, lambda g: (g,) + (0,) * len(shape))
    outs = [
        ((shards, 4 * (D_V // shards), 512), BF),
        ((3, nodes, D_V), F32),
        ((table - nodes, 3 * D_V), BF),
    ]
    return pl.pallas_call(
        skip_refs(functools.partial(vector_backward_kernel, shards), 14, len(before)),
        grid=(NEIGH // GROUP,),
        in_specs=[
            steps(1, rows),
            slots(nodes, 3),
            steps(3, rows),
            slots(3, nodes, H_P),
            slots(nodes, H_P),
            slots(3, nodes, D_V),
            whole((3, nodes, D_V)),
            whole((H_P, D_V)),
            whole((3, table, D_V)),
            whole((3, nodes, D_V)),
            whole((D_V, H_P)),
            whole((D_V, H_P)),
            whole((shards, 64, D_S // shards)),
            whole((8, D_S)),
        ]
        + [pl.BlockSpec(memory_space=pl.ANY)] * len(before),
        out_specs=[whole(shape) for shape, kind in outs],
        out_shape=[jax.ShapeDtypeStruct(shape, kind) for shape, kind in outs],
        scratch_shapes=[
            pltpu.VMEM((3, table + 16, H_P), F32),
            pltpu.VMEM((3, nodes, H_P), F32),
            pltpu.VMEM((D_V, H_P), F32),
            pltpu.VMEM((3, rows, D_V), BF),
            pltpu.VMEM((3, rows, H_P), BF),
        ],
        compiler_params=pltpu.CompilerParams(vmem_limit_bytes=VMEM_LIMIT),
        cost_estimate=pl.CostEstimate(
            flops=2 * NEIGH * nodes * 3 * H_P * (table + 2 * D_V), bytes_accessed=30 << 20,
            transcendentals=NEIGH * nodes * D_V,
        ),
        name="vector_backward",
    )(
        near_row, ev_col, ev_row, hidden, ratio, update, gvone, vout, table_v, node_vector,
        vec_source, vec_target, rest, gains, *before,
    )


def flip(count, bit):
    return [(i, i ^ bit) for i in range(count)]


def own_index():
    space = lax.axis_index("space")
    dp = lax.axis_index("dp")
    return {"core": space % 2, "z_lo": space // 2 % 2, "z_hi": space // 4, "x": dp % 2, "y": dp // 2}


STEP_OF = {
    "core": ("space", 8, 1), "z_lo": ("space", 8, 2), "z_hi": ("space", 8, 4),
    "x": ("dp", 4, 1), "y": ("dp", 4, 2),
}


def swap(values, way):
    axis, count, bit = STEP_OF[way]
    return lax.ppermute(values, axis, flip(count, bit))


def halve(values, way, dim):
    mine = own_index()[way]
    away = lax.dynamic_index_in_dim(values, 1 - mine, dim, False)
    kept = lax.dynamic_index_in_dim(values, mine, dim, False)
    return (kept.astype(F32) + swap(away, way).astype(F32)).astype(BF)


def reduce_core(packed):
    shards, rows, width = packed.shape
    return halve(packed.reshape(shards // 2, 2, rows, width), "core", 1)


def reduce_first(values):
    quads, rows, width = values.shape
    parts = values.reshape(quads, 2, 2, rows // 4, width)
    return halve(parts[:, 0], "x", 1), halve(parts[:, 1], "y", 1)


def reduce_second(pair):
    quads, rows, width = pair[0].shape
    shape = (quads, 2, rows // 2, width)
    return halve(pair[0].reshape(shape), "y", 1), halve(pair[1].reshape(shape), "x", 1)


def reduce_z(values):
    quads, rows, width = values.shape
    values = halve(values.reshape(2, 2, rows, width), "z_lo", 1)
    return halve(values, "z_hi", 0)


def join(values, way, axis=0):
    other = swap(values, way)
    mine = own_index()[way]
    return jnp.stack([jnp.where(mine == 0, values, other), jnp.where(mine == 0, other, values)], axis)


def gather_plane(first, second):
    first = join(join(first, "y"), "x")
    second = join(join(second, "x"), "y")
    return jnp.concatenate([first.reshape(-1, 512), second.reshape(-1, 512)], 0)


def full_block(shape):
    return pl.BlockSpec(shape, lambda: (0,) * len(shape))


def lead_product(former, latter):
    return lax.dot_general(
        former, latter, (((0,), (0,)), ((), ())), preferred_element_type=F32
    )


def swap_halves(values):
    return pltpu.roll(values, 64, 1)


def lower_half(shape):
    return lax.broadcasted_iota(jnp.int32, shape, 1) < 64


def pack_tall(tile, odd):
    rows = tile.shape[0] // 2
    top, low = tile[:rows], tile[rows:]
    side = lower_half((rows, 128))
    if odd:
        return jnp.where(side, swap_halves(top), low)
    return jnp.where(side, top, swap_halves(low))


def unpack_tall(block):
    rows = block.shape[0]
    side = lower_half((rows, 128))
    return jnp.concatenate(
        [jnp.where(side, block, 0.0), jnp.where(side, swap_halves(block), 0.0)], 0
    )


def centre(values):
    centred = values - jnp.mean(values, axis=-1, keepdims=True)
    inverse = lax.rsqrt(jnp.mean(centred * centred, axis=-1, keepdims=True) + 1e-05)
    return centred * inverse, inverse


def centre_back(hat, inverse, grad):
    return inverse * (
        grad
        - jnp.mean(grad, axis=-1, keepdims=True)
        - hat * jnp.mean(grad * hat, axis=-1, keepdims=True)
    )


def power_of(parts):
    return parts[0] * parts[0] + parts[1] * parts[1] + parts[2] * parts[2]


def node_forward_kernel(
    ns_ref, nv_ref, as_ref, av_ref, ng_ref, fv_ref, fs_ref, fu_ref, we_ref, ag_ref, wq_ref,
    s1_ref, v1_ref, ffin_ref, ffh_ref, ffp_ref, ffu_ref, v2_ref, emb_ref, sz_ref, ain_ref, out_ref,
):
    nodes = ns_ref.shape[0]
    s1 = ns_ref[...].astype(F32) + as_ref[...]
    s1_ref[...] = s1
    hat, unused = centre(s1)
    normed_s = hat * ng_ref[...]
    v1 = [nv_ref[c].astype(F32) + av_ref[c] for c in range(3)]
    scale = lax.rsqrt(jnp.mean(power_of(v1), axis=-1, keepdims=True) + 1e-05)
    normed_v = [v * scale for v in v1]
    ffh = [product(v.astype(BF), fv_ref[...]) for v in normed_v]
    power = power_of(ffh) + 1.0
    ffin_ref[:, pl.ds(0, D_S)] = normed_s.astype(BF)
    ffin_ref[:, pl.ds(D_S, D_V)] = (power * lax.rsqrt(power)).astype(BF)
    ffp = product(ffin_ref[...], fs_ref[...])
    ffu = [product(h.astype(BF), fu_ref[...]) for h in ffh]
    for c in range(3):
        v1_ref[c] = v1[c]
        ffh_ref[c] = ffh[c]
        ffu_ref[c] = ffu[c]
    ffp_ref[...] = ffp
    s2 = normed_s + ffp * sigmoid(ffp)
    power = power_of(ffu) + 1.0
    gate = sigmoid(power * lax.rsqrt(power))
    v2 = [normed_v[c] + ffu[c] * gate for c in range(3)]
    for c in range(3):
        v2_ref[c] = v2[c]
    power = power_of(v2) + 1.0
    emb_ref[:, pl.ds(0, D_S)] = s2.astype(BF)
    emb_ref[:, pl.ds(D_S, D_V)] = (power * lax.rsqrt(power)).astype(BF)
    sz = product(emb_ref[...], we_ref[...])
    sz_ref[...] = sz
    hat, unused = centre(sz)
    attn_in = (hat * ag_ref[...]).astype(BF)
    ain_ref[...] = attn_in
    q, k, v = [product(attn_in, wq_ref[:, pl.ds(n * D_MODEL, D_MODEL)]) for n in range(3)]
    pack_heads(q, k, v, out_ref)


def pack_heads(q, k, v, out_ref):
    nodes = q.shape[0]
    side = lower_half((nodes, 128))
    for pair in range(HEADS // 2):
        cols = slice(pair * 128, pair * 128 + 128)
        qp, kp, vp = q[:, cols], k[:, cols], v[:, cols]
        even = jnp.where(side, qp, swap_halves(kp))
        odd = jnp.where(side, swap_halves(qp), kp)
        for n, block in enumerate((even, odd)):
            head = 2 * pair + n
            out_ref[head, pl.ds(0, nodes), :] = block.astype(BF)
            out_ref[head, pl.ds(nodes, nodes // 2), :] = pack_tall(vp, n == 1).astype(BF)


def node_forward(node_scalar, node_vector, agg_s, agg_v, *weights):
    nodes = node_scalar.shape[0]
    outs = [
        ((nodes, D_S), F32),
        ((3, nodes, D_V), F32),
        ((nodes, D_S + D_V), BF),
        ((3, nodes, D_V), F32),
        ((nodes, D_S), F32),
        ((3, nodes, D_V), F32),
        ((3, nodes, D_V), F32),
        ((nodes, D_S + D_V), BF),
        ((nodes, D_MODEL), F32),
        ((nodes, D_MODEL), BF),
        ((HEADS, nodes + nodes // 2, 128), BF),
    ]
    return pl.pallas_call(
        node_forward_kernel,
        out_shape=[jax.ShapeDtypeStruct(shape, kind) for shape, kind in outs],
        compiler_params=pltpu.CompilerParams(vmem_limit_bytes=VMEM_LIMIT),
        name="node_forward",
    )(node_scalar, node_vector, agg_s, agg_v, *weights)


def exchange_kernel(spaces, x_ref, y_ref, send_sem, recv_sem, own_sem):
    me = lax.axis_index("space")
    barrier = pltpu.get_barrier_semaphore()
    peers = [lax.rem(me + d, spaces) for d in range(1, spaces)]
    for peer in peers:
        pl.semaphore_signal(barrier, inc=1, device_id={"space": peer}, device_id_type=MESH)
    own = pltpu.make_async_copy(x_ref.at[me], y_ref.at[me], own_sem)
    own.start()
    pl.semaphore_wait(barrier, spaces - 1)
    copies = []
    for n, peer in enumerate(peers):
        copies.append(
            pltpu.make_async_remote_copy(
                src_ref=x_ref.at[peer],
                dst_ref=y_ref.at[me],
                send_sem=send_sem.at[n],
                recv_sem=recv_sem.at[n],
                device_id={"space": peer},
                device_id_type=MESH,
            )
        )
        copies[-1].start()
    own.wait()
    for copy in copies:
        copy.wait()


def exchange(values, collective_id):
    spaces = values.shape[0]
    return pl.pallas_call(
        functools.partial(exchange_kernel, spaces),
        out_shape=jax.ShapeDtypeStruct(values.shape, values.dtype),
        in_specs=[pl.BlockSpec(memory_space=pl.ANY)],
        out_specs=pl.BlockSpec(memory_space=pl.ANY),
        scratch_shapes=[
            pltpu.SemaphoreType.DMA((spaces - 1,)),
            pltpu.SemaphoreType.DMA((spaces - 1,)),
            pltpu.SemaphoreType.DMA,
        ],
        compiler_params=pltpu.CompilerParams(collective_id=collective_id, has_side_effects=True),
        name="exchange",
    )(values)


def split_heads(x_ref, nodes):
    spaces = x_ref.shape[0]
    both = x_ref[:, pl.ds(0, nodes), :].reshape(spaces * nodes, 128).astype(F32)
    queries = jnp.where(lower_half(both.shape), both, 0.0).astype(BF)
    keys = swap_halves(both).astype(BF)
    values = jnp.concatenate(
        [unpack_tall(x_ref[d, pl.ds(nodes, nodes // 2), :].astype(F32)) for d in range(spaces)], 0
    ).astype(BF)
    return queries, keys, values


def attend_kernel(x_ref, id_ref, probs_ref, att_ref, out_ref):
    spaces = x_ref.shape[0]
    nodes = x_ref.shape[1] * 2 // 3
    count = spaces * nodes
    queries, keys, values = split_heads(x_ref, nodes)
    row_ids = id_ref[...]
    column_ids = jnp.transpose(jnp.broadcast_to(row_ids, (8, count)))[:, 0:1]
    block = 2 * nodes
    for first in range(0, count, block):
        scores = product_back(queries[first : first + block], keys) * HEAD_DIM ** (-0.5)
        same = column_ids[first : first + block] == row_ids
        scores = jnp.where(same, scores, -1000000000.0)
        shifted = jnp.exp(scores - jnp.max(scores, axis=-1, keepdims=True))
        probs = (shifted / jnp.sum(shifted, axis=-1, keepdims=True)).astype(BF)
        probs_ref[pl.ds(first, block), :] = probs
        att = product(probs, values)
        att_ref[pl.ds(first, block), :] = att
        for n in range(block // nodes):
            tile = att[n * nodes : (n + 1) * nodes]
            out_ref[first // nodes + n] = pack_tall(tile, False).astype(BF)


def attend(heads_in, ids):
    spaces, tall, unused = heads_in.shape
    nodes = tall * 2 // 3
    count = spaces * nodes
    outs = [((count, count), BF), ((count, 128), F32), ((spaces, nodes // 2, 128), BF)]
    return pl.pallas_call(
        attend_kernel,
        out_shape=[jax.ShapeDtypeStruct(shape, kind) for shape, kind in outs],
        compiler_params=pltpu.CompilerParams(vmem_limit_bytes=VMEM_LIMIT),
        name="attend",
    )(heads_in, ids)


def attend_backward_kernel(x_ref, probs_ref, att_ref, g_ref, out_ref, gs_scr):
    spaces = x_ref.shape[0]
    nodes = x_ref.shape[1] * 2 // 3
    count = spaces * nodes
    queries, keys, values = split_heads(x_ref, nodes)
    grad = jnp.concatenate(
        [unpack_tall(g_ref[d].astype(F32)) for d in range(spaces)], 0
    )
    dots = jnp.sum(grad * att_ref[...], axis=-1, keepdims=True)
    grad = grad.astype(BF)
    block = 2 * nodes
    scale = HEAD_DIM ** (-0.5)
    grad_queries = []
    for first in range(0, count, block):
        grad_probs = product_back(grad[first : first + block], values)
        part = probs_ref[pl.ds(first, block), :].astype(F32)
        grad_scores = (part * (grad_probs - dots[first : first + block])).astype(BF)
        gs_scr[pl.ds(first, block), :] = grad_scores
        grad_queries.append(product(grad_scores, keys))
    grad_queries = jnp.concatenate(grad_queries, 0) * scale
    grad_keys = jnp.transpose(lead_product(queries, gs_scr[...])) * scale
    grad_values = jnp.transpose(lead_product(grad, probs_ref[...]))
    side = lower_half((nodes, 128))
    for d in range(spaces):
        rows = slice(d * nodes, (d + 1) * nodes)
        out_ref[d, pl.ds(0, nodes), :] = jnp.where(
            side, grad_queries[rows], swap_halves(grad_keys[rows])
        ).astype(BF)
        out_ref[d, pl.ds(nodes, nodes // 2), :] = pack_tall(grad_values[rows], False).astype(BF)


def attend_backward(heads_in, probs, att, grad_in, *before):
    count = probs.shape[0]
    return pl.pallas_call(
        skip_refs(attend_backward_kernel, 4, len(before)),
        in_specs=[pl.BlockSpec(memory_space=pltpu.VMEM)] * 4
        + [pl.BlockSpec(memory_space=pl.ANY)] * len(before),
        out_shape=jax.ShapeDtypeStruct(heads_in.shape, BF),
        scratch_shapes=[pltpu.VMEM((count, count), BF)],
        compiler_params=pltpu.CompilerParams(vmem_limit_bytes=VMEM_LIMIT),
        name="attend_backward",
    )(heads_in, probs, att, grad_in, *before)


def merge_heads(block_ref, first, half):
    tiles = []
    for pair in range(HEADS // 2):
        even = unpack_tall(block_ref[2 * pair, pl.ds(first, half), :].astype(F32))
        odd = unpack_tall(block_ref[2 * pair + 1, pl.ds(first, half), :].astype(F32))
        tiles.append(even + swap_halves(odd))
    return jnp.concatenate(tiles, 1)


def feed_kernel(
    att_ref, sz_ref, wo_ref, fg_ref, wu_ref, wd_ref, cot_ref,
    out_ref, pack_ref, gatt_ref, gs1_ref, attr_ref, gbr_ref, ggain_ref, gelu_scr, gup_scr,
):
    nodes = sz_ref.shape[0]
    shards = pack_ref.shape[0]
    att = merge_heads(att_ref, 0, nodes // 2).astype(BF)
    attr_ref[...] = att
    stream_one = sz_ref[...] + product(att, wo_ref[...])
    hat, inverse = centre(stream_one)
    ffn_in = (hat * fg_ref[...]).astype(BF)
    ffn = wu_ref.shape[1]
    cot = cot_ref[...]
    for start in range(0, ffn, 512):
        cols = pl.ds(start, 512)
        x = product(ffn_in, wu_ref[:, cols])
        cdf = 0.5 * (1.0 + lax.erf(x * (0.5**0.5)))
        gelu_scr[:, cols] = (x * cdf).astype(BF)
        slope = cdf + x * jnp.exp(-0.5 * x * x) * ((0.5 / math.pi) ** 0.5)
        gup_scr[:, cols] = (product_back(cot, wd_ref[cols, :]) * slope).astype(BF)
    out_ref[...] = (stream_one + product(gelu_scr[...], wd_ref[...])).astype(BF)
    grad_in = product_back(gup_scr[...], wu_ref[...])
    ggain_ref[...] = jnp.sum(grad_in * hat, axis=0, keepdims=True)
    grad_one = cot.astype(F32) + centre_back(hat, inverse, grad_in * fg_ref[...])
    gs1_ref[...] = grad_one
    branch = grad_one.astype(BF)
    gbr_ref[...] = branch
    grad_att = product_back(branch, wo_ref[...])
    for head in range(HEADS):
        tile = grad_att[:, head // 2 * 128 : head // 2 * 128 + 128]
        gatt_ref[head] = pack_tall(tile, head % 2 == 1).astype(BF)
    tall = ffn // shards
    for start in range(0, ffn, 512):
        block = lead_product(gelu_scr[:, pl.ds(start, 512)], cot).astype(BF)
        for n in range(512 // tall):
            pack_ref[start // tall + n, pl.ds(0, tall), :] = block[n * tall : (n + 1) * tall]
        block = lead_product(ffn_in, gup_scr[:, pl.ds(start, 512)]).astype(BF)
        low = D_MODEL // shards
        for p in range(shards):
            pack_ref[p, pl.ds(tall + start // 512 * low, low), :] = block[p * low : (p + 1) * low]


def feed(att_in, stream_zero, w_out, gain, w_up, w_down, cotangent):
    nodes = stream_zero.shape[0]
    shards = att_in.shape[0]
    ffn = w_up.shape[1]
    tall = ffn // shards + (ffn // 512) * (D_MODEL // shards)
    outs = [
        ((nodes, D_MODEL), BF),
        ((shards, tall, 512), BF),
        (att_in.shape, BF),
        ((nodes, D_MODEL), F32),
        ((nodes, D_MODEL), BF),
        ((nodes, D_MODEL), BF),
        ((1, D_MODEL), F32),
    ]
    return pl.pallas_call(
        feed_kernel,
        out_shape=[jax.ShapeDtypeStruct(shape, kind) for shape, kind in outs],
        scratch_shapes=[pltpu.VMEM((nodes, ffn), BF), pltpu.VMEM((nodes, ffn), BF)],
        compiler_params=pltpu.CompilerParams(vmem_limit_bytes=VMEM_LIMIT),
        name="feed",
    )(att_in, stream_zero, w_out, gain, w_up, w_down, cotangent)


def node_backward_kernel(
    gq_ref, gs1_ref, attr_ref, gbr_ref, s1_ref, v1_ref, ffin_ref, ffh_ref, ffp_ref, ffu_ref, v2_ref,
    emb_ref, sz_ref, ain_ref, ng_ref, fv_ref, fs_ref, fu_ref, we_ref, ag_ref, wq_ref, fgain_ref,
    pack_ref, gsone_ref, gvone_ref, gains_ref,
):
    nodes = gs1_ref.shape[0]
    shards = pack_ref.shape[0]
    side = lower_half((nodes, 128))
    tiles = [[], []]
    for pair in range(HEADS // 2):
        even = gq_ref[2 * pair, pl.ds(0, nodes), :].astype(F32)
        odd = gq_ref[2 * pair + 1, pl.ds(0, nodes), :].astype(F32)
        tiles[0].append(jnp.where(side, even, swap_halves(odd)))
        tiles[1].append(jnp.where(side, swap_halves(even), odd))
    grads = [jnp.concatenate(tile, 1).astype(BF) for tile in tiles]
    grads.append(merge_heads(gq_ref, nodes, nodes // 2).astype(BF))
    attn_in = ain_ref[...]
    grad_in = None
    low = D_MODEL // shards
    base = 0

    def put(grad, height):
        nonlocal base
        grad = grad.astype(BF)
        for p in range(shards):
            pack_ref[p, pl.ds(base, height), :] = grad[p * height : (p + 1) * height]
        base += height

    for n in range(3):
        one = product_back(grads[n], wq_ref[:, pl.ds(n * D_MODEL, D_MODEL)])
        grad_in = one if grad_in is None else grad_in + one
        put(lead_product(attn_in, grads[n]), low)
    put(lead_product(attr_ref[...], gbr_ref[...]), low)
    hat, inverse = centre(sz_ref[...])
    grad_attn_gain = jnp.sum(grad_in * hat, axis=0, keepdims=True)
    stream = gs1_ref[...] + centre_back(hat, inverse, grad_in * ag_ref[...])
    stream = stream.astype(BF)
    put(lead_product(emb_ref[...], stream), (D_S + D_V) // shards)
    grad_emb = product_back(stream, we_ref[...])
    grad_s2, grad_len = grad_emb[:, :D_S], grad_emb[:, D_S:]
    v2 = [v2_ref[c] for c in range(3)]
    factor = grad_len * lax.rsqrt(power_of(v2) + 1.0)
    grad_v2 = [factor * v for v in v2]
    x = ffp_ref[...]
    s = sigmoid(x)
    grad_pre = (grad_s2 * (s + x * s * (1.0 - s))).astype(BF)
    for start in range(0, D_S, 512):
        put(lead_product(ffin_ref[...], grad_pre[:, start : start + 512]), (D_S + D_V) // shards)
    grad_ffin = product_back(grad_pre, fs_ref[...])
    z = [ffu_ref[c] for c in range(3)]
    power = power_of(z) + 1.0
    inverse = lax.rsqrt(power)
    s = sigmoid(power * inverse)
    dot = z[0] * grad_v2[0] + z[1] * grad_v2[1] + z[2] * grad_v2[2]
    factor = dot * inverse * (s * (1.0 - s))
    grad_up = [(grad_v2[c] * s + z[c] * factor).astype(BF) for c in range(3)]
    h = [ffh_ref[c] for c in range(3)]
    factor = grad_ffin[:, D_S:] * lax.rsqrt(power_of(h) + 1.0)
    v1 = [v1_ref[c] for c in range(3)]
    scale = lax.rsqrt(jnp.mean(power_of(v1), axis=-1, keepdims=True) + 1e-05)
    up_total = vec_total = None
    grad_nv = []
    for c in range(3):
        one = lead_product(h[c].astype(BF), grad_up[c])
        up_total = one if up_total is None else up_total + one
        grad_h = (product_back(grad_up[c], fu_ref[...]) + factor * h[c]).astype(BF)
        one = lead_product((v1[c] * scale).astype(BF), grad_h)
        vec_total = one if vec_total is None else vec_total + one
        grad_nv.append(grad_v2[c] + product_back(grad_h, fv_ref[...]))
    put(jnp.concatenate([vec_total, up_total], 1), D_V // shards)
    grad_ns = grad_s2 + grad_ffin[:, :D_S]
    hat, inverse = centre(s1_ref[...])
    grad_norm_gain = jnp.sum(grad_ns * hat, axis=0, keepdims=True)
    gsone_ref[...] = centre_back(hat, inverse, grad_ns * ng_ref[...])
    dot = grad_nv[0] * v1[0] + grad_nv[1] * v1[1] + grad_nv[2] * v1[2]
    dot = jnp.mean(dot, axis=-1, keepdims=True) * scale * scale
    for c in range(3):
        gvone_ref[c] = scale * (grad_nv[c] - v1[c] * dot)
    gains_ref[...] = jnp.zeros_like(gains_ref)
    gains_ref[0:1, :] = grad_norm_gain
    for p in range(shards):
        pair = slice(p // 2 * 128, p // 2 * 128 + 128)
        left = jnp.broadcast_to(grad_attn_gain[:, pair], (8, 128))
        right = jnp.broadcast_to(fgain_ref[:, pair], (8, 128))
        if p % 2 == 0:
            both = jnp.where(lower_half((8, 128)), left, swap_halves(right))
        else:
            both = jnp.where(lower_half((8, 128)), swap_halves(left), right)
        gains_ref[1:2, pl.ds(p * 128, 128)] = both[0:1]


def node_backward(grad_heads, *values, before=()):
    nodes = values[0].shape[0]
    shards = grad_heads.shape[0]
    tall = 4 * (D_MODEL // shards) + 3 * ((D_S + D_V) // shards) + D_V // shards
    outs = [
        ((shards, tall, 512), BF),
        ((nodes, D_S), F32),
        ((3, nodes, D_V), F32),
        ((8, D_S), F32),
    ]
    seen = 1 + len(values)
    return pl.pallas_call(
        skip_refs(node_backward_kernel, seen, len(before)),
        in_specs=[pl.BlockSpec(memory_space=pltpu.VMEM)] * seen
        + [pl.BlockSpec(memory_space=pl.ANY)] * len(before),
        out_shape=[jax.ShapeDtypeStruct(shape, kind) for shape, kind in outs],
        compiler_params=pltpu.CompilerParams(vmem_limit_bytes=VMEM_LIMIT),
        name="node_backward",
    )(grad_heads, *values, *before)


def pad_to(values, size, axis):
    pads = [(0, 0)] * values.ndim
    pads[axis] = (0, size - values.shape[axis])
    return jnp.pad(values, pads)


def fold(blocks, width=512):
    shards, rows, columns = blocks.shape
    parts = columns // width
    return jnp.moveaxis(blocks.reshape(shards, rows, parts, width), 2, 1).reshape(
        shards, parts * rows, width
    )


def unfold(rows_in, rows, columns, width=512):
    parts = columns // width
    return jnp.moveaxis(rows_in.reshape(parts, rows, width), 0, 1).reshape(rows, columns)


def unfold_lanes(rows_in):
    rows, width = rows_in.shape
    return jnp.moveaxis(rows_in.reshape(rows, width // 128, 128), 1, 0).reshape(-1, 128)


def body(
    node_scalar, node_vector, edge_scalar, edge_vector, neighbours, send_rows, complex_id, cotangent,
    w_node, w_edge, w_norms, vec_node, vec_edge, vec_out, norm_gain, ff_vec, ff_scalar, ff_up,
    w_embed, attn_gain, w_qkv, w_out, ffn_gain, w_up, w_down,
):
    local_rows = node_scalar.shape[0]
    spaces = lax.axis_size("space")
    extra_rows = spaces * CAP
    table_count = local_rows + extra_rows
    all_nodes = complex_id.shape[0]
    steps = NEIGH // GROUP

    sent_index = send_rows[0].reshape(-1)
    sent_live = sent_index >= 0
    pick = sent_index[:, None] == jnp.arange(local_rows, dtype=jnp.int32)[None, :]
    pick = pick.astype(BF)
    flat_nodes = jnp.concatenate([node_scalar] + [node_vector[c] for c in range(3)], 1)
    outgoing = product(pick, flat_nodes).astype(BF).reshape(spaces, CAP, D_S + 3 * D_V)
    incoming = lax.all_to_all(outgoing, "space", split_axis=0, concat_axis=0, tiled=True)
    incoming = incoming.reshape(extra_rows, D_S + 3 * D_V)
    table_s = jnp.concatenate([node_scalar, incoming[:, :D_S]], 0)
    table_v = jnp.stack(
        [
            jnp.concatenate(
                [node_vector[c], incoming[:, D_S + c * D_V : D_S + (c + 1) * D_V]], 0
            )
            for c in range(3)
        ]
    )
    vec_source = pad_to(vec_node[:, :H_V], H_P, 1)
    vec_target = pad_to(vec_node[:, H_V:], H_P, 1)
    a_source = product(table_s, w_node[:, :D_S]).astype(BF)
    b_target = product(node_scalar, w_node[:, D_S:])
    p_source = product(table_v, vec_source).astype(BF)
    q_target = product(node_vector, vec_target)
    ve_row = pad_to(vec_edge.astype(F32), H_P, 1)
    vout = pad_to(vec_out, H_P, 0)
    wn_mix = pad_to(jnp.concatenate([w_norms, w_edge], 0), H_P, 0)
    mix = jnp.concatenate([a_source, wn_mix], 0)

    near = neighbours.T
    near_col = near[:, :, None]
    near_row = near.reshape(steps, 1, GROUP * local_rows)
    es_k = edge_scalar.reshape(local_rows, NEIGH, D_E).transpose(1, 0, 2)
    es_pad = jnp.pad(es_k, ((0, 0), (0, 0), (1, 128 - 1 - D_E)))
    ev_k = edge_vector.reshape(3, local_rows, NEIGH)
    ev_col = ev_k.transpose(2, 1, 0).astype(F32)
    ev_row = ev_k.transpose(2, 0, 1).reshape(steps, GROUP, 3, local_rows)
    ev_row = ev_row.transpose(0, 2, 1, 3).reshape(steps, 3, GROUP * local_rows)

    agg_s, agg_v, hidden, lx, dsilu, update = edge_forward(
        near_col, es_pad, ev_col, mix, b_target, p_source, q_target, ve_row, vout
    )

    if spaces == HEADS and lax.axis_size("dp") == 4 and local_rows == 128:
        row_of = lambda gain: gain.astype(F32)[None]
        s1, v1, ffin, ffh, ffp, ffu, v2, emb, sz, ain, heads_out = node_forward(
            node_scalar, node_vector, agg_s, agg_v, row_of(norm_gain), ff_vec, ff_scalar, ff_up,
            w_embed, row_of(attn_gain), w_qkv,
        )
        heads_in = exchange(heads_out, 0)
        probs, att, att_out = attend(heads_in, complex_id[None])
        stream_out, first_share, gatt, gs1, attr, gbr, fgain = feed(
            exchange(att_out, 1), sz, w_out, row_of(ffn_gain), w_up, w_down, cotangent
        )
        first = reduce_core(first_share)
        gatt_in = exchange(gatt, 1)
        grad_heads = exchange(attend_backward(heads_in, probs, att, gatt_in, first), 0)
        first = reduce_first(first)
        middle_share, gsone, gvone, gains = node_backward(
            grad_heads, gs1, attr, gbr, s1, v1, ffin, ffh, ffp, ffu, v2, emb, sz, ain,
            row_of(norm_gain), ff_vec, ff_scalar, ff_up, w_embed, row_of(attn_gain), w_qkv, fgain,
            before=first,
        )
        middle = reduce_core(middle_share)
        first = reduce_second(first)
        ratio, second_share, rest, gscal, back_s = scalar_backward(
            spaces, near_row, lx, dsilu, gsone, wn_mix, table_s, node_scalar, w_node,
            middle, *first,
        )
        second = reduce_core(second_share)
        middle = reduce_first(middle)
        third_share, gvec, back_v = vector_backward(
            spaces, near_row, ev_col, ev_row, hidden, ratio, update, gvone, vout,
            table_v, node_vector, vec_source, vec_target, rest, gains, second, *middle,
        )
        second = reduce_first(second)
        middle = reduce_second(middle)
        third = reduce_first(reduce_core(third_share))
        back = jnp.concatenate([back_s, back_v], 1).reshape(spaces, CAP, D_S + 3 * D_V)
        got = exchange(back, 2)
        got = got.reshape(extra_rows, D_S + 3 * D_V)
        got = jnp.where(sent_live[:, None], got, 0)
        added = lax.dot_general(pick, got, (((0,), (0,)), ((), ())), preferred_element_type=F32)
        grad_scalar = gscal + added[:, :D_S]
        grad_vector = gvec + jnp.moveaxis(added[:, D_S:].reshape(local_rows, 3, D_V), 1, 0)
        late = reduce_second(tuple(jnp.concatenate(two, 1) for two in zip(second, third)))
        shares = [first_share, middle_share, second_share, third_share]
        eighths = [share.shape[1] // 8 for share in shares]
        rest_of = eighths[2] + eighths[3]
        reduced = reduce_z(jnp.concatenate(first + middle + late, 1))
        cuts = [0]
        for rows in (eighths[0], eighths[0], eighths[1], eighths[1], rest_of, rest_of):
            cuts.append(cuts[-1] + rows)
        pieces = [reduced[lo:hi] for lo, hi in zip(cuts, cuts[1:])]
        gathered_x = join(join(jnp.concatenate(pieces[0::2], 0), "y"), "x").reshape(4, -1, 512)
        gathered_y = join(join(jnp.concatenate(pieces[1::2], 0), "x"), "y").reshape(4, -1, 512)

        def rows_of(lo, hi, start, stop, outer):
            halves = [
                part[:, start:stop].reshape(outer, -1, 512)[:, lo:hi].reshape(-1, 512)
                for part in (gathered_x, gathered_y)
            ]
            return jnp.concatenate(halves, 0).astype(F32)

        early = eighths[0] + eighths[1]
        first_sum = rows_of(0, eighths[0], 0, eighths[0], 4)
        middle_sum = rows_of(0, eighths[1], eighths[0], early, 4)
        second_sum = rows_of(0, 2 * eighths[2], early, early + rest_of, 2)
        third_sum = rows_of(2 * eighths[2], 2 * rest_of, early, early + rest_of, 2)

        def taker(rows_in):
            at = [0]

            def take(rows, cols, blocks=1):
                part = rows_in[at[0] : at[0] + rows * blocks]
                at[0] += rows * blocks
                return unfold(part, rows, cols) if blocks > 1 else part

            return take

        take = taker(first_sum)
        out_down = take(w_down.shape[0] // spaces, 512)
        out_up = take(D_MODEL // spaces, 2048, 4)
        take = taker(middle_sum)
        out_qkv = take(D_MODEL // spaces, 1536, 3)
        out_out = take(D_MODEL // spaces, 512)
        out_embed = take((D_S + D_V) // spaces, 512)
        out_ffs = take((D_S + D_V) // spaces, 1024, 2)
        both = take(D_V // spaces, 512)
        out_ffv, out_ffu = both[:, :D_V], both[:, D_V:]
        take = taker(second_sum)
        node_ab = take(D_S // spaces, 2048, 4)
        norms_main = unfold_lanes(take(128, 512))
        take = taker(third_sum)
        vec_a = take(D_V // spaces, 512)
        vec_b = take(D_V // spaces, 512)
        vout_t = take(D_V // spaces, 512)
        tails = take(D_V // spaces, 512)
        out_vec_node = jnp.concatenate([vec_a, tails[:, 0:1], vec_b, tails[:, 1:2]], 1)
        out_vec_out = jnp.concatenate([vout_t, tails[:, 2:3]], 1).T
        misc = tails[:, 256:384]
        return (
            stream_out,
            grad_scalar.astype(BF),
            grad_vector.astype(BF),
            node_ab,
            tails[:, 128:256],
            jnp.concatenate([norms_main, misc[0:1]], 0),
            out_vec_node,
            misc[1:6].reshape(1, 640)[:, :H_V],
            out_vec_out,
            misc[6],
            out_ffv,
            out_ffs,
            out_ffu,
            out_embed,
            misc[7, :64],
            out_qkv,
            out_out,
            misc[7, 64:],
            out_up,
            out_down,
        )

    scalar_one = node_scalar.astype(F32) + agg_s
    vector_one = node_vector.astype(F32) + agg_v
    gain_norm = norm_gain.astype(F32)
    normed_s = layer_norm(scalar_one, gain_norm)
    normed_v = vector_norm(vector_one)
    normed_vr = normed_v.astype(BF)
    ff_hidden = product(normed_vr, ff_vec)
    ff_hidden_r = ff_hidden.astype(BF)
    ff_length = length_plus(ff_hidden)
    ff_input = jnp.concatenate([normed_s.astype(BF), ff_length.astype(BF)], -1)
    ff_preact = product(ff_input, ff_scalar)
    ff_update = product(ff_hidden_r, ff_up)
    scalar_two = normed_s + jax.nn.silu(ff_preact)
    vector_two = normed_v + vector_gate(ff_update)
    embed_input = jnp.concatenate([scalar_two.astype(BF), length_plus(vector_two).astype(BF)], -1)
    stream_zero = product(embed_input, w_embed)
    gain_attn = attn_gain.astype(F32)
    attn_in = layer_norm(stream_zero, gain_attn).astype(BF)
    qkv = product(attn_in, w_qkv).astype(BF)
    queries = qkv[:, :D_MODEL]
    keys_own = qkv[:, D_MODEL : 2 * D_MODEL]
    values_own = qkv[:, 2 * D_MODEL :]
    full_qkv = lax.all_gather(qkv, "space", axis=0, tiled=True)
    heads = lambda values: values.reshape(values.shape[0], HEADS, HEAD_DIM)
    full_queries = heads(full_qkv[:, :D_MODEL])
    full_keys = heads(full_qkv[:, D_MODEL : 2 * D_MODEL])
    full_values = heads(full_qkv[:, 2 * D_MODEL :])
    position = lax.axis_index("space")
    own_ids = lax.dynamic_slice_in_dim(complex_id, position * local_rows, local_rows, 0)
    same = own_ids[:, None] == complex_id[None, :]
    score_scale = HEAD_DIM ** (-0.5)
    scores = jnp.einsum("qhd,khd->hqk", heads(queries), full_keys, preferred_element_type=F32)
    scores = jnp.where(same[None], scores * score_scale, -1000000000.0)
    row_peak = jnp.max(scores, axis=-1, keepdims=True)
    shifted = jnp.exp(scores - row_peak)
    totals = jnp.sum(shifted, axis=-1, keepdims=True)
    probs = shifted / totals
    log_total = row_peak + jnp.log(totals)
    attended = jnp.einsum(
        "hqk,khd->qhd", probs.astype(BF), full_values, preferred_element_type=F32
    ).reshape(local_rows, D_MODEL)
    attended_r = attended.astype(BF)
    stream_one = stream_zero + product(attended_r, w_out)
    gain_ffn = ffn_gain.astype(F32)
    ffn_in = layer_norm(stream_one, gain_ffn).astype(BF)
    hidden_up = product(ffn_in, w_up)
    gelu_r = gelu_exact(hidden_up).astype(BF)
    stream_out = (stream_one + product(gelu_r, w_down)).astype(BF)
    grad_w_down = product_lead(gelu_r, cotangent)
    grad_gelu = product_back(cotangent, w_down)
    grad_up_r = pullback(gelu_exact, hidden_up, grad_gelu).astype(BF)
    grad_w_up = product_lead(ffn_in, grad_up_r)
    grad_ffn_in = product_back(grad_up_r, w_up)
    unused, ffn_pull = jax.vjp(layer_norm, stream_one, gain_ffn)
    grad_stream_ln, grad_ffn_gain = ffn_pull(grad_ffn_in)
    grad_stream_one = cotangent.astype(F32) + grad_stream_ln
    grad_branch = grad_stream_one.astype(BF)
    grad_w_out = product_lead(attended_r, grad_branch)
    grad_attended = product_back(grad_branch, w_out).astype(BF)
    row_dots = jnp.sum(heads(grad_attended).astype(F32) * heads(attended), axis=-1).T

    def halves(values):
        high = lax.reduce_precision(values, exponent_bits=8, mantissa_bits=7)
        return [high.astype(BF), (values - high).astype(BF)]

    numbers = jnp.concatenate(halves(log_total[:, :, 0]) + halves(row_dots), 0)
    packed = jnp.concatenate([grad_attended, pad_to(numbers.T, 128, 1)], 1)
    full_packed = lax.all_gather(packed, "space", axis=0, tiled=True)
    full_grad = heads(full_packed[:, :D_MODEL])
    numbers = full_packed[:, D_MODEL : D_MODEL + 4 * HEADS].astype(F32).T
    full_log = numbers[:HEADS] + numbers[HEADS : 2 * HEADS]
    full_dots = numbers[2 * HEADS : 3 * HEADS] + numbers[3 * HEADS :]

    grad_probs = jnp.einsum(
        "qhd,khd->hqk", heads(grad_attended), full_values, preferred_element_type=F32
    )
    grad_scores = (probs * (grad_probs - row_dots[:, :, None])).astype(BF)
    grad_query = jnp.einsum("hqk,khd->qhd", grad_scores, full_keys, preferred_element_type=F32)
    own_scores = jnp.einsum(
        "khd,qhd->hkq", heads(keys_own), full_queries, preferred_element_type=F32
    )
    own_scores = jnp.where(same[None], own_scores * score_scale, -1000000000.0)
    own_probs = jnp.exp(own_scores - full_log[:, None, :])
    own_grad_probs = jnp.einsum(
        "khd,qhd->hkq", heads(values_own), full_grad, preferred_element_type=F32
    )
    own_grad_scores = (own_probs * (own_grad_probs - full_dots[:, None, :])).astype(BF)
    grad_keys = jnp.einsum(
        "hkq,qhd->khd", own_grad_scores, full_queries, preferred_element_type=F32
    )
    grad_values = jnp.einsum(
        "hkq,qhd->khd", own_probs.astype(BF), full_grad, preferred_element_type=F32
    )
    flat = lambda values: values.reshape(local_rows, D_MODEL)
    grad_qkv = jnp.concatenate(
        [flat(grad_query) * score_scale, flat(grad_keys) * score_scale, flat(grad_values)], -1
    ).astype(BF)
    grad_w_qkv = product_lead(attn_in, grad_qkv)
    grad_attn_in = product_back(grad_qkv, w_qkv)
    unused, attn_pull = jax.vjp(layer_norm, stream_zero, gain_attn)
    grad_zero_ln, grad_attn_gain = attn_pull(grad_attn_in)
    grad_stream_r = (grad_stream_one + grad_zero_ln).astype(BF)
    grad_w_embed = product_lead(embed_input, grad_stream_r)
    grad_embed_in = product_back(grad_stream_r, w_embed)
    grad_vector_two = pullback(length_plus, vector_two, grad_embed_in[:, D_S:])
    grad_ff_pre = pullback(jax.nn.silu, ff_preact, grad_embed_in[:, :D_S]).astype(BF)
    grad_ff_scalar = product_lead(ff_input, grad_ff_pre)
    grad_ff_input = product_back(grad_ff_pre, ff_scalar)
    grad_ff_update = pullback(vector_gate, ff_update, grad_vector_two).astype(BF)
    grad_ff_up = product_lead(ff_hidden_r, grad_ff_update)
    grad_ff_hidden = (
        product_back(grad_ff_update, ff_up)
        + pullback(length_plus, ff_hidden, grad_ff_input[:, D_S:])
    ).astype(BF)
    grad_ff_vec = product_lead(normed_vr, grad_ff_hidden)
    grad_normed_v = grad_vector_two + product_back(grad_ff_hidden, ff_vec)
    grad_normed_s = grad_embed_in[:, :D_S] + grad_ff_input[:, :D_S]
    unused, norm_pull = jax.vjp(layer_norm, scalar_one, gain_norm)
    grad_scalar_one, grad_norm_gain = norm_pull(grad_normed_s)
    grad_vector_one = pullback(vector_norm, vector_one, grad_normed_v)

    shard = lambda grad: grad.astype(BF).reshape((spaces, grad.shape[0] // spaces) + grad.shape[1:])
    gains = jnp.concatenate(
        [shard(grad_norm_gain), shard(grad_attn_gain), shard(grad_ffn_gain)], 1
    )
    gains = pad_to(pad_to(gains, 512, 1)[:, None, :], 16, 1)
    first_share = jnp.concatenate(
        [
            shard(grad_w_down),
            fold(shard(grad_w_up)),
            fold(shard(grad_w_qkv)),
            shard(grad_w_out),
            shard(grad_w_embed),
            fold(shard(grad_ff_scalar)),
            jnp.concatenate([shard(grad_ff_vec), shard(grad_ff_up)], 2),
            gains,
        ],
        1,
    )
    first_sum = lax.psum_scatter(first_share, "space", scatter_dimension=0, tiled=False)
    first_sum = lax.psum(first_sum, "dp").astype(F32)

    grad_a, grad_mix, grad_b, grad_p, grad_q, grad_vout = edge_backward(
        near_row, ev_col, ev_row, hidden, lx, dsilu, update,
        grad_scalar_one * (1.0 / NEIGH), grad_vector_one * (1.0 / NEIGH), wn_mix, vout, table_count,
    )
    grad_vedge = jnp.sum(grad_p[:, table_count], 0)[:H_V]
    grad_vec_edge = lax.psum(grad_vedge[None, :], ("dp", "space"))
    grad_a_r = grad_a.astype(BF)
    grad_p_r = grad_p[:, :table_count].astype(BF)
    grad_b_r = grad_b.astype(BF)
    grad_q_r = grad_q.astype(BF)
    grad_node_a = product_lead(table_s, grad_a_r)
    grad_node_b = product_lead(node_scalar, grad_b_r)
    grad_vec_a = product_lead(table_v, grad_p_r)
    grad_vec_b = product_lead(node_vector, grad_q_r)
    grad_table_scalar = product_back(grad_a_r, w_node[:, :D_S])
    grad_table_vector = product_back(grad_p_r, vec_source)
    grad_scalar = (
        grad_scalar_one + product_back(grad_b_r, w_node[:, D_S:]) + grad_table_scalar[:local_rows]
    )
    grad_vector = (
        grad_vector_one + product_back(grad_q_r, vec_target) + grad_table_vector[:, :local_rows]
    )
    back = jnp.concatenate(
        [grad_table_scalar[local_rows:]] + [grad_table_vector[c, local_rows:] for c in range(3)], 1
    )
    back = back.astype(BF).reshape(spaces, CAP, D_S + 3 * D_V)
    got = lax.all_to_all(back, "space", split_axis=0, concat_axis=0, tiled=True)
    got = got.reshape(extra_rows, D_S + 3 * D_V)
    got = jnp.where(sent_live[:, None], got, 0)
    added = lax.dot_general(pick, got, (((0,), (0,)), ((), ())), preferred_element_type=F32)
    grad_scalar = grad_scalar + added[:, :D_S]
    grad_vector = grad_vector + jnp.moveaxis(
        added[:, D_S:].reshape(local_rows, 3, D_V), 1, 0
    )

    columns = lambda grad: jnp.moveaxis(
        grad.reshape(grad.shape[0], spaces, grad.shape[1] // spaces), 1, 0
    )
    mix_block = columns(grad_mix.astype(BF))
    mix_width = D_S // spaces
    mix_rows = H_P * mix_width // 512
    second_share = jnp.concatenate(
        [
            fold(shard(grad_node_a)),
            fold(shard(grad_node_b)),
            mix_block.reshape(spaces, mix_rows, 512),
            shard(grad_vec_a)[:, :, :512],
            shard(grad_vec_b)[:, :, :512],
            shard(grad_vout)[:, :, :512],
            jnp.concatenate(
                [
                    shard(grad_vec_a)[:, :, 512:],
                    shard(grad_vec_b)[:, :, 512:],
                    shard(grad_vout)[:, :, 512:],
                    jnp.zeros((spaces, D_V // spaces, 128), BF),
                ],
                2,
            ),
        ],
        1,
    )
    second_sum = lax.psum_scatter(second_share, "space", scatter_dimension=0, tiled=False)
    second_sum = lax.psum(second_sum, "dp").astype(F32)

    def taker(rows_in):
        at = [0]

        def take(rows, cols, blocks=1):
            part = rows_in[at[0] : at[0] + rows * blocks]
            at[0] += rows * blocks
            return unfold(part, rows, cols) if blocks > 1 else part

        return take

    take = taker(first_sum)
    out_down = take(grad_w_down.shape[0] // spaces, 512)
    out_up = take(D_MODEL // spaces, 2048, 4)
    out_qkv = take(D_MODEL // spaces, 1536, 3)
    out_out = take(D_MODEL // spaces, 512)
    out_embed = take((D_S + D_V) // spaces, 512)
    out_ffs = take((D_S + D_V) // spaces, 1024, 2)
    both = take(D_V // spaces, 512)
    out_ffv, out_ffu = both[:, :D_V], both[:, D_V:]
    gain_row = take(16, 512)[0]
    cuts = [D_S // spaces, D_MODEL // spaces, D_MODEL // spaces]
    out_gn = gain_row[: cuts[0]]
    out_ga = gain_row[cuts[0] : cuts[0] + cuts[1]]
    out_gf = gain_row[cuts[0] + cuts[1] : sum(cuts)]
    take = taker(second_sum)
    node_a = take(D_S // spaces, 1024, 2)
    node_b = take(D_S // spaces, 1024, 2)
    mixed = take(mix_rows, 512).reshape(H_P, mix_width)
    vec_a = take(D_V // spaces, 512)
    vec_b = take(D_V // spaces, 512)
    vout_t = take(D_V // spaces, 512)
    tails = take(D_V // spaces, 512)
    out_vec_node = jnp.concatenate([vec_a, tails[:, :1], vec_b, tails[:, 128:129]], 1)
    out_vec_out = jnp.concatenate([vout_t, tails[:, 256:257]], 1).T
    return (
        stream_out,
        grad_scalar.astype(BF),
        grad_vector.astype(BF),
        jnp.concatenate([node_a, node_b], 1),
        mixed[H_V : H_V + D_E],
        mixed[:H_V],
        out_vec_node,
        grad_vec_edge,
        out_vec_out,
        out_gn,
        out_ffv,
        out_ffs,
        out_ffu,
        out_embed,
        out_ga,
        out_qkv,
        out_out,
        out_gf,
        out_up,
        out_down,
    )


def solution(mesh):
    rows = P(("dp", "space"), None)
    component = P(None, ("dp", "space"), None)
    return jax.shard_map(
        body,
        mesh=mesh,
        in_specs=(
            rows, component, rows, P(None, ("dp", "space")), rows,
            P(("dp", "space"), None, None), P("dp"), rows,
        ) + (P(),) * 17,
        out_specs=(
            rows, rows, component, P("space", None), P(None, "space"), P(None, "space"),
            P("space", None), P(), P(None, "space"), P("space"), P("space", None),
            P("space", None), P("space", None), P("space", None), P("space"), P("space", None),
            P("space", None), P("space"), P("space", None), P("space", None),
        ),
        check_vma=False,
    )
```

```python
import functools
import math

import jax
import jax.numpy as jnp
from jax import lax
from jax.experimental import pallas as pl
from jax.experimental.pallas import tpu as pltpu
from jax.sharding import PartitionSpec as P

D_S = 1024
D_V = 256
H_V = 513
H_P = 640
D_E = 32
NEIGH = 30
D_MODEL = 512
HEADS = 8
HEAD_DIM = 64
CAP = 16
GROUP = 5
VMEM_LIMIT = 60 * 1024 * 1024

MESH = pl.DeviceIdType.MESH
BF = jnp.bfloat16
F32 = jnp.float32


def layer_norm(values, gain_row):
    centred = values - jnp.mean(values, axis=-1, keepdims=True)
    spread = jnp.mean(centred * centred, axis=-1, keepdims=True)
    return centred * lax.rsqrt(spread + 1e-05) * gain_row


def vector_norm(vectors):
    mean_power = jnp.mean(jnp.sum(vectors * vectors, axis=0), axis=-1, keepdims=True)
    return vectors * lax.rsqrt(mean_power + 1e-05)[None]


def length_plus(vectors):
    return jnp.sqrt(jnp.sum(vectors * vectors, axis=0) + 1.0)


def vector_gate(vectors):
    return vectors * jax.nn.sigmoid(length_plus(vectors))[None]


def gelu_exact(values):
    return jax.nn.gelu(values, approximate=False)


def product(former, latter):
    return jnp.dot(former, latter, preferred_element_type=F32)


def product_lead(former, latter):
    leading = tuple(range(former.ndim - 1))
    return lax.dot_general(
        former, latter, ((leading, leading), ((), ())), preferred_element_type=F32
    )


def product_back(former, latter):
    return lax.dot_general(
        former, latter, (((former.ndim - 1,), (1,)), ((), ())), preferred_element_type=F32
    )


def pullback(function, at_point, cotangent_in):
    unused, puller = jax.vjp(function, at_point)
    return puller(cotangent_in)[0]


def sigmoid(values):
    return 0.5 * jnp.tanh(0.5 * values) + 0.5


LANE_BLOCKS = ((0, 256), (256, 256), (512, 128))
ROW_TILE = 64


def edge_forward_kernel(
    near_ref, es_ref, ev_ref, a_ref, b_ref, p_ref, q_ref, ve_ref, vo_ref,
    aggs_ref, aggv_ref, h_ref, lx_ref, ds_ref, z_ref, x_scr,
):
    nodes = b_ref.shape[0]
    table = p_ref.shape[1]
    rows = GROUP * nodes
    idx = near_ref[...].reshape(rows, 1)
    x_scr[:, :table] = (idx == lax.broadcasted_iota(jnp.int32, (rows, table), 1)).astype(BF)
    one_hot = x_scr[:, :table]
    for start, width in LANE_BLOCKS:
        cols = pl.ds(start, width)
        gathered = [product(one_hot, p_ref[c, :, cols]) for c in range(3)]
        for k in range(GROUP):
            for first in range(0, nodes, ROW_TILE):
                at = k * nodes + first
                evk = ev_ref[k, pl.ds(first, ROW_TILE), :]
                total = None
                for c in range(3):
                    h = (
                        gathered[c][at : at + ROW_TILE]
                        + q_ref[c, pl.ds(first, ROW_TILE), cols]
                        + evk[:, c : c + 1] * ve_ref[:, cols]
                    )
                    h_ref[k, c, pl.ds(first, ROW_TILE), cols] = h.astype(BF)
                    total = h * h + 1.0 if total is None else total + h * h
                length = total * lax.rsqrt(total)
                if start == 512:
                    lane = lax.broadcasted_iota(jnp.int32, (ROW_TILE, width), 1)
                    length = jnp.where(
                        lane == 0, length, es_ref[k, pl.ds(first, ROW_TILE), :].astype(F32)
                    )
                length = length.astype(BF)
                x_scr[pl.ds(at, ROW_TILE), pl.ds(table + start, width)] = length
                lx_ref[k, pl.ds(first, ROW_TILE), cols] = length

    @pl.when(pl.program_id(0) == 0)
    def _():
        aggs_ref[...] = jnp.zeros_like(aggs_ref)
        aggv_ref[...] = jnp.zeros_like(aggv_ref)

    full = x_scr[...]
    for start in range(0, D_S, 256):
        cols = pl.ds(start, 256)
        pre = product(full, a_ref[:, cols])
        for first in range(0, nodes, ROW_TILE):
            part = pl.ds(first, ROW_TILE)
            acc = None
            for k in range(GROUP):
                at = k * nodes + first
                x = pre[at : at + ROW_TILE] + b_ref[part, cols]
                s = sigmoid(x)
                y = x * s
                ds_ref[k, part, cols] = (s + y * (1.0 - s)).astype(BF)
                acc = y if acc is None else acc + y
            aggs_ref[part, cols] += acc * (1.0 / NEIGH)
    ups = [
        product(h_ref[:, c, :, :].reshape(rows, H_P), vo_ref[...]) for c in range(3)
    ]
    for first in range(0, nodes, ROW_TILE):
        part = pl.ds(first, ROW_TILE)
        acc = [None] * 3
        for k in range(GROUP):
            at = k * nodes + first
            z = [ups[c][at : at + ROW_TILE] for c in range(3)]
            power = z[0] * z[0] + z[1] * z[1] + z[2] * z[2] + 1.0
            s = sigmoid(power * lax.rsqrt(power))
            for c in range(3):
                z_ref[k, c, part, :] = z[c].astype(BF)
                gated = z[c] * s
                acc[c] = gated if acc[c] is None else acc[c] + gated
        for c in range(3):
            aggv_ref[c, part, :] += acc[c] * (1.0 / NEIGH)


def edge_forward(near_col, es_pad, ev_col, mix, b_target, p_source, q_target, ve_row, vout):
    nodes = b_target.shape[0]
    table = p_source.shape[1]
    whole = lambda shape: pl.BlockSpec(shape, lambda g: (0,) * len(shape))
    slots = lambda *shape: pl.BlockSpec((GROUP,) + shape, lambda g: (g,) + (0,) * len(shape))
    return pl.pallas_call(
        edge_forward_kernel,
        grid=(NEIGH // GROUP,),
        in_specs=[
            slots(nodes, 1),
            slots(nodes, 128),
            slots(nodes, 3),
            whole((table + H_P, D_S)),
            whole((nodes, D_S)),
            whole((3, table, H_P)),
            whole((3, nodes, H_P)),
            whole((1, H_P)),
            whole((H_P, D_V)),
        ],
        out_specs=[
            whole((nodes, D_S)),
            whole((3, nodes, D_V)),
            slots(3, nodes, H_P),
            slots(nodes, H_P),
            slots(nodes, D_S),
            slots(3, nodes, D_V),
        ],
        out_shape=[
            jax.ShapeDtypeStruct((nodes, D_S), F32),
            jax.ShapeDtypeStruct((3, nodes, D_V), F32),
            jax.ShapeDtypeStruct((NEIGH, 3, nodes, H_P), BF),
            jax.ShapeDtypeStruct((NEIGH, nodes, H_P), BF),
            jax.ShapeDtypeStruct((NEIGH, nodes, D_S), BF),
            jax.ShapeDtypeStruct((NEIGH, 3, nodes, D_V), BF),
        ],
        scratch_shapes=[pltpu.VMEM((GROUP * nodes, table + H_P), BF)],
        compiler_params=pltpu.CompilerParams(vmem_limit_bytes=VMEM_LIMIT),
        name="edge_forward",
    )(near_col, es_pad, ev_col, mix, b_target, p_source, q_target, ve_row, vout)


def edge_backward_kernel(
    near_ref, ev_ref, evr_ref, h_ref, lx_ref, ds_ref, z_ref, gs_ref, gv_ref, wn_ref, vo_ref,
    ga_ref, gw_ref, gb_ref, gp_ref, gq_ref, gvo_ref, pre_scr, up_scr, gh_scr,
):
    nodes = gs_ref.shape[0]
    table = ga_ref.shape[0]
    rows = GROUP * nodes

    @pl.when(pl.program_id(0) == 0)
    def _():
        for ref in (ga_ref, gw_ref, gb_ref, gp_ref, gq_ref, gvo_ref):
            ref[...] = jnp.zeros_like(ref)

    for start in range(0, D_S, 256):
        cols = pl.ds(start, 256)
        for first in range(0, nodes, ROW_TILE):
            part = pl.ds(first, ROW_TILE)
            share = gs_ref[part, cols]
            acc = None
            for k in range(GROUP):
                g = (ds_ref[k, part, cols].astype(F32) * share).astype(BF)
                pre_scr[pl.ds(k * nodes + first, ROW_TILE), cols] = g
                g = g.astype(F32)
                acc = g if acc is None else acc + g
            gb_ref[part, cols] += acc
    for first in range(0, nodes, ROW_TILE):
        part = pl.ds(first, ROW_TILE)
        share = [gv_ref[c, part, :] for c in range(3)]
        for k in range(GROUP):
            z = [z_ref[k, c, part, :].astype(F32) for c in range(3)]
            power = z[0] * z[0] + z[1] * z[1] + z[2] * z[2] + 1.0
            inverse = lax.rsqrt(power)
            s = sigmoid(power * inverse)
            dot = z[0] * share[0] + z[1] * share[1] + z[2] * share[2]
            factor = dot * inverse * (s * (1.0 - s))
            for c in range(3):
                up_scr[c, pl.ds(k * nodes + first, ROW_TILE), :] = (
                    share[c] * s + z[c] * factor
                ).astype(BF)

    near = near_ref[0]
    one_hot = (lax.broadcasted_iota(jnp.int32, (table, rows), 0) == near).astype(BF)
    grad_pre = pre_scr[...]
    ga_ref[...] += product(one_hot, grad_pre)
    lx = lx_ref[...].reshape(rows, H_P)
    gw_ref[...] += lax.dot_general(
        lx, grad_pre, (((0,), (0,)), ((), ())), preferred_element_type=F32
    )
    for start, width in LANE_BLOCKS:
        cols = pl.ds(start, width)
        grad_length = product_back(grad_pre, wn_ref[cols, :])
        grad_direct = [product_back(up_scr[c], vo_ref[cols, :]) for c in range(3)]
        for first in range(0, nodes, ROW_TILE):
            part = pl.ds(first, ROW_TILE)
            acc = [None] * 3
            for k in range(GROUP):
                at = k * nodes + first
                ratio = grad_length[at : at + ROW_TILE] * pl.reciprocal(
                    lx_ref[k, part, cols].astype(F32), approx=True
                )
                if start == 512:
                    lane = lax.broadcasted_iota(jnp.int32, (ROW_TILE, width), 1)
                    ratio = jnp.where(lane == 0, ratio, 0.0)
                for c in range(3):
                    g = grad_direct[c][at : at + ROW_TILE] + ratio * h_ref[
                        k, c, part, cols
                    ].astype(F32)
                    gh_scr[c, pl.ds(at, ROW_TILE), cols] = g.astype(BF)
                    acc[c] = g if acc[c] is None else acc[c] + g
            for c in range(3):
                gq_ref[c, part, cols] += acc[c]
    for c in range(3):
        evr = jnp.broadcast_to(evr_ref[0, c : c + 1, :], (16, rows))
        lead = jnp.concatenate([one_hot, evr.astype(BF)], axis=0)
        gp_ref[c] += product(lead, gh_scr[c])
        gvo_ref[...] += lax.dot_general(
            up_scr[c],
            h_ref[:, c, :, :].reshape(rows, H_P),
            (((0,), (0,)), ((), ())),
            preferred_element_type=F32,
        )


def edge_backward(near_row, ev_col, ev_row, hidden, lx, dsilu, update, gs, gv, wn, vout, table):
    nodes = gs.shape[0]
    rows = GROUP * nodes
    whole = lambda shape: pl.BlockSpec(shape, lambda g: (0,) * len(shape))
    slots = lambda *shape: pl.BlockSpec((GROUP,) + shape, lambda g: (g,) + (0,) * len(shape))
    steps = lambda *shape: pl.BlockSpec((1,) + shape, lambda g: (g,) + (0,) * len(shape))
    outs = [
        (table, D_S),
        (H_P, D_S),
        (nodes, D_S),
        (3, table + 16, H_P),
        (3, nodes, H_P),
        (D_V, H_P),
    ]
    return pl.pallas_call(
        edge_backward_kernel,
        grid=(NEIGH // GROUP,),
        in_specs=[
            steps(1, rows),
            slots(nodes, 3),
            steps(3, rows),
            slots(3, nodes, H_P),
            slots(nodes, H_P),
            slots(nodes, D_S),
            slots(3, nodes, D_V),
            whole((nodes, D_S)),
            whole((3, nodes, D_V)),
            whole((H_P, D_S)),
            whole((H_P, D_V)),
        ],
        out_specs=[whole(shape) for shape in outs],
        out_shape=[jax.ShapeDtypeStruct(shape, F32) for shape in outs],
        scratch_shapes=[
            pltpu.VMEM((rows, D_S), BF),
            pltpu.VMEM((3, rows, D_V), BF),
            pltpu.VMEM((3, rows, H_P), BF),
        ],
        compiler_params=pltpu.CompilerParams(vmem_limit_bytes=VMEM_LIMIT),
        name="edge_backward",
    )(near_row, ev_col, ev_row, hidden, lx, dsilu, update, gs, gv, wn, vout)


AT_AIN, AT_EMB, AT_FFIN, AT_FFH, AT_NV, FAC_NODE = 0, 512, 1792, 3072, 3840, 4608
AT_GELU, AT_GUP, AT_FIN, AT_COT, AT_ATT, AT_GBR, FAC_FEED = 0, 2048, 4096, 4608, 5120, 5632, 6144
AT_GQKV, AT_STREAM, AT_GPRE, AT_GFU, AT_GFH, FAC_BACK = 0, 1536, 2048, 3072, 3840, 4608
ROWS_F, ROWS_M, ROWS_S, ROWS_T = 512, 768, 640, 128

def full_block(shape):
    return pl.BlockSpec(shape, lambda: (0,) * len(shape))


def lead_product(former, latter):
    return lax.dot_general(
        former, latter, (((0,), (0,)), ((), ())), preferred_element_type=F32
    )


def swap_halves(values):
    return pltpu.roll(values, 64, 1)


def lower_half(shape):
    return lax.broadcasted_iota(jnp.int32, shape, 1) < 64


def pack_tall(tile, odd):
    rows = tile.shape[0] // 2
    top, low = tile[:rows], tile[rows:]
    side = lower_half((rows, 128))
    if odd:
        return jnp.where(side, swap_halves(top), low)
    return jnp.where(side, top, swap_halves(low))


def unpack_tall(block):
    rows = block.shape[0]
    side = lower_half((rows, 128))
    return jnp.concatenate(
        [jnp.where(side, block, 0.0), jnp.where(side, swap_halves(block), 0.0)], 0
    )


def centre(values):
    centred = values - jnp.mean(values, axis=-1, keepdims=True)
    inverse = lax.rsqrt(jnp.mean(centred * centred, axis=-1, keepdims=True) + 1e-05)
    return centred * inverse, inverse


def centre_back(hat, inverse, grad):
    return inverse * (
        grad
        - jnp.mean(grad, axis=-1, keepdims=True)
        - hat * jnp.mean(grad * hat, axis=-1, keepdims=True)
    )


def power_of(parts):
    return parts[0] * parts[0] + parts[1] * parts[1] + parts[2] * parts[2]


def node_forward_kernel(
    ns_ref, nv_ref, as_ref, av_ref, ng_ref, fv_ref, fs_ref, fu_ref, we_ref, ag_ref, wq_ref,
    s1_ref, v1_ref, ffh_ref, ffp_ref, ffu_ref, v2_ref, sz_ref, fac_ref, out_ref,
):
    nodes = ns_ref.shape[0]
    s1 = ns_ref[...].astype(F32) + as_ref[...]
    s1_ref[...] = s1
    hat, unused = centre(s1)
    normed_s = hat * ng_ref[...]
    v1 = [nv_ref[c].astype(F32) + av_ref[c] for c in range(3)]
    scale = lax.rsqrt(jnp.mean(power_of(v1), axis=-1, keepdims=True) + 1e-05)
    normed_v = [v * scale for v in v1]
    ffh = [product(v.astype(BF), fv_ref[...]) for v in normed_v]
    power = power_of(ffh) + 1.0
    fac_ref[:, pl.ds(AT_FFIN, D_S)] = normed_s.astype(BF)
    fac_ref[:, pl.ds(AT_FFIN + D_S, D_V)] = (power * lax.rsqrt(power)).astype(BF)
    ffp = product(fac_ref[:, pl.ds(AT_FFIN, D_S + D_V)], fs_ref[...])
    ffu = [product(h.astype(BF), fu_ref[...]) for h in ffh]
    for c in range(3):
        v1_ref[c] = v1[c]
        fac_ref[:, pl.ds(AT_FFH + c * D_V, D_V)] = ffh[c].astype(BF)
        fac_ref[:, pl.ds(AT_NV + c * D_V, D_V)] = normed_v[c].astype(BF)
        ffh_ref[c] = ffh[c]
        ffu_ref[c] = ffu[c]
    ffp_ref[...] = ffp
    s2 = normed_s + ffp * sigmoid(ffp)
    power = power_of(ffu) + 1.0
    gate = sigmoid(power * lax.rsqrt(power))
    v2 = [normed_v[c] + ffu[c] * gate for c in range(3)]
    for c in range(3):
        v2_ref[c] = v2[c]
    power = power_of(v2) + 1.0
    fac_ref[:, pl.ds(AT_EMB, D_S)] = s2.astype(BF)
    fac_ref[:, pl.ds(AT_EMB + D_S, D_V)] = (power * lax.rsqrt(power)).astype(BF)
    sz = product(fac_ref[:, pl.ds(AT_EMB, D_S + D_V)], we_ref[...])
    sz_ref[...] = sz
    hat, unused = centre(sz)
    attn_in = (hat * ag_ref[...]).astype(BF)
    fac_ref[:, pl.ds(AT_AIN, D_MODEL)] = attn_in
    q, k, v = [product(attn_in, wq_ref[:, pl.ds(n * D_MODEL, D_MODEL)]) for n in range(3)]
    pack_heads(q, k, v, out_ref)


def pack_heads(q, k, v, out_ref):
    nodes = q.shape[0]
    side = lower_half((nodes, 128))
    for pair in range(HEADS // 2):
        cols = slice(pair * 128, pair * 128 + 128)
        qp, kp, vp = q[:, cols], k[:, cols], v[:, cols]
        even = jnp.where(side, qp, swap_halves(kp))
        odd = jnp.where(side, swap_halves(qp), kp)
        for n, block in enumerate((even, odd)):
            head = 2 * pair + n
            out_ref[head, pl.ds(0, nodes), :] = block.astype(BF)
            out_ref[head, pl.ds(nodes, nodes // 2), :] = pack_tall(vp, n == 1).astype(BF)


def node_forward(node_scalar, node_vector, agg_s, agg_v, *weights):
    nodes = node_scalar.shape[0]
    outs = [
        ((nodes, D_S), F32),
        ((3, nodes, D_V), F32),
        ((3, nodes, D_V), F32),
        ((nodes, D_S), F32),
        ((3, nodes, D_V), F32),
        ((3, nodes, D_V), F32),
        ((nodes, D_MODEL), F32),
        ((nodes, FAC_NODE), BF),
        ((HEADS, nodes + nodes // 2, 128), BF),
    ]
    return pl.pallas_call(
        node_forward_kernel,
        out_shape=[jax.ShapeDtypeStruct(shape, kind) for shape, kind in outs],
        compiler_params=pltpu.CompilerParams(vmem_limit_bytes=VMEM_LIMIT),
        name="node_forward",
    )(node_scalar, node_vector, agg_s, agg_v, *weights)


def split_heads(x_ref, nodes):
    spaces = x_ref.shape[0]
    both = x_ref[:, pl.ds(0, nodes), :].reshape(spaces * nodes, 128).astype(F32)
    queries = jnp.where(lower_half(both.shape), both, 0.0).astype(BF)
    keys = swap_halves(both).astype(BF)
    values = jnp.concatenate(
        [unpack_tall(x_ref[d, pl.ds(nodes, nodes // 2), :].astype(F32)) for d in range(spaces)], 0
    ).astype(BF)
    return queries, keys, values


def attend_kernel(x_ref, id_ref, probs_ref, att_ref, out_ref):
    spaces = x_ref.shape[0]
    nodes = x_ref.shape[1] * 2 // 3
    count = spaces * nodes
    queries, keys, values = split_heads(x_ref, nodes)
    row_ids = id_ref[...]
    column_ids = jnp.transpose(jnp.broadcast_to(row_ids, (8, count)))[:, 0:1]
    block = 2 * nodes
    for first in range(0, count, block):
        scores = product_back(queries[first : first + block], keys) * HEAD_DIM ** (-0.5)
        same = column_ids[first : first + block] == row_ids
        scores = jnp.where(same, scores, -1000000000.0)
        shifted = jnp.exp(scores - jnp.max(scores, axis=-1, keepdims=True))
        probs = (shifted / jnp.sum(shifted, axis=-1, keepdims=True)).astype(BF)
        probs_ref[pl.ds(first, block), :] = probs
        att = product(probs, values)
        att_ref[pl.ds(first, block), :] = att
        for n in range(block // nodes):
            tile = att[n * nodes : (n + 1) * nodes]
            out_ref[first // nodes + n] = pack_tall(tile, False).astype(BF)


def attend(heads_in, ids):
    spaces, tall, unused = heads_in.shape
    nodes = tall * 2 // 3
    count = spaces * nodes
    outs = [((count, count), BF), ((count, 128), F32), ((spaces, nodes // 2, 128), BF)]
    return pl.pallas_call(
        attend_kernel,
        out_shape=[jax.ShapeDtypeStruct(shape, kind) for shape, kind in outs],
        compiler_params=pltpu.CompilerParams(vmem_limit_bytes=VMEM_LIMIT),
        name="attend",
    )(heads_in, ids)


def attend_backward_kernel(x_ref, probs_ref, att_ref, g_ref, out_ref, gs_scr):
    spaces = x_ref.shape[0]
    nodes = x_ref.shape[1] * 2 // 3
    count = spaces * nodes
    queries, keys, values = split_heads(x_ref, nodes)
    grad = jnp.concatenate(
        [unpack_tall(g_ref[d].astype(F32)) for d in range(spaces)], 0
    )
    dots = jnp.sum(grad * att_ref[...], axis=-1, keepdims=True)
    grad = grad.astype(BF)
    block = 2 * nodes
    scale = HEAD_DIM ** (-0.5)
    grad_queries = []
    for first in range(0, count, block):
        grad_probs = product_back(grad[first : first + block], values)
        part = probs_ref[pl.ds(first, block), :].astype(F32)
        grad_scores = (part * (grad_probs - dots[first : first + block])).astype(BF)
        gs_scr[pl.ds(first, block), :] = grad_scores
        grad_queries.append(product(grad_scores, keys))
    grad_queries = jnp.concatenate(grad_queries, 0) * scale
    grad_keys = jnp.transpose(lead_product(queries, gs_scr[...])) * scale
    grad_values = jnp.transpose(lead_product(grad, probs_ref[...]))
    side = lower_half((nodes, 128))
    for d in range(spaces):
        rows = slice(d * nodes, (d + 1) * nodes)
        out_ref[d, pl.ds(0, nodes), :] = jnp.where(
            side, grad_queries[rows], swap_halves(grad_keys[rows])
        ).astype(BF)
        out_ref[d, pl.ds(nodes, nodes // 2), :] = pack_tall(grad_values[rows], False).astype(BF)


def attend_backward(heads_in, probs, att, grad_in):
    count = probs.shape[0]
    return pl.pallas_call(
        attend_backward_kernel,
        out_shape=jax.ShapeDtypeStruct(heads_in.shape, BF),
        scratch_shapes=[pltpu.VMEM((count, count), BF)],
        compiler_params=pltpu.CompilerParams(vmem_limit_bytes=VMEM_LIMIT),
        name="attend_backward",
    )(heads_in, probs, att, grad_in)


def merge_heads(block_ref, first, half):
    tiles = []
    for pair in range(HEADS // 2):
        even = unpack_tall(block_ref[2 * pair, pl.ds(first, half), :].astype(F32))
        odd = unpack_tall(block_ref[2 * pair + 1, pl.ds(first, half), :].astype(F32))
        tiles.append(even + swap_halves(odd))
    return jnp.concatenate(tiles, 1)


def feed_kernel(
    att_ref, sz_ref, wo_ref, fg_ref, wu_ref, wd_ref, cot_ref,
    out_ref, gatt_ref, gs1_ref, ggain_ref, fac_ref,
):
    nodes = sz_ref.shape[0]
    att = merge_heads(att_ref, 0, nodes // 2).astype(BF)
    fac_ref[:, pl.ds(AT_ATT, D_MODEL)] = att
    stream_one = sz_ref[...] + product(att, wo_ref[...])
    hat, inverse = centre(stream_one)
    ffn_in = (hat * fg_ref[...]).astype(BF)
    fac_ref[:, pl.ds(AT_FIN, D_MODEL)] = ffn_in
    ffn = wu_ref.shape[1]
    cot = cot_ref[...]
    fac_ref[:, pl.ds(AT_COT, D_MODEL)] = cot
    for start in range(0, ffn, 512):
        cols = pl.ds(start, 512)
        x = product(ffn_in, wu_ref[:, cols])
        cdf = 0.5 * (1.0 + lax.erf(x * (0.5**0.5)))
        fac_ref[:, pl.ds(AT_GELU + start, 512)] = (x * cdf).astype(BF)
        slope = cdf + x * jnp.exp(-0.5 * x * x) * ((0.5 / math.pi) ** 0.5)
        fac_ref[:, pl.ds(AT_GUP + start, 512)] = (
            product_back(cot, wd_ref[cols, :]) * slope
        ).astype(BF)
    out_ref[...] = (
        stream_one + product(fac_ref[:, pl.ds(AT_GELU, ffn)], wd_ref[...])
    ).astype(BF)
    grad_in = product_back(fac_ref[:, pl.ds(AT_GUP, ffn)], wu_ref[...])
    ggain_ref[...] = jnp.sum(grad_in * hat, axis=0, keepdims=True)
    grad_one = cot.astype(F32) + centre_back(hat, inverse, grad_in * fg_ref[...])
    gs1_ref[...] = grad_one
    branch = grad_one.astype(BF)
    fac_ref[:, pl.ds(AT_GBR, D_MODEL)] = branch
    grad_att = product_back(branch, wo_ref[...])
    for head in range(HEADS):
        tile = grad_att[:, head // 2 * 128 : head // 2 * 128 + 128]
        gatt_ref[head] = pack_tall(tile, head % 2 == 1).astype(BF)


def feed(att_in, stream_zero, w_out, gain, w_up, w_down, cotangent):
    nodes = stream_zero.shape[0]
    outs = [
        ((nodes, D_MODEL), BF),
        (att_in.shape, BF),
        ((nodes, D_MODEL), F32),
        ((1, D_MODEL), F32),
        ((nodes, FAC_FEED), BF),
    ]
    return pl.pallas_call(
        feed_kernel,
        out_shape=[jax.ShapeDtypeStruct(shape, kind) for shape, kind in outs],
        compiler_params=pltpu.CompilerParams(vmem_limit_bytes=VMEM_LIMIT),
        name="feed",
    )(att_in, stream_zero, w_out, gain, w_up, w_down, cotangent)


def core_columns(values, core):
    values = values.astype(F32)
    side = lower_half((values.shape[0], 128))
    tiles = []
    for n in range(0, 512, 256):
        one, two = values[:, n : n + 128], values[:, n + 128 : n + 256]
        even = jnp.where(side, one, swap_halves(two))
        odd = jnp.where(side, swap_halves(one), two)
        tiles.append(jnp.where(core == 0, even, odd))
    return jnp.concatenate(tiles, 1).astype(BF)


def both_rows(own_ref, other_ref, start, width):
    return jnp.concatenate(
        [own_ref[:, pl.ds(start, width)], other_ref[:, pl.ds(start, width)]], 0
    )


def feed_grads_kernel(own_ref, other_ref, pack_ref):
    quads = pack_ref.shape[0]
    core = lax.rem(lax.axis_index("space"), 2)
    cot = both_rows(own_ref, other_ref, AT_COT, D_MODEL)
    for z in range(quads):
        start = pl.multiple_of(AT_GELU + (2 * z + core) * 256, 256)
        block = lead_product(both_rows(own_ref, other_ref, start, 256), cot)
        pack_ref[z, pl.ds(0, 256), :] = block.astype(BF)
    left = core_columns(both_rows(own_ref, other_ref, AT_FIN, D_MODEL), core)
    for n in range(4):
        block = lead_product(left, both_rows(own_ref, other_ref, AT_GUP + n * 512, 512)).astype(BF)
        for z in range(quads):
            pack_ref[z, pl.ds(256 + n * 64, 64), :] = block[z * 64 : (z + 1) * 64]


def feed_grads(own, other, quads):
    return pl.pallas_call(
        feed_grads_kernel,
        out_shape=jax.ShapeDtypeStruct((quads, ROWS_F, 512), BF),
        compiler_params=pltpu.CompilerParams(vmem_limit_bytes=VMEM_LIMIT),
        name="feed_grads",
    )(own, other)


def node_grads_kernel(
    node_ref, node_other, back_ref, back_other, feed_ref, feed_other, pack_ref, tall_scr, low_scr
):
    quads = pack_ref.shape[0]
    core = lax.rem(lax.axis_index("space"), 2)
    left = core_columns(both_rows(node_ref, node_other, AT_AIN, D_MODEL), core)
    pairs = [
        (left, both_rows(back_ref, back_other, AT_GQKV + n * D_MODEL, D_MODEL)) for n in range(3)
    ]
    pairs.append(
        (
            core_columns(both_rows(feed_ref, feed_other, AT_ATT, D_MODEL), core),
            both_rows(feed_ref, feed_other, AT_GBR, D_MODEL),
        )
    )
    for n, (one, two) in enumerate(pairs):
        block = lead_product(one, two).astype(BF)
        for z in range(quads):
            pack_ref[z, pl.ds(n * 64, 64), :] = block[z * 64 : (z + 1) * 64]
    emb = both_rows(node_ref, node_other, AT_EMB, D_S + D_V)
    ffin = both_rows(node_ref, node_other, AT_FFIN, D_S + D_V)
    rights = [(emb, back_ref, back_other, AT_STREAM)]
    rights += [(ffin, back_ref, back_other, AT_GPRE + n * 512) for n in range(2)]
    for n, (one, own, other, start) in enumerate(rights):
        tall_scr[...] = lead_product(one, both_rows(own, other, start, 512)).astype(BF)
        for z in range(quads):
            rows = pl.ds(pl.multiple_of((2 * z + core) * 160, 32), 160)
            pack_ref[z, pl.ds(256 + n * 160, 160), :] = tall_scr[rows, :]
    vec = up = None
    for c in range(3):
        one = lead_product(
            both_rows(node_ref, node_other, AT_NV + c * D_V, D_V),
            both_rows(back_ref, back_other, AT_GFH + c * D_V, D_V),
        )
        vec = one if vec is None else vec + one
        one = lead_product(
            both_rows(node_ref, node_other, AT_FFH + c * D_V, D_V),
            both_rows(back_ref, back_other, AT_GFU + c * D_V, D_V),
        )
        up = one if up is None else up + one
    low_scr[...] = jnp.concatenate([vec, up], 1).astype(BF)
    for z in range(quads):
        rows = pl.ds(pl.multiple_of((2 * z + core) * 32, 32), 32)
        pack_ref[z, pl.ds(736, 32), :] = low_scr[rows, :]


def node_grads(quads, *factors):
    return pl.pallas_call(
        node_grads_kernel,
        out_shape=jax.ShapeDtypeStruct((quads, ROWS_M, 512), BF),
        scratch_shapes=[pltpu.VMEM((D_S + D_V, 512), BF), pltpu.VMEM((D_V, 512), BF)],
        compiler_params=pltpu.CompilerParams(vmem_limit_bytes=VMEM_LIMIT),
        name="node_grads",
    )(*factors)


def node_backward_kernel(
    gq_ref, gs1_ref, s1_ref, v1_ref, ffh_ref, ffp_ref, ffu_ref, v2_ref,
    sz_ref, ng_ref, fv_ref, fs_ref, fu_ref, we_ref, ag_ref, wq_ref, fgain_ref,
    gsone_ref, gvone_ref, gains_ref, back_ref,
):
    nodes = gs1_ref.shape[0]
    shards = gq_ref.shape[0]
    side = lower_half((nodes, 128))
    tiles = [[], []]
    for pair in range(HEADS // 2):
        even = gq_ref[2 * pair, pl.ds(0, nodes), :].astype(F32)
        odd = gq_ref[2 * pair + 1, pl.ds(0, nodes), :].astype(F32)
        tiles[0].append(jnp.where(side, even, swap_halves(odd)))
        tiles[1].append(jnp.where(side, swap_halves(even), odd))
    grads = [jnp.concatenate(tile, 1).astype(BF) for tile in tiles]
    grads.append(merge_heads(gq_ref, nodes, nodes // 2).astype(BF))
    for n in range(3):
        back_ref[:, pl.ds(AT_GQKV + n * D_MODEL, D_MODEL)] = grads[n]
    grad_in = product_back(back_ref[:, pl.ds(AT_GQKV, 3 * D_MODEL)], wq_ref[...])
    hat, inverse = centre(sz_ref[...])
    grad_attn_gain = jnp.sum(grad_in * hat, axis=0, keepdims=True)
    stream = gs1_ref[...] + centre_back(hat, inverse, grad_in * ag_ref[...])
    stream = stream.astype(BF)
    back_ref[:, pl.ds(AT_STREAM, D_MODEL)] = stream
    grad_emb = product_back(stream, we_ref[...])
    grad_s2, grad_len = grad_emb[:, :D_S], grad_emb[:, D_S:]
    v2 = [v2_ref[c] for c in range(3)]
    factor = grad_len * lax.rsqrt(power_of(v2) + 1.0)
    grad_v2 = [factor * v for v in v2]
    x = ffp_ref[...]
    s = sigmoid(x)
    grad_pre = (grad_s2 * (s + x * s * (1.0 - s))).astype(BF)
    back_ref[:, pl.ds(AT_GPRE, D_S)] = grad_pre
    grad_ffin = product_back(grad_pre, fs_ref[...])
    z = [ffu_ref[c] for c in range(3)]
    power = power_of(z) + 1.0
    inverse = lax.rsqrt(power)
    s = sigmoid(power * inverse)
    dot = z[0] * grad_v2[0] + z[1] * grad_v2[1] + z[2] * grad_v2[2]
    factor = dot * inverse * (s * (1.0 - s))
    grad_up = [(grad_v2[c] * s + z[c] * factor).astype(BF) for c in range(3)]
    h = [ffh_ref[c] for c in range(3)]
    factor = grad_ffin[:, D_S:] * lax.rsqrt(power_of(h) + 1.0)
    v1 = [v1_ref[c] for c in range(3)]
    scale = lax.rsqrt(jnp.mean(power_of(v1), axis=-1, keepdims=True) + 1e-05)
    grad_nv = []
    for c in range(3):
        back_ref[:, pl.ds(AT_GFU + c * D_V, D_V)] = grad_up[c]
        grad_h = (product_back(grad_up[c], fu_ref[...]) + factor * h[c]).astype(BF)
        back_ref[:, pl.ds(AT_GFH + c * D_V, D_V)] = grad_h
        grad_nv.append(grad_v2[c] + product_back(grad_h, fv_ref[...]))
    grad_ns = grad_s2 + grad_ffin[:, :D_S]
    hat, inverse = centre(s1_ref[...])
    grad_norm_gain = jnp.sum(grad_ns * hat, axis=0, keepdims=True)
    gsone_ref[...] = centre_back(hat, inverse, grad_ns * ng_ref[...])
    dot = grad_nv[0] * v1[0] + grad_nv[1] * v1[1] + grad_nv[2] * v1[2]
    dot = jnp.mean(dot, axis=-1, keepdims=True) * scale * scale
    for c in range(3):
        gvone_ref[c] = scale * (grad_nv[c] - v1[c] * dot)
    gains_ref[...] = jnp.zeros_like(gains_ref)
    gains_ref[0:1, :] = grad_norm_gain
    for p in range(shards):
        pair = slice(p // 2 * 128, p // 2 * 128 + 128)
        left = jnp.broadcast_to(grad_attn_gain[:, pair], (8, 128))
        right = jnp.broadcast_to(fgain_ref[:, pair], (8, 128))
        if p % 2 == 0:
            both = jnp.where(lower_half((8, 128)), left, swap_halves(right))
        else:
            both = jnp.where(lower_half((8, 128)), swap_halves(left), right)
        gains_ref[1:2, pl.ds(p * 128, 128)] = both[0:1]


def node_backward(grad_heads, *values):
    nodes = values[0].shape[0]
    outs = [
        ((nodes, D_S), F32),
        ((3, nodes, D_V), F32),
        ((8, D_S), F32),
        ((nodes, FAC_BACK), BF),
    ]
    return pl.pallas_call(
        node_backward_kernel,
        out_shape=[jax.ShapeDtypeStruct(shape, kind) for shape, kind in outs],
        compiler_params=pltpu.CompilerParams(vmem_limit_bytes=VMEM_LIMIT),
        name="node_backward",
    )(grad_heads, *values)


def place():
    dp, space = lax.axis_index("dp"), lax.axis_index("space")
    return {"x": lax.rem(dp, 2), "y": dp // 2, "z": space // 2, "core": lax.rem(space, 2)}


def peer(way, shift=1):
    at = place()
    if way == "x":
        return {"dp": 2 * at["y"] + 1 - at["x"]}
    if way == "y":
        return {"dp": 2 * (1 - at["y"]) + at["x"]}
    if way == "diagonal":
        return {"dp": 2 * (1 - at["y"]) + 1 - at["x"]}
    if way == "core":
        return {"space": 2 * at["z"] + 1 - at["core"]}
    if way == "z":
        return {"space": 2 * lax.rem(at["z"] + shift, 4) + at["core"]}
    return {"space": lax.rem(lax.axis_index("space") + shift, lax.axis_size("space"))}


def greet(peers):
    barrier = pltpu.get_barrier_semaphore()
    for one in peers:
        pl.semaphore_signal(barrier, inc=1, device_id=one, device_id_type=MESH)
    pl.semaphore_wait(barrier, len(peers))


class Wires:
    def __init__(self, send_sem, recv_sem):
        self.send_sem, self.recv_sem, self.used = send_sem, recv_sem, 0

    def copy(self, source, target, to):
        n = self.used
        self.used += 1
        return pltpu.make_async_remote_copy(
            src_ref=source,
            dst_ref=target,
            send_sem=self.send_sem.at[n],
            recv_sem=self.recv_sem.at[n],
            device_id=to,
            device_id_type=MESH,
        )


def rows_at(ref, start, count):
    return ref.at[:, pl.ds(start, count), :]


def first_cut(wires, share_ref, got_ref):
    at = place()
    quarter = share_ref.shape[1] // 4
    return [
        wires.copy(rows_at(share_ref, (1 - at["x"]) * quarter, quarter), got_ref.at[0], peer("x")),
        wires.copy(
            rows_at(share_ref, (3 - at["y"]) * quarter, quarter), got_ref.at[1], peer("y")
        ),
    ]


def first_add(share_ref, got_ref, sum_ref):
    at = place()
    quarter = share_ref.shape[1] // 4
    for n, start in enumerate((at["x"] * quarter, (2 + at["y"]) * quarter)):
        own = share_ref[:, pl.ds(pl.multiple_of(start, 16), quarter), :]
        sum_ref[n] = (own.astype(F32) + got_ref[n].astype(F32)).astype(BF)


def second_cut(wires, sum_ref, got_ref):
    at = place()
    eighth = sum_ref.shape[2] // 2
    return [
        wires.copy(
            rows_at(sum_ref.at[0], (1 - at["y"]) * eighth, eighth), got_ref.at[0], peer("y")
        ),
        wires.copy(
            rows_at(sum_ref.at[1], (1 - at["x"]) * eighth, eighth), got_ref.at[1], peer("x")
        ),
    ]


def second_add(sum_ref, got_ref, out_ref, base=0):
    at = place()
    eighth = sum_ref.shape[2] // 2
    for n, start in enumerate((at["y"] * eighth, at["x"] * eighth)):
        own = sum_ref[n, :, pl.ds(pl.multiple_of(start, 16), eighth), :]
        out_ref[:, pl.ds(base + n * eighth, eighth), :] = (
            own.astype(F32) + got_ref[n].astype(F32)
        ).astype(BF)


def z_send(wires, part_ref, got_ref):
    at = place()
    return [
        wires.copy(
            part_ref.at[lax.rem(at["z"] + shift, 4)], got_ref.at[shift - 1], peer("z", shift)
        )
        for shift in (1, 2, 3)
    ]


def z_add(part_ref, got_ref):
    total = part_ref[place()["z"]].astype(F32)
    for n in range(3):
        total = total + got_ref[n].astype(F32)
    return total.astype(BF)


def start_all(copies):
    for copy in copies:
        copy.start()
    return copies


def wait_all(copies):
    for copy in copies:
        copy.wait()


def links_kernel(blocks, pairs, cut, *refs):
    refs = list(refs)
    take = lambda count: [refs.pop(0) for unused in range(count)]
    x_refs = take(blocks)
    pair_refs = take(pairs)
    share_refs = take(1 if cut else 0)
    y_refs = take(blocks)
    pair_outs = take(pairs)
    cut_outs = take(1 if cut else 0)
    send_sem, recv_sem, own_sem = take(3)
    got_refs = take(1 if cut else 0)
    wires = Wires(send_sem, recv_sem)
    spaces = lax.axis_size("space")
    ring = [peer("group", shift) for shift in range(1, spaces)] if blocks else []
    greeted = ring + ([] if blocks or not pairs else [peer("core")])
    greet(greeted + ([peer("x"), peer("y")] if cut else []))
    me = lax.axis_index("space")
    copies = []
    for x_ref, y_ref in zip(x_refs, y_refs):
        copies += start_all(
            [
                wires.copy(x_ref.at[lax.rem(me + n + 1, spaces)], y_ref.at[me], ring[n])
                for n in range(spaces - 1)
            ]
        )
    cuts = []
    if cut == 1:
        cuts = start_all(first_cut(wires, share_refs[0], got_refs[0]))
    if cut == 2:
        cuts = start_all(second_cut(wires, share_refs[0], got_refs[0]))
    for source, target in zip(pair_refs, pair_outs):
        copies += start_all([wires.copy(source, target, peer("core"))])
    for x_ref, y_ref in zip(x_refs, y_refs):
        own = pltpu.make_async_copy(x_ref.at[me], y_ref.at[me], own_sem)
        own.start()
        own.wait()
    wait_all(cuts)
    if cut == 1:
        first_add(share_refs[0], got_refs[0], cut_outs[0])
    if cut == 2:
        second_add(share_refs[0], got_refs[0], cut_outs[0])
    wait_all(copies)


def links(collective_id, blocks=None, pairs=(), cut=0, share=None):
    hbm = pl.BlockSpec(memory_space=pl.ANY)
    vmem = pl.BlockSpec(memory_space=pltpu.VMEM)
    operands = ([] if blocks is None else [blocks]) + list(pairs)
    outs = [jax.ShapeDtypeStruct(one.shape, one.dtype) for one in operands]
    in_specs = [hbm] * len(operands)
    out_specs = [hbm] * len(operands)
    scratch = []
    count = len(pairs) + (0 if blocks is None else blocks.shape[0] - 1)
    if cut == 1:
        quads, rows, width = share.shape
        shape = (2, quads, rows // 4, width)
        outs.append(jax.ShapeDtypeStruct(shape, BF))
        scratch = [pltpu.VMEM(shape, BF)]
    if cut == 2:
        unused, quads, rows, width = share.shape
        outs.append(jax.ShapeDtypeStruct((quads, rows, width), BF))
        scratch = [pltpu.VMEM((2, quads, rows // 2, width), BF)]
    if cut:
        operands.append(share)
        in_specs.append(vmem)
        out_specs.append(vmem)
        count += 2
    return pl.pallas_call(
        functools.partial(links_kernel, 0 if blocks is None else 1, len(pairs), cut),
        out_shape=outs,
        in_specs=in_specs,
        out_specs=out_specs,
        scratch_shapes=[
            pltpu.SemaphoreType.DMA((count,)),
            pltpu.SemaphoreType.DMA((count,)),
            pltpu.SemaphoreType.DMA,
        ]
        + scratch,
        compiler_params=pltpu.CompilerParams(
            collective_id=collective_id, has_side_effects=True, vmem_limit_bytes=VMEM_LIMIT
        ),
        name="links",
    )(*operands)


def scalar_backward_kernel(
    near_ref, lx_ref, ds_ref, gsone_ref, wn_ref, ts_ref, ns_ref, wnode_ref, tso_ref, nso_ref,
    m_ref, f_ref,
    ratio_ref, pack_ref, rest_ref, gscal_ref, back_ref, m2_ref, ffin_ref,
    ga_ref, gw_ref, gb_ref, pre_scr, grads_scr, grads_got, mix_scr, mix_got, rest_scr, rest_got,
    m_got, m_sum, m_got2, f_got, send_sem, recv_sem,
):
    nodes = gsone_ref.shape[0]
    table = ts_ref.shape[0]
    rows = GROUP * nodes
    quads = pack_ref.shape[0]
    step = pl.program_id(0)
    last = pl.num_programs(0) - 1
    wires = Wires(send_sem, recv_sem)
    f_copies = z_send(wires, f_ref, f_got)
    m_copies = first_cut(wires, m_ref, m_got)
    m_copies2 = second_cut(wires, m_sum, m_got2)
    pair_copies = [
        wires.copy(source, target, peer("core"))
        for source, target in ((grads_scr, grads_got), (mix_scr, mix_got), (rest_scr, rest_got))
    ]

    @pl.when(step == 0)
    def _():
        greet([peer("x"), peer("y"), peer("core")] + [peer("z", shift) for shift in (1, 2, 3)])
        start_all(m_copies)
        start_all(f_copies)
        for ref in (ga_ref, gw_ref, gb_ref):
            ref[...] = jnp.zeros_like(ref)

    @pl.when(step == 4)
    def _():
        wait_all(m_copies)
        first_add(m_ref, m_got, m_sum)
        start_all(m_copies2)

    for start in range(0, D_S, 256):
        cols = pl.ds(start, 256)
        for first in range(0, nodes, ROW_TILE):
            part = pl.ds(first, ROW_TILE)
            share = gsone_ref[part, cols] * (1.0 / NEIGH)
            acc = None
            for k in range(GROUP):
                g = (ds_ref[k, part, cols].astype(F32) * share).astype(BF)
                pre_scr[pl.ds(k * nodes + first, ROW_TILE), cols] = g
                g = g.astype(F32)
                acc = g if acc is None else acc + g
            gb_ref[part, cols] += acc
    one_hot = (lax.broadcasted_iota(jnp.int32, (table, rows), 0) == near_ref[0]).astype(BF)
    grad_pre = pre_scr[...]
    ga_ref[...] += product(one_hot, grad_pre)
    lx = lx_ref[...].reshape(rows, H_P)
    gw_ref[...] += lead_product(lx, grad_pre)
    for start, width in LANE_BLOCKS:
        cols = pl.ds(start, width)
        grad_length = product_back(grad_pre, wn_ref[cols, :])
        for first in range(0, nodes, ROW_TILE):
            part = pl.ds(first, ROW_TILE)
            for k in range(GROUP):
                at = k * nodes + first
                ratio = grad_length[at : at + ROW_TILE] * pl.reciprocal(
                    lx_ref[k, part, cols].astype(F32), approx=True
                )
                if start == 512:
                    lane = lax.broadcasted_iota(jnp.int32, (ROW_TILE, width), 1)
                    ratio = jnp.where(lane == 0, ratio, 0.0)
                ratio_ref[k, part, cols] = ratio.astype(BF)

    @pl.when(step == last)
    def _():
        core = place()["core"]
        grads_scr[pl.ds(0, table), :] = ga_ref[...].astype(BF)
        grads_scr[pl.ds(table, nodes), :] = gb_ref[...].astype(BF)
        for z in range(quads):
            away = pl.ds(pl.multiple_of((2 * z + 1 - core) * 128, 128), 128)
            for r in range(4):
                mix_scr[z, :, pl.ds(r * 128, 128)] = gw_ref[pl.ds(r * 128, 128), away].astype(BF)
            rest_scr[z] = gw_ref[pl.ds(512, 64), away].astype(BF)
        start_all(pair_copies)
        ga = grads_scr[pl.ds(0, table), :]
        gb = grads_scr[pl.ds(table, nodes), :]
        projected = product_back(ga, wnode_ref[:, pl.ds(0, D_S)])
        gscal_ref[...] = (
            gsone_ref[...] + product_back(gb, wnode_ref[:, pl.ds(D_S, D_S)]) + projected[:nodes]
        )
        back_ref[...] = projected[nodes:].astype(BF)
        wait_all(pair_copies)
        gao = grads_got[pl.ds(0, table), :]
        gbo = grads_got[pl.ds(table, nodes), :]
        for z in range(quads):
            own = pl.ds(pl.multiple_of((2 * z + core) * 128, 128), 128)
            for half, (left, right, lefto, righto) in enumerate(
                ((ts_ref, ga, tso_ref, gao), (ns_ref, gb, nso_ref, gbo))
            ):
                block = lead_product(left[:, own], right) + lead_product(lefto[:, own], righto)
                block = block.astype(BF)
                for n in range(2):
                    pack_ref[z, pl.ds((2 * half + n) * 128, 128), :] = block[
                        :, n * 512 : (n + 1) * 512
                    ]
            for r in range(4):
                lanes = pl.ds(r * 128, 128)
                pack_ref[z, pl.ds(512, 128), lanes] = (
                    gw_ref[pl.ds(r * 128, 128), own] + mix_got[z, :, lanes].astype(F32)
                ).astype(BF)
            rest_ref[z] = gw_ref[pl.ds(512, 64), own] + rest_got[z].astype(F32)
        wait_all(m_copies2)
        second_add(m_sum, m_got2, m2_ref)
        wait_all(f_copies)
        ffin_ref[...] = z_add(f_ref, f_got)


def scalar_backward(near_row, lx, dsilu, gsone, wn, ts, ns, w_node, ts_other, ns_other, m, f):
    nodes = gsone.shape[0]
    table = ts.shape[0]
    quads = m.shape[0]
    rows = GROUP * nodes
    once = pl.Buffered(1)
    whole = lambda shape: pl.BlockSpec(shape, lambda g: (0,) * len(shape), pipeline_mode=once)
    slots = lambda *shape: pl.BlockSpec((GROUP,) + shape, lambda g: (g,) + (0,) * len(shape))
    steps = lambda *shape: pl.BlockSpec((1,) + shape, lambda g: (g,) + (0,) * len(shape))
    outs = [
        ((quads, ROWS_S, 512), BF),
        ((quads, 64, 128), F32),
        ((nodes, D_S), F32),
        ((table - nodes, D_S), BF),
        ((quads, ROWS_M // 4, 512), BF),
        ((ROWS_F // 4, 512), BF),
    ]
    return pl.pallas_call(
        scalar_backward_kernel,
        grid=(NEIGH // GROUP,),
        in_specs=[steps(1, rows), slots(nodes, H_P), slots(nodes, D_S)]
        + [whole(one.shape) for one in (gsone, wn, ts, ns, w_node, ts_other, ns_other, m, f)],
        out_specs=[slots(nodes, H_P)] + [whole(shape) for shape, kind in outs],
        out_shape=[jax.ShapeDtypeStruct((NEIGH, nodes, H_P), BF)]
        + [jax.ShapeDtypeStruct(shape, kind) for shape, kind in outs],
        scratch_shapes=[
            pltpu.VMEM((table, D_S), F32),
            pltpu.VMEM((H_P, D_S), F32),
            pltpu.VMEM((nodes, D_S), F32),
            pltpu.VMEM((rows, D_S), BF),
            pltpu.VMEM((table + nodes, D_S), BF),
            pltpu.VMEM((table + nodes, D_S), BF),
            pltpu.VMEM((quads, 128, 512), BF),
            pltpu.VMEM((quads, 128, 512), BF),
            pltpu.VMEM((quads, 64, 128), BF),
            pltpu.VMEM((quads, 64, 128), BF),
            pltpu.VMEM((2, quads, ROWS_M // 4, 512), BF),
            pltpu.VMEM((2, quads, ROWS_M // 4, 512), BF),
            pltpu.VMEM((2, quads, ROWS_M // 8, 512), BF),
            pltpu.VMEM((3, ROWS_F // 4, 512), BF),
            pltpu.SemaphoreType.DMA((10,)),
            pltpu.SemaphoreType.DMA((10,)),
        ],
        compiler_params=pltpu.CompilerParams(
            collective_id=5, has_side_effects=True, vmem_limit_bytes=VMEM_LIMIT
        ),
        name="scalar_backward",
    )(near_row, lx, dsilu, gsone, wn, ts, ns, w_node, ts_other, ns_other, m, f)


def vector_backward_kernel(
    near_ref, ev_ref, evr_ref, h_ref, ratio_ref, z_ref, gvone_ref, vo_ref, tv_ref,
    nv_ref, vs_ref, vt_ref, rest_ref, gains_ref, s_ref, m_ref, f_ref, backs_ref,
    plane_ref, gvec_ref, got_ref, gp_ref, gq_ref, gvo_ref, up_scr, gh_scr,
    s_got, s_sum, s_got2, s_part, s_gotz, m_gotz, t_scr, t_got, t_half, t_got1, t_sum, t_got2,
    t_part, t_gotz, back_scr, fin_scr, own_sem, send_sem, recv_sem,
):
    nodes = gvone_ref.shape[1]
    table = tv_ref.shape[1]
    rows = GROUP * nodes
    spaces = lax.axis_size("space")
    quads = spaces // 2
    step = pl.program_id(0)
    last = pl.num_programs(0) - 1
    at = place()
    me = lax.axis_index("space")
    mine = 2 * at["x"] + at["y"]
    wires = Wires(send_sem, recv_sem)
    early, late = ROWS_F // 4 + ROWS_M // 4, ROWS_S // 4 + ROWS_T // 4
    ring = [peer("group", shift) for shift in range(1, spaces)]
    plane = [peer("x"), peer("y"), peer("diagonal")]
    s_copies = first_cut(wires, s_ref, s_got)
    s_copies2 = second_cut(wires, s_sum, s_got2)
    s_copiesz = z_send(wires, s_part, s_gotz)
    m_copiesz = z_send(wires, m_ref, m_gotz)
    early_rows, late_rows = pl.ds(0, early), pl.ds(early, late)
    early_copies = [
        wires.copy(fin_scr.at[early_rows, :], plane_ref.at[mine, early_rows, :], to) for to in plane
    ]
    late_copies = [
        wires.copy(fin_scr.at[late_rows, :], plane_ref.at[mine, late_rows, :], to) for to in plane
    ]
    back_copies = [
        wires.copy(back_scr.at[lax.rem(me + n + 1, spaces)], got_ref.at[me], ring[n])
        for n in range(spaces - 1)
    ]
    t_pair = [wires.copy(t_scr.at[:, 1 - at["core"]], t_got, peer("core"))]
    t_copies = first_cut(wires, t_half, t_got1)
    t_copies2 = second_cut(wires, t_sum, t_got2)
    t_copiesz = z_send(wires, t_part, t_gotz)

    @pl.when(step == 0)
    def _():
        greet(ring + plane)
        start_all(s_copies)
        start_all(m_copiesz)
        for ref in (gp_ref, gq_ref, gvo_ref):
            ref[...] = jnp.zeros_like(ref)

    @pl.when(step == 3)
    def _():
        wait_all(s_copies)
        first_add(s_ref, s_got, s_sum)
        start_all(s_copies2)

    @pl.when(step == last)
    def _():
        wait_all(s_copies2)
        second_add(s_sum, s_got2, s_part)
        start_all(s_copiesz)
        wait_all(m_copiesz)
        fin_scr[pl.ds(0, ROWS_F // 4), :] = f_ref[...]
        fin_scr[pl.ds(ROWS_F // 4, ROWS_M // 4), :] = z_add(m_ref, m_gotz)
        start_all(early_copies)

    for first in range(0, nodes, ROW_TILE):
        part = pl.ds(first, ROW_TILE)
        share = [gvone_ref[c, part, :] * (1.0 / NEIGH) for c in range(3)]
        for k in range(GROUP):
            z = [z_ref[k, c, part, :].astype(F32) for c in range(3)]
            power = power_of(z) + 1.0
            inverse = lax.rsqrt(power)
            s = sigmoid(power * inverse)
            dot = z[0] * share[0] + z[1] * share[1] + z[2] * share[2]
            factor = dot * inverse * (s * (1.0 - s))
            for c in range(3):
                up_scr[c, pl.ds(k * nodes + first, ROW_TILE), :] = (
                    share[c] * s + z[c] * factor
                ).astype(BF)
    for start, width in LANE_BLOCKS:
        cols = pl.ds(start, width)
        grad_direct = [product_back(up_scr[c], vo_ref[cols, :]) for c in range(3)]
        for first in range(0, nodes, ROW_TILE):
            part = pl.ds(first, ROW_TILE)
            acc = [None] * 3
            for k in range(GROUP):
                row = k * nodes + first
                ratio = ratio_ref[k, part, cols].astype(F32)
                for c in range(3):
                    g = grad_direct[c][row : row + ROW_TILE] + ratio * h_ref[
                        k, c, part, cols
                    ].astype(F32)
                    gh_scr[c, pl.ds(row, ROW_TILE), cols] = g.astype(BF)
                    acc[c] = g if acc[c] is None else acc[c] + g
            for c in range(3):
                gq_ref[c, part, cols] += acc[c]
    one_hot = (lax.broadcasted_iota(jnp.int32, (table, rows), 0) == near_ref[0]).astype(BF)
    for c in range(3):
        evr = jnp.broadcast_to(evr_ref[0, c : c + 1, :], (16, rows))
        lead = jnp.concatenate([one_hot, evr.astype(BF)], axis=0)
        gp_ref[c] += product(lead, gh_scr[c])
        gvo_ref[...] += lead_product(up_scr[c], h_ref[:, c, :, :].reshape(rows, H_P))

    @pl.when(step == last)
    def _():
        tall = D_V // spaces
        gp = [gp_ref[c, pl.ds(0, table), :].astype(BF) for c in range(3)]
        gq = [gq_ref[c].astype(BF) for c in range(3)]
        for d in range(spaces):
            back_scr[d, :, pl.ds(0, D_S)] = backs_ref[pl.ds(d * CAP, CAP), :]
        for c in range(3):
            projected = product_back(gp[c], vs_ref[...])
            gvec_ref[c] = gvone_ref[c] + product_back(gq[c], vt_ref[...]) + projected[:nodes]
            for d in range(spaces):
                back_scr[d, :, pl.ds(D_S + c * D_V, D_V)] = projected[
                    nodes + d * CAP : nodes + (d + 1) * CAP
                ].astype(BF)
        start_all(back_copies)
        own = pltpu.make_async_copy(back_scr.at[me], got_ref.at[me], own_sem)
        own.start()
        grads = []
        for lead_ref, right in ((tv_ref, gp), (nv_ref, gq)):
            total = None
            for c in range(3):
                one = lead_product(lead_ref[c], right[c])
                total = one if total is None else total + one
            grads.append(total)
        grads.append(gvo_ref[...])
        lane = lax.broadcasted_iota(jnp.int32, (D_V, 128), 1)
        tails = jnp.zeros((D_V, 128), F32)
        for n, grad in enumerate(grads):
            for p in range(spaces):
                t_scr[p // 2, p % 2, pl.ds(n * tall, tall), :] = grad[
                    p * tall : (p + 1) * tall, :512
                ].astype(BF)
            tails = tails + jnp.where(
                lane == n, jnp.broadcast_to(grad[:, 512:513], (D_V, 128)), 0.0
            )
        tails = tails.astype(BF)
        vedge = gp_ref[0, pl.ds(table, 8), :] + gp_ref[1, pl.ds(table, 8), :]
        vedge = vedge + gp_ref[2, pl.ds(table, 8), :]
        row = lax.broadcasted_iota(jnp.int32, (tall, 128), 0)
        below = pl.ds(3 * tall, tall)
        for p in range(spaces):
            rest = jnp.where(at["core"] == p % 2, rest_ref[p // 2], 0.0)
            t_scr[p // 2, p % 2, below, pl.ds(0, 128)] = tails[p * tall : (p + 1) * tall]
            t_scr[p // 2, p % 2, below, pl.ds(128, 128)] = rest[1 : 1 + tall].astype(BF)
            extra = jnp.where(row == 0, jnp.broadcast_to(rest[0:1], (tall, 128)), 0.0)
            for n in range(5):
                piece = jnp.broadcast_to(vedge[0:1, n * 128 : (n + 1) * 128], (tall, 128))
                extra = jnp.where(row == 1 + n, piece, extra)
            for n in range(2):
                piece = jnp.broadcast_to(
                    gains_ref[n : n + 1, p * 128 : (p + 1) * 128], (tall, 128)
                )
                extra = jnp.where(row == 6 + n, piece, extra)
            t_scr[p // 2, p % 2, below, pl.ds(256, 128)] = extra.astype(BF)
            t_scr[p // 2, p % 2, below, pl.ds(384, 128)] = jnp.zeros((tall, 128), BF)
        start_all(t_pair)
        wait_all(t_pair)
        t_half[...] = (t_scr[:, at["core"]].astype(F32) + t_got[...].astype(F32)).astype(BF)
        start_all(t_copies)
        wait_all(t_copies)
        first_add(t_half, t_got1, t_sum)
        start_all(t_copies2)
        wait_all(t_copies2)
        second_add(t_sum, t_got2, t_part)
        start_all(t_copiesz)
        wait_all(s_copiesz)
        fin_scr[pl.ds(early, ROWS_S // 4), :] = z_add(s_part, s_gotz)
        wait_all(t_copiesz)
        fin_scr[pl.ds(early + ROWS_S // 4, ROWS_T // 4), :] = z_add(t_part, t_gotz)
        start_all(late_copies)
        own.wait()
        own_plane = pltpu.make_async_copy(fin_scr, plane_ref.at[mine], own_sem)
        own_plane.start()
        own_plane.wait()
        wait_all(back_copies)
        wait_all(early_copies)
        wait_all(late_copies)


def vector_backward(
    near_row, ev_col, ev_row, hidden, ratio, update, gvone, vout, tv, nv, vs, vt, rest, gains,
    s, m, f, back,
):
    nodes = gvone.shape[1]
    table = tv.shape[1]
    quads = s.shape[0]
    spaces = 2 * quads
    rows = GROUP * nodes
    once = pl.Buffered(1)
    whole = lambda shape: pl.BlockSpec(shape, lambda g: (0,) * len(shape), pipeline_mode=once)
    slots = lambda *shape: pl.BlockSpec((GROUP,) + shape, lambda g: (g,) + (0,) * len(shape))
    steps = lambda *shape: pl.BlockSpec((1,) + shape, lambda g: (g,) + (0,) * len(shape))
    outs = [
        ((4, (ROWS_F + ROWS_M + ROWS_S + ROWS_T) // 4, 512), BF),
        ((3, nodes, D_V), F32),
        ((spaces, CAP, D_S + 3 * D_V), BF),
    ]
    bits = lambda *shape: pltpu.VMEM(shape, BF)
    return pl.pallas_call(
        vector_backward_kernel,
        grid=(NEIGH // GROUP,),
        in_specs=[
            steps(1, rows),
            slots(nodes, 3),
            steps(3, rows),
            slots(3, nodes, H_P),
            slots(nodes, H_P),
            slots(3, nodes, D_V),
        ]
        + [whole(one.shape) for one in (gvone, vout, tv, nv, vs, vt, rest, gains, s, m, f, back)],
        out_specs=[
            pl.BlockSpec(memory_space=pl.ANY),
            whole(outs[1][0]),
            pl.BlockSpec(memory_space=pl.ANY),
        ],
        out_shape=[jax.ShapeDtypeStruct(shape, kind) for shape, kind in outs],
        scratch_shapes=[
            pltpu.VMEM((3, table + 16, H_P), F32),
            pltpu.VMEM((3, nodes, H_P), F32),
            pltpu.VMEM((D_V, H_P), F32),
            bits(3, rows, D_V),
            bits(3, rows, H_P),
            bits(2, quads, ROWS_S // 4, 512),
            bits(2, quads, ROWS_S // 4, 512),
            bits(2, quads, ROWS_S // 8, 512),
            bits(quads, ROWS_S // 4, 512),
            bits(3, ROWS_S // 4, 512),
            bits(3, ROWS_M // 4, 512),
            bits(quads, 2, ROWS_T, 512),
            bits(quads, ROWS_T, 512),
            bits(quads, ROWS_T, 512),
            bits(2, quads, ROWS_T // 4, 512),
            bits(2, quads, ROWS_T // 4, 512),
            bits(2, quads, ROWS_T // 8, 512),
            bits(quads, ROWS_T // 4, 512),
            bits(3, ROWS_T // 4, 512),
            bits(spaces, CAP, D_S + 3 * D_V),
            bits((ROWS_F + ROWS_M + ROWS_S + ROWS_T) // 4, 512),
            pltpu.SemaphoreType.DMA,
            pltpu.SemaphoreType.DMA((31,)),
            pltpu.SemaphoreType.DMA((31,)),
        ],
        compiler_params=pltpu.CompilerParams(
            collective_id=6, has_side_effects=True, vmem_limit_bytes=VMEM_LIMIT
        ),
        name="vector_backward",
    )(
        near_row, ev_col, ev_row, hidden, ratio, update, gvone, vout, tv, nv, vs, vt, rest, gains,
        s, m, f, back,
    )


def finish_kernel(
    plane_ref, got_ref, pick_ref, gscal_ref, gvec_ref,
    gs_ref, gv_ref, node_ref, edge_ref, norms_ref, vnode_ref, vedge_ref, vout_ref, ffv_ref, ffs_ref,
    ffu_ref, embed_ref, qkv_ref, out_ref, up_ref, down_ref, gains_ref, row_scr,
):
    base = 0
    for rows in (ROWS_F, ROWS_M, ROWS_S, ROWS_T):
        eighth = rows // 8
        for half, order in enumerate(((0, 1, 2, 3), (0, 2, 1, 3))):
            for n, q in enumerate(order):
                row_scr[pl.ds(4 * base + (4 * half + n) * eighth, eighth), :] = plane_ref[
                    q, pl.ds(base + half * eighth, eighth), :
                ]
        base += rows // 4

    def take(start, rows, lane=0, width=512):
        return row_scr[pl.ds(start, rows), pl.ds(lane, width)].astype(F32)

    at = 0
    down_ref[...] = take(at, 256)
    for n in range(4):
        up_ref[:, pl.ds(n * 512, 512)] = take(at + 256 + n * 64, 64)
    at = ROWS_F
    for n in range(3):
        qkv_ref[:, pl.ds(n * 512, 512)] = take(at + n * 64, 64)
    out_ref[...] = take(at + 192, 64)
    embed_ref[...] = take(at + 256, 160)
    for n in range(2):
        ffs_ref[:, pl.ds(n * 512, 512)] = take(at + 416 + n * 160, 160)
    ffv_ref[...] = take(at + 736, 32, 0, 256)
    ffu_ref[...] = take(at + 736, 32, 256, 256)
    at += ROWS_M
    for n in range(4):
        node_ref[:, pl.ds(n * 512, 512)] = take(at + n * 128, 128)
        norms_ref[pl.ds(n * 128, 128), :] = take(at + 512, 128, n * 128, 128)
    at += ROWS_S
    tails = take(at + 96, 32, 0, 128)
    edge_ref[...] = take(at + 96, 32, 128, 128)
    extra = take(at + 96, 32, 256, 128)
    norms_ref[pl.ds(512, 1), :] = extra[0:1]
    for n in range(5):
        width = min(128, H_V - n * 128)
        vedge_ref[:, pl.ds(n * 128, width)] = extra[1 + n : 2 + n, :width]
    gains_ref[...] = extra[0:8]
    vnode_ref[:, pl.ds(0, 512)] = take(at, 32)
    wide = jnp.concatenate([take(at + 32, 32), jnp.zeros((32, 128), F32)], 1)
    lane = lax.broadcasted_iota(jnp.int32, (32, 640), 1)
    wide = pltpu.roll(wide, 1, 1)
    wide = jnp.where(lane == 0, tails[:, 0:1], wide)
    wide = jnp.where(lane == 513, tails[:, 1:2], wide)
    vnode_ref[:, pl.ds(512, 514)] = wide[:, :514]
    flat = jnp.concatenate([take(at + 64, 32), jnp.zeros((96, 512), F32)], 0)
    vout_ref[pl.ds(0, 512), :] = jnp.transpose(flat)[:, :32]
    flat = jnp.concatenate([tails, jnp.zeros((96, 128), F32)], 0)
    vout_ref[pl.ds(512, 1), :] = jnp.transpose(flat)[2:3, :32]
    got = got_ref[...].reshape(pick_ref.shape[0], D_S + 3 * D_V)
    live = jnp.sum(pick_ref[...].astype(F32), axis=-1, keepdims=True) > 0.0
    got = jnp.where(live, got.astype(F32), 0.0).astype(BF)
    added = lead_product(pick_ref[...], got)
    gs_ref[...] = (gscal_ref[...] + added[:, :D_S]).astype(BF)
    for c in range(3):
        gv_ref[c] = (
            gvec_ref[c] + added[:, D_S + c * D_V : D_S + (c + 1) * D_V]
        ).astype(BF)


def finish(plane, got, pick, gscal, gvec):
    nodes = gscal.shape[0]
    outs = [
        ((nodes, D_S), BF),
        ((3, nodes, D_V), BF),
        ((128, 2048), F32),
        ((32, 128), F32),
        ((513, 128), F32),
        ((32, 1026), F32),
        ((1, 513), F32),
        ((513, 32), F32),
        ((32, 256), F32),
        ((160, 1024), F32),
        ((32, 256), F32),
        ((160, 512), F32),
        ((64, 1536), F32),
        ((64, 512), F32),
        ((64, 2048), F32),
        ((256, 512), F32),
        ((8, 128), F32),
    ]
    return pl.pallas_call(
        finish_kernel,
        out_shape=[jax.ShapeDtypeStruct(shape, kind) for shape, kind in outs],
        scratch_shapes=[pltpu.VMEM((ROWS_F + ROWS_M + ROWS_S + ROWS_T, 512), BF)],
        compiler_params=pltpu.CompilerParams(vmem_limit_bytes=VMEM_LIMIT),
        name="finish",
    )(plane, got, pick, gscal, gvec)


def pad_to(values, size, axis):
    pads = [(0, 0)] * values.ndim
    pads[axis] = (0, size - values.shape[axis])
    return jnp.pad(values, pads)


def fold(blocks, width=512):
    shards, rows, columns = blocks.shape
    parts = columns // width
    return jnp.moveaxis(blocks.reshape(shards, rows, parts, width), 2, 1).reshape(
        shards, parts * rows, width
    )


def unfold(rows_in, rows, columns, width=512):
    parts = columns // width
    return jnp.moveaxis(rows_in.reshape(parts, rows, width), 0, 1).reshape(rows, columns)


def body(
    node_scalar, node_vector, edge_scalar, edge_vector, neighbours, send_rows, complex_id, cotangent,
    w_node, w_edge, w_norms, vec_node, vec_edge, vec_out, norm_gain, ff_vec, ff_scalar, ff_up,
    w_embed, attn_gain, w_qkv, w_out, ffn_gain, w_up, w_down,
):
    local_rows = node_scalar.shape[0]
    spaces = lax.axis_size("space")
    extra_rows = spaces * CAP
    table_count = local_rows + extra_rows
    all_nodes = complex_id.shape[0]
    steps = NEIGH // GROUP

    sent_index = send_rows[0].reshape(-1)
    sent_live = sent_index >= 0
    pick = sent_index[:, None] == jnp.arange(local_rows, dtype=jnp.int32)[None, :]
    pick = pick.astype(BF)
    flat_nodes = jnp.concatenate([node_scalar] + [node_vector[c] for c in range(3)], 1)
    outgoing = product(pick, flat_nodes).astype(BF).reshape(spaces, CAP, D_S + 3 * D_V)
    incoming = lax.all_to_all(outgoing, "space", split_axis=0, concat_axis=0, tiled=True)
    incoming = incoming.reshape(extra_rows, D_S + 3 * D_V)
    table_s = jnp.concatenate([node_scalar, incoming[:, :D_S]], 0)
    table_v = jnp.stack(
        [
            jnp.concatenate(
                [node_vector[c], incoming[:, D_S + c * D_V : D_S + (c + 1) * D_V]], 0
            )
            for c in range(3)
        ]
    )
    vec_source = pad_to(vec_node[:, :H_V], H_P, 1)
    vec_target = pad_to(vec_node[:, H_V:], H_P, 1)
    a_source = product(table_s, w_node[:, :D_S]).astype(BF)
    b_target = product(node_scalar, w_node[:, D_S:])
    p_source = product(table_v, vec_source).astype(BF)
    q_target = product(node_vector, vec_target)
    ve_row = pad_to(vec_edge.astype(F32), H_P, 1)
    vout = pad_to(vec_out, H_P, 0)
    wn_mix = pad_to(jnp.concatenate([w_norms, w_edge], 0), H_P, 0)
    mix = jnp.concatenate([a_source, wn_mix], 0)

    near = neighbours.T
    near_col = near[:, :, None]
    near_row = near.reshape(steps, 1, GROUP * local_rows)
    es_k = edge_scalar.reshape(local_rows, NEIGH, D_E).transpose(1, 0, 2)
    es_pad = jnp.pad(es_k, ((0, 0), (0, 0), (1, 128 - 1 - D_E)))
    ev_k = edge_vector.reshape(3, local_rows, NEIGH)
    ev_col = ev_k.transpose(2, 1, 0).astype(F32)
    ev_row = ev_k.transpose(2, 0, 1).reshape(steps, GROUP, 3, local_rows)
    ev_row = ev_row.transpose(0, 2, 1, 3).reshape(steps, 3, GROUP * local_rows)

    agg_s, agg_v, hidden, lx, dsilu, update = edge_forward(
        near_col, es_pad, ev_col, mix, b_target, p_source, q_target, ve_row, vout
    )

    if spaces == HEADS and lax.axis_size("dp") == 4 and local_rows == 128:
        row_of = lambda gain: gain.astype(F32)[None]
        quads = spaces // 2
        s1, v1, ffh, ffp, ffu, v2, sz, fac_node, heads_out = node_forward(
            node_scalar, node_vector, agg_s, agg_v, row_of(norm_gain), ff_vec, ff_scalar, ff_up,
            w_embed, row_of(attn_gain), w_qkv,
        )
        heads_in, fac_node_o, table_o, node_o = links(0, heads_out, (fac_node, table_s, node_scalar))
        probs, att, att_out = attend(heads_in, complex_id[None])
        (att_in,) = links(1, att_out)
        stream_out, gatt, gs1, fgain, fac_feed = feed(
            att_in, sz, w_out, row_of(ffn_gain), w_up, w_down, cotangent
        )
        gatt_in, fac_feed_o = links(2, gatt, (fac_feed,))
        first = feed_grads(fac_feed, fac_feed_o, quads)
        grad_heads, first = links(
            3, attend_backward(heads_in, probs, att, gatt_in), cut=1, share=first
        )
        gsone, gvone, gains, fac_back = node_backward(
            grad_heads, gs1, s1, v1, ffh, ffp, ffu, v2, sz,
            row_of(norm_gain), ff_vec, ff_scalar, ff_up, w_embed, row_of(attn_gain), w_qkv, fgain,
        )
        fac_back_o, first = links(4, pairs=(fac_back,), cut=2, share=first)
        middle = node_grads(
            quads, fac_node, fac_node_o, fac_back, fac_back_o, fac_feed, fac_feed_o
        )
        ratio, second, rest, gscal, back_s, middle, first = scalar_backward(
            near_row, lx, dsilu, gsone, wn_mix, table_s, node_scalar, w_node, table_o, node_o,
            middle, first,
        )
        plane, gvec, got = vector_backward(
            near_row, ev_col, ev_row, hidden, ratio, update, gvone, vout, table_v, node_vector,
            vec_source, vec_target, rest, gains, second, middle, first, back_s,
        )
        (
            grad_scalar, grad_vector, out_node, out_edge, out_norms, out_vnode, out_vedge, out_vout,
            out_ffv, out_ffs, out_ffu, out_embed, out_qkv, out_out, out_up, out_down, rows,
        ) = finish(plane, got, pick, gscal, gvec)
        return (
            stream_out, grad_scalar, grad_vector, out_node, out_edge, out_norms, out_vnode,
            out_vedge, out_vout, rows[6], out_ffv, out_ffs, out_ffu, out_embed, rows[7, :64],
            out_qkv, out_out, rows[7, 64:], out_up, out_down,
        )

    scalar_one = node_scalar.astype(F32) + agg_s
    vector_one = node_vector.astype(F32) + agg_v
    gain_norm = norm_gain.astype(F32)
    normed_s = layer_norm(scalar_one, gain_norm)
    normed_v = vector_norm(vector_one)
    normed_vr = normed_v.astype(BF)
    ff_hidden = product(normed_vr, ff_vec)
    ff_hidden_r = ff_hidden.astype(BF)
    ff_length = length_plus(ff_hidden)
    ff_input = jnp.concatenate([normed_s.astype(BF), ff_length.astype(BF)], -1)
    ff_preact = product(ff_input, ff_scalar)
    ff_update = product(ff_hidden_r, ff_up)
    scalar_two = normed_s + jax.nn.silu(ff_preact)
    vector_two = normed_v + vector_gate(ff_update)
    embed_input = jnp.concatenate([scalar_two.astype(BF), length_plus(vector_two).astype(BF)], -1)
    stream_zero = product(embed_input, w_embed)
    gain_attn = attn_gain.astype(F32)
    attn_in = layer_norm(stream_zero, gain_attn).astype(BF)
    qkv = product(attn_in, w_qkv).astype(BF)
    queries = qkv[:, :D_MODEL]
    keys_own = qkv[:, D_MODEL : 2 * D_MODEL]
    values_own = qkv[:, 2 * D_MODEL :]
    full_qkv = lax.all_gather(qkv, "space", axis=0, tiled=True)
    heads = lambda values: values.reshape(values.shape[0], HEADS, HEAD_DIM)
    full_queries = heads(full_qkv[:, :D_MODEL])
    full_keys = heads(full_qkv[:, D_MODEL : 2 * D_MODEL])
    full_values = heads(full_qkv[:, 2 * D_MODEL :])
    position = lax.axis_index("space")
    own_ids = lax.dynamic_slice_in_dim(complex_id, position * local_rows, local_rows, 0)
    same = own_ids[:, None] == complex_id[None, :]
    score_scale = HEAD_DIM ** (-0.5)
    scores = jnp.einsum("qhd,khd->hqk", heads(queries), full_keys, preferred_element_type=F32)
    scores = jnp.where(same[None], scores * score_scale, -1000000000.0)
    row_peak = jnp.max(scores, axis=-1, keepdims=True)
    shifted = jnp.exp(scores - row_peak)
    totals = jnp.sum(shifted, axis=-1, keepdims=True)
    probs = shifted / totals
    log_total = row_peak + jnp.log(totals)
    attended = jnp.einsum(
        "hqk,khd->qhd", probs.astype(BF), full_values, preferred_element_type=F32
    ).reshape(local_rows, D_MODEL)
    attended_r = attended.astype(BF)
    stream_one = stream_zero + product(attended_r, w_out)
    gain_ffn = ffn_gain.astype(F32)
    ffn_in = layer_norm(stream_one, gain_ffn).astype(BF)
    hidden_up = product(ffn_in, w_up)
    gelu_r = gelu_exact(hidden_up).astype(BF)
    stream_out = (stream_one + product(gelu_r, w_down)).astype(BF)
    grad_w_down = product_lead(gelu_r, cotangent)
    grad_gelu = product_back(cotangent, w_down)
    grad_up_r = pullback(gelu_exact, hidden_up, grad_gelu).astype(BF)
    grad_w_up = product_lead(ffn_in, grad_up_r)
    grad_ffn_in = product_back(grad_up_r, w_up)
    unused, ffn_pull = jax.vjp(layer_norm, stream_one, gain_ffn)
    grad_stream_ln, grad_ffn_gain = ffn_pull(grad_ffn_in)
    grad_stream_one = cotangent.astype(F32) + grad_stream_ln
    grad_branch = grad_stream_one.astype(BF)
    grad_w_out = product_lead(attended_r, grad_branch)
    grad_attended = product_back(grad_branch, w_out).astype(BF)
    row_dots = jnp.sum(heads(grad_attended).astype(F32) * heads(attended), axis=-1).T

    def halves(values):
        high = lax.reduce_precision(values, exponent_bits=8, mantissa_bits=7)
        return [high.astype(BF), (values - high).astype(BF)]

    numbers = jnp.concatenate(halves(log_total[:, :, 0]) + halves(row_dots), 0)
    packed = jnp.concatenate([grad_attended, pad_to(numbers.T, 128, 1)], 1)
    full_packed = lax.all_gather(packed, "space", axis=0, tiled=True)
    full_grad = heads(full_packed[:, :D_MODEL])
    numbers = full_packed[:, D_MODEL : D_MODEL + 4 * HEADS].astype(F32).T
    full_log = numbers[:HEADS] + numbers[HEADS : 2 * HEADS]
    full_dots = numbers[2 * HEADS : 3 * HEADS] + numbers[3 * HEADS :]

    grad_probs = jnp.einsum(
        "qhd,khd->hqk", heads(grad_attended), full_values, preferred_element_type=F32
    )
    grad_scores = (probs * (grad_probs - row_dots[:, :, None])).astype(BF)
    grad_query = jnp.einsum("hqk,khd->qhd", grad_scores, full_keys, preferred_element_type=F32)
    own_scores = jnp.einsum(
        "khd,qhd->hkq", heads(keys_own), full_queries, preferred_element_type=F32
    )
    own_scores = jnp.where(same[None], own_scores * score_scale, -1000000000.0)
    own_probs = jnp.exp(own_scores - full_log[:, None, :])
    own_grad_probs = jnp.einsum(
        "khd,qhd->hkq", heads(values_own), full_grad, preferred_element_type=F32
    )
    own_grad_scores = (own_probs * (own_grad_probs - full_dots[:, None, :])).astype(BF)
    grad_keys = jnp.einsum(
        "hkq,qhd->khd", own_grad_scores, full_queries, preferred_element_type=F32
    )
    grad_values = jnp.einsum(
        "hkq,qhd->khd", own_probs.astype(BF), full_grad, preferred_element_type=F32
    )
    flat = lambda values: values.reshape(local_rows, D_MODEL)
    grad_qkv = jnp.concatenate(
        [flat(grad_query) * score_scale, flat(grad_keys) * score_scale, flat(grad_values)], -1
    ).astype(BF)
    grad_w_qkv = product_lead(attn_in, grad_qkv)
    grad_attn_in = product_back(grad_qkv, w_qkv)
    unused, attn_pull = jax.vjp(layer_norm, stream_zero, gain_attn)
    grad_zero_ln, grad_attn_gain = attn_pull(grad_attn_in)
    grad_stream_r = (grad_stream_one + grad_zero_ln).astype(BF)
    grad_w_embed = product_lead(embed_input, grad_stream_r)
    grad_embed_in = product_back(grad_stream_r, w_embed)
    grad_vector_two = pullback(length_plus, vector_two, grad_embed_in[:, D_S:])
    grad_ff_pre = pullback(jax.nn.silu, ff_preact, grad_embed_in[:, :D_S]).astype(BF)
    grad_ff_scalar = product_lead(ff_input, grad_ff_pre)
    grad_ff_input = product_back(grad_ff_pre, ff_scalar)
    grad_ff_update = pullback(vector_gate, ff_update, grad_vector_two).astype(BF)
    grad_ff_up = product_lead(ff_hidden_r, grad_ff_update)
    grad_ff_hidden = (
        product_back(grad_ff_update, ff_up)
        + pullback(length_plus, ff_hidden, grad_ff_input[:, D_S:])
    ).astype(BF)
    grad_ff_vec = product_lead(normed_vr, grad_ff_hidden)
    grad_normed_v = grad_vector_two + product_back(grad_ff_hidden, ff_vec)
    grad_normed_s = grad_embed_in[:, :D_S] + grad_ff_input[:, :D_S]
    unused, norm_pull = jax.vjp(layer_norm, scalar_one, gain_norm)
    grad_scalar_one, grad_norm_gain = norm_pull(grad_normed_s)
    grad_vector_one = pullback(vector_norm, vector_one, grad_normed_v)

    shard = lambda grad: grad.astype(BF).reshape((spaces, grad.shape[0] // spaces) + grad.shape[1:])
    gains = jnp.concatenate(
        [shard(grad_norm_gain), shard(grad_attn_gain), shard(grad_ffn_gain)], 1
    )
    gains = pad_to(pad_to(gains, 512, 1)[:, None, :], 16, 1)
    first_share = jnp.concatenate(
        [
            shard(grad_w_down),
            fold(shard(grad_w_up)),
            fold(shard(grad_w_qkv)),
            shard(grad_w_out),
            shard(grad_w_embed),
            fold(shard(grad_ff_scalar)),
            jnp.concatenate([shard(grad_ff_vec), shard(grad_ff_up)], 2),
            gains,
        ],
        1,
    )
    first_sum = lax.psum_scatter(first_share, "space", scatter_dimension=0, tiled=False)
    first_sum = lax.psum(first_sum, "dp").astype(F32)

    grad_a, grad_mix, grad_b, grad_p, grad_q, grad_vout = edge_backward(
        near_row, ev_col, ev_row, hidden, lx, dsilu, update,
        grad_scalar_one * (1.0 / NEIGH), grad_vector_one * (1.0 / NEIGH), wn_mix, vout, table_count,
    )
    grad_vedge = jnp.sum(grad_p[:, table_count], 0)[:H_V]
    grad_vec_edge = lax.psum(grad_vedge[None, :], ("dp", "space"))
    grad_a_r = grad_a.astype(BF)
    grad_p_r = grad_p[:, :table_count].astype(BF)
    grad_b_r = grad_b.astype(BF)
    grad_q_r = grad_q.astype(BF)
    grad_node_a = product_lead(table_s, grad_a_r)
    grad_node_b = product_lead(node_scalar, grad_b_r)
    grad_vec_a = product_lead(table_v, grad_p_r)
    grad_vec_b = product_lead(node_vector, grad_q_r)
    grad_table_scalar = product_back(grad_a_r, w_node[:, :D_S])
    grad_table_vector = product_back(grad_p_r, vec_source)
    grad_scalar = (
        grad_scalar_one + product_back(grad_b_r, w_node[:, D_S:]) + grad_table_scalar[:local_rows]
    )
    grad_vector = (
        grad_vector_one + product_back(grad_q_r, vec_target) + grad_table_vector[:, :local_rows]
    )
    back = jnp.concatenate(
        [grad_table_scalar[local_rows:]] + [grad_table_vector[c, local_rows:] for c in range(3)], 1
    )
    back = back.astype(BF).reshape(spaces, CAP, D_S + 3 * D_V)
    got = lax.all_to_all(back, "space", split_axis=0, concat_axis=0, tiled=True)
    got = got.reshape(extra_rows, D_S + 3 * D_V)
    got = jnp.where(sent_live[:, None], got, 0)
    added = lax.dot_general(pick, got, (((0,), (0,)), ((), ())), preferred_element_type=F32)
    grad_scalar = grad_scalar + added[:, :D_S]
    grad_vector = grad_vector + jnp.moveaxis(
        added[:, D_S:].reshape(local_rows, 3, D_V), 1, 0
    )

    columns = lambda grad: jnp.moveaxis(
        grad.reshape(grad.shape[0], spaces, grad.shape[1] // spaces), 1, 0
    )
    mix_block = columns(grad_mix.astype(BF))
    mix_width = D_S // spaces
    mix_rows = H_P * mix_width // 512
    second_share = jnp.concatenate(
        [
            fold(shard(grad_node_a)),
            fold(shard(grad_node_b)),
            mix_block.reshape(spaces, mix_rows, 512),
            shard(grad_vec_a)[:, :, :512],
            shard(grad_vec_b)[:, :, :512],
            shard(grad_vout)[:, :, :512],
            jnp.concatenate(
                [
                    shard(grad_vec_a)[:, :, 512:],
                    shard(grad_vec_b)[:, :, 512:],
                    shard(grad_vout)[:, :, 512:],
                    jnp.zeros((spaces, D_V // spaces, 128), BF),
                ],
                2,
            ),
        ],
        1,
    )
    second_sum = lax.psum_scatter(second_share, "space", scatter_dimension=0, tiled=False)
    second_sum = lax.psum(second_sum, "dp").astype(F32)

    def taker(rows_in):
        at = [0]

        def take(rows, cols, blocks=1):
            part = rows_in[at[0] : at[0] + rows * blocks]
            at[0] += rows * blocks
            return unfold(part, rows, cols) if blocks > 1 else part

        return take

    take = taker(first_sum)
    out_down = take(grad_w_down.shape[0] // spaces, 512)
    out_up = take(D_MODEL // spaces, 2048, 4)
    out_qkv = take(D_MODEL // spaces, 1536, 3)
    out_out = take(D_MODEL // spaces, 512)
    out_embed = take((D_S + D_V) // spaces, 512)
    out_ffs = take((D_S + D_V) // spaces, 1024, 2)
    both = take(D_V // spaces, 512)
    out_ffv, out_ffu = both[:, :D_V], both[:, D_V:]
    gain_row = take(16, 512)[0]
    cuts = [D_S // spaces, D_MODEL // spaces, D_MODEL // spaces]
    out_gn = gain_row[: cuts[0]]
    out_ga = gain_row[cuts[0] : cuts[0] + cuts[1]]
    out_gf = gain_row[cuts[0] + cuts[1] : sum(cuts)]
    take = taker(second_sum)
    node_a = take(D_S // spaces, 1024, 2)
    node_b = take(D_S // spaces, 1024, 2)
    mixed = take(mix_rows, 512).reshape(H_P, mix_width)
    vec_a = take(D_V // spaces, 512)
    vec_b = take(D_V // spaces, 512)
    vout_t = take(D_V // spaces, 512)
    tails = take(D_V // spaces, 512)
    out_vec_node = jnp.concatenate([vec_a, tails[:, :1], vec_b, tails[:, 128:129]], 1)
    out_vec_out = jnp.concatenate([vout_t, tails[:, 256:257]], 1).T
    return (
        stream_out,
        grad_scalar.astype(BF),
        grad_vector.astype(BF),
        jnp.concatenate([node_a, node_b], 1),
        mixed[H_V : H_V + D_E],
        mixed[:H_V],
        out_vec_node,
        grad_vec_edge,
        out_vec_out,
        out_gn,
        out_ffv,
        out_ffs,
        out_ffu,
        out_embed,
        out_ga,
        out_qkv,
        out_out,
        out_gf,
        out_up,
        out_down,
    )


def solution(mesh):
    rows = P(("dp", "space"), None)
    component = P(None, ("dp", "space"), None)
    return jax.shard_map(
        body,
        mesh=mesh,
        in_specs=(
            rows, component, rows, P(None, ("dp", "space")), rows,
            P(("dp", "space"), None, None), P("dp"), rows,
        ) + (P(),) * 17,
        out_specs=(
            rows, rows, component, P("space", None), P(None, "space"), P(None, "space"),
            P("space", None), P(), P(None, "space"), P("space"), P("space", None),
            P("space", None), P("space", None), P("space", None), P("space"), P("space", None),
            P("space", None), P("space"), P("space", None), P("space", None),
        ),
        check_vma=False,
    )
```

```python
import functools
import math

import jax
import jax.numpy as jnp
from jax import lax
from jax.experimental import pallas as pl
from jax.experimental.pallas import tpu as pltpu
from jax.sharding import PartitionSpec as P

D_S = 1024
D_V = 256
H_V = 513
H_P = 640
D_E = 32
NEIGH = 30
D_MODEL = 512
HEADS = 8
HEAD_DIM = 64
CAP = 16
GROUP = 5
VMEM_LIMIT = 60 * 1024 * 1024

MESH = pl.DeviceIdType.MESH
BF = jnp.bfloat16
F32 = jnp.float32


def layer_norm(values, gain_row):
    centred = values - jnp.mean(values, axis=-1, keepdims=True)
    spread = jnp.mean(centred * centred, axis=-1, keepdims=True)
    return centred * lax.rsqrt(spread + 1e-05) * gain_row


def vector_norm(vectors):
    mean_power = jnp.mean(jnp.sum(vectors * vectors, axis=0), axis=-1, keepdims=True)
    return vectors * lax.rsqrt(mean_power + 1e-05)[None]


def length_plus(vectors):
    return jnp.sqrt(jnp.sum(vectors * vectors, axis=0) + 1.0)


def vector_gate(vectors):
    return vectors * jax.nn.sigmoid(length_plus(vectors))[None]


def gelu_exact(values):
    return jax.nn.gelu(values, approximate=False)


def product(former, latter):
    return jnp.dot(former, latter, preferred_element_type=F32)


def product_lead(former, latter):
    leading = tuple(range(former.ndim - 1))
    return lax.dot_general(
        former, latter, ((leading, leading), ((), ())), preferred_element_type=F32
    )


def product_back(former, latter):
    return lax.dot_general(
        former, latter, (((former.ndim - 1,), (1,)), ((), ())), preferred_element_type=F32
    )


def pullback(function, at_point, cotangent_in):
    unused, puller = jax.vjp(function, at_point)
    return puller(cotangent_in)[0]


def sigmoid(values):
    return 0.5 * jnp.tanh(0.5 * values) + 0.5


LANE_BLOCKS = ((0, 256), (256, 256), (512, 128))
ROW_TILE = 64


def edge_forward_kernel(
    near_ref, es_ref, ev_ref, a_ref, b_ref, p_ref, q_ref, ve_ref, vo_ref,
    aggs_ref, aggv_ref, h_ref, lx_ref, ds_ref, z_ref, x_scr,
):
    nodes = b_ref.shape[0]
    table = p_ref.shape[1]
    rows = GROUP * nodes
    idx = near_ref[...].reshape(rows, 1)
    x_scr[:, :table] = (idx == lax.broadcasted_iota(jnp.int32, (rows, table), 1)).astype(BF)
    one_hot = x_scr[:, :table]
    for start, width in LANE_BLOCKS:
        cols = pl.ds(start, width)
        gathered = [product(one_hot, p_ref[c, :, cols]) for c in range(3)]
        for k in range(GROUP):
            for first in range(0, nodes, ROW_TILE):
                at = k * nodes + first
                evk = ev_ref[k, pl.ds(first, ROW_TILE), :]
                total = None
                for c in range(3):
                    h = (
                        gathered[c][at : at + ROW_TILE]
                        + q_ref[c, pl.ds(first, ROW_TILE), cols]
                        + evk[:, c : c + 1] * ve_ref[:, cols]
                    )
                    h_ref[k, c, pl.ds(first, ROW_TILE), cols] = h.astype(BF)
                    total = h * h + 1.0 if total is None else total + h * h
                length = total * lax.rsqrt(total)
                if start == 512:
                    lane = lax.broadcasted_iota(jnp.int32, (ROW_TILE, width), 1)
                    length = jnp.where(
                        lane == 0, length, es_ref[k, pl.ds(first, ROW_TILE), :].astype(F32)
                    )
                length = length.astype(BF)
                x_scr[pl.ds(at, ROW_TILE), pl.ds(table + start, width)] = length
                lx_ref[k, pl.ds(first, ROW_TILE), cols] = length

    @pl.when(pl.program_id(0) == 0)
    def _():
        aggs_ref[...] = jnp.zeros_like(aggs_ref)
        aggv_ref[...] = jnp.zeros_like(aggv_ref)

    full = x_scr[...]
    for start in range(0, D_S, 256):
        cols = pl.ds(start, 256)
        pre = product(full, a_ref[:, cols])
        for first in range(0, nodes, ROW_TILE):
            part = pl.ds(first, ROW_TILE)
            acc = None
            for k in range(GROUP):
                at = k * nodes + first
                x = pre[at : at + ROW_TILE] + b_ref[part, cols]
                s = sigmoid(x)
                y = x * s
                ds_ref[k, part, cols] = (s + y * (1.0 - s)).astype(BF)
                acc = y if acc is None else acc + y
            aggs_ref[part, cols] += acc * (1.0 / NEIGH)
    ups = [
        product(h_ref[:, c, :, :].reshape(rows, H_P), vo_ref[...]) for c in range(3)
    ]
    for first in range(0, nodes, ROW_TILE):
        part = pl.ds(first, ROW_TILE)
        acc = [None] * 3
        for k in range(GROUP):
            at = k * nodes + first
            z = [ups[c][at : at + ROW_TILE] for c in range(3)]
            power = z[0] * z[0] + z[1] * z[1] + z[2] * z[2] + 1.0
            s = sigmoid(power * lax.rsqrt(power))
            for c in range(3):
                z_ref[k, c, part, :] = z[c].astype(BF)
                gated = z[c] * s
                acc[c] = gated if acc[c] is None else acc[c] + gated
        for c in range(3):
            aggv_ref[c, part, :] += acc[c] * (1.0 / NEIGH)


def edge_forward(near_col, es_pad, ev_col, mix, b_target, p_source, q_target, ve_row, vout):
    nodes = b_target.shape[0]
    table = p_source.shape[1]
    whole = lambda shape: pl.BlockSpec(shape, lambda g: (0,) * len(shape))
    slots = lambda *shape: pl.BlockSpec((GROUP,) + shape, lambda g: (g,) + (0,) * len(shape))
    return pl.pallas_call(
        edge_forward_kernel,
        grid=(NEIGH // GROUP,),
        in_specs=[
            slots(nodes, 1),
            slots(nodes, 128),
            slots(nodes, 3),
            whole((table + H_P, D_S)),
            whole((nodes, D_S)),
            whole((3, table, H_P)),
            whole((3, nodes, H_P)),
            whole((1, H_P)),
            whole((H_P, D_V)),
        ],
        out_specs=[
            whole((nodes, D_S)),
            whole((3, nodes, D_V)),
            slots(3, nodes, H_P),
            slots(nodes, H_P),
            slots(nodes, D_S),
            slots(3, nodes, D_V),
        ],
        out_shape=[
            jax.ShapeDtypeStruct((nodes, D_S), F32),
            jax.ShapeDtypeStruct((3, nodes, D_V), F32),
            jax.ShapeDtypeStruct((NEIGH, 3, nodes, H_P), BF),
            jax.ShapeDtypeStruct((NEIGH, nodes, H_P), BF),
            jax.ShapeDtypeStruct((NEIGH, nodes, D_S), BF),
            jax.ShapeDtypeStruct((NEIGH, 3, nodes, D_V), BF),
        ],
        scratch_shapes=[pltpu.VMEM((GROUP * nodes, table + H_P), BF)],
        compiler_params=pltpu.CompilerParams(vmem_limit_bytes=VMEM_LIMIT),
        name="edge_forward",
    )(near_col, es_pad, ev_col, mix, b_target, p_source, q_target, ve_row, vout)


def message_kernel(
    near_ref, es_ref, ev_ref, a_ref, b_ref, p_ref, q_ref, ve_ref, vo_ref,
    aggs_ref, aggv_ref, h_ref, lx_ref, ds_ref, z_ref, x_scr, turn_scr,
):
    nodes = b_ref.shape[0]
    table = p_ref.shape[1]
    rows = GROUP * nodes
    first_slot = pl.program_id(0) * GROUP

    @pl.when(pl.program_id(0) == 0)
    def _():
        for n in range(4):
            ref = near_ref if n == 3 else ev_ref.at[n]
            turn_scr[n, pl.ds(0, NEIGH), :] = ref[...].astype(F32)
            turn_scr[n] = jnp.transpose(turn_scr[n])

    back = lax.rem(128 - first_slot, 128)
    ev = [pltpu.roll(turn_scr[n], back, 1) for n in range(4)]
    slots = ev[3]
    places = lax.broadcasted_iota(jnp.int32, (nodes, table), 1).astype(F32)
    edges_in = []
    for k in range(GROUP):
        x_scr[pl.ds(k * nodes, nodes), :table] = (slots[:, k : k + 1] == places).astype(BF)
        rows_in = pl.ds(pl.multiple_of((first_slot + k) * D_E, D_E), D_E)
        edges_in.append(
            jnp.transpose(
                jnp.concatenate(
                    [
                        jnp.zeros((16, nodes), F32),
                        es_ref[rows_in, :].astype(F32),
                        jnp.zeros((112 - D_E, nodes), F32),
                    ],
                    0,
                )
            )
        )
    one_hot = x_scr[:, :table]
    for start, width in LANE_BLOCKS:
        cols = pl.ds(start, width)
        gathered = [product(one_hot, p_ref[c, :, cols]) for c in range(3)]
        for k in range(GROUP):
            for first in range(0, nodes, ROW_TILE):
                at = k * nodes + first
                total = None
                for c in range(3):
                    h = (
                        gathered[c][at : at + ROW_TILE]
                        + q_ref[c, pl.ds(first, ROW_TILE), cols]
                        + ev[c][first : first + ROW_TILE, k : k + 1]
                        * ve_ref[:, pl.ds(D_S + 2 * D_MODEL + start, width)]
                    )
                    h_ref[k, c, pl.ds(first, ROW_TILE), cols] = h.astype(BF)
                    total = h * h + 1.0 if total is None else total + h * h
                length = total * lax.rsqrt(total)
                if start == 512:
                    lane = lax.broadcasted_iota(jnp.int32, (ROW_TILE, width), 1)
                    length = jnp.where(
                        lane == 0, length, edges_in[k][first : first + ROW_TILE]
                    )
                length = length.astype(BF)
                x_scr[pl.ds(at, ROW_TILE), pl.ds(table + start, width)] = length
                lx_ref[k, pl.ds(first, ROW_TILE), cols] = length

    @pl.when(pl.program_id(0) == 0)
    def _():
        aggs_ref[...] = jnp.zeros_like(aggs_ref)
        aggv_ref[...] = jnp.zeros_like(aggv_ref)

    full = x_scr[...]
    for start in range(0, D_S, 256):
        cols = pl.ds(start, 256)
        pre = product(full, a_ref[:, cols])
        for first in range(0, nodes, ROW_TILE):
            part = pl.ds(first, ROW_TILE)
            acc = None
            for k in range(GROUP):
                at = k * nodes + first
                x = pre[at : at + ROW_TILE] + b_ref[part, cols]
                s = sigmoid(x)
                y = x * s
                ds_ref[k, part, cols] = (s + y * (1.0 - s)).astype(BF)
                acc = y if acc is None else acc + y
            aggs_ref[part, cols] += acc * (1.0 / NEIGH)
    ups = [
        product(h_ref[:, c, :, :].reshape(rows, H_P), vo_ref[...]) for c in range(3)
    ]
    for first in range(0, nodes, ROW_TILE):
        part = pl.ds(first, ROW_TILE)
        acc = [None] * 3
        for k in range(GROUP):
            at = k * nodes + first
            z = [ups[c][at : at + ROW_TILE] for c in range(3)]
            power = z[0] * z[0] + z[1] * z[1] + z[2] * z[2] + 1.0
            s = sigmoid(power * lax.rsqrt(power))
            for c in range(3):
                z_ref[k, c, part, :] = z[c].astype(BF)
                gated = z[c] * s
                acc[c] = gated if acc[c] is None else acc[c] + gated
        for c in range(3):
            aggv_ref[c, part, :] += acc[c] * (1.0 / NEIGH)


def message(near, edge_scalar, ev, mix, b_target, p_source, q_target, ve_row, vout):
    nodes = b_target.shape[0]
    table = p_source.shape[1]
    whole = lambda shape: pl.BlockSpec(shape, lambda g: (0,) * len(shape))
    slots = lambda *shape: pl.BlockSpec((GROUP,) + shape, lambda g: (g,) + (0,) * len(shape))
    return pl.pallas_call(
        message_kernel,
        grid=(NEIGH // GROUP,),
        in_specs=[
            whole(near.shape),
            whole(edge_scalar.shape),
            whole(ev.shape),
            whole((table + H_P, D_S)),
            whole((nodes, D_S)),
            whole((3, table, H_P)),
            whole((3, nodes, H_P)),
            whole(ve_row.shape),
            whole((H_P, D_V)),
        ],
        out_specs=[
            whole((nodes, D_S)),
            whole((3, nodes, D_V)),
            slots(3, nodes, H_P),
            slots(nodes, H_P),
            slots(nodes, D_S),
            slots(3, nodes, D_V),
        ],
        out_shape=[
            jax.ShapeDtypeStruct((nodes, D_S), F32),
            jax.ShapeDtypeStruct((3, nodes, D_V), F32),
            jax.ShapeDtypeStruct((NEIGH, 3, nodes, H_P), BF),
            jax.ShapeDtypeStruct((NEIGH, nodes, H_P), BF),
            jax.ShapeDtypeStruct((NEIGH, nodes, D_S), BF),
            jax.ShapeDtypeStruct((NEIGH, 3, nodes, D_V), BF),
        ],
        scratch_shapes=[
            pltpu.VMEM((GROUP * nodes, table + H_P), BF),
            pltpu.VMEM((4, 128, nodes), F32),
        ],
        compiler_params=pltpu.CompilerParams(vmem_limit_bytes=VMEM_LIMIT),
        name="message",
    )(near, edge_scalar, ev, mix, b_target, p_source, q_target, ve_row, vout)


def edge_backward_kernel(
    near_ref, ev_ref, evr_ref, h_ref, lx_ref, ds_ref, z_ref, gs_ref, gv_ref, wn_ref, vo_ref,
    ga_ref, gw_ref, gb_ref, gp_ref, gq_ref, gvo_ref, pre_scr, up_scr, gh_scr,
):
    nodes = gs_ref.shape[0]
    table = ga_ref.shape[0]
    rows = GROUP * nodes

    @pl.when(pl.program_id(0) == 0)
    def _():
        for ref in (ga_ref, gw_ref, gb_ref, gp_ref, gq_ref, gvo_ref):
            ref[...] = jnp.zeros_like(ref)

    for start in range(0, D_S, 256):
        cols = pl.ds(start, 256)
        for first in range(0, nodes, ROW_TILE):
            part = pl.ds(first, ROW_TILE)
            share = gs_ref[part, cols]
            acc = None
            for k in range(GROUP):
                g = (ds_ref[k, part, cols].astype(F32) * share).astype(BF)
                pre_scr[pl.ds(k * nodes + first, ROW_TILE), cols] = g
                g = g.astype(F32)
                acc = g if acc is None else acc + g
            gb_ref[part, cols] += acc
    for first in range(0, nodes, ROW_TILE):
        part = pl.ds(first, ROW_TILE)
        share = [gv_ref[c, part, :] for c in range(3)]
        for k in range(GROUP):
            z = [z_ref[k, c, part, :].astype(F32) for c in range(3)]
            power = z[0] * z[0] + z[1] * z[1] + z[2] * z[2] + 1.0
            inverse = lax.rsqrt(power)
            s = sigmoid(power * inverse)
            dot = z[0] * share[0] + z[1] * share[1] + z[2] * share[2]
            factor = dot * inverse * (s * (1.0 - s))
            for c in range(3):
                up_scr[c, pl.ds(k * nodes + first, ROW_TILE), :] = (
                    share[c] * s + z[c] * factor
                ).astype(BF)

    near = near_ref[0]
    one_hot = (lax.broadcasted_iota(jnp.int32, (table, rows), 0) == near).astype(BF)
    grad_pre = pre_scr[...]
    ga_ref[...] += product(one_hot, grad_pre)
    lx = lx_ref[...].reshape(rows, H_P)
    gw_ref[...] += lax.dot_general(
        lx, grad_pre, (((0,), (0,)), ((), ())), preferred_element_type=F32
    )
    for start, width in LANE_BLOCKS:
        cols = pl.ds(start, width)
        grad_length = product_back(grad_pre, wn_ref[cols, :])
        grad_direct = [product_back(up_scr[c], vo_ref[cols, :]) for c in range(3)]
        for first in range(0, nodes, ROW_TILE):
            part = pl.ds(first, ROW_TILE)
            acc = [None] * 3
            for k in range(GROUP):
                at = k * nodes + first
                ratio = grad_length[at : at + ROW_TILE] * pl.reciprocal(
                    lx_ref[k, part, cols].astype(F32), approx=True
                )
                if start == 512:
                    lane = lax.broadcasted_iota(jnp.int32, (ROW_TILE, width), 1)
                    ratio = jnp.where(lane == 0, ratio, 0.0)
                for c in range(3):
                    g = grad_direct[c][at : at + ROW_TILE] + ratio * h_ref[
                        k, c, part, cols
                    ].astype(F32)
                    gh_scr[c, pl.ds(at, ROW_TILE), cols] = g.astype(BF)
                    acc[c] = g if acc[c] is None else acc[c] + g
            for c in range(3):
                gq_ref[c, part, cols] += acc[c]
    for c in range(3):
        evr = jnp.broadcast_to(evr_ref[0, c : c + 1, :], (16, rows))
        lead = jnp.concatenate([one_hot, evr.astype(BF)], axis=0)
        gp_ref[c] += product(lead, gh_scr[c])
        gvo_ref[...] += lax.dot_general(
            up_scr[c],
            h_ref[:, c, :, :].reshape(rows, H_P),
            (((0,), (0,)), ((), ())),
            preferred_element_type=F32,
        )


def edge_backward(near_row, ev_col, ev_row, hidden, lx, dsilu, update, gs, gv, wn, vout, table):
    nodes = gs.shape[0]
    rows = GROUP * nodes
    whole = lambda shape: pl.BlockSpec(shape, lambda g: (0,) * len(shape))
    slots = lambda *shape: pl.BlockSpec((GROUP,) + shape, lambda g: (g,) + (0,) * len(shape))
    steps = lambda *shape: pl.BlockSpec((1,) + shape, lambda g: (g,) + (0,) * len(shape))
    outs = [
        (table, D_S),
        (H_P, D_S),
        (nodes, D_S),
        (3, table + 16, H_P),
        (3, nodes, H_P),
        (D_V, H_P),
    ]
    return pl.pallas_call(
        edge_backward_kernel,
        grid=(NEIGH // GROUP,),
        in_specs=[
            steps(1, rows),
            slots(nodes, 3),
            steps(3, rows),
            slots(3, nodes, H_P),
            slots(nodes, H_P),
            slots(nodes, D_S),
            slots(3, nodes, D_V),
            whole((nodes, D_S)),
            whole((3, nodes, D_V)),
            whole((H_P, D_S)),
            whole((H_P, D_V)),
        ],
        out_specs=[whole(shape) for shape in outs],
        out_shape=[jax.ShapeDtypeStruct(shape, F32) for shape in outs],
        scratch_shapes=[
            pltpu.VMEM((rows, D_S), BF),
            pltpu.VMEM((3, rows, D_V), BF),
            pltpu.VMEM((3, rows, H_P), BF),
        ],
        compiler_params=pltpu.CompilerParams(vmem_limit_bytes=VMEM_LIMIT),
        name="edge_backward",
    )(near_row, ev_col, ev_row, hidden, lx, dsilu, update, gs, gv, wn, vout)


AT_AIN, AT_EMB, AT_FFIN, AT_FFH, AT_NV, FAC_NODE = 0, 512, 1792, 3072, 3840, 4608
AT_GELU, AT_GUP, AT_FIN, AT_COT, AT_ATT, AT_GBR, FAC_FEED = 0, 2048, 4096, 4608, 5120, 5632, 6144
AT_GQKV, AT_STREAM, AT_GPRE, AT_GFU, AT_GFH, FAC_BACK = 0, 1536, 2048, 3072, 3840, 4608
ROWS_F, ROWS_M, ROWS_S, ROWS_T = 512, 768, 640, 128

def full_block(shape):
    return pl.BlockSpec(shape, lambda: (0,) * len(shape))


def lead_product(former, latter):
    return lax.dot_general(
        former, latter, (((0,), (0,)), ((), ())), preferred_element_type=F32
    )


def swap_halves(values):
    return pltpu.roll(values, 64, 1)


def lower_half(shape):
    return lax.broadcasted_iota(jnp.int32, shape, 1) < 64


def pack_tall(tile, odd):
    rows = tile.shape[0] // 2
    top, low = tile[:rows], tile[rows:]
    side = lower_half((rows, 128))
    if odd:
        return jnp.where(side, swap_halves(top), low)
    return jnp.where(side, top, swap_halves(low))


def unpack_tall(block):
    rows = block.shape[0]
    side = lower_half((rows, 128))
    return jnp.concatenate(
        [jnp.where(side, block, 0.0), jnp.where(side, swap_halves(block), 0.0)], 0
    )


def centre(values):
    centred = values - jnp.mean(values, axis=-1, keepdims=True)
    inverse = lax.rsqrt(jnp.mean(centred * centred, axis=-1, keepdims=True) + 1e-05)
    return centred * inverse, inverse


def centre_back(hat, inverse, grad):
    return inverse * (
        grad
        - jnp.mean(grad, axis=-1, keepdims=True)
        - hat * jnp.mean(grad * hat, axis=-1, keepdims=True)
    )


def power_of(parts):
    return parts[0] * parts[0] + parts[1] * parts[1] + parts[2] * parts[2]


def node_forward_kernel(
    ns_ref, nv_ref, as_ref, av_ref, ng_ref, fv_ref, fs_ref, fu_ref, we_ref, ag_ref, wq_ref,
    s1_ref, v1_ref, ffh_ref, ffp_ref, ffu_ref, v2_ref, sz_ref, fac_ref, out_ref,
):
    nodes = ns_ref.shape[0]
    s1 = ns_ref[...].astype(F32) + as_ref[...]
    s1_ref[...] = s1
    hat, unused = centre(s1)
    normed_s = hat * ng_ref[...]
    v1 = [nv_ref[c].astype(F32) + av_ref[c] for c in range(3)]
    scale = lax.rsqrt(jnp.mean(power_of(v1), axis=-1, keepdims=True) + 1e-05)
    normed_v = [v * scale for v in v1]
    ffh = [product(v.astype(BF), fv_ref[...]) for v in normed_v]
    power = power_of(ffh) + 1.0
    fac_ref[:, pl.ds(AT_FFIN, D_S)] = normed_s.astype(BF)
    fac_ref[:, pl.ds(AT_FFIN + D_S, D_V)] = (power * lax.rsqrt(power)).astype(BF)
    ffp = product(fac_ref[:, pl.ds(AT_FFIN, D_S + D_V)], fs_ref[...])
    ffu = [product(h.astype(BF), fu_ref[...]) for h in ffh]
    for c in range(3):
        v1_ref[c] = v1[c]
        fac_ref[:, pl.ds(AT_FFH + c * D_V, D_V)] = ffh[c].astype(BF)
        fac_ref[:, pl.ds(AT_NV + c * D_V, D_V)] = normed_v[c].astype(BF)
        ffh_ref[c] = ffh[c]
        ffu_ref[c] = ffu[c]
    ffp_ref[...] = ffp
    s2 = normed_s + ffp * sigmoid(ffp)
    power = power_of(ffu) + 1.0
    gate = sigmoid(power * lax.rsqrt(power))
    v2 = [normed_v[c] + ffu[c] * gate for c in range(3)]
    for c in range(3):
        v2_ref[c] = v2[c]
    power = power_of(v2) + 1.0
    fac_ref[:, pl.ds(AT_EMB, D_S)] = s2.astype(BF)
    fac_ref[:, pl.ds(AT_EMB + D_S, D_V)] = (power * lax.rsqrt(power)).astype(BF)
    sz = product(fac_ref[:, pl.ds(AT_EMB, D_S + D_V)], we_ref[...])
    sz_ref[...] = sz
    hat, unused = centre(sz)
    attn_in = (hat * ag_ref[...]).astype(BF)
    fac_ref[:, pl.ds(AT_AIN, D_MODEL)] = attn_in
    q, k, v = [product(attn_in, wq_ref[:, pl.ds(n * D_MODEL, D_MODEL)]) for n in range(3)]
    pack_heads(q, k, v, out_ref)


def pack_heads(q, k, v, out_ref):
    nodes = q.shape[0]
    side = lower_half((nodes, 128))
    for pair in range(HEADS // 2):
        cols = slice(pair * 128, pair * 128 + 128)
        qp, kp, vp = q[:, cols], k[:, cols], v[:, cols]
        even = jnp.where(side, qp, swap_halves(kp))
        odd = jnp.where(side, swap_halves(qp), kp)
        for n, block in enumerate((even, odd)):
            head = 2 * pair + n
            out_ref[head, pl.ds(0, nodes), :] = block.astype(BF)
            out_ref[head, pl.ds(nodes, nodes // 2), :] = pack_tall(vp, n == 1).astype(BF)


def split_heads(x_ref, nodes):
    spaces = x_ref.shape[0]
    both = x_ref[:, pl.ds(0, nodes), :].reshape(spaces * nodes, 128).astype(F32)
    queries = jnp.where(lower_half(both.shape), both, 0.0).astype(BF)
    keys = swap_halves(both).astype(BF)
    values = jnp.concatenate(
        [unpack_tall(x_ref[d, pl.ds(nodes, nodes // 2), :].astype(F32)) for d in range(spaces)], 0
    ).astype(BF)
    return queries, keys, values


def attend_kernel(x_ref, id_ref, probs_ref, att_ref, out_ref):
    spaces = x_ref.shape[0]
    nodes = x_ref.shape[1] * 2 // 3
    count = spaces * nodes
    queries, keys, values = split_heads(x_ref, nodes)
    row_ids = id_ref[...]
    column_ids = jnp.transpose(jnp.broadcast_to(row_ids, (8, count)))[:, 0:1]
    block = 2 * nodes
    for first in range(0, count, block):
        scores = product_back(queries[first : first + block], keys) * HEAD_DIM ** (-0.5)
        same = column_ids[first : first + block] == row_ids
        scores = jnp.where(same, scores, -1000000000.0)
        shifted = jnp.exp(scores - jnp.max(scores, axis=-1, keepdims=True))
        probs = (shifted / jnp.sum(shifted, axis=-1, keepdims=True)).astype(BF)
        probs_ref[pl.ds(first, block), :] = probs
        att = product(probs, values)
        att_ref[pl.ds(first, block), :] = att
        for n in range(block // nodes):
            tile = att[n * nodes : (n + 1) * nodes]
            out_ref[first // nodes + n] = pack_tall(tile, False).astype(BF)


def attend_backward_kernel(x_ref, probs_ref, att_ref, g_ref, out_ref, gs_scr):
    spaces = x_ref.shape[0]
    nodes = x_ref.shape[1] * 2 // 3
    count = spaces * nodes
    queries, keys, values = split_heads(x_ref, nodes)
    grad = jnp.concatenate(
        [unpack_tall(g_ref[d].astype(F32)) for d in range(spaces)], 0
    )
    dots = jnp.sum(grad * att_ref[...], axis=-1, keepdims=True)
    grad = grad.astype(BF)
    block = 2 * nodes
    scale = HEAD_DIM ** (-0.5)
    grad_queries = []
    for first in range(0, count, block):
        grad_probs = product_back(grad[first : first + block], values)
        part = probs_ref[pl.ds(first, block), :].astype(F32)
        grad_scores = (part * (grad_probs - dots[first : first + block])).astype(BF)
        gs_scr[pl.ds(first, block), :] = grad_scores
        grad_queries.append(product(grad_scores, keys))
    grad_queries = jnp.concatenate(grad_queries, 0) * scale
    grad_keys = jnp.transpose(lead_product(queries, gs_scr[...])) * scale
    grad_values = jnp.transpose(lead_product(grad, probs_ref[...]))
    side = lower_half((nodes, 128))
    for d in range(spaces):
        rows = slice(d * nodes, (d + 1) * nodes)
        out_ref[d, pl.ds(0, nodes), :] = jnp.where(
            side, grad_queries[rows], swap_halves(grad_keys[rows])
        ).astype(BF)
        out_ref[d, pl.ds(nodes, nodes // 2), :] = pack_tall(grad_values[rows], False).astype(BF)


def merge_heads(block_ref, first, half):
    tiles = []
    for pair in range(HEADS // 2):
        even = unpack_tall(block_ref[2 * pair, pl.ds(first, half), :].astype(F32))
        odd = unpack_tall(block_ref[2 * pair + 1, pl.ds(first, half), :].astype(F32))
        tiles.append(even + swap_halves(odd))
    return jnp.concatenate(tiles, 1)


def feed_kernel(
    att_ref, sz_ref, wo_ref, fg_ref, wu_ref, wd_ref, cot_ref,
    out_ref, gatt_ref, gs1_ref, ggain_ref, fac_ref,
):
    nodes = sz_ref.shape[0]
    att = merge_heads(att_ref, 0, nodes // 2).astype(BF)
    fac_ref[:, pl.ds(AT_ATT, D_MODEL)] = att
    stream_one = sz_ref[...] + product(att, wo_ref[...])
    hat, inverse = centre(stream_one)
    ffn_in = (hat * fg_ref[...]).astype(BF)
    fac_ref[:, pl.ds(AT_FIN, D_MODEL)] = ffn_in
    ffn = wu_ref.shape[1]
    cot = cot_ref[...]
    fac_ref[:, pl.ds(AT_COT, D_MODEL)] = cot
    for start in range(0, ffn, 512):
        cols = pl.ds(start, 512)
        x = product(ffn_in, wu_ref[:, cols])
        cdf = 0.5 * (1.0 + lax.erf(x * (0.5**0.5)))
        fac_ref[:, pl.ds(AT_GELU + start, 512)] = (x * cdf).astype(BF)
        slope = cdf + x * jnp.exp(-0.5 * x * x) * ((0.5 / math.pi) ** 0.5)
        fac_ref[:, pl.ds(AT_GUP + start, 512)] = (
            product_back(cot, wd_ref[cols, :]) * slope
        ).astype(BF)
    out_ref[...] = (
        stream_one + product(fac_ref[:, pl.ds(AT_GELU, ffn)], wd_ref[...])
    ).astype(BF)
    grad_in = product_back(fac_ref[:, pl.ds(AT_GUP, ffn)], wu_ref[...])
    ggain_ref[...] = jnp.sum(grad_in * hat, axis=0, keepdims=True)
    grad_one = cot.astype(F32) + centre_back(hat, inverse, grad_in * fg_ref[...])
    gs1_ref[...] = grad_one
    branch = grad_one.astype(BF)
    fac_ref[:, pl.ds(AT_GBR, D_MODEL)] = branch
    grad_att = product_back(branch, wo_ref[...])
    for head in range(HEADS):
        tile = grad_att[:, head // 2 * 128 : head // 2 * 128 + 128]
        gatt_ref[head] = pack_tall(tile, head % 2 == 1).astype(BF)


def core_columns(values, core):
    values = values.astype(F32)
    side = lower_half((values.shape[0], 128))
    tiles = []
    for n in range(0, 512, 256):
        one, two = values[:, n : n + 128], values[:, n + 128 : n + 256]
        even = jnp.where(side, one, swap_halves(two))
        odd = jnp.where(side, swap_halves(one), two)
        tiles.append(jnp.where(core == 0, even, odd))
    return jnp.concatenate(tiles, 1).astype(BF)


def both_rows(own_ref, other_ref, start, width):
    return jnp.concatenate(
        [own_ref[:, pl.ds(start, width)], other_ref[:, pl.ds(start, width)]], 0
    )


def feed_grads_kernel(own_ref, other_ref, pack_ref):
    quads = pack_ref.shape[0]
    core = lax.rem(lax.axis_index("space"), 2)
    cot = both_rows(own_ref, other_ref, AT_COT, D_MODEL)
    for z in range(quads):
        start = pl.multiple_of(AT_GELU + (2 * z + core) * 256, 256)
        block = lead_product(both_rows(own_ref, other_ref, start, 256), cot)
        pack_ref[z, pl.ds(0, 256), :] = block.astype(BF)
    left = core_columns(both_rows(own_ref, other_ref, AT_FIN, D_MODEL), core)
    for n in range(4):
        block = lead_product(left, both_rows(own_ref, other_ref, AT_GUP + n * 512, 512)).astype(BF)
        for z in range(quads):
            pack_ref[z, pl.ds(256 + n * 64, 64), :] = block[z * 64 : (z + 1) * 64]


def node_grads_kernel(
    node_ref, node_other, back_ref, back_other, feed_ref, feed_other, pack_ref, tall_scr, low_scr
):
    quads = pack_ref.shape[0]
    core = lax.rem(lax.axis_index("space"), 2)
    left = core_columns(both_rows(node_ref, node_other, AT_AIN, D_MODEL), core)
    pairs = [
        (left, both_rows(back_ref, back_other, AT_GQKV + n * D_MODEL, D_MODEL)) for n in range(3)
    ]
    pairs.append(
        (
            core_columns(both_rows(feed_ref, feed_other, AT_ATT, D_MODEL), core),
            both_rows(feed_ref, feed_other, AT_GBR, D_MODEL),
        )
    )
    for n, (one, two) in enumerate(pairs):
        block = lead_product(one, two).astype(BF)
        for z in range(quads):
            pack_ref[z, pl.ds(n * 64, 64), :] = block[z * 64 : (z + 1) * 64]
    emb = both_rows(node_ref, node_other, AT_EMB, D_S + D_V)
    ffin = both_rows(node_ref, node_other, AT_FFIN, D_S + D_V)
    rights = [(emb, back_ref, back_other, AT_STREAM)]
    rights += [(ffin, back_ref, back_other, AT_GPRE + n * 512) for n in range(2)]
    for n, (one, own, other, start) in enumerate(rights):
        tall_scr[...] = lead_product(one, both_rows(own, other, start, 512)).astype(BF)
        for z in range(quads):
            rows = pl.ds(pl.multiple_of((2 * z + core) * 160, 32), 160)
            pack_ref[z, pl.ds(256 + n * 160, 160), :] = tall_scr[rows, :]
    vec = up = None
    for c in range(3):
        one = lead_product(
            both_rows(node_ref, node_other, AT_NV + c * D_V, D_V),
            both_rows(back_ref, back_other, AT_GFH + c * D_V, D_V),
        )
        vec = one if vec is None else vec + one
        one = lead_product(
            both_rows(node_ref, node_other, AT_FFH + c * D_V, D_V),
            both_rows(back_ref, back_other, AT_GFU + c * D_V, D_V),
        )
        up = one if up is None else up + one
    low_scr[...] = jnp.concatenate([vec, up], 1).astype(BF)
    for z in range(quads):
        rows = pl.ds(pl.multiple_of((2 * z + core) * 32, 32), 32)
        pack_ref[z, pl.ds(736, 32), :] = low_scr[rows, :]


def node_backward_kernel(
    gq_ref, gs1_ref, s1_ref, v1_ref, ffh_ref, ffp_ref, ffu_ref, v2_ref,
    sz_ref, ng_ref, fv_ref, fs_ref, fu_ref, we_ref, ag_ref, wq_ref, fgain_ref,
    gsone_ref, gvone_ref, gains_ref, back_ref,
):
    nodes = gs1_ref.shape[0]
    shards = gq_ref.shape[0]
    side = lower_half((nodes, 128))
    tiles = [[], []]
    for pair in range(HEADS // 2):
        even = gq_ref[2 * pair, pl.ds(0, nodes), :].astype(F32)
        odd = gq_ref[2 * pair + 1, pl.ds(0, nodes), :].astype(F32)
        tiles[0].append(jnp.where(side, even, swap_halves(odd)))
        tiles[1].append(jnp.where(side, swap_halves(even), odd))
    grads = [jnp.concatenate(tile, 1).astype(BF) for tile in tiles]
    grads.append(merge_heads(gq_ref, nodes, nodes // 2).astype(BF))
    for n in range(3):
        back_ref[:, pl.ds(AT_GQKV + n * D_MODEL, D_MODEL)] = grads[n]
    grad_in = product_back(back_ref[:, pl.ds(AT_GQKV, 3 * D_MODEL)], wq_ref[...])
    hat, inverse = centre(sz_ref[...])
    grad_attn_gain = jnp.sum(grad_in * hat, axis=0, keepdims=True)
    stream = gs1_ref[...] + centre_back(hat, inverse, grad_in * ag_ref[...])
    stream = stream.astype(BF)
    back_ref[:, pl.ds(AT_STREAM, D_MODEL)] = stream
    grad_emb = product_back(stream, we_ref[...])
    grad_s2, grad_len = grad_emb[:, :D_S], grad_emb[:, D_S:]
    v2 = [v2_ref[c] for c in range(3)]
    factor = grad_len * lax.rsqrt(power_of(v2) + 1.0)
    grad_v2 = [factor * v for v in v2]
    x = ffp_ref[...]
    s = sigmoid(x)
    grad_pre = (grad_s2 * (s + x * s * (1.0 - s))).astype(BF)
    back_ref[:, pl.ds(AT_GPRE, D_S)] = grad_pre
    grad_ffin = product_back(grad_pre, fs_ref[...])
    z = [ffu_ref[c] for c in range(3)]
    power = power_of(z) + 1.0
    inverse = lax.rsqrt(power)
    s = sigmoid(power * inverse)
    dot = z[0] * grad_v2[0] + z[1] * grad_v2[1] + z[2] * grad_v2[2]
    factor = dot * inverse * (s * (1.0 - s))
    grad_up = [(grad_v2[c] * s + z[c] * factor).astype(BF) for c in range(3)]
    h = [ffh_ref[c] for c in range(3)]
    factor = grad_ffin[:, D_S:] * lax.rsqrt(power_of(h) + 1.0)
    v1 = [v1_ref[c] for c in range(3)]
    scale = lax.rsqrt(jnp.mean(power_of(v1), axis=-1, keepdims=True) + 1e-05)
    grad_nv = []
    for c in range(3):
        back_ref[:, pl.ds(AT_GFU + c * D_V, D_V)] = grad_up[c]
        grad_h = (product_back(grad_up[c], fu_ref[...]) + factor * h[c]).astype(BF)
        back_ref[:, pl.ds(AT_GFH + c * D_V, D_V)] = grad_h
        grad_nv.append(grad_v2[c] + product_back(grad_h, fv_ref[...]))
    grad_ns = grad_s2 + grad_ffin[:, :D_S]
    hat, inverse = centre(s1_ref[...])
    grad_norm_gain = jnp.sum(grad_ns * hat, axis=0, keepdims=True)
    gsone_ref[...] = centre_back(hat, inverse, grad_ns * ng_ref[...])
    dot = grad_nv[0] * v1[0] + grad_nv[1] * v1[1] + grad_nv[2] * v1[2]
    dot = jnp.mean(dot, axis=-1, keepdims=True) * scale * scale
    for c in range(3):
        gvone_ref[c] = scale * (grad_nv[c] - v1[c] * dot)
    gains_ref[...] = jnp.zeros_like(gains_ref)
    gains_ref[0:1, :] = grad_norm_gain
    for p in range(shards):
        pair = slice(p // 2 * 128, p // 2 * 128 + 128)
        left = jnp.broadcast_to(grad_attn_gain[:, pair], (8, 128))
        right = jnp.broadcast_to(fgain_ref[:, pair], (8, 128))
        if p % 2 == 0:
            both = jnp.where(lower_half((8, 128)), left, swap_halves(right))
        else:
            both = jnp.where(lower_half((8, 128)), swap_halves(left), right)
        gains_ref[1:2, pl.ds(p * 128, 128)] = both[0:1]


def place():
    dp, space = lax.axis_index("dp"), lax.axis_index("space")
    return {"x": lax.rem(dp, 2), "y": dp // 2, "z": space // 2, "core": lax.rem(space, 2)}


def peer(way, shift=1):
    at = place()
    if way == "x":
        return {"dp": 2 * at["y"] + 1 - at["x"]}
    if way == "y":
        return {"dp": 2 * (1 - at["y"]) + at["x"]}
    if way == "diagonal":
        return {"dp": 2 * (1 - at["y"]) + 1 - at["x"]}
    if way == "core":
        return {"space": 2 * at["z"] + 1 - at["core"]}
    if way == "z":
        return {"space": 2 * lax.rem(at["z"] + shift, 4) + at["core"]}
    return {"space": lax.rem(lax.axis_index("space") + shift, lax.axis_size("space"))}


def greet(peers):
    barrier = pltpu.get_barrier_semaphore()
    for one in peers:
        pl.semaphore_signal(barrier, inc=1, device_id=one, device_id_type=MESH)
    pl.semaphore_wait(barrier, len(peers))


class Wires:
    def __init__(self, send_sem, recv_sem):
        self.send_sem, self.recv_sem, self.used = send_sem, recv_sem, 0

    def copy(self, source, target, to):
        n = self.used
        self.used += 1
        return pltpu.make_async_remote_copy(
            src_ref=source,
            dst_ref=target,
            send_sem=self.send_sem.at[n],
            recv_sem=self.recv_sem.at[n],
            device_id=to,
            device_id_type=MESH,
        )


def rows_at(ref, start, count):
    return ref.at[:, pl.ds(start, count), :]


def first_cut(wires, share_ref, got_ref):
    at = place()
    quarter = share_ref.shape[1] // 4
    return [
        wires.copy(rows_at(share_ref, (1 - at["x"]) * quarter, quarter), got_ref.at[0], peer("x")),
        wires.copy(
            rows_at(share_ref, (3 - at["y"]) * quarter, quarter), got_ref.at[1], peer("y")
        ),
    ]


def own_quarters(share_ref, own_ref, sems):
    at = place()
    quarter = share_ref.shape[1] // 4
    starts = (at["x"] * quarter, (2 + at["y"]) * quarter)
    return [
        pltpu.make_async_copy(rows_at(share_ref, start, quarter), own_ref.at[n], sems.at[n])
        for n, start in enumerate(starts)
    ]


def first_add(own_ref, got_ref, sum_ref):
    for n in range(2):
        sum_ref[n] = (own_ref[n].astype(F32) + got_ref[n].astype(F32)).astype(BF)


def first_add_whole(share_ref, got_ref, sum_ref):
    at = place()
    quarter = share_ref.shape[1] // 4
    for n, start in enumerate((at["x"] * quarter, (2 + at["y"]) * quarter)):
        own = share_ref[:, pl.ds(pl.multiple_of(start, 16), quarter), :]
        sum_ref[n] = (own.astype(F32) + got_ref[n].astype(F32)).astype(BF)


def second_cut(wires, sum_ref, got_ref):
    at = place()
    eighth = sum_ref.shape[2] // 2
    return [
        wires.copy(
            rows_at(sum_ref.at[0], (1 - at["y"]) * eighth, eighth), got_ref.at[0], peer("y")
        ),
        wires.copy(
            rows_at(sum_ref.at[1], (1 - at["x"]) * eighth, eighth), got_ref.at[1], peer("x")
        ),
    ]


def second_add(sum_ref, got_ref, out_ref, base=0):
    at = place()
    eighth = sum_ref.shape[2] // 2
    for n, start in enumerate((at["y"] * eighth, at["x"] * eighth)):
        own = sum_ref[n, :, pl.ds(pl.multiple_of(start, 16), eighth), :]
        out_ref[:, pl.ds(base + n * eighth, eighth), :] = (
            own.astype(F32) + got_ref[n].astype(F32)
        ).astype(BF)


def z_send(wires, part_ref, got_ref):
    at = place()
    return [
        wires.copy(
            part_ref.at[lax.rem(at["z"] + shift, 4)], got_ref.at[shift - 1], peer("z", shift)
        )
        for shift in (1, 2, 3)
    ]


def z_add(own, got_ref):
    total = own.astype(F32)
    for n in range(3):
        total = total + got_ref[n].astype(F32)
    return total.astype(BF)


def start_all(copies):
    for copy in copies:
        copy.start()
    return copies


def wait_all(copies):
    for copy in copies:
        copy.wait()


def sent_row(sent_ref, scr):
    spaces = sent_ref.shape[0]
    scr[...] = jnp.zeros_like(scr)
    scr[pl.ds(0, spaces), pl.ds(0, CAP)] = sent_ref[...].astype(F32)
    row = scr[0:1, :]
    for d in range(1, spaces):
        row = row + pltpu.roll(scr[d : d + 1, :], d * CAP, 1)
    return row


def pick_matrix(row, nodes):
    places = lax.broadcasted_iota(jnp.int32, (nodes, row.shape[1]), 0).astype(F32)
    return (places == row).astype(BF)


def prepare_kernel(
    ns_ref, nv_ref, sent_ref, vn_ref, we_ref, vout_ref, norms_ref, wnode_hbm,
    b_ref, p_ref, q_ref, ts_ref, tv_ref, vs_ref, vt_ref, vo_ref, mix_ref, wn_ref,
    wnode, row_scr, vt_scr, out_scr, in_scr, send_sem, recv_sem, load_sem,
):
    nodes = ns_ref.shape[0]
    table = ts_ref.shape[0]
    spaces = lax.axis_size("space")
    me = lax.axis_index("space")
    wires = Wires(send_sem, recv_sem)
    ring = [peer("group", shift) for shift in range(1, spaces)]
    load = pltpu.make_async_copy(wnode_hbm, wnode, load_sem)
    load.start()
    pick = pick_matrix(sent_row(sent_ref, row_scr), nodes)
    rows = lead_product(pick, ns_ref[...]).astype(BF)
    for d in range(spaces):
        out_scr[d, :, pl.ds(0, D_S)] = rows[d * CAP : (d + 1) * CAP]
    for c in range(3):
        rows = lead_product(pick, nv_ref[c]).astype(BF)
        for d in range(spaces):
            out_scr[d, :, pl.ds(D_S + c * D_V, D_V)] = rows[d * CAP : (d + 1) * CAP]
    greet(ring)
    copies = start_all(
        [
            wires.copy(out_scr.at[lax.rem(me + n + 1, spaces)], in_scr.at[me], ring[n])
            for n in range(spaces - 1)
        ]
    )
    in_scr[me] = out_scr[me]
    vs_ref[pl.ds(0, 512), :] = vn_ref[pl.ds(0, 512), :]
    vt_scr[...] = jnp.zeros_like(vt_scr)
    vt_scr[pl.ds(0, H_V + 1), :] = vn_ref[pl.ds(512, H_V + 1), :].astype(F32)
    row = lax.broadcasted_iota(jnp.int32, (H_P, D_V), 0)
    vt_ref[...] = jnp.where(row < H_V, pltpu.roll(vt_scr[...], H_P - 1, 0), 0.0).astype(BF)
    low = row[: H_P - 512]
    first = jnp.broadcast_to(vt_scr[0:1, :], low.shape)
    vs_ref[pl.ds(512, H_P - 512), :] = jnp.where(low == 0, first, 0.0).astype(BF)
    vo_ref[pl.ds(0, 512), :] = vout_ref[pl.ds(0, 512), :]
    first = jnp.broadcast_to(vout_ref[pl.ds(512, 1), :].astype(F32), low.shape)
    vo_ref[pl.ds(512, H_P - 512), :] = jnp.where(low == 0, first, 0.0).astype(BF)
    for c in range(3):
        q_ref[c] = product_back(nv_ref[c], vt_ref[...])
        p_ref[c, pl.ds(0, nodes), :] = product_back(nv_ref[c], vs_ref[...]).astype(BF)
        tv_ref[c, pl.ds(0, nodes), :] = nv_ref[c]
    ts_ref[pl.ds(0, nodes), :] = ns_ref[...]
    first = jnp.broadcast_to(norms_ref[pl.ds(512, 1), :].astype(F32), (16, D_S))
    row = lax.broadcasted_iota(jnp.int32, (16, D_S), 0)
    wn_ref[pl.ds(0, 512), :] = norms_ref[pl.ds(0, 512), :]
    wn_ref[pl.ds(512, 16), :] = jnp.where(row == 0, first, 0.0).astype(BF)
    wn_ref[pl.ds(528, D_E), :] = we_ref[...]
    wn_ref[pl.ds(528 + D_E, H_P - 528 - D_E), :] = jnp.zeros((H_P - 528 - D_E, D_S), BF)
    mix_ref[pl.ds(table, H_P), :] = wn_ref[...]
    load.wait()
    b_ref[...] = product(ns_ref[...], wnode[:, pl.ds(D_S, D_S)])
    mix_ref[pl.ds(0, nodes), :] = product(ns_ref[...], wnode[:, pl.ds(0, D_S)]).astype(BF)
    wait_all(copies)
    got = in_scr[...].reshape(spaces * CAP, D_S + 3 * D_V)
    ts_ref[pl.ds(nodes, table - nodes), :] = got[:, :D_S]
    mix_ref[pl.ds(nodes, table - nodes), :] = product(
        got[:, :D_S], wnode[:, pl.ds(0, D_S)]
    ).astype(BF)
    for c in range(3):
        rows = got[:, D_S + c * D_V : D_S + (c + 1) * D_V]
        tv_ref[c, pl.ds(nodes, table - nodes), :] = rows
        p_ref[c, pl.ds(nodes, table - nodes), :] = product_back(rows, vs_ref[...]).astype(BF)


def prepare(node_scalar, node_vector, sent, vec_node, w_edge, vec_out, w_norms, w_node):
    nodes = node_scalar.shape[0]
    spaces = sent.shape[0]
    table = nodes + spaces * CAP
    hbm = pl.BlockSpec(memory_space=pl.ANY)
    vmem = pl.BlockSpec(memory_space=pltpu.VMEM)
    outs = [
        ((nodes, D_S), F32),
        ((3, table, H_P), BF),
        ((3, nodes, H_P), F32),
        ((table, D_S), BF),
        ((3, table, D_V), BF),
        ((H_P, D_V), BF),
        ((H_P, D_V), BF),
        ((H_P, D_V), BF),
        ((table + H_P, D_S), BF),
        ((H_P, D_S), BF),
    ]
    blocks = (spaces, CAP, D_S + 3 * D_V)
    return pl.pallas_call(
        prepare_kernel,
        out_shape=[jax.ShapeDtypeStruct(shape, kind) for shape, kind in outs],
        in_specs=[vmem] * 7 + [hbm],
        out_specs=[vmem] * 10,
        scratch_shapes=[
            pltpu.VMEM(w_node.shape, BF),
            pltpu.VMEM((8, 128), F32),
            pltpu.VMEM((H_P, D_V), F32),
            pltpu.VMEM(blocks, BF),
            pltpu.VMEM(blocks, BF),
            pltpu.SemaphoreType.DMA((spaces - 1,)),
            pltpu.SemaphoreType.DMA((spaces - 1,)),
            pltpu.SemaphoreType.DMA,
        ],
        compiler_params=pltpu.CompilerParams(
            collective_id=3, has_side_effects=True, vmem_limit_bytes=VMEM_LIMIT
        ),
        name="prepare",
    )(node_scalar, node_vector, sent, vec_node, w_edge, vec_out, w_norms, w_node)


def middle_kernel(
    ns_ref, nv_ref, as_ref, av_ref, gains_in, fv_ref, fs_ref, fu_ref, we_ref, wq_ref, id_ref, cot_ref, wo_hbm, wu_hbm, wd_hbm, ts_hbm, ns_hbm,
    out_ref, gsone_ref, gvone_ref, gains_ref, m_ref, f_ref, tso_hbm, nso_hbm,
    s1, v1, ffh, ffp, ffu, v2, sz, fac_node, fac_node_o, heads_out, heads_in,
    probs, att, att_out, att_in, wo_ref, wu_ref, wd_ref, gatt, gatt_in, gs1, fgain,
    fac_feed, fac_feed_o, gs_scr, ghead, ghead_in, fac_back, fac_back_o,
    first, first_got, first_sum, first_got2, tall_scr, low_scr,
    send_sem, recv_sem, load_sem,
):
    spaces = lax.axis_size("space")
    quads = spaces // 2
    me = lax.axis_index("space")
    ng_ref = gains_in.at[:, pl.ds(0, D_S)]
    ag_ref = gains_in.at[:, pl.ds(D_S, D_MODEL)]
    fg_ref = gains_in.at[:, pl.ds(D_S + D_MODEL, D_MODEL)]
    wires = Wires(send_sem, recv_sem)
    ring = [peer("group", shift) for shift in range(1, spaces)]

    def exchange(source, target):
        return [
            wires.copy(source.at[lax.rem(me + n + 1, spaces)], target.at[me], ring[n])
            for n in range(spaces - 1)
        ]

    def keep(source, target):
        target[me] = source[me]

    loads = [
        pltpu.make_async_copy(source, target, load_sem.at[n])
        for n, (source, target) in enumerate(
            ((wo_hbm, wo_ref), (wu_hbm, wu_ref), (wd_hbm, wd_ref))
        )
    ]
    start_all(loads)
    greet(ring + [peer("x"), peer("y")])
    swaps = start_all(
        [wires.copy(ts_hbm, tso_hbm, peer("core")), wires.copy(ns_hbm, nso_hbm, peer("core"))]
    )
    node_forward_kernel(
        ns_ref, nv_ref, as_ref, av_ref, ng_ref, fv_ref, fs_ref, fu_ref, we_ref, ag_ref, wq_ref,
        s1, v1, ffh, ffp, ffu, v2, sz, fac_node, heads_out,
    )
    copies = start_all(exchange(heads_out, heads_in))
    swaps += start_all([wires.copy(fac_node, fac_node_o, peer("core"))])
    keep(heads_out, heads_in)
    wait_all(copies)
    attend_kernel(heads_in, id_ref, probs, att, att_out)
    copies = start_all(exchange(att_out, att_in))
    keep(att_out, att_in)
    wait_all(loads)
    wait_all(copies)
    feed_kernel(
        att_in, sz, wo_ref, fg_ref, wu_ref, wd_ref, cot_ref, out_ref, gatt, gs1, fgain, fac_feed
    )
    copies = start_all(exchange(gatt, gatt_in))
    feed_swap = start_all([wires.copy(fac_feed, fac_feed_o, peer("core"))])
    keep(gatt, gatt_in)
    wait_all(copies)
    attend_backward_kernel(heads_in, probs, att, gatt_in, ghead, gs_scr)
    copies = start_all(exchange(ghead, ghead_in))
    keep(ghead, ghead_in)
    wait_all(feed_swap)
    feed_grads_kernel(fac_feed, fac_feed_o, first)
    cuts = start_all(first_cut(wires, first, first_got))
    wait_all(copies)
    node_backward_kernel(
        ghead_in, gs1, s1, v1, ffh, ffp, ffu, v2, sz,
        ng_ref, fv_ref, fs_ref, fu_ref, we_ref, ag_ref, wq_ref, fgain,
        gsone_ref, gvone_ref, gains_ref, fac_back,
    )
    swaps += start_all([wires.copy(fac_back, fac_back_o, peer("core"))])
    wait_all(cuts)
    first_add_whole(first, first_got, first_sum)
    cuts = start_all(second_cut(wires, first_sum, first_got2))
    wait_all(swaps)
    node_grads_kernel(
        fac_node, fac_node_o, fac_back, fac_back_o, fac_feed, fac_feed_o, m_ref, tall_scr, low_scr
    )
    wait_all(cuts)
    second_add(first_sum, first_got2, f_ref)


def middle(vmem_operands, hbm_operands, table_s, node_scalar, quads):
    nodes = node_scalar.shape[0]
    spaces = 2 * quads
    count = spaces * nodes
    hbm = pl.BlockSpec(memory_space=pl.ANY)
    vmem = pl.BlockSpec(memory_space=pltpu.VMEM)
    operands = tuple(vmem_operands) + tuple(hbm_operands) + (table_s, node_scalar)
    bits = lambda *shape: pltpu.VMEM(shape, BF)
    wide = lambda *shape: pltpu.VMEM(shape, F32)
    packed = (spaces, nodes + nodes // 2, 128)
    small = (spaces, nodes // 2, 128)
    outs = [
        ((nodes, D_MODEL), BF),
        ((nodes, D_S), F32),
        ((3, nodes, D_V), F32),
        ((8, D_S), F32),
        ((quads, ROWS_M, 512), BF),
        ((quads, ROWS_F // 4, 512), BF),
        (table_s.shape, BF),
        (node_scalar.shape, BF),
    ]
    wires = 4 * (spaces - 1) + 9
    return pl.pallas_call(
        middle_kernel,
        out_shape=[jax.ShapeDtypeStruct(shape, kind) for shape, kind in outs],
        in_specs=[vmem] * len(vmem_operands) + [hbm] * (len(hbm_operands) + 2),
        out_specs=[vmem] * 6 + [hbm] * 2,
        scratch_shapes=[
            wide(nodes, D_S), wide(3, nodes, D_V), wide(3, nodes, D_V), wide(nodes, D_S),
            wide(3, nodes, D_V), wide(3, nodes, D_V), wide(nodes, D_MODEL),
            bits(nodes, FAC_NODE), bits(nodes, FAC_NODE), bits(*packed), bits(*packed),
            bits(count, count), wide(count, 128), bits(*small), bits(*small),
        ]
        + [bits(*one.shape) for one in hbm_operands]
        + [
            bits(*small), bits(*small), wide(nodes, D_MODEL), wide(1, D_MODEL),
            bits(nodes, FAC_FEED), bits(nodes, FAC_FEED), bits(count, count),
            bits(*packed), bits(*packed), bits(nodes, FAC_BACK), bits(nodes, FAC_BACK),
            bits(quads, ROWS_F, 512), bits(2, quads, ROWS_F // 4, 512),
            bits(2, quads, ROWS_F // 4, 512), bits(2, quads, ROWS_F // 8, 512),
            bits(D_S + D_V, 512), bits(D_V, 512),
            pltpu.SemaphoreType.DMA((wires,)),
            pltpu.SemaphoreType.DMA((wires,)),
            pltpu.SemaphoreType.DMA((len(hbm_operands),)),
        ],
        compiler_params=pltpu.CompilerParams(
            collective_id=0, has_side_effects=True, vmem_limit_bytes=VMEM_LIMIT
        ),
        name="middle",
    )(*operands)


def slot_rows(rows_scr, first_slot, nodes):
    return jnp.concatenate([rows_scr[pl.ds(first_slot + k, 1), :] for k in range(GROUP)], 1)


def one_hot_rows(rows_scr, first_slot, table, nodes):
    row = slot_rows(rows_scr, first_slot, nodes)
    return (lax.broadcasted_iota(jnp.int32, (table, row.shape[1]), 0).astype(F32) == row).astype(BF)


def keep_rows(ref, rows_scr):
    rows_scr[pl.ds(0, ref.shape[0]), :] = ref[...].astype(F32)


def scalar_backward_kernel(
    near_ref, lx_ref, ds_ref, gsone_ref, wn_ref, ts_hbm, ns_hbm, wnode_hbm, tso_hbm, nso_hbm,
    m_ref, f_ref,
    ratio_ref, pack_ref, rest_ref, gscal_ref, back_ref, m2_ref, ffin_ref,
    ga_ref, gw_ref, gb_ref, pre_scr, grads_scr, grads_got, mix_scr, mix_got, rest_scr, rest_got,
    m_own, m_got, m_sum, m_got2, f_own, f_got, ts_ref, ns_ref, wnode_ref, tso_ref, nso_ref,
    send_sem, recv_sem, load_sem, near_scr,
):
    nodes = gsone_ref.shape[0]
    table = ts_ref.shape[0]
    rows = GROUP * nodes
    quads = pack_ref.shape[0]
    step = pl.program_id(0)
    last = pl.num_programs(0) - 1
    wires = Wires(send_sem, recv_sem)
    f_copies = z_send(wires, f_ref, f_got)
    m_copies = first_cut(wires, m_ref, m_got)
    pairs = (
        (ts_hbm, ts_ref), (ns_hbm, ns_ref), (wnode_hbm, wnode_ref), (tso_hbm, tso_ref),
        (nso_hbm, nso_ref), (f_ref.at[place()["z"]], f_own),
    )
    loads = [
        pltpu.make_async_copy(source, target, load_sem.at[2 + n])
        for n, (source, target) in enumerate(pairs)
    ]
    m_loads = own_quarters(m_ref, m_own, load_sem)
    m_copies2 = second_cut(wires, m_sum, m_got2)
    pair_copies = [
        wires.copy(source, target, peer("core"))
        for source, target in ((grads_scr, grads_got), (mix_scr, mix_got), (rest_scr, rest_got))
    ]

    @pl.when(step == 0)
    def _():
        greet([peer("x"), peer("y"), peer("core")] + [peer("z", shift) for shift in (1, 2, 3)])
        start_all(m_copies)
        start_all(f_copies)
        start_all(m_loads)
        start_all(loads)
        keep_rows(near_ref, near_scr)
        for ref in (ga_ref, gw_ref, gb_ref):
            ref[...] = jnp.zeros_like(ref)

    @pl.when(step == 4)
    def _():
        wait_all(m_loads)
        wait_all(m_copies)
        first_add(m_own, m_got, m_sum)
        start_all(m_copies2)

    for start in range(0, D_S, 256):
        cols = pl.ds(start, 256)
        for first in range(0, nodes, ROW_TILE):
            part = pl.ds(first, ROW_TILE)
            share = gsone_ref[part, cols] * (1.0 / NEIGH)
            acc = None
            for k in range(GROUP):
                g = (ds_ref[k, part, cols].astype(F32) * share).astype(BF)
                pre_scr[pl.ds(k * nodes + first, ROW_TILE), cols] = g
                g = g.astype(F32)
                acc = g if acc is None else acc + g
            gb_ref[part, cols] += acc
    one_hot = one_hot_rows(near_scr, step * GROUP, table, nodes)
    grad_pre = pre_scr[...]
    ga_ref[...] += product(one_hot, grad_pre)
    lx = lx_ref[...].reshape(rows, H_P)
    gw_ref[...] += lead_product(lx, grad_pre)
    for start, width in LANE_BLOCKS:
        cols = pl.ds(start, width)
        grad_length = product_back(grad_pre, wn_ref[cols, :])
        for first in range(0, nodes, ROW_TILE):
            part = pl.ds(first, ROW_TILE)
            for k in range(GROUP):
                at = k * nodes + first
                ratio = grad_length[at : at + ROW_TILE] * pl.reciprocal(
                    lx_ref[k, part, cols].astype(F32), approx=True
                )
                if start == 512:
                    lane = lax.broadcasted_iota(jnp.int32, (ROW_TILE, width), 1)
                    ratio = jnp.where(lane == 0, ratio, 0.0)
                ratio_ref[k, part, cols] = ratio.astype(BF)

    @pl.when(step == last)
    def _():
        core = place()["core"]
        grads_scr[pl.ds(0, table), :] = ga_ref[...].astype(BF)
        grads_scr[pl.ds(table, nodes), :] = gb_ref[...].astype(BF)
        for z in range(quads):
            away = pl.ds(pl.multiple_of((2 * z + 1 - core) * 128, 128), 128)
            for r in range(4):
                mix_scr[z, :, pl.ds(r * 128, 128)] = gw_ref[pl.ds(r * 128, 128), away].astype(BF)
            rest_scr[z] = gw_ref[pl.ds(512, 64), away].astype(BF)
        start_all(pair_copies)
        wait_all(loads)
        ga = grads_scr[pl.ds(0, table), :]
        gb = grads_scr[pl.ds(table, nodes), :]
        projected = product_back(ga, wnode_ref[:, pl.ds(0, D_S)])
        gscal_ref[...] = (
            gsone_ref[...] + product_back(gb, wnode_ref[:, pl.ds(D_S, D_S)]) + projected[:nodes]
        )
        back_ref[...] = projected[nodes:].astype(BF)
        wait_all(pair_copies)
        gao = grads_got[pl.ds(0, table), :]
        gbo = grads_got[pl.ds(table, nodes), :]
        for z in range(quads):
            own = pl.ds(pl.multiple_of((2 * z + core) * 128, 128), 128)
            for half, (left, right, lefto, righto) in enumerate(
                ((ts_ref, ga, tso_ref, gao), (ns_ref, gb, nso_ref, gbo))
            ):
                block = lead_product(left[:, own], right) + lead_product(lefto[:, own], righto)
                block = block.astype(BF)
                for n in range(2):
                    pack_ref[z, pl.ds((2 * half + n) * 128, 128), :] = block[
                        :, n * 512 : (n + 1) * 512
                    ]
            for r in range(4):
                lanes = pl.ds(r * 128, 128)
                pack_ref[z, pl.ds(512, 128), lanes] = (
                    gw_ref[pl.ds(r * 128, 128), own] + mix_got[z, :, lanes].astype(F32)
                ).astype(BF)
            rest_ref[z] = gw_ref[pl.ds(512, 64), own] + rest_got[z].astype(F32)
        wait_all(m_copies2)
        second_add(m_sum, m_got2, m2_ref)
        wait_all(f_copies)
        ffin_ref[...] = z_add(f_own[...], f_got)


def scalar_backward(near, lx, dsilu, gsone, wn, ts, ns, w_node, ts_other, ns_other, m, f):
    nodes = gsone.shape[0]
    table = ts.shape[0]
    quads = m.shape[0]
    rows = GROUP * nodes
    once = pl.Buffered(1)
    whole = lambda shape: pl.BlockSpec(shape, lambda g: (0,) * len(shape), pipeline_mode=once)
    slots = lambda *shape: pl.BlockSpec((GROUP,) + shape, lambda g: (g,) + (0,) * len(shape))
    steps = lambda *shape: pl.BlockSpec((1,) + shape, lambda g: (g,) + (0,) * len(shape))
    outs = [
        ((quads, ROWS_S, 512), BF),
        ((quads, 64, 128), F32),
        ((nodes, D_S), F32),
        ((table - nodes, D_S), BF),
        ((quads, ROWS_M // 4, 512), BF),
        ((ROWS_F // 4, 512), BF),
    ]
    return pl.pallas_call(
        scalar_backward_kernel,
        grid=(NEIGH // GROUP,),
        in_specs=[whole(near.shape), slots(nodes, H_P), slots(nodes, D_S)]
        + [whole(one.shape) for one in (gsone, wn)]
        + [pl.BlockSpec(memory_space=pl.ANY)] * 7,
        out_specs=[slots(nodes, H_P)] + [whole(shape) for shape, kind in outs],
        out_shape=[jax.ShapeDtypeStruct((NEIGH, nodes, H_P), BF)]
        + [jax.ShapeDtypeStruct(shape, kind) for shape, kind in outs],
        scratch_shapes=[
            pltpu.VMEM((table, D_S), F32),
            pltpu.VMEM((H_P, D_S), F32),
            pltpu.VMEM((nodes, D_S), F32),
            pltpu.VMEM((rows, D_S), BF),
            pltpu.VMEM((table + nodes, D_S), BF),
            pltpu.VMEM((table + nodes, D_S), BF),
            pltpu.VMEM((quads, 128, 512), BF),
            pltpu.VMEM((quads, 128, 512), BF),
            pltpu.VMEM((quads, 64, 128), BF),
            pltpu.VMEM((quads, 64, 128), BF),
            pltpu.VMEM((2, quads, ROWS_M // 4, 512), BF),
            pltpu.VMEM((2, quads, ROWS_M // 4, 512), BF),
            pltpu.VMEM((2, quads, ROWS_M // 4, 512), BF),
            pltpu.VMEM((2, quads, ROWS_M // 8, 512), BF),
            pltpu.VMEM((ROWS_F // 4, 512), BF),
            pltpu.VMEM((3, ROWS_F // 4, 512), BF),
        ]
        + [pltpu.VMEM(one.shape, BF) for one in (ts, ns, w_node, ts_other, ns_other)]
        + [
            pltpu.SemaphoreType.DMA((10,)),
            pltpu.SemaphoreType.DMA((10,)),
            pltpu.SemaphoreType.DMA((8,)),
            pltpu.VMEM((32, 128), F32),
        ],
        compiler_params=pltpu.CompilerParams(
            collective_id=1, has_side_effects=True, vmem_limit_bytes=VMEM_LIMIT
        ),
        name="scalar_backward",
    )(near, lx, dsilu, gsone, wn, ts, ns, w_node, ts_other, ns_other, m, f)


def vector_backward_kernel(
    near_ref, ev_ref, h_ref, ratio_ref, z_ref, gvone_ref, vo_ref, tv_ref,
    nv_ref, vs_ref, vt_ref, rest_ref, gains_ref, s_ref, m_ref, f_ref, backs_ref,
    plane_ref, gvec_ref, got_ref, gp_ref, gq_ref, gvo_ref, up_scr, gh_scr,
    s_own, s_got, s_sum, s_got2, s_part, s_gotz, m_own, m_gotz, t_scr, t_got, t_half, t_got1, t_sum, t_got2,
    t_part, t_gotz, back_scr, fin_scr, own_sem, send_sem, recv_sem, load_sem, near_scr, ev_scr,
):
    nodes = gvone_ref.shape[1]
    table = tv_ref.shape[1]
    rows = GROUP * nodes
    spaces = lax.axis_size("space")
    quads = spaces // 2
    step = pl.program_id(0)
    last = pl.num_programs(0) - 1
    at = place()
    me = lax.axis_index("space")
    mine = 2 * at["x"] + at["y"]
    wires = Wires(send_sem, recv_sem)
    early, late = ROWS_F // 4 + ROWS_M // 4, ROWS_S // 4 + ROWS_T // 4
    ring = [peer("group", shift) for shift in range(1, spaces)]
    plane = [peer("x"), peer("y"), peer("diagonal")]
    s_copies = first_cut(wires, s_ref, s_got)
    s_copies2 = second_cut(wires, s_sum, s_got2)
    s_copiesz = z_send(wires, s_part, s_gotz)
    m_copiesz = z_send(wires, m_ref, m_gotz)
    early_rows, late_rows = pl.ds(0, early), pl.ds(early, late)
    early_copies = [
        wires.copy(fin_scr.at[early_rows, :], plane_ref.at[mine, early_rows, :], to) for to in plane
    ]
    late_copies = [
        wires.copy(fin_scr.at[late_rows, :], plane_ref.at[mine, late_rows, :], to) for to in plane
    ]
    back_scalar, back_vector = pl.ds(0, D_S), pl.ds(D_S, 3 * D_V)
    scalar_copies = [
        wires.copy(
            backs_ref.at[pl.ds(lax.rem(me + n + 1, spaces) * CAP, CAP), :],
            got_ref.at[me, :, back_scalar],
            ring[n],
        )
        for n in range(spaces - 1)
    ]
    back_copies = [
        wires.copy(
            back_scr.at[lax.rem(me + n + 1, spaces)], got_ref.at[me, :, back_vector], ring[n]
        )
        for n in range(spaces - 1)
    ]
    s_loads = own_quarters(s_ref, s_own, load_sem)
    m_load = pltpu.make_async_copy(m_ref.at[at["z"]], m_own, load_sem.at[2])
    f_load = pltpu.make_async_copy(f_ref, fin_scr.at[pl.ds(0, ROWS_F // 4), :], load_sem.at[3])
    own_scalar = pltpu.make_async_copy(
        backs_ref.at[pl.ds(me * CAP, CAP), :], got_ref.at[me, :, back_scalar], load_sem.at[4]
    )
    t_pair = [wires.copy(t_scr.at[:, 1 - at["core"]], t_got, peer("core"))]
    t_copies = first_cut(wires, t_half, t_got1)
    t_copies2 = second_cut(wires, t_sum, t_got2)
    t_copiesz = z_send(wires, t_part, t_gotz)

    @pl.when(step == 0)
    def _():
        greet(ring + plane)
        start_all(s_copies)
        start_all(m_copiesz)
        start_all(s_loads + [m_load, f_load, own_scalar])
        keep_rows(near_ref, near_scr)
        for c in range(3):
            keep_rows(ev_ref.at[c], ev_scr.at[c])
        for ref in (gp_ref, gq_ref, gvo_ref):
            ref[...] = jnp.zeros_like(ref)

    @pl.when(step == 3)
    def _():
        wait_all(s_loads)
        wait_all(s_copies)
        first_add(s_own, s_got, s_sum)
        start_all(s_copies2)
        start_all(scalar_copies)

    @pl.when(step == 4)
    def _():
        wait_all([m_load, f_load])
        wait_all(m_copiesz)
        fin_scr[pl.ds(ROWS_F // 4, ROWS_M // 4), :] = z_add(m_own[...], m_gotz)
        start_all(early_copies)

    @pl.when(step == last)
    def _():
        wait_all(s_copies2)
        second_add(s_sum, s_got2, s_part)
        start_all(s_copiesz)

    for first in range(0, nodes, ROW_TILE):
        part = pl.ds(first, ROW_TILE)
        share = [gvone_ref[c, part, :] * (1.0 / NEIGH) for c in range(3)]
        for k in range(GROUP):
            z = [z_ref[k, c, part, :].astype(F32) for c in range(3)]
            power = power_of(z) + 1.0
            inverse = lax.rsqrt(power)
            s = sigmoid(power * inverse)
            dot = z[0] * share[0] + z[1] * share[1] + z[2] * share[2]
            factor = dot * inverse * (s * (1.0 - s))
            for c in range(3):
                up_scr[c, pl.ds(k * nodes + first, ROW_TILE), :] = (
                    share[c] * s + z[c] * factor
                ).astype(BF)
    for start, width in LANE_BLOCKS:
        cols = pl.ds(start, width)
        grad_direct = [product_back(up_scr[c], vo_ref[cols, :]) for c in range(3)]
        for first in range(0, nodes, ROW_TILE):
            part = pl.ds(first, ROW_TILE)
            acc = [None] * 3
            for k in range(GROUP):
                row = k * nodes + first
                ratio = ratio_ref[k, part, cols].astype(F32)
                for c in range(3):
                    g = grad_direct[c][row : row + ROW_TILE] + ratio * h_ref[
                        k, c, part, cols
                    ].astype(F32)
                    gh_scr[c, pl.ds(row, ROW_TILE), cols] = g.astype(BF)
                    acc[c] = g if acc[c] is None else acc[c] + g
            for c in range(3):
                gq_ref[c, part, cols] += acc[c]
    one_hot = one_hot_rows(near_scr, step * GROUP, table, nodes)
    for c in range(3):
        evr = jnp.broadcast_to(slot_rows(ev_scr.at[c], step * GROUP, nodes), (16, rows))
        lead = jnp.concatenate([one_hot, evr.astype(BF)], axis=0)
        gp_ref[c] += product(lead, gh_scr[c])
        gvo_ref[...] += lead_product(up_scr[c], h_ref[:, c, :, :].reshape(rows, H_P))

    @pl.when(step == last)
    def _():
        tall = D_V // spaces
        gp = [gp_ref[c, pl.ds(0, table), :].astype(BF) for c in range(3)]
        gq = [gq_ref[c].astype(BF) for c in range(3)]
        for c in range(3):
            projected = product(gp[c], vs_ref[...])
            gvec_ref[c] = gvone_ref[c] + product(gq[c], vt_ref[...]) + projected[:nodes]
            for d in range(spaces):
                back_scr[d, :, pl.ds(c * D_V, D_V)] = projected[
                    nodes + d * CAP : nodes + (d + 1) * CAP
                ].astype(BF)
        start_all(back_copies)
        own = pltpu.make_async_copy(
            back_scr.at[me], got_ref.at[me, :, back_vector], load_sem.at[5]
        )
        own.start()
        grads = []
        for lead_ref, right in ((tv_ref, gp), (nv_ref, gq)):
            total = None
            for c in range(3):
                one = lead_product(lead_ref[c], right[c])
                total = one if total is None else total + one
            grads.append(total)
        grads.append(gvo_ref[...])
        lane = lax.broadcasted_iota(jnp.int32, (D_V, 128), 1)
        tails = jnp.zeros((D_V, 128), F32)
        for n, grad in enumerate(grads):
            for p in range(spaces):
                t_scr[p // 2, p % 2, pl.ds(n * tall, tall), :] = grad[
                    p * tall : (p + 1) * tall, :512
                ].astype(BF)
            tails = tails + jnp.where(
                lane == n, jnp.broadcast_to(grad[:, 512:513], (D_V, 128)), 0.0
            )
        tails = tails.astype(BF)
        vedge = gp_ref[0, pl.ds(table, 8), :] + gp_ref[1, pl.ds(table, 8), :]
        vedge = vedge + gp_ref[2, pl.ds(table, 8), :]
        row = lax.broadcasted_iota(jnp.int32, (tall, 128), 0)
        below = pl.ds(3 * tall, tall)
        for p in range(spaces):
            rest = jnp.where(at["core"] == p % 2, rest_ref[p // 2], 0.0)
            t_scr[p // 2, p % 2, below, pl.ds(0, 128)] = tails[p * tall : (p + 1) * tall]
            t_scr[p // 2, p % 2, below, pl.ds(128, 128)] = rest[16 : 16 + tall].astype(BF)
            extra = jnp.where(row == 0, jnp.broadcast_to(rest[0:1], (tall, 128)), 0.0)
            for n in range(5):
                piece = jnp.broadcast_to(vedge[0:1, n * 128 : (n + 1) * 128], (tall, 128))
                extra = jnp.where(row == 1 + n, piece, extra)
            for n in range(2):
                piece = jnp.broadcast_to(
                    gains_ref[n : n + 1, p * 128 : (p + 1) * 128], (tall, 128)
                )
                extra = jnp.where(row == 6 + n, piece, extra)
            t_scr[p // 2, p % 2, below, pl.ds(256, 128)] = extra.astype(BF)
            t_scr[p // 2, p % 2, below, pl.ds(384, 128)] = jnp.zeros((tall, 128), BF)
        start_all(t_pair)
        wait_all(t_pair)
        t_half[...] = (t_scr[:, at["core"]].astype(F32) + t_got[...].astype(F32)).astype(BF)
        start_all(t_copies)
        wait_all(t_copies)
        first_add_whole(t_half, t_got1, t_sum)
        start_all(t_copies2)
        wait_all(t_copies2)
        second_add(t_sum, t_got2, t_part)
        start_all(t_copiesz)
        wait_all(s_copiesz)
        fin_scr[pl.ds(early, ROWS_S // 4), :] = z_add(s_part[at["z"]], s_gotz)
        wait_all(t_copiesz)
        fin_scr[pl.ds(early + ROWS_S // 4, ROWS_T // 4), :] = z_add(t_part[at["z"]], t_gotz)
        start_all(late_copies)
        own.wait()
        own_scalar.wait()
        wait_all(scalar_copies)
        own_plane = pltpu.make_async_copy(fin_scr, plane_ref.at[mine], own_sem)
        own_plane.start()
        own_plane.wait()
        wait_all(back_copies)
        wait_all(early_copies)
        wait_all(late_copies)


def vector_backward(
    near, ev, hidden, ratio, update, gvone, vout, tv, nv, vs, vt, rest, gains,
    s, m, f, back,
):
    nodes = gvone.shape[1]
    table = tv.shape[1]
    quads = s.shape[0]
    spaces = 2 * quads
    rows = GROUP * nodes
    once = pl.Buffered(1)
    whole = lambda shape: pl.BlockSpec(shape, lambda g: (0,) * len(shape), pipeline_mode=once)
    slots = lambda *shape: pl.BlockSpec((GROUP,) + shape, lambda g: (g,) + (0,) * len(shape))
    steps = lambda *shape: pl.BlockSpec((1,) + shape, lambda g: (g,) + (0,) * len(shape))
    outs = [
        ((4, (ROWS_F + ROWS_M + ROWS_S + ROWS_T) // 4, 512), BF),
        ((3, nodes, D_V), F32),
        ((spaces, CAP, D_S + 3 * D_V), BF),
    ]
    bits = lambda *shape: pltpu.VMEM(shape, BF)
    return pl.pallas_call(
        vector_backward_kernel,
        grid=(NEIGH // GROUP,),
        in_specs=[
            whole(near.shape),
            whole(ev.shape),
            slots(3, nodes, H_P),
            slots(nodes, H_P),
            slots(3, nodes, D_V),
        ]
        + [whole(one.shape) for one in (gvone, vout, tv, nv, vs, vt, rest, gains)]
        + [pl.BlockSpec(memory_space=pl.ANY)] * 4,
        out_specs=[
            pl.BlockSpec(memory_space=pl.ANY),
            whole(outs[1][0]),
            pl.BlockSpec(memory_space=pl.ANY),
        ],
        out_shape=[jax.ShapeDtypeStruct(shape, kind) for shape, kind in outs],
        scratch_shapes=[
            pltpu.VMEM((3, table + 16, H_P), F32),
            pltpu.VMEM((3, nodes, H_P), F32),
            pltpu.VMEM((D_V, H_P), F32),
            bits(3, rows, D_V),
            bits(3, rows, H_P),
            bits(2, quads, ROWS_S // 4, 512),
            bits(2, quads, ROWS_S // 4, 512),
            bits(2, quads, ROWS_S // 4, 512),
            bits(2, quads, ROWS_S // 8, 512),
            bits(quads, ROWS_S // 4, 512),
            bits(3, ROWS_S // 4, 512),
            bits(ROWS_M // 4, 512),
            bits(3, ROWS_M // 4, 512),
            bits(quads, 2, ROWS_T, 512),
            bits(quads, ROWS_T, 512),
            bits(quads, ROWS_T, 512),
            bits(2, quads, ROWS_T // 4, 512),
            bits(2, quads, ROWS_T // 4, 512),
            bits(2, quads, ROWS_T // 8, 512),
            bits(quads, ROWS_T // 4, 512),
            bits(3, ROWS_T // 4, 512),
            bits(spaces, CAP, 3 * D_V),
            bits((ROWS_F + ROWS_M + ROWS_S + ROWS_T) // 4, 512),
            pltpu.SemaphoreType.DMA,
            pltpu.SemaphoreType.DMA((38,)),
            pltpu.SemaphoreType.DMA((38,)),
            pltpu.SemaphoreType.DMA((6,)),
            pltpu.VMEM((32, 128), F32),
            pltpu.VMEM((3, 32, 128), F32),
        ],
        compiler_params=pltpu.CompilerParams(
            collective_id=2, has_side_effects=True, vmem_limit_bytes=VMEM_LIMIT
        ),
        name="vector_backward",
    )(
        near, ev, hidden, ratio, update, gvone, vout, tv, nv, vs, vt, rest, gains,
        s, m, f, back,
    )


def finish_kernel(
    plane_ref, got_ref, sent_ref, gscal_ref, gvec_ref,
    gs_ref, gv_ref, node_ref, edge_ref, norms_ref, vnode_ref, vedge_ref, vout_ref, ffv_ref, ffs_ref,
    ffu_ref, embed_ref, qkv_ref, out_ref, up_ref, down_ref, gains_ref, row_scr, sent_scr,
):
    base = 0
    for rows in (ROWS_F, ROWS_M, ROWS_S, ROWS_T):
        eighth = rows // 8
        for half, order in enumerate(((0, 1, 2, 3), (0, 2, 1, 3))):
            for n, q in enumerate(order):
                row_scr[pl.ds(4 * base + (4 * half + n) * eighth, eighth), :] = plane_ref[
                    q, pl.ds(base + half * eighth, eighth), :
                ]
        base += rows // 4

    def take(start, rows, lane=0, width=512):
        return row_scr[pl.ds(start, rows), pl.ds(lane, width)].astype(F32)

    at = 0
    down_ref[...] = take(at, 256)
    for n in range(4):
        up_ref[:, pl.ds(n * 512, 512)] = take(at + 256 + n * 64, 64)
    at = ROWS_F
    for n in range(3):
        qkv_ref[:, pl.ds(n * 512, 512)] = take(at + n * 64, 64)
    out_ref[...] = take(at + 192, 64)
    embed_ref[...] = take(at + 256, 160)
    for n in range(2):
        ffs_ref[:, pl.ds(n * 512, 512)] = take(at + 416 + n * 160, 160)
    ffv_ref[...] = take(at + 736, 32, 0, 256)
    ffu_ref[...] = take(at + 736, 32, 256, 256)
    at += ROWS_M
    for n in range(4):
        node_ref[:, pl.ds(n * 512, 512)] = take(at + n * 128, 128)
        norms_ref[pl.ds(n * 128, 128), :] = take(at + 512, 128, n * 128, 128)
    at += ROWS_S
    tails = take(at + 96, 32, 0, 128)
    edge_ref[...] = take(at + 96, 32, 128, 128)
    extra = take(at + 96, 32, 256, 128)
    norms_ref[pl.ds(512, 1), :] = extra[0:1]
    for n in range(5):
        width = min(128, H_V - n * 128)
        vedge_ref[:, pl.ds(n * 128, width)] = extra[1 + n : 2 + n, :width]
    gains_ref[...] = extra[0:8]
    vnode_ref[:, pl.ds(0, 512)] = take(at, 32)
    wide = jnp.concatenate([take(at + 32, 32), jnp.zeros((32, 128), F32)], 1)
    lane = lax.broadcasted_iota(jnp.int32, (32, 640), 1)
    wide = pltpu.roll(wide, 1, 1)
    wide = jnp.where(lane == 0, tails[:, 0:1], wide)
    wide = jnp.where(lane == 513, tails[:, 1:2], wide)
    vnode_ref[:, pl.ds(512, 514)] = wide[:, :514]
    flat = jnp.concatenate([take(at + 64, 32), jnp.zeros((96, 512), F32)], 0)
    vout_ref[pl.ds(0, 512), :] = jnp.transpose(flat)[:, :32]
    flat = jnp.concatenate([tails, jnp.zeros((96, 128), F32)], 0)
    vout_ref[pl.ds(512, 1), :] = jnp.transpose(flat)[2:3, :32]
    nodes = gscal_ref.shape[0]
    slots = got_ref.shape[0] * got_ref.shape[1]
    got = got_ref[...].reshape(slots, D_S + 3 * D_V)
    pick = pick_matrix(sent_row(sent_ref, sent_scr), nodes)
    added = product(pick, got)
    gs_ref[...] = (gscal_ref[...] + added[:, :D_S]).astype(BF)
    for c in range(3):
        gv_ref[c] = (
            gvec_ref[c] + added[:, D_S + c * D_V : D_S + (c + 1) * D_V]
        ).astype(BF)


def finish(plane, got, sent, gscal, gvec):
    nodes = gscal.shape[0]
    outs = [
        ((nodes, D_S), BF),
        ((3, nodes, D_V), BF),
        ((128, 2048), F32),
        ((32, 128), F32),
        ((513, 128), F32),
        ((32, 1026), F32),
        ((1, 513), F32),
        ((513, 32), F32),
        ((32, 256), F32),
        ((160, 1024), F32),
        ((32, 256), F32),
        ((160, 512), F32),
        ((64, 1536), F32),
        ((64, 512), F32),
        ((64, 2048), F32),
        ((256, 512), F32),
        ((8, 128), F32),
    ]
    return pl.pallas_call(
        finish_kernel,
        out_shape=[jax.ShapeDtypeStruct(shape, kind) for shape, kind in outs],
        scratch_shapes=[
            pltpu.VMEM((ROWS_F + ROWS_M + ROWS_S + ROWS_T, 512), BF),
            pltpu.VMEM((8, 128), F32),
        ],
        compiler_params=pltpu.CompilerParams(vmem_limit_bytes=VMEM_LIMIT),
        name="finish",
    )(plane, got, sent, gscal, gvec)


def pad_to(values, size, axis):
    pads = [(0, 0)] * values.ndim
    pads[axis] = (0, size - values.shape[axis])
    return jnp.pad(values, pads)


def fold(blocks, width=512):
    shards, rows, columns = blocks.shape
    parts = columns // width
    return jnp.moveaxis(blocks.reshape(shards, rows, parts, width), 2, 1).reshape(
        shards, parts * rows, width
    )


def unfold(rows_in, rows, columns, width=512):
    parts = columns // width
    return jnp.moveaxis(rows_in.reshape(parts, rows, width), 0, 1).reshape(rows, columns)


def body(
    node_scalar, node_vector, edge_scalar, edge_vector, neighbours, send_rows, complex_id, cotangent,
    w_node, w_edge, w_norms, vec_node, vec_edge, vec_out, norm_gain, ff_vec, ff_scalar, ff_up,
    w_embed, attn_gain, w_qkv, w_out, ffn_gain, w_up, w_down,
):
    local_rows = node_scalar.shape[0]
    spaces = lax.axis_size("space")
    extra_rows = spaces * CAP
    table_count = local_rows + extra_rows
    all_nodes = complex_id.shape[0]
    steps = NEIGH // GROUP

    if spaces == HEADS and lax.axis_size("dp") == 4 and local_rows == 128:
        quads = spaces // 2
        sent = send_rows[0]
        near = neighbours.T
        ev = edge_vector.reshape(3, local_rows, NEIGH).transpose(0, 2, 1).astype(F32)
        gain_row = jnp.concatenate(
            [norm_gain, attn_gain, ffn_gain, vec_edge[0], jnp.zeros((H_P - H_V,), BF)]
        )
        gain_row = gain_row.astype(F32)[None]
        (
            b_target, p_source, q_target, table_s, table_v, vec_source, vec_target, vout, mix, wn_mix,
        ) = prepare(
            node_scalar, node_vector, sent, vec_node.T, w_edge, vec_out, w_norms, w_node
        )
        agg_s, agg_v, hidden, lx, dsilu, update = message(
            near, edge_scalar.T, ev, mix, b_target, p_source, q_target, gain_row, vout
        )
        stream_out, gsone, gvone, gains, middle_share, first_share, table_o, node_o = middle(
            (
                node_scalar, node_vector, agg_s, agg_v, gain_row, ff_vec, ff_scalar, ff_up,
                w_embed, w_qkv, complex_id[None], cotangent,
            ),
            (w_out, w_up, w_down), table_s, node_scalar, quads,
        )
        ratio, second_share, rest, gscal, back_s, middle_part, first_part = scalar_backward(
            near, lx, dsilu, gsone, wn_mix, table_s, node_scalar, w_node, table_o, node_o,
            middle_share, first_share,
        )
        plane, gvec, got = vector_backward(
            near, ev, hidden, ratio, update, gvone, vout, table_v, node_vector,
            vec_source, vec_target, rest, gains, second_share, middle_part, first_part, back_s,
        )
        (
            grad_scalar, grad_vector, out_node, out_edge, out_norms, out_vnode, out_vedge, out_vout,
            out_ffv, out_ffs, out_ffu, out_embed, out_qkv, out_out, out_up, out_down, rows,
        ) = finish(plane, got, sent, gscal, gvec)
        return (
            stream_out, grad_scalar, grad_vector, out_node, out_edge, out_norms, out_vnode,
            out_vedge, out_vout, rows[6], out_ffv, out_ffs, out_ffu, out_embed, rows[7, :64],
            out_qkv, out_out, rows[7, 64:], out_up, out_down,
        )

    sent_index = send_rows[0].reshape(-1)
    sent_live = sent_index >= 0
    pick = sent_index[:, None] == jnp.arange(local_rows, dtype=jnp.int32)[None, :]
    pick = pick.astype(BF)
    flat_nodes = jnp.concatenate([node_scalar] + [node_vector[c] for c in range(3)], 1)
    outgoing = product(pick, flat_nodes).astype(BF).reshape(spaces, CAP, D_S + 3 * D_V)
    incoming = lax.all_to_all(outgoing, "space", split_axis=0, concat_axis=0, tiled=True)
    incoming = incoming.reshape(extra_rows, D_S + 3 * D_V)
    table_s = jnp.concatenate([node_scalar, incoming[:, :D_S]], 0)
    table_v = jnp.stack(
        [
            jnp.concatenate(
                [node_vector[c], incoming[:, D_S + c * D_V : D_S + (c + 1) * D_V]], 0
            )
            for c in range(3)
        ]
    )
    vec_source = pad_to(vec_node[:, :H_V], H_P, 1)
    vec_target = pad_to(vec_node[:, H_V:], H_P, 1)
    a_source = product(table_s, w_node[:, :D_S]).astype(BF)
    b_target = product(node_scalar, w_node[:, D_S:])
    p_source = product(table_v, vec_source).astype(BF)
    q_target = product(node_vector, vec_target)
    ve_row = pad_to(vec_edge.astype(F32), H_P, 1)
    vout = pad_to(vec_out, H_P, 0)
    wn_mix = pad_to(jnp.concatenate([w_norms, w_edge], 0), H_P, 0)
    mix = jnp.concatenate([a_source, wn_mix], 0)

    near = neighbours.T
    near_col = near[:, :, None]
    near_row = near.reshape(steps, 1, GROUP * local_rows)
    es_k = edge_scalar.reshape(local_rows, NEIGH, D_E).transpose(1, 0, 2)
    es_pad = jnp.pad(es_k, ((0, 0), (0, 0), (1, 128 - 1 - D_E)))
    ev_k = edge_vector.reshape(3, local_rows, NEIGH)
    ev_col = ev_k.transpose(2, 1, 0).astype(F32)
    ev_row = ev_k.transpose(2, 0, 1).reshape(steps, GROUP, 3, local_rows)
    ev_row = ev_row.transpose(0, 2, 1, 3).reshape(steps, 3, GROUP * local_rows)

    agg_s, agg_v, hidden, lx, dsilu, update = edge_forward(
        near_col, es_pad, ev_col, mix, b_target, p_source, q_target, ve_row, vout
    )

    scalar_one = node_scalar.astype(F32) + agg_s
    vector_one = node_vector.astype(F32) + agg_v
    gain_norm = norm_gain.astype(F32)
    normed_s = layer_norm(scalar_one, gain_norm)
    normed_v = vector_norm(vector_one)
    normed_vr = normed_v.astype(BF)
    ff_hidden = product(normed_vr, ff_vec)
    ff_hidden_r = ff_hidden.astype(BF)
    ff_length = length_plus(ff_hidden)
    ff_input = jnp.concatenate([normed_s.astype(BF), ff_length.astype(BF)], -1)
    ff_preact = product(ff_input, ff_scalar)
    ff_update = product(ff_hidden_r, ff_up)
    scalar_two = normed_s + jax.nn.silu(ff_preact)
    vector_two = normed_v + vector_gate(ff_update)
    embed_input = jnp.concatenate([scalar_two.astype(BF), length_plus(vector_two).astype(BF)], -1)
    stream_zero = product(embed_input, w_embed)
    gain_attn = attn_gain.astype(F32)
    attn_in = layer_norm(stream_zero, gain_attn).astype(BF)
    qkv = product(attn_in, w_qkv).astype(BF)
    queries = qkv[:, :D_MODEL]
    keys_own = qkv[:, D_MODEL : 2 * D_MODEL]
    values_own = qkv[:, 2 * D_MODEL :]
    full_qkv = lax.all_gather(qkv, "space", axis=0, tiled=True)
    heads = lambda values: values.reshape(values.shape[0], HEADS, HEAD_DIM)
    full_queries = heads(full_qkv[:, :D_MODEL])
    full_keys = heads(full_qkv[:, D_MODEL : 2 * D_MODEL])
    full_values = heads(full_qkv[:, 2 * D_MODEL :])
    position = lax.axis_index("space")
    own_ids = lax.dynamic_slice_in_dim(complex_id, position * local_rows, local_rows, 0)
    same = own_ids[:, None] == complex_id[None, :]
    score_scale = HEAD_DIM ** (-0.5)
    scores = jnp.einsum("qhd,khd->hqk", heads(queries), full_keys, preferred_element_type=F32)
    scores = jnp.where(same[None], scores * score_scale, -1000000000.0)
    row_peak = jnp.max(scores, axis=-1, keepdims=True)
    shifted = jnp.exp(scores - row_peak)
    totals = jnp.sum(shifted, axis=-1, keepdims=True)
    probs = shifted / totals
    log_total = row_peak + jnp.log(totals)
    attended = jnp.einsum(
        "hqk,khd->qhd", probs.astype(BF), full_values, preferred_element_type=F32
    ).reshape(local_rows, D_MODEL)
    attended_r = attended.astype(BF)
    stream_one = stream_zero + product(attended_r, w_out)
    gain_ffn = ffn_gain.astype(F32)
    ffn_in = layer_norm(stream_one, gain_ffn).astype(BF)
    hidden_up = product(ffn_in, w_up)
    gelu_r = gelu_exact(hidden_up).astype(BF)
    stream_out = (stream_one + product(gelu_r, w_down)).astype(BF)
    grad_w_down = product_lead(gelu_r, cotangent)
    grad_gelu = product_back(cotangent, w_down)
    grad_up_r = pullback(gelu_exact, hidden_up, grad_gelu).astype(BF)
    grad_w_up = product_lead(ffn_in, grad_up_r)
    grad_ffn_in = product_back(grad_up_r, w_up)
    unused, ffn_pull = jax.vjp(layer_norm, stream_one, gain_ffn)
    grad_stream_ln, grad_ffn_gain = ffn_pull(grad_ffn_in)
    grad_stream_one = cotangent.astype(F32) + grad_stream_ln
    grad_branch = grad_stream_one.astype(BF)
    grad_w_out = product_lead(attended_r, grad_branch)
    grad_attended = product_back(grad_branch, w_out).astype(BF)
    row_dots = jnp.sum(heads(grad_attended).astype(F32) * heads(attended), axis=-1).T

    def halves(values):
        high = lax.reduce_precision(values, exponent_bits=8, mantissa_bits=7)
        return [high.astype(BF), (values - high).astype(BF)]

    numbers = jnp.concatenate(halves(log_total[:, :, 0]) + halves(row_dots), 0)
    packed = jnp.concatenate([grad_attended, pad_to(numbers.T, 128, 1)], 1)
    full_packed = lax.all_gather(packed, "space", axis=0, tiled=True)
    full_grad = heads(full_packed[:, :D_MODEL])
    numbers = full_packed[:, D_MODEL : D_MODEL + 4 * HEADS].astype(F32).T
    full_log = numbers[:HEADS] + numbers[HEADS : 2 * HEADS]
    full_dots = numbers[2 * HEADS : 3 * HEADS] + numbers[3 * HEADS :]

    grad_probs = jnp.einsum(
        "qhd,khd->hqk", heads(grad_attended), full_values, preferred_element_type=F32
    )
    grad_scores = (probs * (grad_probs - row_dots[:, :, None])).astype(BF)
    grad_query = jnp.einsum("hqk,khd->qhd", grad_scores, full_keys, preferred_element_type=F32)
    own_scores = jnp.einsum(
        "khd,qhd->hkq", heads(keys_own), full_queries, preferred_element_type=F32
    )
    own_scores = jnp.where(same[None], own_scores * score_scale, -1000000000.0)
    own_probs = jnp.exp(own_scores - full_log[:, None, :])
    own_grad_probs = jnp.einsum(
        "khd,qhd->hkq", heads(values_own), full_grad, preferred_element_type=F32
    )
    own_grad_scores = (own_probs * (own_grad_probs - full_dots[:, None, :])).astype(BF)
    grad_keys = jnp.einsum(
        "hkq,qhd->khd", own_grad_scores, full_queries, preferred_element_type=F32
    )
    grad_values = jnp.einsum(
        "hkq,qhd->khd", own_probs.astype(BF), full_grad, preferred_element_type=F32
    )
    flat = lambda values: values.reshape(local_rows, D_MODEL)
    grad_qkv = jnp.concatenate(
        [flat(grad_query) * score_scale, flat(grad_keys) * score_scale, flat(grad_values)], -1
    ).astype(BF)
    grad_w_qkv = product_lead(attn_in, grad_qkv)
    grad_attn_in = product_back(grad_qkv, w_qkv)
    unused, attn_pull = jax.vjp(layer_norm, stream_zero, gain_attn)
    grad_zero_ln, grad_attn_gain = attn_pull(grad_attn_in)
    grad_stream_r = (grad_stream_one + grad_zero_ln).astype(BF)
    grad_w_embed = product_lead(embed_input, grad_stream_r)
    grad_embed_in = product_back(grad_stream_r, w_embed)
    grad_vector_two = pullback(length_plus, vector_two, grad_embed_in[:, D_S:])
    grad_ff_pre = pullback(jax.nn.silu, ff_preact, grad_embed_in[:, :D_S]).astype(BF)
    grad_ff_scalar = product_lead(ff_input, grad_ff_pre)
    grad_ff_input = product_back(grad_ff_pre, ff_scalar)
    grad_ff_update = pullback(vector_gate, ff_update, grad_vector_two).astype(BF)
    grad_ff_up = product_lead(ff_hidden_r, grad_ff_update)
    grad_ff_hidden = (
        product_back(grad_ff_update, ff_up)
        + pullback(length_plus, ff_hidden, grad_ff_input[:, D_S:])
    ).astype(BF)
    grad_ff_vec = product_lead(normed_vr, grad_ff_hidden)
    grad_normed_v = grad_vector_two + product_back(grad_ff_hidden, ff_vec)
    grad_normed_s = grad_embed_in[:, :D_S] + grad_ff_input[:, :D_S]
    unused, norm_pull = jax.vjp(layer_norm, scalar_one, gain_norm)
    grad_scalar_one, grad_norm_gain = norm_pull(grad_normed_s)
    grad_vector_one = pullback(vector_norm, vector_one, grad_normed_v)

    shard = lambda grad: grad.astype(BF).reshape((spaces, grad.shape[0] // spaces) + grad.shape[1:])
    gains = jnp.concatenate(
        [shard(grad_norm_gain), shard(grad_attn_gain), shard(grad_ffn_gain)], 1
    )
    gains = pad_to(pad_to(gains, 512, 1)[:, None, :], 16, 1)
    first_share = jnp.concatenate(
        [
            shard(grad_w_down),
            fold(shard(grad_w_up)),
            fold(shard(grad_w_qkv)),
            shard(grad_w_out),
            shard(grad_w_embed),
            fold(shard(grad_ff_scalar)),
            jnp.concatenate([shard(grad_ff_vec), shard(grad_ff_up)], 2),
            gains,
        ],
        1,
    )
    first_sum = lax.psum_scatter(first_share, "space", scatter_dimension=0, tiled=False)
    first_sum = lax.psum(first_sum, "dp").astype(F32)

    grad_a, grad_mix, grad_b, grad_p, grad_q, grad_vout = edge_backward(
        near_row, ev_col, ev_row, hidden, lx, dsilu, update,
        grad_scalar_one * (1.0 / NEIGH), grad_vector_one * (1.0 / NEIGH), wn_mix, vout, table_count,
    )
    grad_vedge = jnp.sum(grad_p[:, table_count], 0)[:H_V]
    grad_vec_edge = lax.psum(grad_vedge[None, :], ("dp", "space"))
    grad_a_r = grad_a.astype(BF)
    grad_p_r = grad_p[:, :table_count].astype(BF)
    grad_b_r = grad_b.astype(BF)
    grad_q_r = grad_q.astype(BF)
    grad_node_a = product_lead(table_s, grad_a_r)
    grad_node_b = product_lead(node_scalar, grad_b_r)
    grad_vec_a = product_lead(table_v, grad_p_r)
    grad_vec_b = product_lead(node_vector, grad_q_r)
    grad_table_scalar = product_back(grad_a_r, w_node[:, :D_S])
    grad_table_vector = product_back(grad_p_r, vec_source)
    grad_scalar = (
        grad_scalar_one + product_back(grad_b_r, w_node[:, D_S:]) + grad_table_scalar[:local_rows]
    )
    grad_vector = (
        grad_vector_one + product_back(grad_q_r, vec_target) + grad_table_vector[:, :local_rows]
    )
    back = jnp.concatenate(
        [grad_table_scalar[local_rows:]] + [grad_table_vector[c, local_rows:] for c in range(3)], 1
    )
    back = back.astype(BF).reshape(spaces, CAP, D_S + 3 * D_V)
    got = lax.all_to_all(back, "space", split_axis=0, concat_axis=0, tiled=True)
    got = got.reshape(extra_rows, D_S + 3 * D_V)
    got = jnp.where(sent_live[:, None], got, 0)
    added = lax.dot_general(pick, got, (((0,), (0,)), ((), ())), preferred_element_type=F32)
    grad_scalar = grad_scalar + added[:, :D_S]
    grad_vector = grad_vector + jnp.moveaxis(
        added[:, D_S:].reshape(local_rows, 3, D_V), 1, 0
    )

    columns = lambda grad: jnp.moveaxis(
        grad.reshape(grad.shape[0], spaces, grad.shape[1] // spaces), 1, 0
    )
    mix_block = columns(grad_mix.astype(BF))
    mix_width = D_S // spaces
    mix_rows = H_P * mix_width // 512
    second_share = jnp.concatenate(
        [
            fold(shard(grad_node_a)),
            fold(shard(grad_node_b)),
            mix_block.reshape(spaces, mix_rows, 512),
            shard(grad_vec_a)[:, :, :512],
            shard(grad_vec_b)[:, :, :512],
            shard(grad_vout)[:, :, :512],
            jnp.concatenate(
                [
                    shard(grad_vec_a)[:, :, 512:],
                    shard(grad_vec_b)[:, :, 512:],
                    shard(grad_vout)[:, :, 512:],
                    jnp.zeros((spaces, D_V // spaces, 128), BF),
                ],
                2,
            ),
        ],
        1,
    )
    second_sum = lax.psum_scatter(second_share, "space", scatter_dimension=0, tiled=False)
    second_sum = lax.psum(second_sum, "dp").astype(F32)

    def taker(rows_in):
        at = [0]

        def take(rows, cols, blocks=1):
            part = rows_in[at[0] : at[0] + rows * blocks]
            at[0] += rows * blocks
            return unfold(part, rows, cols) if blocks > 1 else part

        return take

    take = taker(first_sum)
    out_down = take(grad_w_down.shape[0] // spaces, 512)
    out_up = take(D_MODEL // spaces, 2048, 4)
    out_qkv = take(D_MODEL // spaces, 1536, 3)
    out_out = take(D_MODEL // spaces, 512)
    out_embed = take((D_S + D_V) // spaces, 512)
    out_ffs = take((D_S + D_V) // spaces, 1024, 2)
    both = take(D_V // spaces, 512)
    out_ffv, out_ffu = both[:, :D_V], both[:, D_V:]
    gain_row = take(16, 512)[0]
    cuts = [D_S // spaces, D_MODEL // spaces, D_MODEL // spaces]
    out_gn = gain_row[: cuts[0]]
    out_ga = gain_row[cuts[0] : cuts[0] + cuts[1]]
    out_gf = gain_row[cuts[0] + cuts[1] : sum(cuts)]
    take = taker(second_sum)
    node_a = take(D_S // spaces, 1024, 2)
    node_b = take(D_S // spaces, 1024, 2)
    mixed = take(mix_rows, 512).reshape(H_P, mix_width)
    vec_a = take(D_V // spaces, 512)
    vec_b = take(D_V // spaces, 512)
    vout_t = take(D_V // spaces, 512)
    tails = take(D_V // spaces, 512)
    out_vec_node = jnp.concatenate([vec_a, tails[:, :1], vec_b, tails[:, 128:129]], 1)
    out_vec_out = jnp.concatenate([vout_t, tails[:, 256:257]], 1).T
    return (
        stream_out,
        grad_scalar.astype(BF),
        grad_vector.astype(BF),
        jnp.concatenate([node_a, node_b], 1),
        mixed[H_V : H_V + D_E],
        mixed[:H_V],
        out_vec_node,
        grad_vec_edge,
        out_vec_out,
        out_gn,
        out_ffv,
        out_ffs,
        out_ffu,
        out_embed,
        out_ga,
        out_qkv,
        out_out,
        out_gf,
        out_up,
        out_down,
    )


def solution(mesh):
    rows = P(("dp", "space"), None)
    component = P(None, ("dp", "space"), None)
    return jax.shard_map(
        body,
        mesh=mesh,
        in_specs=(
            rows, component, rows, P(None, ("dp", "space")), rows,
            P(("dp", "space"), None, None), P("dp"), rows,
        ) + (P(),) * 17,
        out_specs=(
            rows, rows, component, P("space", None), P(None, "space"), P(None, "space"),
            P("space", None), P(), P(None, "space"), P("space"), P("space", None),
            P("space", None), P("space", None), P("space", None), P("space"), P("space", None),
            P("space", None), P("space"), P("space", None), P("space", None),
        ),
        check_vma=False,
    )
```

```python
import functools
import math

import jax
import jax.numpy as jnp
from jax import lax
from jax.experimental import pallas as pl
from jax.experimental.pallas import tpu as pltpu
from jax.sharding import PartitionSpec as P

D_S = 1024
D_V = 256
H_V = 513
H_P = 640
D_E = 32
NEIGH = 30
D_MODEL = 512
HEADS = 8
HEAD_DIM = 64
CAP = 16
GROUP = 5
VMEM_LIMIT = 60 * 1024 * 1024

MESH = pl.DeviceIdType.MESH
BF = jnp.bfloat16
F32 = jnp.float32


def layer_norm(values, gain_row):
    centred = values - jnp.mean(values, axis=-1, keepdims=True)
    spread = jnp.mean(centred * centred, axis=-1, keepdims=True)
    return centred * lax.rsqrt(spread + 1e-05) * gain_row


def vector_norm(vectors):
    mean_power = jnp.mean(jnp.sum(vectors * vectors, axis=0), axis=-1, keepdims=True)
    return vectors * lax.rsqrt(mean_power + 1e-05)[None]


def length_plus(vectors):
    return jnp.sqrt(jnp.sum(vectors * vectors, axis=0) + 1.0)


def vector_gate(vectors):
    return vectors * jax.nn.sigmoid(length_plus(vectors))[None]


def gelu_exact(values):
    return jax.nn.gelu(values, approximate=False)


def product(former, latter):
    return jnp.dot(former, latter, preferred_element_type=F32)


def product_lead(former, latter):
    leading = tuple(range(former.ndim - 1))
    return lax.dot_general(
        former, latter, ((leading, leading), ((), ())), preferred_element_type=F32
    )


def product_back(former, latter):
    return lax.dot_general(
        former, latter, (((former.ndim - 1,), (1,)), ((), ())), preferred_element_type=F32
    )


def pullback(function, at_point, cotangent_in):
    unused, puller = jax.vjp(function, at_point)
    return puller(cotangent_in)[0]


def sigmoid(values):
    return 0.5 * jnp.tanh(0.5 * values) + 0.5


LANE_BLOCKS = ((0, 256), (256, 256), (512, 128))
ROW_TILE = 64


def edge_forward_kernel(
    near_ref, es_ref, ev_ref, a_ref, b_ref, p_ref, q_ref, ve_ref, vo_ref,
    aggs_ref, aggv_ref, h_ref, lx_ref, ds_ref, z_ref, x_scr,
):
    nodes = b_ref.shape[0]
    table = p_ref.shape[1]
    rows = GROUP * nodes
    idx = near_ref[...].reshape(rows, 1)
    x_scr[:, :table] = (idx == lax.broadcasted_iota(jnp.int32, (rows, table), 1)).astype(BF)
    one_hot = x_scr[:, :table]
    for start, width in LANE_BLOCKS:
        cols = pl.ds(start, width)
        gathered = [product(one_hot, p_ref[c, :, cols]) for c in range(3)]
        for k in range(GROUP):
            for first in range(0, nodes, ROW_TILE):
                at = k * nodes + first
                evk = ev_ref[k, pl.ds(first, ROW_TILE), :]
                total = None
                for c in range(3):
                    h = (
                        gathered[c][at : at + ROW_TILE]
                        + q_ref[c, pl.ds(first, ROW_TILE), cols]
                        + evk[:, c : c + 1] * ve_ref[:, cols]
                    )
                    h_ref[k, c, pl.ds(first, ROW_TILE), cols] = h.astype(BF)
                    total = h * h + 1.0 if total is None else total + h * h
                length = total * lax.rsqrt(total)
                if start == 512:
                    lane = lax.broadcasted_iota(jnp.int32, (ROW_TILE, width), 1)
                    length = jnp.where(
                        lane == 0, length, es_ref[k, pl.ds(first, ROW_TILE), :].astype(F32)
                    )
                length = length.astype(BF)
                x_scr[pl.ds(at, ROW_TILE), pl.ds(table + start, width)] = length
                lx_ref[k, pl.ds(first, ROW_TILE), cols] = length

    @pl.when(pl.program_id(0) == 0)
    def _():
        aggs_ref[...] = jnp.zeros_like(aggs_ref)
        aggv_ref[...] = jnp.zeros_like(aggv_ref)

    full = x_scr[...]
    for start in range(0, D_S, 256):
        cols = pl.ds(start, 256)
        pre = product(full, a_ref[:, cols])
        for first in range(0, nodes, ROW_TILE):
            part = pl.ds(first, ROW_TILE)
            acc = None
            for k in range(GROUP):
                at = k * nodes + first
                x = pre[at : at + ROW_TILE] + b_ref[part, cols]
                s = sigmoid(x)
                y = x * s
                ds_ref[k, part, cols] = (s + y * (1.0 - s)).astype(BF)
                acc = y if acc is None else acc + y
            aggs_ref[part, cols] += acc * (1.0 / NEIGH)
    ups = [
        product(h_ref[:, c, :, :].reshape(rows, H_P), vo_ref[...]) for c in range(3)
    ]
    for first in range(0, nodes, ROW_TILE):
        part = pl.ds(first, ROW_TILE)
        acc = [None] * 3
        for k in range(GROUP):
            at = k * nodes + first
            z = [ups[c][at : at + ROW_TILE] for c in range(3)]
            power = z[0] * z[0] + z[1] * z[1] + z[2] * z[2] + 1.0
            s = sigmoid(power * lax.rsqrt(power))
            for c in range(3):
                z_ref[k, c, part, :] = z[c].astype(BF)
                gated = z[c] * s
                acc[c] = gated if acc[c] is None else acc[c] + gated
        for c in range(3):
            aggv_ref[c, part, :] += acc[c] * (1.0 / NEIGH)


def edge_forward(near_col, es_pad, ev_col, mix, b_target, p_source, q_target, ve_row, vout):
    nodes = b_target.shape[0]
    table = p_source.shape[1]
    whole = lambda shape: pl.BlockSpec(shape, lambda g: (0,) * len(shape))
    slots = lambda *shape: pl.BlockSpec((GROUP,) + shape, lambda g: (g,) + (0,) * len(shape))
    return pl.pallas_call(
        edge_forward_kernel,
        grid=(NEIGH // GROUP,),
        in_specs=[
            slots(nodes, 1),
            slots(nodes, 128),
            slots(nodes, 3),
            whole((table + H_P, D_S)),
            whole((nodes, D_S)),
            whole((3, table, H_P)),
            whole((3, nodes, H_P)),
            whole((1, H_P)),
            whole((H_P, D_V)),
        ],
        out_specs=[
            whole((nodes, D_S)),
            whole((3, nodes, D_V)),
            slots(3, nodes, H_P),
            slots(nodes, H_P),
            slots(nodes, D_S),
            slots(3, nodes, D_V),
        ],
        out_shape=[
            jax.ShapeDtypeStruct((nodes, D_S), F32),
            jax.ShapeDtypeStruct((3, nodes, D_V), F32),
            jax.ShapeDtypeStruct((NEIGH, 3, nodes, H_P), BF),
            jax.ShapeDtypeStruct((NEIGH, nodes, H_P), BF),
            jax.ShapeDtypeStruct((NEIGH, nodes, D_S), BF),
            jax.ShapeDtypeStruct((NEIGH, 3, nodes, D_V), BF),
        ],
        scratch_shapes=[pltpu.VMEM((GROUP * nodes, table + H_P), BF)],
        compiler_params=pltpu.CompilerParams(vmem_limit_bytes=VMEM_LIMIT),
        name="edge_forward",
    )(near_col, es_pad, ev_col, mix, b_target, p_source, q_target, ve_row, vout)


def message_kernel(
    near_ref, es_ref, ev_ref, a_ref, b_ref, p_ref, q_ref, ve_ref, vo_ref,
    aggs_ref, aggv_ref, h_ref, lx_ref, ds_ref, z_ref, x_scr, turn_scr,
):
    nodes = b_ref.shape[0]
    table = p_ref.shape[1]
    rows = GROUP * nodes
    first_slot = pl.program_id(0) * GROUP

    @pl.when(pl.program_id(0) == 0)
    def _():
        for n in range(4):
            ref = near_ref if n == 3 else ev_ref.at[n]
            turn_scr[n, pl.ds(0, NEIGH), :] = ref[...].astype(F32)
            turn_scr[n] = jnp.transpose(turn_scr[n])

    back = lax.rem(128 - first_slot, 128)
    ev = [pltpu.roll(turn_scr[n], back, 1) for n in range(4)]
    slots = ev[3]
    places = lax.broadcasted_iota(jnp.int32, (nodes, table), 1).astype(F32)
    edges_in = []
    for k in range(GROUP):
        x_scr[pl.ds(k * nodes, nodes), :table] = (slots[:, k : k + 1] == places).astype(BF)
        rows_in = pl.ds(pl.multiple_of((first_slot + k) * D_E, D_E), D_E)
        edges_in.append(
            jnp.transpose(
                jnp.concatenate(
                    [
                        jnp.zeros((16, nodes), F32),
                        es_ref[rows_in, :].astype(F32),
                        jnp.zeros((112 - D_E, nodes), F32),
                    ],
                    0,
                )
            )
        )
    one_hot = x_scr[:, :table]
    for start, width in LANE_BLOCKS:
        cols = pl.ds(start, width)
        gathered = [product(one_hot, p_ref[c, :, cols]) for c in range(3)]
        for k in range(GROUP):
            for first in range(0, nodes, ROW_TILE):
                at = k * nodes + first
                total = None
                for c in range(3):
                    h = (
                        gathered[c][at : at + ROW_TILE]
                        + q_ref[c, pl.ds(first, ROW_TILE), cols]
                        + ev[c][first : first + ROW_TILE, k : k + 1]
                        * ve_ref[:, pl.ds(D_S + 2 * D_MODEL + start, width)]
                    )
                    h_ref[k, c, pl.ds(first, ROW_TILE), cols] = h.astype(BF)
                    total = h * h + 1.0 if total is None else total + h * h
                length = total * lax.rsqrt(total)
                if start == 512:
                    lane = lax.broadcasted_iota(jnp.int32, (ROW_TILE, width), 1)
                    length = jnp.where(
                        lane == 0, length, edges_in[k][first : first + ROW_TILE]
                    )
                length = length.astype(BF)
                x_scr[pl.ds(at, ROW_TILE), pl.ds(table + start, width)] = length
                lx_ref[k, pl.ds(first, ROW_TILE), cols] = length

    @pl.when(pl.program_id(0) == 0)
    def _():
        aggs_ref[...] = jnp.zeros_like(aggs_ref)
        aggv_ref[...] = jnp.zeros_like(aggv_ref)

    full = x_scr[...]
    for start in range(0, D_S, 256):
        cols = pl.ds(start, 256)
        pre = product(full, a_ref[:, cols])
        for first in range(0, nodes, ROW_TILE):
            part = pl.ds(first, ROW_TILE)
            acc = None
            for k in range(GROUP):
                at = k * nodes + first
                x = pre[at : at + ROW_TILE] + b_ref[part, cols]
                s = sigmoid(x)
                y = x * s
                ds_ref[k, part, cols] = (s + y * (1.0 - s)).astype(BF)
                acc = y if acc is None else acc + y
            aggs_ref[part, cols] += acc * (1.0 / NEIGH)
    ups = [
        product(h_ref[:, c, :, :].reshape(rows, H_P), vo_ref[...]) for c in range(3)
    ]
    for first in range(0, nodes, ROW_TILE):
        part = pl.ds(first, ROW_TILE)
        acc = [None] * 3
        for k in range(GROUP):
            at = k * nodes + first
            z = [ups[c][at : at + ROW_TILE] for c in range(3)]
            power = z[0] * z[0] + z[1] * z[1] + z[2] * z[2] + 1.0
            s = sigmoid(power * lax.rsqrt(power))
            for c in range(3):
                z_ref[k, c, part, :] = z[c].astype(BF)
                gated = z[c] * s
                acc[c] = gated if acc[c] is None else acc[c] + gated
        for c in range(3):
            aggv_ref[c, part, :] += acc[c] * (1.0 / NEIGH)


def message(near, edge_scalar, ev, mix, b_target, p_source, q_target, ve_row, vout):
    nodes = b_target.shape[0]
    table = p_source.shape[1]
    whole = lambda shape: pl.BlockSpec(shape, lambda g: (0,) * len(shape))
    slots = lambda *shape: pl.BlockSpec((GROUP,) + shape, lambda g: (g,) + (0,) * len(shape))
    return pl.pallas_call(
        message_kernel,
        grid=(NEIGH // GROUP,),
        in_specs=[
            whole(near.shape),
            whole(edge_scalar.shape),
            whole(ev.shape),
            whole((table + H_P, D_S)),
            whole((nodes, D_S)),
            whole((3, table, H_P)),
            whole((3, nodes, H_P)),
            whole(ve_row.shape),
            whole((H_P, D_V)),
        ],
        out_specs=[
            whole((nodes, D_S)),
            whole((3, nodes, D_V)),
            slots(3, nodes, H_P),
            slots(nodes, H_P),
            slots(nodes, D_S),
            slots(3, nodes, D_V),
        ],
        out_shape=[
            jax.ShapeDtypeStruct((nodes, D_S), F32),
            jax.ShapeDtypeStruct((3, nodes, D_V), F32),
            jax.ShapeDtypeStruct((NEIGH, 3, nodes, H_P), BF),
            jax.ShapeDtypeStruct((NEIGH, nodes, H_P), BF),
            jax.ShapeDtypeStruct((NEIGH, nodes, D_S), BF),
            jax.ShapeDtypeStruct((NEIGH, 3, nodes, D_V), BF),
        ],
        scratch_shapes=[
            pltpu.VMEM((GROUP * nodes, table + H_P), BF),
            pltpu.VMEM((4, 128, nodes), F32),
        ],
        compiler_params=pltpu.CompilerParams(vmem_limit_bytes=VMEM_LIMIT),
        name="message",
    )(near, edge_scalar, ev, mix, b_target, p_source, q_target, ve_row, vout)


def edge_backward_kernel(
    near_ref, ev_ref, evr_ref, h_ref, lx_ref, ds_ref, z_ref, gs_ref, gv_ref, wn_ref, vo_ref,
    ga_ref, gw_ref, gb_ref, gp_ref, gq_ref, gvo_ref, pre_scr, up_scr, gh_scr,
):
    nodes = gs_ref.shape[0]
    table = ga_ref.shape[0]
    rows = GROUP * nodes

    @pl.when(pl.program_id(0) == 0)
    def _():
        for ref in (ga_ref, gw_ref, gb_ref, gp_ref, gq_ref, gvo_ref):
            ref[...] = jnp.zeros_like(ref)

    for start in range(0, D_S, 256):
        cols = pl.ds(start, 256)
        for first in range(0, nodes, ROW_TILE):
            part = pl.ds(first, ROW_TILE)
            share = gs_ref[part, cols]
            acc = None
            for k in range(GROUP):
                g = (ds_ref[k, part, cols].astype(F32) * share).astype(BF)
                pre_scr[pl.ds(k * nodes + first, ROW_TILE), cols] = g
                g = g.astype(F32)
                acc = g if acc is None else acc + g
            gb_ref[part, cols] += acc
    for first in range(0, nodes, ROW_TILE):
        part = pl.ds(first, ROW_TILE)
        share = [gv_ref[c, part, :] for c in range(3)]
        for k in range(GROUP):
            z = [z_ref[k, c, part, :].astype(F32) for c in range(3)]
            power = z[0] * z[0] + z[1] * z[1] + z[2] * z[2] + 1.0
            inverse = lax.rsqrt(power)
            s = sigmoid(power * inverse)
            dot = z[0] * share[0] + z[1] * share[1] + z[2] * share[2]
            factor = dot * inverse * (s * (1.0 - s))
            for c in range(3):
                up_scr[c, pl.ds(k * nodes + first, ROW_TILE), :] = (
                    share[c] * s + z[c] * factor
                ).astype(BF)

    near = near_ref[0]
    one_hot = (lax.broadcasted_iota(jnp.int32, (table, rows), 0) == near).astype(BF)
    grad_pre = pre_scr[...]
    ga_ref[...] += product(one_hot, grad_pre)
    lx = lx_ref[...].reshape(rows, H_P)
    gw_ref[...] += lax.dot_general(
        lx, grad_pre, (((0,), (0,)), ((), ())), preferred_element_type=F32
    )
    for start, width in LANE_BLOCKS:
        cols = pl.ds(start, width)
        grad_length = product_back(grad_pre, wn_ref[cols, :])
        grad_direct = [product_back(up_scr[c], vo_ref[cols, :]) for c in range(3)]
        for first in range(0, nodes, ROW_TILE):
            part = pl.ds(first, ROW_TILE)
            acc = [None] * 3
            for k in range(GROUP):
                at = k * nodes + first
                ratio = grad_length[at : at + ROW_TILE] * pl.reciprocal(
                    lx_ref[k, part, cols].astype(F32), approx=True
                )
                if start == 512:
                    lane = lax.broadcasted_iota(jnp.int32, (ROW_TILE, width), 1)
                    ratio = jnp.where(lane == 0, ratio, 0.0)
                for c in range(3):
                    g = grad_direct[c][at : at + ROW_TILE] + ratio * h_ref[
                        k, c, part, cols
                    ].astype(F32)
                    gh_scr[c, pl.ds(at, ROW_TILE), cols] = g.astype(BF)
                    acc[c] = g if acc[c] is None else acc[c] + g
            for c in range(3):
                gq_ref[c, part, cols] += acc[c]
    for c in range(3):
        evr = jnp.broadcast_to(evr_ref[0, c : c + 1, :], (16, rows))
        lead = jnp.concatenate([one_hot, evr.astype(BF)], axis=0)
        gp_ref[c] += product(lead, gh_scr[c])
        gvo_ref[...] += lax.dot_general(
            up_scr[c],
            h_ref[:, c, :, :].reshape(rows, H_P),
            (((0,), (0,)), ((), ())),
            preferred_element_type=F32,
        )


def edge_backward(near_row, ev_col, ev_row, hidden, lx, dsilu, update, gs, gv, wn, vout, table):
    nodes = gs.shape[0]
    rows = GROUP * nodes
    whole = lambda shape: pl.BlockSpec(shape, lambda g: (0,) * len(shape))
    slots = lambda *shape: pl.BlockSpec((GROUP,) + shape, lambda g: (g,) + (0,) * len(shape))
    steps = lambda *shape: pl.BlockSpec((1,) + shape, lambda g: (g,) + (0,) * len(shape))
    outs = [
        (table, D_S),
        (H_P, D_S),
        (nodes, D_S),
        (3, table + 16, H_P),
        (3, nodes, H_P),
        (D_V, H_P),
    ]
    return pl.pallas_call(
        edge_backward_kernel,
        grid=(NEIGH // GROUP,),
        in_specs=[
            steps(1, rows),
            slots(nodes, 3),
            steps(3, rows),
            slots(3, nodes, H_P),
            slots(nodes, H_P),
            slots(nodes, D_S),
            slots(3, nodes, D_V),
            whole((nodes, D_S)),
            whole((3, nodes, D_V)),
            whole((H_P, D_S)),
            whole((H_P, D_V)),
        ],
        out_specs=[whole(shape) for shape in outs],
        out_shape=[jax.ShapeDtypeStruct(shape, F32) for shape in outs],
        scratch_shapes=[
            pltpu.VMEM((rows, D_S), BF),
            pltpu.VMEM((3, rows, D_V), BF),
            pltpu.VMEM((3, rows, H_P), BF),
        ],
        compiler_params=pltpu.CompilerParams(vmem_limit_bytes=VMEM_LIMIT),
        name="edge_backward",
    )(near_row, ev_col, ev_row, hidden, lx, dsilu, update, gs, gv, wn, vout)


AT_AIN, AT_EMB, AT_FFIN, AT_FFH, AT_NV, FAC_NODE = 0, 512, 1792, 3072, 3840, 4608
AT_GELU, AT_GUP, AT_FIN, AT_COT, AT_ATT, AT_GBR, FAC_FEED = 0, 2048, 4096, 4608, 5120, 5632, 6144
AT_GQKV, AT_STREAM, AT_GPRE, AT_GFU, AT_GFH, FAC_BACK = 0, 1536, 2048, 3072, 3840, 4608
ROWS_F, ROWS_A, ROWS_N, ROWS_S, ROWS_B, ROWS_V = ALL_ROWS = (512, 256, 512, 256, 384, 128)
ROWS_E = ROWS_F // 4

def full_block(shape):
    return pl.BlockSpec(shape, lambda: (0,) * len(shape))


def lead_product(former, latter):
    return lax.dot_general(
        former, latter, (((0,), (0,)), ((), ())), preferred_element_type=F32
    )


def swap_halves(values):
    return pltpu.roll(values, 64, 1)


def lower_half(shape):
    return lax.broadcasted_iota(jnp.int32, shape, 1) < 64


def pack_tall(tile, odd):
    rows = tile.shape[0] // 2
    top, low = tile[:rows], tile[rows:]
    side = lower_half((rows, 128))
    if odd:
        return jnp.where(side, swap_halves(top), low)
    return jnp.where(side, top, swap_halves(low))


def unpack_tall(block):
    rows = block.shape[0]
    side = lower_half((rows, 128))
    return jnp.concatenate(
        [jnp.where(side, block, 0.0), jnp.where(side, swap_halves(block), 0.0)], 0
    )


def centre(values):
    centred = values - jnp.mean(values, axis=-1, keepdims=True)
    inverse = lax.rsqrt(jnp.mean(centred * centred, axis=-1, keepdims=True) + 1e-05)
    return centred * inverse, inverse


def centre_back(hat, inverse, grad):
    return inverse * (
        grad
        - jnp.mean(grad, axis=-1, keepdims=True)
        - hat * jnp.mean(grad * hat, axis=-1, keepdims=True)
    )


def power_of(parts):
    return parts[0] * parts[0] + parts[1] * parts[1] + parts[2] * parts[2]


def node_forward_kernel(
    ns_ref, nv_ref, as_ref, av_ref, ng_ref, fv_ref, fs_ref, fu_ref, we_ref, ag_ref, wq_ref,
    s1_ref, v1_ref, ffh_ref, ffp_ref, ffu_ref, v2_ref, sz_ref, fac_ref, out_ref, with_keys,
):
    nodes = ns_ref.shape[0]
    s1 = ns_ref[...].astype(F32) + as_ref[...]
    s1_ref[...] = s1
    hat, unused = centre(s1)
    normed_s = hat * ng_ref[...]
    v1 = [nv_ref[c].astype(F32) + av_ref[c] for c in range(3)]
    scale = lax.rsqrt(jnp.mean(power_of(v1), axis=-1, keepdims=True) + 1e-05)
    normed_v = [v * scale for v in v1]
    ffh = [product(v.astype(BF), fv_ref[...]) for v in normed_v]
    power = power_of(ffh) + 1.0
    fac_ref[:, pl.ds(AT_FFIN, D_S)] = normed_s.astype(BF)
    fac_ref[:, pl.ds(AT_FFIN + D_S, D_V)] = (power * lax.rsqrt(power)).astype(BF)
    ffp = product(fac_ref[:, pl.ds(AT_FFIN, D_S + D_V)], fs_ref[...])
    ffu = [product(h.astype(BF), fu_ref[...]) for h in ffh]
    for c in range(3):
        v1_ref[c] = v1[c]
        fac_ref[:, pl.ds(AT_FFH + c * D_V, D_V)] = ffh[c].astype(BF)
        fac_ref[:, pl.ds(AT_NV + c * D_V, D_V)] = normed_v[c].astype(BF)
        ffh_ref[c] = ffh[c]
        ffu_ref[c] = ffu[c]
    ffp_ref[...] = ffp
    s2 = normed_s + ffp * sigmoid(ffp)
    power = power_of(ffu) + 1.0
    gate = sigmoid(power * lax.rsqrt(power))
    v2 = [normed_v[c] + ffu[c] * gate for c in range(3)]
    for c in range(3):
        v2_ref[c] = v2[c]
    power = power_of(v2) + 1.0
    fac_ref[:, pl.ds(AT_EMB, D_S)] = s2.astype(BF)
    fac_ref[:, pl.ds(AT_EMB + D_S, D_V)] = (power * lax.rsqrt(power)).astype(BF)
    sz = product(fac_ref[:, pl.ds(AT_EMB, D_S + D_V)], we_ref[...])
    sz_ref[...] = sz
    hat, unused = centre(sz)
    attn_in = (hat * ag_ref[...]).astype(BF)
    fac_ref[:, pl.ds(AT_AIN, D_MODEL)] = attn_in
    q, k = [product(attn_in, wq_ref[:, pl.ds(n * D_MODEL, D_MODEL)]) for n in range(2)]
    side = lower_half((nodes, 128))
    for pair in range(HEADS // 2):
        cols = slice(pair * 128, pair * 128 + 128)
        qp, kp = q[:, cols], k[:, cols]
        even = jnp.where(side, qp, swap_halves(kp))
        odd = jnp.where(side, swap_halves(qp), kp)
        for n, block in enumerate((even, odd)):
            out_ref[2 * pair + n, pl.ds(0, nodes), :] = block.astype(BF)
    with_keys()
    v = product(attn_in, wq_ref[:, pl.ds(2 * D_MODEL, D_MODEL)])
    for head in range(HEADS):
        tile = v[:, head // 2 * 128 : head // 2 * 128 + 128]
        out_ref[head, pl.ds(nodes, nodes // 2), :] = pack_tall(tile, head % 2 == 1).astype(BF)


def split_heads(x_ref, nodes):
    spaces = x_ref.shape[0]
    both = x_ref[:, pl.ds(0, nodes), :].reshape(spaces * nodes, 128).astype(F32)
    queries = jnp.where(lower_half(both.shape), both, 0.0).astype(BF)
    keys = swap_halves(both).astype(BF)
    return queries, keys


def split_values(x_ref, nodes):
    spaces = x_ref.shape[0]
    return jnp.concatenate(
        [unpack_tall(x_ref[d, pl.ds(nodes, nodes // 2), :].astype(F32)) for d in range(spaces)], 0
    ).astype(BF)


def attend_kernel(x_ref, id_ref, probs_ref, att_ref, out_ref, with_probs):
    spaces = x_ref.shape[0]
    nodes = x_ref.shape[1] * 2 // 3
    count = spaces * nodes
    queries, keys = split_heads(x_ref, nodes)
    row_ids = id_ref[...]
    column_ids = jnp.transpose(jnp.broadcast_to(row_ids, (8, count)))[:, 0:1]
    block = 2 * nodes
    for first in range(0, count, block):
        scores = product_back(queries[first : first + block], keys) * HEAD_DIM ** (-0.5)
        same = column_ids[first : first + block] == row_ids
        scores = jnp.where(same, scores, -1000000000.0)
        shifted = jnp.exp(scores - jnp.max(scores, axis=-1, keepdims=True))
        probs = (shifted / jnp.sum(shifted, axis=-1, keepdims=True)).astype(BF)
        probs_ref[pl.ds(first, block), :] = probs
    with_probs()
    values = split_values(x_ref, nodes)
    for first in range(0, count, block):
        att = product(probs_ref[pl.ds(first, block), :], values)
        att_ref[pl.ds(first, block), :] = att
        for n in range(block // nodes):
            tile = att[n * nodes : (n + 1) * nodes]
            out_ref[first // nodes + n] = pack_tall(tile, False).astype(BF)


def attend_backward_kernel(x_ref, probs_ref, att_ref, g_ref, out_ref, gs_scr, with_values):
    spaces = x_ref.shape[0]
    nodes = x_ref.shape[1] * 2 // 3
    count = spaces * nodes
    queries, keys = split_heads(x_ref, nodes)
    values = split_values(x_ref, nodes)
    grad = jnp.concatenate(
        [unpack_tall(g_ref[d].astype(F32)) for d in range(spaces)], 0
    )
    dots = jnp.sum(grad * att_ref[...], axis=-1, keepdims=True)
    grad = grad.astype(BF)
    grad_values = jnp.transpose(lead_product(grad, probs_ref[...]))
    for d in range(spaces):
        tile = grad_values[d * nodes : (d + 1) * nodes]
        out_ref[d, pl.ds(nodes, nodes // 2), :] = pack_tall(tile, False).astype(BF)
    with_values()
    block = 2 * nodes
    scale = HEAD_DIM ** (-0.5)
    grad_queries = []
    for first in range(0, count, block):
        grad_probs = product_back(grad[first : first + block], values)
        part = probs_ref[pl.ds(first, block), :].astype(F32)
        grad_scores = (part * (grad_probs - dots[first : first + block])).astype(BF)
        gs_scr[pl.ds(first, block), :] = grad_scores
        grad_queries.append(product(grad_scores, keys))
    grad_queries = jnp.concatenate(grad_queries, 0) * scale
    grad_keys = jnp.transpose(lead_product(queries, gs_scr[...])) * scale
    side = lower_half((nodes, 128))
    for d in range(spaces):
        rows = slice(d * nodes, (d + 1) * nodes)
        out_ref[d, pl.ds(0, nodes), :] = jnp.where(
            side, grad_queries[rows], swap_halves(grad_keys[rows])
        ).astype(BF)


def merge_heads(block_ref, first, half):
    tiles = []
    for pair in range(HEADS // 2):
        even = unpack_tall(block_ref[2 * pair, pl.ds(first, half), :].astype(F32))
        odd = unpack_tall(block_ref[2 * pair + 1, pl.ds(first, half), :].astype(F32))
        tiles.append(even + swap_halves(odd))
    return jnp.concatenate(tiles, 1)


def feed_kernel(
    att_ref, sz_ref, wo_ref, fg_ref, wu_ref, wd_ref, cot_ref,
    out_ref, gatt_ref, gs1_ref, ggain_ref, fac_ref, with_up,
):
    nodes = sz_ref.shape[0]
    att = merge_heads(att_ref, 0, nodes // 2).astype(BF)
    fac_ref[:, pl.ds(AT_ATT, D_MODEL)] = att
    stream_one = sz_ref[...] + product(att, wo_ref[...])
    hat, inverse = centre(stream_one)
    ffn_in = (hat * fg_ref[...]).astype(BF)
    fac_ref[:, pl.ds(AT_FIN, D_MODEL)] = ffn_in
    ffn = wu_ref.shape[1]
    cot = cot_ref[...]
    fac_ref[:, pl.ds(AT_COT, D_MODEL)] = cot
    for start in range(0, ffn, 512):
        cols = pl.ds(start, 512)
        x = product(ffn_in, wu_ref[:, cols])
        cdf = 0.5 * (1.0 + lax.erf(x * (0.5**0.5)))
        fac_ref[:, pl.ds(AT_GELU + start, 512)] = (x * cdf).astype(BF)
        slope = cdf + x * jnp.exp(-0.5 * x * x) * ((0.5 / math.pi) ** 0.5)
        fac_ref[:, pl.ds(AT_GUP + start, 512)] = (
            product_back(cot, wd_ref[cols, :]) * slope
        ).astype(BF)
    with_up()
    out_ref[...] = (
        stream_one + product(fac_ref[:, pl.ds(AT_GELU, ffn)], wd_ref[...])
    ).astype(BF)
    grad_in = product_back(fac_ref[:, pl.ds(AT_GUP, ffn)], wu_ref[...])
    ggain_ref[...] = jnp.sum(grad_in * hat, axis=0, keepdims=True)
    grad_one = cot.astype(F32) + centre_back(hat, inverse, grad_in * fg_ref[...])
    gs1_ref[...] = grad_one
    branch = grad_one.astype(BF)
    fac_ref[:, pl.ds(AT_GBR, D_MODEL)] = branch
    grad_att = product_back(branch, wo_ref[...])
    for head in range(HEADS):
        tile = grad_att[:, head // 2 * 128 : head // 2 * 128 + 128]
        gatt_ref[head] = pack_tall(tile, head % 2 == 1).astype(BF)


def core_columns(values, core):
    values = values.astype(F32)
    side = lower_half((values.shape[0], 128))
    tiles = []
    for n in range(0, 512, 256):
        one, two = values[:, n : n + 128], values[:, n + 128 : n + 256]
        even = jnp.where(side, one, swap_halves(two))
        odd = jnp.where(side, swap_halves(one), two)
        tiles.append(jnp.where(core == 0, even, odd))
    return jnp.concatenate(tiles, 1).astype(BF)


def both_rows(own_ref, other_ref, start, width):
    return jnp.concatenate(
        [own_ref[:, pl.ds(start, width)], other_ref[:, pl.ds(start, width)]], 0
    )


def feed_grads_kernel(own_ref, other_ref, pack_ref):
    quads = pack_ref.shape[0]
    core = lax.rem(lax.axis_index("space"), 2)
    cot = both_rows(own_ref, other_ref, AT_COT, D_MODEL)
    for z in range(quads):
        start = pl.multiple_of(AT_GELU + (2 * z + core) * 256, 256)
        block = lead_product(both_rows(own_ref, other_ref, start, 256), cot)
        pack_ref[z, pl.ds(0, 256), :] = block.astype(BF)
    left = core_columns(both_rows(own_ref, other_ref, AT_FIN, D_MODEL), core)
    for n in range(4):
        block = lead_product(left, both_rows(own_ref, other_ref, AT_GUP + n * 512, 512)).astype(BF)
        for z in range(quads):
            pack_ref[z, pl.ds(256 + n * 64, 64), :] = block[z * 64 : (z + 1) * 64]


def attention_grads(node_ref, node_other, back_ref, back_other, feed_ref, feed_other, pack_ref):
    quads = pack_ref.shape[0]
    core = lax.rem(lax.axis_index("space"), 2)
    left = core_columns(both_rows(node_ref, node_other, AT_AIN, D_MODEL), core)
    pairs = [
        (left, both_rows(back_ref, back_other, AT_GQKV + n * D_MODEL, D_MODEL)) for n in range(3)
    ]
    pairs.append(
        (
            core_columns(both_rows(feed_ref, feed_other, AT_ATT, D_MODEL), core),
            both_rows(feed_ref, feed_other, AT_GBR, D_MODEL),
        )
    )
    for n, (one, two) in enumerate(pairs):
        block = lead_product(one, two).astype(BF)
        for z in range(quads):
            pack_ref[z, pl.ds(n * 64, 64), :] = block[z * 64 : (z + 1) * 64]


def node_grads(node_ref, node_other, back_ref, back_other, pack_ref, tall_scr, low_scr):
    quads = pack_ref.shape[0]
    core = lax.rem(lax.axis_index("space"), 2)
    emb = both_rows(node_ref, node_other, AT_EMB, D_S + D_V)
    ffin = both_rows(node_ref, node_other, AT_FFIN, D_S + D_V)
    rights = [(emb, back_ref, back_other, AT_STREAM)]
    rights += [(ffin, back_ref, back_other, AT_GPRE + n * 512) for n in range(2)]
    for n, (one, own, other, start) in enumerate(rights):
        tall_scr[...] = lead_product(one, both_rows(own, other, start, 512)).astype(BF)
        for z in range(quads):
            rows = pl.ds(pl.multiple_of((2 * z + core) * 160, 32), 160)
            pack_ref[z, pl.ds(n * 160, 160), :] = tall_scr[rows, :]
    vec = up = None
    for c in range(3):
        one = lead_product(
            both_rows(node_ref, node_other, AT_NV + c * D_V, D_V),
            both_rows(back_ref, back_other, AT_GFH + c * D_V, D_V),
        )
        vec = one if vec is None else vec + one
        one = lead_product(
            both_rows(node_ref, node_other, AT_FFH + c * D_V, D_V),
            both_rows(back_ref, back_other, AT_GFU + c * D_V, D_V),
        )
        up = one if up is None else up + one
    low_scr[...] = jnp.concatenate([vec, up], 1).astype(BF)
    for z in range(quads):
        rows = pl.ds(pl.multiple_of((2 * z + core) * 32, 32), 32)
        pack_ref[z, pl.ds(480, 32), :] = low_scr[rows, :]


def node_backward_kernel(
    gq_ref, gs1_ref, s1_ref, v1_ref, ffh_ref, ffp_ref, ffu_ref, v2_ref,
    sz_ref, ng_ref, fv_ref, fs_ref, fu_ref, we_ref, ag_ref, wq_ref, fgain_ref,
    gsone_ref, gvone_ref, gains_ref, back_ref, with_qkv,
):
    nodes = gs1_ref.shape[0]
    shards = gq_ref.shape[0]
    side = lower_half((nodes, 128))
    tiles = [[], []]
    for pair in range(HEADS // 2):
        even = gq_ref[2 * pair, pl.ds(0, nodes), :].astype(F32)
        odd = gq_ref[2 * pair + 1, pl.ds(0, nodes), :].astype(F32)
        tiles[0].append(jnp.where(side, even, swap_halves(odd)))
        tiles[1].append(jnp.where(side, swap_halves(even), odd))
    grads = [jnp.concatenate(tile, 1).astype(BF) for tile in tiles]
    grads.append(merge_heads(gq_ref, nodes, nodes // 2).astype(BF))
    for n in range(3):
        back_ref[:, pl.ds(AT_GQKV + n * D_MODEL, D_MODEL)] = grads[n]
    with_qkv()
    grad_in = product_back(back_ref[:, pl.ds(AT_GQKV, 3 * D_MODEL)], wq_ref[...])
    hat, inverse = centre(sz_ref[...])
    grad_attn_gain = jnp.sum(grad_in * hat, axis=0, keepdims=True)
    stream = gs1_ref[...] + centre_back(hat, inverse, grad_in * ag_ref[...])
    stream = stream.astype(BF)
    back_ref[:, pl.ds(AT_STREAM, D_MODEL)] = stream
    grad_emb = product_back(stream, we_ref[...])
    grad_s2, grad_len = grad_emb[:, :D_S], grad_emb[:, D_S:]
    v2 = [v2_ref[c] for c in range(3)]
    factor = grad_len * lax.rsqrt(power_of(v2) + 1.0)
    grad_v2 = [factor * v for v in v2]
    x = ffp_ref[...]
    s = sigmoid(x)
    grad_pre = (grad_s2 * (s + x * s * (1.0 - s))).astype(BF)
    back_ref[:, pl.ds(AT_GPRE, D_S)] = grad_pre
    grad_ffin = product_back(grad_pre, fs_ref[...])
    z = [ffu_ref[c] for c in range(3)]
    power = power_of(z) + 1.0
    inverse = lax.rsqrt(power)
    s = sigmoid(power * inverse)
    dot = z[0] * grad_v2[0] + z[1] * grad_v2[1] + z[2] * grad_v2[2]
    factor = dot * inverse * (s * (1.0 - s))
    grad_up = [(grad_v2[c] * s + z[c] * factor).astype(BF) for c in range(3)]
    h = [ffh_ref[c] for c in range(3)]
    factor = grad_ffin[:, D_S:] * lax.rsqrt(power_of(h) + 1.0)
    v1 = [v1_ref[c] for c in range(3)]
    scale = lax.rsqrt(jnp.mean(power_of(v1), axis=-1, keepdims=True) + 1e-05)
    grad_nv = []
    for c in range(3):
        back_ref[:, pl.ds(AT_GFU + c * D_V, D_V)] = grad_up[c]
        grad_h = (product_back(grad_up[c], fu_ref[...]) + factor * h[c]).astype(BF)
        back_ref[:, pl.ds(AT_GFH + c * D_V, D_V)] = grad_h
        grad_nv.append(grad_v2[c] + product_back(grad_h, fv_ref[...]))
    grad_ns = grad_s2 + grad_ffin[:, :D_S]
    hat, inverse = centre(s1_ref[...])
    grad_norm_gain = jnp.sum(grad_ns * hat, axis=0, keepdims=True)
    gsone_ref[...] = centre_back(hat, inverse, grad_ns * ng_ref[...])
    dot = grad_nv[0] * v1[0] + grad_nv[1] * v1[1] + grad_nv[2] * v1[2]
    dot = jnp.mean(dot, axis=-1, keepdims=True) * scale * scale
    for c in range(3):
        gvone_ref[c] = scale * (grad_nv[c] - v1[c] * dot)
    gains_ref[...] = jnp.zeros_like(gains_ref)
    gains_ref[0:1, :] = grad_norm_gain
    for p in range(shards):
        pair = slice(p // 2 * 128, p // 2 * 128 + 128)
        left = jnp.broadcast_to(grad_attn_gain[:, pair], (8, 128))
        right = jnp.broadcast_to(fgain_ref[:, pair], (8, 128))
        if p % 2 == 0:
            both = jnp.where(lower_half((8, 128)), left, swap_halves(right))
        else:
            both = jnp.where(lower_half((8, 128)), swap_halves(left), right)
        gains_ref[1:2, pl.ds(p * 128, 128)] = both[0:1]


BACKWARD_LIMIT = 62 * 1024 * 1024

def place():
    dp, space = lax.axis_index("dp"), lax.axis_index("space")
    return {"x": lax.rem(dp, 2), "y": dp // 2, "z": space // 2, "core": lax.rem(space, 2)}


def peer(way, shift=1):
    at = place()
    if way == "x":
        return {"dp": 2 * at["y"] + 1 - at["x"]}
    if way == "y":
        return {"dp": 2 * (1 - at["y"]) + at["x"]}
    if way == "diagonal":
        return {"dp": 2 * (1 - at["y"]) + 1 - at["x"]}
    if way == "core":
        return {"space": 2 * at["z"] + 1 - at["core"]}
    if way == "z":
        return {"space": 2 * lax.rem(at["z"] + shift, 4) + at["core"]}
    return {"space": lax.rem(lax.axis_index("space") + shift, lax.axis_size("space"))}


def greet(peers):
    barrier = pltpu.get_barrier_semaphore()
    for one in peers:
        pl.semaphore_signal(barrier, inc=1, device_id=one, device_id_type=MESH)
    pl.semaphore_wait(barrier, len(peers))


class Wires:
    def __init__(self, send_sem, recv_sem):
        self.send_sem, self.recv_sem, self.used = send_sem, recv_sem, 0

    def copy(self, source, target, to):
        n = self.used
        self.used += 1
        return pltpu.make_async_remote_copy(
            src_ref=source,
            dst_ref=target,
            send_sem=self.send_sem.at[n],
            recv_sem=self.recv_sem.at[n],
            device_id=to,
            device_id_type=MESH,
        )


def rows_at(ref, start, count):
    return ref.at[:, pl.ds(start, count), :]


def first_cut(wires, share_ref, got_ref):
    at = place()
    quarter = share_ref.shape[1] // 4
    return [
        wires.copy(rows_at(share_ref, (1 - at["x"]) * quarter, quarter), got_ref.at[0], peer("x")),
        wires.copy(
            rows_at(share_ref, (3 - at["y"]) * quarter, quarter), got_ref.at[1], peer("y")
        ),
    ]


def own_quarters(share_ref, own_ref, sems):
    at = place()
    quarter = share_ref.shape[1] // 4
    starts = (at["x"] * quarter, (2 + at["y"]) * quarter)
    return [
        pltpu.make_async_copy(rows_at(share_ref, start, quarter), own_ref.at[n], sems[n])
        for n, start in enumerate(starts)
    ]


def first_add(own_ref, got_ref, sum_ref):
    for n in range(2):
        sum_ref[n] = (own_ref[n].astype(F32) + got_ref[n].astype(F32)).astype(BF)


def first_add_whole(share_ref, got_ref, sum_ref):
    at = place()
    quarter = share_ref.shape[1] // 4
    for n, start in enumerate((at["x"] * quarter, (2 + at["y"]) * quarter)):
        own = share_ref[:, pl.ds(pl.multiple_of(start, 16), quarter), :]
        sum_ref[n] = (own.astype(F32) + got_ref[n].astype(F32)).astype(BF)


def second_cut(wires, sum_ref, got_ref):
    at = place()
    eighth = sum_ref.shape[2] // 2
    return [
        wires.copy(
            rows_at(sum_ref.at[0], (1 - at["y"]) * eighth, eighth), got_ref.at[0], peer("y")
        ),
        wires.copy(
            rows_at(sum_ref.at[1], (1 - at["x"]) * eighth, eighth), got_ref.at[1], peer("x")
        ),
    ]


def second_add(sum_ref, got_ref, out_ref, base=0):
    at = place()
    eighth = sum_ref.shape[2] // 2
    for n, start in enumerate((at["y"] * eighth, at["x"] * eighth)):
        own = sum_ref[n, :, pl.ds(pl.multiple_of(start, 16), eighth), :]
        out_ref[:, pl.ds(base + n * eighth, eighth), :] = (
            own.astype(F32) + got_ref[n].astype(F32)
        ).astype(BF)


def z_send(wires, part_ref, got_ref):
    at = place()
    return [
        wires.copy(
            part_ref.at[lax.rem(at["z"] + shift, 4)], got_ref.at[shift - 1], peer("z", shift)
        )
        for shift in (1, 2, 3)
    ]


def z_add(own, got_ref):
    total = own.astype(F32)
    for n in range(3):
        total = total + got_ref[n].astype(F32)
    return total.astype(BF)


class Share:
    def __init__(self, wires, packed, own, refs, loads=()):
        self.packed, self.own, self.loads = packed, own, list(loads)
        self.got, self.sum, self.got2, self.part, self.gotz = refs
        self.copies = first_cut(wires, packed, self.got)
        self.copies2 = second_cut(wires, self.sum, self.got2)
        self.copiesz = z_send(wires, self.part, self.gotz)

    def start(self):
        start_all(self.loads + self.copies)

    def cut(self):
        wait_all(self.loads + self.copies)
        if self.own is None:
            first_add_whole(self.packed, self.got, self.sum)
        else:
            first_add(self.own, self.got, self.sum)
        start_all(self.copies2)

    def spread(self):
        wait_all(self.copies2)
        second_add(self.sum, self.got2, self.part)
        start_all(self.copiesz)

    def total(self):
        wait_all(self.copiesz)
        return z_add(self.part[place()["z"]], self.gotz)


def start_all(copies):
    for copy in copies:
        copy.start()
    return copies


def wait_all(copies):
    for copy in copies:
        copy.wait()


def sent_row(sent_ref, scr):
    spaces = sent_ref.shape[0]
    scr[...] = jnp.zeros_like(scr)
    scr[pl.ds(0, spaces), pl.ds(0, CAP)] = sent_ref[...].astype(F32)
    row = scr[0:1, :]
    for d in range(1, spaces):
        row = row + pltpu.roll(scr[d : d + 1, :], d * CAP, 1)
    return row


def pick_matrix(row, nodes):
    places = lax.broadcasted_iota(jnp.int32, (nodes, row.shape[1]), 0).astype(F32)
    return (places == row).astype(BF)


def prepare_kernel(
    ns_ref, nv_ref, sent_ref, vn_ref, we_ref, vout_ref, norms_ref, wnode_hbm,
    b_ref, p_ref, q_ref, ts_ref, tv_ref, vs_ref, vt_ref, vo_ref, mix_ref, wn_ref,
    wnode, row_scr, vt_scr, out_scr, in_scr, send_sem, recv_sem, load_sem,
):
    nodes = ns_ref.shape[0]
    table = ts_ref.shape[0]
    spaces = lax.axis_size("space")
    me = lax.axis_index("space")
    wires = Wires(send_sem, recv_sem)
    ring = [peer("group", shift) for shift in range(1, spaces)]
    load = pltpu.make_async_copy(wnode_hbm, wnode, load_sem)
    load.start()
    pick = pick_matrix(sent_row(sent_ref, row_scr), nodes)
    rows = lead_product(pick, ns_ref[...]).astype(BF)
    for d in range(spaces):
        out_scr[d, :, pl.ds(0, D_S)] = rows[d * CAP : (d + 1) * CAP]
    for c in range(3):
        rows = lead_product(pick, nv_ref[c]).astype(BF)
        for d in range(spaces):
            out_scr[d, :, pl.ds(D_S + c * D_V, D_V)] = rows[d * CAP : (d + 1) * CAP]
    greet(ring)
    copies = start_all(
        [
            wires.copy(out_scr.at[lax.rem(me + n + 1, spaces)], in_scr.at[me], ring[n])
            for n in range(spaces - 1)
        ]
    )
    in_scr[me] = out_scr[me]
    vs_ref[pl.ds(0, 512), :] = vn_ref[pl.ds(0, 512), :]
    vt_scr[...] = jnp.zeros_like(vt_scr)
    vt_scr[pl.ds(0, H_V + 1), :] = vn_ref[pl.ds(512, H_V + 1), :].astype(F32)
    row = lax.broadcasted_iota(jnp.int32, (H_P, D_V), 0)
    vt_ref[...] = jnp.where(row < H_V, pltpu.roll(vt_scr[...], H_P - 1, 0), 0.0).astype(BF)
    low = row[: H_P - 512]
    first = jnp.broadcast_to(vt_scr[0:1, :], low.shape)
    vs_ref[pl.ds(512, H_P - 512), :] = jnp.where(low == 0, first, 0.0).astype(BF)
    vo_ref[pl.ds(0, 512), :] = vout_ref[pl.ds(0, 512), :]
    first = jnp.broadcast_to(vout_ref[pl.ds(512, 1), :].astype(F32), low.shape)
    vo_ref[pl.ds(512, H_P - 512), :] = jnp.where(low == 0, first, 0.0).astype(BF)
    for c in range(3):
        q_ref[c] = product_back(nv_ref[c], vt_ref[...])
        p_ref[c, pl.ds(0, nodes), :] = product_back(nv_ref[c], vs_ref[...]).astype(BF)
        tv_ref[c, pl.ds(0, nodes), :] = nv_ref[c]
    ts_ref[pl.ds(0, nodes), :] = ns_ref[...]
    first = jnp.broadcast_to(norms_ref[pl.ds(512, 1), :].astype(F32), (16, D_S))
    row = lax.broadcasted_iota(jnp.int32, (16, D_S), 0)
    wn_ref[pl.ds(0, 512), :] = norms_ref[pl.ds(0, 512), :]
    wn_ref[pl.ds(512, 16), :] = jnp.where(row == 0, first, 0.0).astype(BF)
    wn_ref[pl.ds(528, D_E), :] = we_ref[...]
    wn_ref[pl.ds(528 + D_E, H_P - 528 - D_E), :] = jnp.zeros((H_P - 528 - D_E, D_S), BF)
    mix_ref[pl.ds(table, H_P), :] = wn_ref[...]
    load.wait()
    b_ref[...] = product(ns_ref[...], wnode[:, pl.ds(D_S, D_S)])
    mix_ref[pl.ds(0, nodes), :] = product(ns_ref[...], wnode[:, pl.ds(0, D_S)]).astype(BF)
    wait_all(copies)
    got = in_scr[...].reshape(spaces * CAP, D_S + 3 * D_V)
    ts_ref[pl.ds(nodes, table - nodes), :] = got[:, :D_S]
    mix_ref[pl.ds(nodes, table - nodes), :] = product(
        got[:, :D_S], wnode[:, pl.ds(0, D_S)]
    ).astype(BF)
    for c in range(3):
        rows = got[:, D_S + c * D_V : D_S + (c + 1) * D_V]
        tv_ref[c, pl.ds(nodes, table - nodes), :] = rows
        p_ref[c, pl.ds(nodes, table - nodes), :] = product_back(rows, vs_ref[...]).astype(BF)


def prepare(node_scalar, node_vector, sent, vec_node, w_edge, vec_out, w_norms, w_node):
    nodes = node_scalar.shape[0]
    spaces = sent.shape[0]
    table = nodes + spaces * CAP
    hbm = pl.BlockSpec(memory_space=pl.ANY)
    vmem = pl.BlockSpec(memory_space=pltpu.VMEM)
    outs = [
        ((nodes, D_S), F32),
        ((3, table, H_P), BF),
        ((3, nodes, H_P), F32),
        ((table, D_S), BF),
        ((3, table, D_V), BF),
        ((H_P, D_V), BF),
        ((H_P, D_V), BF),
        ((H_P, D_V), BF),
        ((table + H_P, D_S), BF),
        ((H_P, D_S), BF),
    ]
    blocks = (spaces, CAP, D_S + 3 * D_V)
    return pl.pallas_call(
        prepare_kernel,
        out_shape=[jax.ShapeDtypeStruct(shape, kind) for shape, kind in outs],
        in_specs=[vmem] * 7 + [hbm],
        out_specs=[vmem] * 10,
        scratch_shapes=[
            pltpu.VMEM(w_node.shape, BF),
            pltpu.VMEM((8, 128), F32),
            pltpu.VMEM((H_P, D_V), F32),
            pltpu.VMEM(blocks, BF),
            pltpu.VMEM(blocks, BF),
            pltpu.SemaphoreType.DMA((spaces - 1,)),
            pltpu.SemaphoreType.DMA((spaces - 1,)),
            pltpu.SemaphoreType.DMA,
        ],
        compiler_params=pltpu.CompilerParams(
            collective_id=3, has_side_effects=True, vmem_limit_bytes=VMEM_LIMIT
        ),
        name="prepare",
    )(node_scalar, node_vector, sent, vec_node, w_edge, vec_out, w_norms, w_node)


def middle_kernel(
    ns_ref, nv_ref, as_ref, av_ref, gains_in, fv_ref, fs_ref, fu_ref, we_ref, wq_ref, id_ref, cot_ref, wo_hbm, wu_hbm, wd_hbm, ts_hbm, ns_hbm,
    out_ref, gsone_ref, gvone_ref, gains_ref, a_ref, m_ref, e_ref, tso_hbm, nso_hbm,
    s1, v1, ffh, ffp, ffu, v2, sz, fac_node, fac_node_o, heads_out, heads_in,
    probs, att, att_out, att_in, wo_ref, wu_ref, wd_ref, gatt, gatt_in, gs1, fgain,
    fac_feed, fac_feed_o, gs_scr, ghead, ghead_in, fac_back, fac_back_o,
    first, first_got, first_sum, first_got2, tall_scr, low_scr,
    send_sem, recv_sem, load_sem,
):
    spaces = lax.axis_size("space")
    quads = spaces // 2
    me = lax.axis_index("space")
    ng_ref = gains_in.at[:, pl.ds(0, D_S)]
    ag_ref = gains_in.at[:, pl.ds(D_S, D_MODEL)]
    fg_ref = gains_in.at[:, pl.ds(D_S + D_MODEL, D_MODEL)]
    wires = Wires(send_sem, recv_sem)
    ring = [peer("group", shift) for shift in range(1, spaces)]

    def exchange(source, target, start=0, count=None):
        rows = pl.ds(start, source.shape[1] if count is None else count)
        return [
            wires.copy(source.at[lax.rem(me + n + 1, spaces), rows], target.at[me, rows], ring[n])
            for n in range(spaces - 1)
        ]

    def keep(source, target):
        target[me] = source[me]

    loads = [
        pltpu.make_async_copy(source, target, load_sem.at[n])
        for n, (source, target) in enumerate(
            ((wo_hbm, wo_ref), (wu_hbm, wu_ref), (wd_hbm, wd_ref))
        )
    ]
    start_all(loads)
    greet(ring + [peer("x"), peer("y")])
    swaps = start_all(
        [wires.copy(ts_hbm, tso_hbm, peer("core")), wires.copy(ns_hbm, nso_hbm, peer("core"))]
    )
    nodes = ns_ref.shape[0]
    key_copies = exchange(heads_out, heads_in, 0, nodes)
    value_copies = exchange(heads_out, heads_in, nodes, nodes // 2)
    grad_key_copies = exchange(ghead, ghead_in, 0, nodes)
    grad_value_copies = exchange(ghead, ghead_in, nodes, nodes // 2)
    start_later = lambda copies: functools.partial(start_all, copies)
    node_forward_kernel(
        ns_ref, nv_ref, as_ref, av_ref, ng_ref, fv_ref, fs_ref, fu_ref, we_ref, ag_ref, wq_ref,
        s1, v1, ffh, ffp, ffu, v2, sz, fac_node, heads_out, start_later(key_copies),
    )
    start_all(value_copies)
    swaps += start_all([wires.copy(fac_node, fac_node_o, peer("core"))])
    keep(heads_out, heads_in)
    wait_all(key_copies)
    attend_kernel(heads_in, id_ref, probs, att, att_out, functools.partial(wait_all, value_copies))
    copies = start_all(exchange(att_out, att_in))
    keep(att_out, att_in)
    wait_all(loads)
    wait_all(copies)
    up_cols, rest_cols = pl.ds(0, AT_ATT), pl.ds(AT_ATT, FAC_FEED - AT_ATT)
    feed_swap = wires.copy(fac_feed.at[:, up_cols], fac_feed_o.at[:, up_cols], peer("core"))
    feed_kernel(
        att_in, sz, wo_ref, fg_ref, wu_ref, wd_ref, cot_ref, out_ref, gatt, gs1, fgain, fac_feed,
        feed_swap.start,
    )
    copies = start_all(exchange(gatt, gatt_in))
    swaps += start_all(
        [wires.copy(fac_feed.at[:, rest_cols], fac_feed_o.at[:, rest_cols], peer("core"))]
    )
    keep(gatt, gatt_in)
    feed_swap.wait()
    feed_grads_kernel(fac_feed, fac_feed_o, first)
    cuts = start_all(first_cut(wires, first, first_got))
    wait_all(copies)
    attend_backward_kernel(
        heads_in, probs, att, gatt_in, ghead, gs_scr, start_later(grad_value_copies)
    )
    copies = start_all(grad_key_copies) + grad_value_copies
    keep(ghead, ghead_in)
    wait_all(cuts)
    first_add_whole(first, first_got, first_sum)
    cuts = start_all(second_cut(wires, first_sum, first_got2))
    wait_all(copies)
    qkv_cols, other_cols = pl.ds(0, AT_STREAM), pl.ds(AT_STREAM, FAC_BACK - AT_STREAM)
    qkv_swap = wires.copy(fac_back.at[:, qkv_cols], fac_back_o.at[:, qkv_cols], peer("core"))

    node_backward_kernel(
        ghead_in, gs1, s1, v1, ffh, ffp, ffu, v2, sz,
        ng_ref, fv_ref, fs_ref, fu_ref, we_ref, ag_ref, wq_ref, fgain,
        gsone_ref, gvone_ref, gains_ref, fac_back, qkv_swap.start,
    )
    swap = start_all(
        [wires.copy(fac_back.at[:, other_cols], fac_back_o.at[:, other_cols], peer("core"))]
    )
    qkv_swap.wait()
    wait_all(swaps)
    attention_grads(fac_node, fac_node_o, fac_back, fac_back_o, fac_feed, fac_feed_o, a_ref)
    wait_all(cuts)
    second_add(first_sum, first_got2, e_ref)
    wait_all(swap)
    node_grads(fac_node, fac_node_o, fac_back, fac_back_o, m_ref, tall_scr, low_scr)


def middle(vmem_operands, hbm_operands, table_s, node_scalar, quads):
    nodes = node_scalar.shape[0]
    spaces = 2 * quads
    count = spaces * nodes
    hbm = pl.BlockSpec(memory_space=pl.ANY)
    vmem = pl.BlockSpec(memory_space=pltpu.VMEM)
    operands = tuple(vmem_operands) + tuple(hbm_operands) + (table_s, node_scalar)
    bits = lambda *shape: pltpu.VMEM(shape, BF)
    wide = lambda *shape: pltpu.VMEM(shape, F32)
    packed = (spaces, nodes + nodes // 2, 128)
    small = (spaces, nodes // 2, 128)
    outs = [
        ((nodes, D_MODEL), BF),
        ((nodes, D_S), F32),
        ((3, nodes, D_V), F32),
        ((8, D_S), F32),
        ((quads, ROWS_A, 512), BF),
        ((quads, ROWS_N, 512), BF),
        ((quads, ROWS_E, 512), BF),
        (table_s.shape, BF),
        (node_scalar.shape, BF),
    ]
    wires = 6 * (spaces - 1) + 12
    return pl.pallas_call(
        middle_kernel,
        out_shape=[jax.ShapeDtypeStruct(shape, kind) for shape, kind in outs],
        in_specs=[vmem] * len(vmem_operands) + [hbm] * (len(hbm_operands) + 2),
        out_specs=[vmem] * 7 + [hbm] * 2,
        scratch_shapes=[
            wide(nodes, D_S), wide(3, nodes, D_V), wide(3, nodes, D_V), wide(nodes, D_S),
            wide(3, nodes, D_V), wide(3, nodes, D_V), wide(nodes, D_MODEL),
            bits(nodes, FAC_NODE), bits(nodes, FAC_NODE), bits(*packed), bits(*packed),
            bits(count, count), wide(count, 128), bits(*small), bits(*small),
        ]
        + [bits(*one.shape) for one in hbm_operands]
        + [
            bits(*small), bits(*small), wide(nodes, D_MODEL), wide(1, D_MODEL),
            bits(nodes, FAC_FEED), bits(nodes, FAC_FEED), bits(count, count),
            bits(*packed), bits(*packed), bits(nodes, FAC_BACK), bits(nodes, FAC_BACK),
            bits(quads, ROWS_F, 512), bits(2, quads, ROWS_F // 4, 512),
            bits(2, quads, ROWS_F // 4, 512), bits(2, quads, ROWS_F // 8, 512),
            bits(D_S + D_V, 512), bits(D_V, 512),
            pltpu.SemaphoreType.DMA((wires,)),
            pltpu.SemaphoreType.DMA((wires,)),
            pltpu.SemaphoreType.DMA((len(hbm_operands),)),
        ],
        compiler_params=pltpu.CompilerParams(
            collective_id=0, has_side_effects=True, vmem_limit_bytes=VMEM_LIMIT
        ),
        name="middle",
    )(*operands)


def slot_rows(rows_scr, first_slot, nodes):
    return jnp.concatenate([rows_scr[pl.ds(first_slot + k, 1), :] for k in range(GROUP)], 1)


def one_hot_rows(rows_scr, first_slot, table, nodes):
    row = slot_rows(rows_scr, first_slot, nodes)
    return (lax.broadcasted_iota(jnp.int32, (table, row.shape[1]), 0).astype(F32) == row).astype(BF)


def keep_rows(ref, rows_scr):
    rows_scr[pl.ds(0, ref.shape[0]), :] = ref[...].astype(F32)


def backward_kernel(
    near_ref, ev_ref, lx_ref, ds_ref, h_ref, z_ref, gsone_ref, wn_ref, gvone_ref, vo_ref, tv_ref,
    nv_ref, vs_ref, vt_ref, gains_ref,
    ts_hbm, ns_hbm, wnode_hbm, tso_hbm, nso_hbm, e_hbm, a_hbm, n_hbm,
    gscal_ref, gvec_ref, plane_hbm, got_hbm,
    near_scr, ev_scr, ga_ref, gw_ref, gb_ref, pre_scr, gp_ref, gq_ref, gvo_ref, up_scr,
    gh_scr, ts_ref, ns_ref, wnode_ref, tso_ref, nso_ref,
    grads_scr, grads_got, mix_scr, mix_got, rest_scr, rest_got, e_own, e_got, a_own, n_own,
    s_scr, b_scr, v_got, backs_scr, backv_scr, fin_scr,
    send_sem, recv_sem, load_sem, *share_refs,
):
    nodes = gsone_ref.shape[0]
    table = ts_ref.shape[0]
    rows = GROUP * nodes
    spaces = lax.axis_size("space")
    quads = spaces // 2
    step = pl.program_id(0)
    half = NEIGH // GROUP
    last = 2 * half - 1
    first_slot = lax.rem(step, half) * GROUP
    at = place()
    core = at["core"]
    me = lax.axis_index("space")
    mine = 2 * at["x"] + at["y"]
    ring = [peer("group", shift) for shift in range(1, spaces)]
    plane = [peer("x"), peer("y"), peer("diagonal")]

    wires = Wires(send_sem, recv_sem)
    own_copy = lambda n, source, target: pltpu.make_async_copy(source, target, load_sem.at[n])
    quarters = lambda share_ref, own_ref, n: own_quarters(
        share_ref, own_ref, [load_sem.at[n], load_sem.at[n + 1]]
    )
    refs = [share_refs[n : n + 5] for n in range(0, len(share_refs), 5)]
    e_copiesz = z_send(wires, e_hbm, e_got)
    share_a = Share(wires, a_hbm, a_own, refs[0], quarters(a_hbm, a_own, 9))
    share_n = Share(wires, n_hbm, n_own, refs[1], quarters(n_hbm, n_own, 11))
    share_s = Share(wires, s_scr, None, refs[2])
    share_b = Share(wires, b_scr, None, refs[3])
    v_scr = s_scr.at[:, pl.ds(0, ROWS_V), :]
    share_v = Share(wires, v_scr, None, refs[4])
    pair_copies = [
        wires.copy(source, target, peer("core"))
        for source, target in ((grads_scr, grads_got), (mix_scr, mix_got), (rest_scr, rest_got))
    ]
    v_pair = n_own
    v_copies = [wires.copy(v_pair.at[1 - core], v_got, peer("core"))]
    bounds = [0]
    for count in ALL_ROWS:
        bounds.append(bounds[-1] + count // 4)
    rows_e, rows_a, rows_n, rows_s, rows_b, rows_v = [
        pl.ds(lo, hi - lo) for lo, hi in zip(bounds, bounds[1:])
    ]
    batches = [(bounds[0], bounds[3]), (bounds[3], bounds[4]), (bounds[4], bounds[5])]
    rounds = [
        [
            wires.copy(fin_scr.at[pl.ds(lo, hi - lo), :], plane_hbm.at[mine, pl.ds(lo, hi - lo), :], to)
            for to in plane[:2]
        ]
        for lo, hi in batches
    ]
    relays = []
    over_x, over_y = 2 * (1 - at["x"]) + at["y"], 2 * at["x"] + 1 - at["y"]
    for lo, hi in batches:
        middle_row = (lo + hi) // 2
        upper, lower = pl.ds(lo, middle_row - lo), pl.ds(middle_row, hi - middle_row)
        relays.append(
            [
                wires.copy(plane_hbm.at[over_x, upper, :], plane_hbm.at[over_x, upper, :], plane[1]),
                wires.copy(plane_hbm.at[over_y, lower, :], plane_hbm.at[over_y, lower, :], plane[0]),
            ]
        )
    last_round = [
        wires.copy(fin_scr.at[rows_v, :], plane_hbm.at[mine, rows_v, :], to) for to in plane
    ]
    back_scalar, back_vector = pl.ds(0, D_S), pl.ds(D_S, 3 * D_V)
    scalar_copies = [
        wires.copy(
            backs_scr.at[lax.rem(me + n + 1, spaces)], got_hbm.at[me, :, back_scalar], ring[n]
        )
        for n in range(spaces - 1)
    ]
    vector_copies = [
        wires.copy(
            backv_scr.at[lax.rem(me + n + 1, spaces)], got_hbm.at[me, :, back_vector], ring[n]
        )
        for n in range(spaces - 1)
    ]
    e_load = own_copy(0, e_hbm.at[at["z"]], e_own)
    loads = [
        own_copy(1 + n, source, target)
        for n, (source, target) in enumerate(
            (
                (ts_hbm, ts_ref), (ns_hbm, ns_ref), (wnode_hbm.at[:, pl.ds(0, D_S)], wnode_ref),
                (tso_hbm, tso_ref),
                (nso_hbm, nso_ref),
            )
        )
    ]
    own_scalar = own_copy(6, backs_scr.at[me], got_hbm.at[me, :, back_scalar])
    own_vector = own_copy(7, backv_scr.at[me], got_hbm.at[me, :, back_vector])
    own_plane = own_copy(8, fin_scr, plane_hbm.at[mine])
    target_load = own_copy(13, wnode_hbm.at[:, pl.ds(D_S, D_S)], wnode_ref)

    def early_total():
        e_load.wait()
        wait_all(e_copiesz)
        fin_scr[rows_e, :] = z_add(e_own[...], e_got)

    def middle_total():
        fin_scr[rows_a, :] = share_a.total()
        fin_scr[rows_n, :] = share_n.total()
        start_all(rounds[0])

    def source_total():
        fin_scr[rows_s, :] = share_s.total()
        start_all(rounds[1])

    def relay(n):
        wait_all(rounds[n])
        start_all(relays[n])

    schedule = {
        (4, 0): [share_a.cut],
        (7, 0): [share_a.spread],
        (7, 1): [share_n.spread],
        (8, 1): [share_s.cut],
        (9, 1): [early_total],
        (10, 0): [share_b.cut],
        (10, 1): [share_s.spread, middle_total],
        (11, 1): [share_b.spread, source_total],
    }

    def carry_on(part):
        for (at_step, at_part), actions in schedule.items():
            if at_part == part:

                @pl.when(step == at_step)
                def _():
                    for action in actions:
                        action()

    @pl.when(step == 0)
    def _():
        greet(ring + plane)
        share_a.start()
        share_n.start()
        start_all(e_copiesz)
        start_all([e_load] + loads)
        keep_rows(near_ref, near_scr)
        for c in range(3):
            keep_rows(ev_ref.at[c], ev_scr.at[c])
        for ref in (ga_ref, gw_ref, gb_ref, gp_ref, gq_ref, gvo_ref):
            ref[...] = jnp.zeros_like(ref)

    carry_on(0)

    @pl.when(step < half)
    def _():
        for start in range(0, D_S, 256):
            cols = pl.ds(start, 256)
            for first in range(0, nodes, ROW_TILE):
                part = pl.ds(first, ROW_TILE)
                share = gsone_ref[part, cols] * (1.0 / NEIGH)
                acc = None
                for k in range(GROUP):
                    g = (ds_ref[k, part, cols].astype(F32) * share).astype(BF)
                    pre_scr[step, pl.ds(k * nodes + first, ROW_TILE), cols] = g
                    g = g.astype(F32)
                    acc = g if acc is None else acc + g
                gb_ref[part, cols] += acc
        one_hot = one_hot_rows(near_scr, first_slot, table, nodes)
        grad_pre = pre_scr[step]
        ga_ref[...] += product(one_hot, grad_pre)
        lx = lx_ref[...].reshape(rows, H_P)
        gw_ref[...] += lead_product(lx, grad_pre)
    @pl.when(step == half - 1)
    def _():
        grads_scr[pl.ds(0, table), :] = ga_ref[...].astype(BF)
        grads_scr[pl.ds(table, nodes), :] = gb_ref[...].astype(BF)
        for z in range(quads):
            away = pl.ds(pl.multiple_of((2 * z + 1 - core) * 128, 128), 128)
            for r in range(4):
                mix_scr[z, :, pl.ds(r * 128, 128)] = gw_ref[pl.ds(r * 128, 128), away].astype(BF)
            rest_scr[z] = gw_ref[pl.ds(512, 64), away].astype(BF)
        start_all(pair_copies)
        wait_all(loads)
        ga = grads_scr[pl.ds(0, table), :]
        projected = product_back(ga, wnode_ref[...])
        target_load.start()
        gscal_ref[...] = gsone_ref[...] + projected[:nodes]
        for d in range(spaces):
            backs_scr[d] = projected[nodes + d * CAP : nodes + (d + 1) * CAP].astype(BF)
        start_all(scalar_copies)
        own_scalar.start()

    @pl.when(step == half)
    def _():
        wait_all(pair_copies)
        grad_rows = pl.ds(0, table), pl.ds(table, nodes)
        for side, (left, lefto, pack) in enumerate(
            ((ts_ref, tso_ref, s_scr), (ns_ref, nso_ref, b_scr))
        ):
            right, righto = grads_scr[grad_rows[side], :], grads_got[grad_rows[side], :]
            for z in range(quads):
                own = pl.ds(pl.multiple_of((2 * z + core) * 128, 128), 128)
                block = lead_product(left[:, own], right) + lead_product(lefto[:, own], righto)
                block = block.astype(BF)
                for n in range(2):
                    pack[z, pl.ds(n * 128, 128), :] = block[:, n * 512 : (n + 1) * 512]
            if side == 0:
                share_n.cut()
                share_s.start()
        for z in range(quads):
            own = pl.ds(pl.multiple_of((2 * z + core) * 128, 128), 128)
            for r in range(4):
                lanes = pl.ds(r * 128, 128)
                b_scr[z, pl.ds(256, 128), lanes] = (
                    gw_ref[pl.ds(r * 128, 128), own] + mix_got[z, :, lanes].astype(F32)
                ).astype(BF)
        share_b.start()
        target_load.wait()
        gscal_ref[...] += product_back(grads_scr[pl.ds(table, nodes), :], wnode_ref[...])

    @pl.when(step >= half)
    def _():
        for first in range(0, nodes, ROW_TILE):
            part = pl.ds(first, ROW_TILE)
            share = [gvone_ref[c, part, :] * (1.0 / NEIGH) for c in range(3)]
            for k in range(GROUP):
                z = [z_ref[k, c, part, :].astype(F32) for c in range(3)]
                power = power_of(z) + 1.0
                inverse = lax.rsqrt(power)
                s = sigmoid(power * inverse)
                dot = z[0] * share[0] + z[1] * share[1] + z[2] * share[2]
                factor = dot * inverse * (s * (1.0 - s))
                for c in range(3):
                    up_scr[c, pl.ds(k * nodes + first, ROW_TILE), :] = (
                        share[c] * s + z[c] * factor
                    ).astype(BF)
        for start, width in LANE_BLOCKS:
            cols = pl.ds(start, width)
            grad_length = product_back(pre_scr[step - half], wn_ref[cols, :])
            grad_direct = [product_back(up_scr[c], vo_ref[cols, :]) for c in range(3)]
            for first in range(0, nodes, ROW_TILE):
                part = pl.ds(first, ROW_TILE)
                acc = [None] * 3
                for k in range(GROUP):
                    row = k * nodes + first
                    ratio = grad_length[row : row + ROW_TILE] * pl.reciprocal(
                        lx_ref[k, part, cols].astype(F32), approx=True
                    )
                    if start == 512:
                        lane = lax.broadcasted_iota(jnp.int32, (ROW_TILE, width), 1)
                        ratio = jnp.where(lane == 0, ratio, 0.0)
                    for c in range(3):
                        g = grad_direct[c][row : row + ROW_TILE] + ratio * h_ref[
                            k, c, part, cols
                        ].astype(F32)
                        gh_scr[c, pl.ds(row, ROW_TILE), cols] = g.astype(BF)
                        acc[c] = g if acc[c] is None else acc[c] + g
                for c in range(3):
                    gq_ref[c, part, cols] += acc[c]
    carry_on(1)

    @pl.when(step >= half)
    def _():
        one_hot = one_hot_rows(near_scr, first_slot, table, nodes)
        for c in range(3):
            evr = jnp.broadcast_to(slot_rows(ev_scr.at[c], first_slot, nodes), (16, rows))
            lead = jnp.concatenate([one_hot, evr.astype(BF)], axis=0)
            gp_ref[c] += product(lead, gh_scr[c])
            gvo_ref[...] += lead_product(up_scr[c], h_ref[:, c, :, :].reshape(rows, H_P))

    @pl.when(step == last)
    def _():
        tall = D_V // spaces
        gp = [gp_ref[c, pl.ds(0, table), :].astype(BF) for c in range(3)]
        gq = [gq_ref[c].astype(BF) for c in range(3)]
        grads = []
        for lead_ref, right in ((tv_ref, gp), (nv_ref, gq)):
            total = None
            for c in range(3):
                one = lead_product(lead_ref[c], right[c])
                total = one if total is None else total + one
            grads.append(total)
        grads.append(gvo_ref[...])
        lane = lax.broadcasted_iota(jnp.int32, (D_V, 128), 1)
        tails = jnp.zeros((D_V, 128), F32)
        for n, grad in enumerate(grads):
            for p in range(spaces):
                v_pair[p % 2, p // 2, pl.ds(n * tall, tall), :] = grad[
                    p * tall : (p + 1) * tall, :512
                ].astype(BF)
            tails = tails + jnp.where(
                lane == n, jnp.broadcast_to(grad[:, 512:513], (D_V, 128)), 0.0
            )
        tails = tails.astype(BF)
        vedge = gp_ref[0, pl.ds(table, 8), :] + gp_ref[1, pl.ds(table, 8), :]
        vedge = vedge + gp_ref[2, pl.ds(table, 8), :]
        row = lax.broadcasted_iota(jnp.int32, (tall, 128), 0)
        below = pl.ds(3 * tall, tall)
        for p in range(spaces):
            own = pl.ds(p * 128, 128)
            rest = gw_ref[pl.ds(512, 64), own] + rest_got[p // 2].astype(F32)
            rest = jnp.where(core == p % 2, rest, 0.0)
            v_pair[p % 2, p // 2, below, pl.ds(0, 128)] = tails[p * tall : (p + 1) * tall]
            v_pair[p % 2, p // 2, below, pl.ds(128, 128)] = rest[16 : 16 + tall].astype(BF)
            extra = jnp.where(row == 0, jnp.broadcast_to(rest[0:1], (tall, 128)), 0.0)
            for n in range(5):
                piece = jnp.broadcast_to(vedge[0:1, n * 128 : (n + 1) * 128], (tall, 128))
                extra = jnp.where(row == 1 + n, piece, extra)
            for n in range(2):
                piece = jnp.broadcast_to(
                    gains_ref[n : n + 1, p * 128 : (p + 1) * 128], (tall, 128)
                )
                extra = jnp.where(row == 6 + n, piece, extra)
            v_pair[p % 2, p // 2, below, pl.ds(256, 128)] = extra.astype(BF)
            v_pair[p % 2, p // 2, below, pl.ds(384, 128)] = jnp.zeros((tall, 128), BF)
        start_all(v_copies)
        for c in range(3):
            projected = product(gp[c], vs_ref[...])
            gvec_ref[c] = gvone_ref[c] + product(gq[c], vt_ref[...]) + projected[:nodes]
            for d in range(spaces):
                backv_scr[d, :, pl.ds(c * D_V, D_V)] = projected[
                    nodes + d * CAP : nodes + (d + 1) * CAP
                ].astype(BF)
        relay(0)
        start_all(vector_copies)
        own_vector.start()
        wait_all(v_copies)
        v_scr[...] = (v_pair[core].astype(F32) + v_got[...].astype(F32)).astype(BF)
        share_v.start()
        share_v.cut()
        fin_scr[rows_b, :] = share_b.total()
        start_all(rounds[2])
        share_v.spread()
        relay(1)
        relay(2)
        fin_scr[rows_v, :] = share_v.total()
        start_all(last_round)
        own_plane.start()
        for copies in relays:
            wait_all(copies)
        wait_all(scalar_copies)
        wait_all(vector_copies)
        own_scalar.wait()
        own_vector.wait()
        own_plane.wait()
        wait_all(last_round)


def backward(blocked, whole_operands, hbm_operands):
    near, ev, lx, dsilu, hidden, update = blocked
    ts, ns, w_node = hbm_operands[:3]
    nodes = ns.shape[0]
    table = ts.shape[0]
    quads = hbm_operands[-1].shape[0]
    spaces = 2 * quads
    rows = GROUP * nodes
    half = NEIGH // GROUP
    once = pl.Buffered(1)
    whole = lambda shape: pl.BlockSpec(shape, lambda g: (0,) * len(shape), pipeline_mode=once)
    early = lambda *shape: pl.BlockSpec(
        (GROUP,) + shape, lambda g: (jnp.minimum(g, half - 1),) + (0,) * len(shape)
    )
    late = lambda *shape: pl.BlockSpec(
        (GROUP,) + shape, lambda g: (jnp.maximum(g - half, 0),) + (0,) * len(shape)
    )
    both = lambda *shape: pl.BlockSpec(
        (GROUP,) + shape, lambda g: (lax.rem(g, half),) + (0,) * len(shape)
    )
    hbm = pl.BlockSpec(memory_space=pl.ANY)
    outs = [
        ((nodes, D_S), F32),
        ((3, nodes, D_V), F32),
        ((4, sum(ALL_ROWS) // 4, 512), BF),
        ((spaces, CAP, D_S + 3 * D_V), BF),
    ]
    bits = lambda *shape: pltpu.VMEM(shape, BF)
    wide = lambda *shape: pltpu.VMEM(shape, F32)
    grads = (table + nodes, D_S)
    pieces = lambda count: [
        bits(2, quads, count // 4, 512), bits(2, quads, count // 4, 512),
        bits(2, quads, count // 8, 512), bits(quads, count // 4, 512), bits(3, count // 4, 512),
    ]
    wires = 57 + 2 * (spaces - 1)
    return pl.pallas_call(
        backward_kernel,
        grid=(2 * half,),
        in_specs=[
            whole(near.shape),
            whole(ev.shape),
            both(nodes, H_P),
            early(nodes, D_S),
            late(3, nodes, H_P),
            late(3, nodes, D_V),
        ]
        + [whole(one.shape) for one in whole_operands]
        + [hbm] * len(hbm_operands),
        out_specs=[whole(outs[0][0]), whole(outs[1][0]), hbm, hbm],
        out_shape=[jax.ShapeDtypeStruct(shape, kind) for shape, kind in outs],
        scratch_shapes=[
            wide(32, 128), wide(3, 32, 128),
            wide(table, D_S), wide(H_P, D_S), wide(nodes, D_S), bits(half, rows, D_S),
            wide(3, table + 16, H_P), wide(3, nodes, H_P), wide(D_V, H_P), bits(3, rows, D_V),
            bits(3, rows, H_P),
        ]
        + [
            bits(*(one.shape if one is not w_node else (D_S, D_S))) for one in hbm_operands[:5]
        ]
        + [
            bits(*grads), bits(*grads), bits(quads, 128, 512), bits(quads, 128, 512),
            bits(quads, 64, 128), bits(quads, 64, 128), bits(ROWS_E, 512), bits(3, ROWS_E, 512),
            bits(2, quads, ROWS_A // 4, 512), bits(2, quads, ROWS_N // 4, 512),
            bits(quads, ROWS_S, 512), bits(quads, ROWS_B, 512),
            bits(quads, ROWS_V, 512),
            bits(spaces, CAP, D_S), bits(spaces, CAP, 3 * D_V), bits(sum(ALL_ROWS) // 4, 512),
            pltpu.SemaphoreType.DMA((wires,)),
            pltpu.SemaphoreType.DMA((wires,)),
            pltpu.SemaphoreType.DMA((14,)),
        ]
        + sum([pieces(count) for count in ALL_ROWS[1:]], []),
        compiler_params=pltpu.CompilerParams(
            collective_id=1, has_side_effects=True, vmem_limit_bytes=BACKWARD_LIMIT
        ),
        name="backward",
    )(*blocked, *whole_operands, *hbm_operands)


def finish_kernel(
    plane_ref, got_ref, sent_ref, gscal_ref, gvec_ref, stream_ref,
    gs_ref, gv_ref, node_ref, edge_ref, norms_ref, vnode_ref, vedge_ref, vout_ref, ffv_ref, ffs_ref,
    ffu_ref, embed_ref, qkv_ref, out_ref, up_ref, down_ref, ngain_ref, again_ref, fgain_ref,
    stream_out_ref, row_scr, sent_scr,
):
    base = 0
    for rows in ALL_ROWS:
        eighth = rows // 8
        for half, order in enumerate(((0, 1, 2, 3), (0, 2, 1, 3))):
            for n, q in enumerate(order):
                row_scr[pl.ds(4 * base + (4 * half + n) * eighth, eighth), :] = plane_ref[
                    q, pl.ds(base + half * eighth, eighth), :
                ]
        base += rows // 4

    def take(start, rows, lane=0, width=512):
        return row_scr[pl.ds(start, rows), pl.ds(lane, width)].astype(F32)

    at = 0
    down_ref[...] = take(at, 256)
    for n in range(4):
        up_ref[:, pl.ds(n * 512, 512)] = take(at + 256 + n * 64, 64)
    at += ROWS_F
    for n in range(3):
        qkv_ref[:, pl.ds(n * 512, 512)] = take(at + n * 64, 64)
    out_ref[...] = take(at + 192, 64)
    at += ROWS_A
    embed_ref[...] = take(at, 160)
    for n in range(2):
        ffs_ref[:, pl.ds(n * 512, 512)] = take(at + 160 + n * 160, 160)
    ffv_ref[...] = take(at + 480, 32, 0, 256)
    ffu_ref[...] = take(at + 480, 32, 256, 256)
    at += ROWS_N
    for n in range(4):
        node_ref[:, pl.ds(n * 512, 512)] = take(at + n * 128, 128)
        norms_ref[pl.ds(n * 128, 128), :] = take(at + 512, 128, n * 128, 128)
    at += ROWS_S + ROWS_B
    tails = take(at + 96, 32, 0, 128)
    edge_ref[...] = take(at + 96, 32, 128, 128)
    extra = take(at + 96, 32, 256, 128)
    norms_ref[pl.ds(512, 1), :] = extra[0:1]
    for n in range(5):
        width = min(128, H_V - n * 128)
        vedge_ref[:, pl.ds(n * 128, width)] = extra[1 + n : 2 + n, :width]
    ngain_ref[...] = extra[6]
    again_ref[...] = extra[7, :64]
    fgain_ref[...] = extra[7, 64:]
    vnode_ref[:, pl.ds(0, 512)] = take(at, 32)
    wide = jnp.concatenate([take(at + 32, 32), jnp.zeros((32, 128), F32)], 1)
    lane = lax.broadcasted_iota(jnp.int32, (32, 640), 1)
    wide = pltpu.roll(wide, 1, 1)
    wide = jnp.where(lane == 0, tails[:, 0:1], wide)
    wide = jnp.where(lane == 513, tails[:, 1:2], wide)
    vnode_ref[:, pl.ds(512, 514)] = wide[:, :514]
    vout_ref[:, pl.ds(0, 512)] = take(at + 64, 32)
    vout_ref[:, pl.ds(512, 1)] = tails[:, 2:3]
    stream_out_ref[...] = stream_ref[...]
    nodes = gscal_ref.shape[0]
    slots = got_ref.shape[0] * got_ref.shape[1]
    got = got_ref[...].reshape(slots, D_S + 3 * D_V)
    pick = pick_matrix(sent_row(sent_ref, sent_scr), nodes)
    added = product(pick, got)
    gs_ref[...] = (gscal_ref[...] + added[:, :D_S]).astype(BF)
    for c in range(3):
        gv_ref[c] = (
            gvec_ref[c] + added[:, D_S + c * D_V : D_S + (c + 1) * D_V]
        ).astype(BF)


def finish(plane, got, sent, gscal, gvec, stream):
    nodes = gscal.shape[0]
    outs = [
        ((nodes, D_S), BF),
        ((3, nodes, D_V), BF),
        ((128, 2048), F32),
        ((32, 128), F32),
        ((513, 128), F32),
        ((32, 1026), F32),
        ((1, 513), F32),
        ((32, 513), F32),
        ((32, 256), F32),
        ((160, 1024), F32),
        ((32, 256), F32),
        ((160, 512), F32),
        ((64, 1536), F32),
        ((64, 512), F32),
        ((64, 2048), F32),
        ((256, 512), F32),
        ((128,), F32),
        ((64,), F32),
        ((64,), F32),
        (stream.shape, BF),
    ]
    return pl.pallas_call(
        finish_kernel,
        out_shape=[jax.ShapeDtypeStruct(shape, kind) for shape, kind in outs],
        scratch_shapes=[
            pltpu.VMEM((sum(ALL_ROWS), 512), BF),
            pltpu.VMEM((8, 128), F32),
        ],
        compiler_params=pltpu.CompilerParams(vmem_limit_bytes=VMEM_LIMIT),
        name="finish",
    )(plane, got, sent, gscal, gvec, stream)


def pad_to(values, size, axis):
    pads = [(0, 0)] * values.ndim
    pads[axis] = (0, size - values.shape[axis])
    return jnp.pad(values, pads)


def fold(blocks, width=512):
    shards, rows, columns = blocks.shape
    parts = columns // width
    return jnp.moveaxis(blocks.reshape(shards, rows, parts, width), 2, 1).reshape(
        shards, parts * rows, width
    )


def unfold(rows_in, rows, columns, width=512):
    parts = columns // width
    return jnp.moveaxis(rows_in.reshape(parts, rows, width), 0, 1).reshape(rows, columns)


def body(
    node_scalar, node_vector, edge_scalar, edge_vector, neighbours, send_rows, complex_id, cotangent,
    w_node, w_edge, w_norms, vec_node, vec_edge, vec_out, norm_gain, ff_vec, ff_scalar, ff_up,
    w_embed, attn_gain, w_qkv, w_out, ffn_gain, w_up, w_down,
):
    local_rows = node_scalar.shape[0]
    spaces = lax.axis_size("space")
    extra_rows = spaces * CAP
    table_count = local_rows + extra_rows
    all_nodes = complex_id.shape[0]
    steps = NEIGH // GROUP

    if spaces == HEADS and lax.axis_size("dp") == 4 and local_rows == 128:
        quads = spaces // 2
        sent = send_rows[0]
        near = neighbours.T
        ev = edge_vector.reshape(3, local_rows, NEIGH).transpose(0, 2, 1).astype(F32)
        gain_row = jnp.concatenate(
            [norm_gain, attn_gain, ffn_gain, vec_edge[0], jnp.zeros((H_P - H_V,), BF)]
        )
        gain_row = gain_row.astype(F32)[None]
        (
            b_target, p_source, q_target, table_s, table_v, vec_source, vec_target, vout, mix, wn_mix,
        ) = prepare(
            node_scalar, node_vector, sent, vec_node.T, w_edge, vec_out, w_norms, w_node
        )
        agg_s, agg_v, hidden, lx, dsilu, update = message(
            near, edge_scalar.T, ev, mix, b_target, p_source, q_target, gain_row, vout
        )
        (
            stream_out, gsone, gvone, gains, attention_share, node_share, early_share, table_o, node_o,
        ) = middle(
            (
                node_scalar, node_vector, agg_s, agg_v, gain_row, ff_vec, ff_scalar, ff_up,
                w_embed, w_qkv, complex_id[None], cotangent,
            ),
            (w_out, w_up, w_down), table_s, node_scalar, quads,
        )
        gscal, gvec, plane, got = backward(
            (near, ev, lx, dsilu, hidden, update),
            (
                gsone, wn_mix, gvone, vout, table_v, node_vector, vec_source, vec_target, gains,
            ),
            (table_s, node_scalar, w_node, table_o, node_o, early_share, attention_share, node_share),
        )
        (
            grad_scalar, grad_vector, out_node, out_edge, out_norms, out_vnode, out_vedge, out_vout,
            out_ffv, out_ffs, out_ffu, out_embed, out_qkv, out_out, out_up, out_down, out_ng, out_ag,
            out_fg, stream_out,
        ) = finish(plane, got, sent, gscal, gvec, stream_out)
        return (
            stream_out, grad_scalar, grad_vector, out_node, out_edge, out_norms, out_vnode,
            out_vedge, out_vout.T, out_ng, out_ffv, out_ffs, out_ffu, out_embed, out_ag,
            out_qkv, out_out, out_fg, out_up, out_down,
        )

    sent_index = send_rows[0].reshape(-1)
    sent_live = sent_index >= 0
    pick = sent_index[:, None] == jnp.arange(local_rows, dtype=jnp.int32)[None, :]
    pick = pick.astype(BF)
    flat_nodes = jnp.concatenate([node_scalar] + [node_vector[c] for c in range(3)], 1)
    outgoing = product(pick, flat_nodes).astype(BF).reshape(spaces, CAP, D_S + 3 * D_V)
    incoming = lax.all_to_all(outgoing, "space", split_axis=0, concat_axis=0, tiled=True)
    incoming = incoming.reshape(extra_rows, D_S + 3 * D_V)
    table_s = jnp.concatenate([node_scalar, incoming[:, :D_S]], 0)
    table_v = jnp.stack(
        [
            jnp.concatenate(
                [node_vector[c], incoming[:, D_S + c * D_V : D_S + (c + 1) * D_V]], 0
            )
            for c in range(3)
        ]
    )
    vec_source = pad_to(vec_node[:, :H_V], H_P, 1)
    vec_target = pad_to(vec_node[:, H_V:], H_P, 1)
    a_source = product(table_s, w_node[:, :D_S]).astype(BF)
    b_target = product(node_scalar, w_node[:, D_S:])
    p_source = product(table_v, vec_source).astype(BF)
    q_target = product(node_vector, vec_target)
    ve_row = pad_to(vec_edge.astype(F32), H_P, 1)
    vout = pad_to(vec_out, H_P, 0)
    wn_mix = pad_to(jnp.concatenate([w_norms, w_edge], 0), H_P, 0)
    mix = jnp.concatenate([a_source, wn_mix], 0)

    near = neighbours.T
    near_col = near[:, :, None]
    near_row = near.reshape(steps, 1, GROUP * local_rows)
    es_k = edge_scalar.reshape(local_rows, NEIGH, D_E).transpose(1, 0, 2)
    es_pad = jnp.pad(es_k, ((0, 0), (0, 0), (1, 128 - 1 - D_E)))
    ev_k = edge_vector.reshape(3, local_rows, NEIGH)
    ev_col = ev_k.transpose(2, 1, 0).astype(F32)
    ev_row = ev_k.transpose(2, 0, 1).reshape(steps, GROUP, 3, local_rows)
    ev_row = ev_row.transpose(0, 2, 1, 3).reshape(steps, 3, GROUP * local_rows)

    agg_s, agg_v, hidden, lx, dsilu, update = edge_forward(
        near_col, es_pad, ev_col, mix, b_target, p_source, q_target, ve_row, vout
    )

    scalar_one = node_scalar.astype(F32) + agg_s
    vector_one = node_vector.astype(F32) + agg_v
    gain_norm = norm_gain.astype(F32)
    normed_s = layer_norm(scalar_one, gain_norm)
    normed_v = vector_norm(vector_one)
    normed_vr = normed_v.astype(BF)
    ff_hidden = product(normed_vr, ff_vec)
    ff_hidden_r = ff_hidden.astype(BF)
    ff_length = length_plus(ff_hidden)
    ff_input = jnp.concatenate([normed_s.astype(BF), ff_length.astype(BF)], -1)
    ff_preact = product(ff_input, ff_scalar)
    ff_update = product(ff_hidden_r, ff_up)
    scalar_two = normed_s + jax.nn.silu(ff_preact)
    vector_two = normed_v + vector_gate(ff_update)
    embed_input = jnp.concatenate([scalar_two.astype(BF), length_plus(vector_two).astype(BF)], -1)
    stream_zero = product(embed_input, w_embed)
    gain_attn = attn_gain.astype(F32)
    attn_in = layer_norm(stream_zero, gain_attn).astype(BF)
    qkv = product(attn_in, w_qkv).astype(BF)
    queries = qkv[:, :D_MODEL]
    keys_own = qkv[:, D_MODEL : 2 * D_MODEL]
    values_own = qkv[:, 2 * D_MODEL :]
    full_qkv = lax.all_gather(qkv, "space", axis=0, tiled=True)
    heads = lambda values: values.reshape(values.shape[0], HEADS, HEAD_DIM)
    full_queries = heads(full_qkv[:, :D_MODEL])
    full_keys = heads(full_qkv[:, D_MODEL : 2 * D_MODEL])
    full_values = heads(full_qkv[:, 2 * D_MODEL :])
    position = lax.axis_index("space")
    own_ids = lax.dynamic_slice_in_dim(complex_id, position * local_rows, local_rows, 0)
    same = own_ids[:, None] == complex_id[None, :]
    score_scale = HEAD_DIM ** (-0.5)
    scores = jnp.einsum("qhd,khd->hqk", heads(queries), full_keys, preferred_element_type=F32)
    scores = jnp.where(same[None], scores * score_scale, -1000000000.0)
    row_peak = jnp.max(scores, axis=-1, keepdims=True)
    shifted = jnp.exp(scores - row_peak)
    totals = jnp.sum(shifted, axis=-1, keepdims=True)
    probs = shifted / totals
    log_total = row_peak + jnp.log(totals)
    attended = jnp.einsum(
        "hqk,khd->qhd", probs.astype(BF), full_values, preferred_element_type=F32
    ).reshape(local_rows, D_MODEL)
    attended_r = attended.astype(BF)
    stream_one = stream_zero + product(attended_r, w_out)
    gain_ffn = ffn_gain.astype(F32)
    ffn_in = layer_norm(stream_one, gain_ffn).astype(BF)
    hidden_up = product(ffn_in, w_up)
    gelu_r = gelu_exact(hidden_up).astype(BF)
    stream_out = (stream_one + product(gelu_r, w_down)).astype(BF)
    grad_w_down = product_lead(gelu_r, cotangent)
    grad_gelu = product_back(cotangent, w_down)
    grad_up_r = pullback(gelu_exact, hidden_up, grad_gelu).astype(BF)
    grad_w_up = product_lead(ffn_in, grad_up_r)
    grad_ffn_in = product_back(grad_up_r, w_up)
    unused, ffn_pull = jax.vjp(layer_norm, stream_one, gain_ffn)
    grad_stream_ln, grad_ffn_gain = ffn_pull(grad_ffn_in)
    grad_stream_one = cotangent.astype(F32) + grad_stream_ln
    grad_branch = grad_stream_one.astype(BF)
    grad_w_out = product_lead(attended_r, grad_branch)
    grad_attended = product_back(grad_branch, w_out).astype(BF)
    row_dots = jnp.sum(heads(grad_attended).astype(F32) * heads(attended), axis=-1).T

    def halves(values):
        high = lax.reduce_precision(values, exponent_bits=8, mantissa_bits=7)
        return [high.astype(BF), (values - high).astype(BF)]

    numbers = jnp.concatenate(halves(log_total[:, :, 0]) + halves(row_dots), 0)
    packed = jnp.concatenate([grad_attended, pad_to(numbers.T, 128, 1)], 1)
    full_packed = lax.all_gather(packed, "space", axis=0, tiled=True)
    full_grad = heads(full_packed[:, :D_MODEL])
    numbers = full_packed[:, D_MODEL : D_MODEL + 4 * HEADS].astype(F32).T
    full_log = numbers[:HEADS] + numbers[HEADS : 2 * HEADS]
    full_dots = numbers[2 * HEADS : 3 * HEADS] + numbers[3 * HEADS :]

    grad_probs = jnp.einsum(
        "qhd,khd->hqk", heads(grad_attended), full_values, preferred_element_type=F32
    )
    grad_scores = (probs * (grad_probs - row_dots[:, :, None])).astype(BF)
    grad_query = jnp.einsum("hqk,khd->qhd", grad_scores, full_keys, preferred_element_type=F32)
    own_scores = jnp.einsum(
        "khd,qhd->hkq", heads(keys_own), full_queries, preferred_element_type=F32
    )
    own_scores = jnp.where(same[None], own_scores * score_scale, -1000000000.0)
    own_probs = jnp.exp(own_scores - full_log[:, None, :])
    own_grad_probs = jnp.einsum(
        "khd,qhd->hkq", heads(values_own), full_grad, preferred_element_type=F32
    )
    own_grad_scores = (own_probs * (own_grad_probs - full_dots[:, None, :])).astype(BF)
    grad_keys = jnp.einsum(
        "hkq,qhd->khd", own_grad_scores, full_queries, preferred_element_type=F32
    )
    grad_values = jnp.einsum(
        "hkq,qhd->khd", own_probs.astype(BF), full_grad, preferred_element_type=F32
    )
    flat = lambda values: values.reshape(local_rows, D_MODEL)
    grad_qkv = jnp.concatenate(
        [flat(grad_query) * score_scale, flat(grad_keys) * score_scale, flat(grad_values)], -1
    ).astype(BF)
    grad_w_qkv = product_lead(attn_in, grad_qkv)
    grad_attn_in = product_back(grad_qkv, w_qkv)
    unused, attn_pull = jax.vjp(layer_norm, stream_zero, gain_attn)
    grad_zero_ln, grad_attn_gain = attn_pull(grad_attn_in)
    grad_stream_r = (grad_stream_one + grad_zero_ln).astype(BF)
    grad_w_embed = product_lead(embed_input, grad_stream_r)
    grad_embed_in = product_back(grad_stream_r, w_embed)
    grad_vector_two = pullback(length_plus, vector_two, grad_embed_in[:, D_S:])
    grad_ff_pre = pullback(jax.nn.silu, ff_preact, grad_embed_in[:, :D_S]).astype(BF)
    grad_ff_scalar = product_lead(ff_input, grad_ff_pre)
    grad_ff_input = product_back(grad_ff_pre, ff_scalar)
    grad_ff_update = pullback(vector_gate, ff_update, grad_vector_two).astype(BF)
    grad_ff_up = product_lead(ff_hidden_r, grad_ff_update)
    grad_ff_hidden = (
        product_back(grad_ff_update, ff_up)
        + pullback(length_plus, ff_hidden, grad_ff_input[:, D_S:])
    ).astype(BF)
    grad_ff_vec = product_lead(normed_vr, grad_ff_hidden)
    grad_normed_v = grad_vector_two + product_back(grad_ff_hidden, ff_vec)
    grad_normed_s = grad_embed_in[:, :D_S] + grad_ff_input[:, :D_S]
    unused, norm_pull = jax.vjp(layer_norm, scalar_one, gain_norm)
    grad_scalar_one, grad_norm_gain = norm_pull(grad_normed_s)
    grad_vector_one = pullback(vector_norm, vector_one, grad_normed_v)

    shard = lambda grad: grad.astype(BF).reshape((spaces, grad.shape[0] // spaces) + grad.shape[1:])
    gains = jnp.concatenate(
        [shard(grad_norm_gain), shard(grad_attn_gain), shard(grad_ffn_gain)], 1
    )
    gains = pad_to(pad_to(gains, 512, 1)[:, None, :], 16, 1)
    first_share = jnp.concatenate(
        [
            shard(grad_w_down),
            fold(shard(grad_w_up)),
            fold(shard(grad_w_qkv)),
            shard(grad_w_out),
            shard(grad_w_embed),
            fold(shard(grad_ff_scalar)),
            jnp.concatenate([shard(grad_ff_vec), shard(grad_ff_up)], 2),
            gains,
        ],
        1,
    )
    first_sum = lax.psum_scatter(first_share, "space", scatter_dimension=0, tiled=False)
    first_sum = lax.psum(first_sum, "dp").astype(F32)

    grad_a, grad_mix, grad_b, grad_p, grad_q, grad_vout = edge_backward(
        near_row, ev_col, ev_row, hidden, lx, dsilu, update,
        grad_scalar_one * (1.0 / NEIGH), grad_vector_one * (1.0 / NEIGH), wn_mix, vout, table_count,
    )
    grad_vedge = jnp.sum(grad_p[:, table_count], 0)[:H_V]
    grad_vec_edge = lax.psum(grad_vedge[None, :], ("dp", "space"))
    grad_a_r = grad_a.astype(BF)
    grad_p_r = grad_p[:, :table_count].astype(BF)
    grad_b_r = grad_b.astype(BF)
    grad_q_r = grad_q.astype(BF)
    grad_node_a = product_lead(table_s, grad_a_r)
    grad_node_b = product_lead(node_scalar, grad_b_r)
    grad_vec_a = product_lead(table_v, grad_p_r)
    grad_vec_b = product_lead(node_vector, grad_q_r)
    grad_table_scalar = product_back(grad_a_r, w_node[:, :D_S])
    grad_table_vector = product_back(grad_p_r, vec_source)
    grad_scalar = (
        grad_scalar_one + product_back(grad_b_r, w_node[:, D_S:]) + grad_table_scalar[:local_rows]
    )
    grad_vector = (
        grad_vector_one + product_back(grad_q_r, vec_target) + grad_table_vector[:, :local_rows]
    )
    back = jnp.concatenate(
        [grad_table_scalar[local_rows:]] + [grad_table_vector[c, local_rows:] for c in range(3)], 1
    )
    back = back.astype(BF).reshape(spaces, CAP, D_S + 3 * D_V)
    got = lax.all_to_all(back, "space", split_axis=0, concat_axis=0, tiled=True)
    got = got.reshape(extra_rows, D_S + 3 * D_V)
    got = jnp.where(sent_live[:, None], got, 0)
    added = lax.dot_general(pick, got, (((0,), (0,)), ((), ())), preferred_element_type=F32)
    grad_scalar = grad_scalar + added[:, :D_S]
    grad_vector = grad_vector + jnp.moveaxis(
        added[:, D_S:].reshape(local_rows, 3, D_V), 1, 0
    )

    columns = lambda grad: jnp.moveaxis(
        grad.reshape(grad.shape[0], spaces, grad.shape[1] // spaces), 1, 0
    )
    mix_block = columns(grad_mix.astype(BF))
    mix_width = D_S // spaces
    mix_rows = H_P * mix_width // 512
    second_share = jnp.concatenate(
        [
            fold(shard(grad_node_a)),
            fold(shard(grad_node_b)),
            mix_block.reshape(spaces, mix_rows, 512),
            shard(grad_vec_a)[:, :, :512],
            shard(grad_vec_b)[:, :, :512],
            shard(grad_vout)[:, :, :512],
            jnp.concatenate(
                [
                    shard(grad_vec_a)[:, :, 512:],
                    shard(grad_vec_b)[:, :, 512:],
                    shard(grad_vout)[:, :, 512:],
                    jnp.zeros((spaces, D_V // spaces, 128), BF),
                ],
                2,
            ),
        ],
        1,
    )
    second_sum = lax.psum_scatter(second_share, "space", scatter_dimension=0, tiled=False)
    second_sum = lax.psum(second_sum, "dp").astype(F32)

    def taker(rows_in):
        at = [0]

        def take(rows, cols, blocks=1):
            part = rows_in[at[0] : at[0] + rows * blocks]
            at[0] += rows * blocks
            return unfold(part, rows, cols) if blocks > 1 else part

        return take

    take = taker(first_sum)
    out_down = take(grad_w_down.shape[0] // spaces, 512)
    out_up = take(D_MODEL // spaces, 2048, 4)
    out_qkv = take(D_MODEL // spaces, 1536, 3)
    out_out = take(D_MODEL // spaces, 512)
    out_embed = take((D_S + D_V) // spaces, 512)
    out_ffs = take((D_S + D_V) // spaces, 1024, 2)
    both = take(D_V // spaces, 512)
    out_ffv, out_ffu = both[:, :D_V], both[:, D_V:]
    gain_row = take(16, 512)[0]
    cuts = [D_S // spaces, D_MODEL // spaces, D_MODEL // spaces]
    out_gn = gain_row[: cuts[0]]
    out_ga = gain_row[cuts[0] : cuts[0] + cuts[1]]
    out_gf = gain_row[cuts[0] + cuts[1] : sum(cuts)]
    take = taker(second_sum)
    node_a = take(D_S // spaces, 1024, 2)
    node_b = take(D_S // spaces, 1024, 2)
    mixed = take(mix_rows, 512).reshape(H_P, mix_width)
    vec_a = take(D_V // spaces, 512)
    vec_b = take(D_V // spaces, 512)
    vout_t = take(D_V // spaces, 512)
    tails = take(D_V // spaces, 512)
    out_vec_node = jnp.concatenate([vec_a, tails[:, :1], vec_b, tails[:, 128:129]], 1)
    out_vec_out = jnp.concatenate([vout_t, tails[:, 256:257]], 1).T
    return (
        stream_out,
        grad_scalar.astype(BF),
        grad_vector.astype(BF),
        jnp.concatenate([node_a, node_b], 1),
        mixed[H_V : H_V + D_E],
        mixed[:H_V],
        out_vec_node,
        grad_vec_edge,
        out_vec_out,
        out_gn,
        out_ffv,
        out_ffs,
        out_ffu,
        out_embed,
        out_ga,
        out_qkv,
        out_out,
        out_gf,
        out_up,
        out_down,
    )


def solution(mesh):
    rows = P(("dp", "space"), None)
    component = P(None, ("dp", "space"), None)
    return jax.shard_map(
        body,
        mesh=mesh,
        in_specs=(
            rows, component, rows, P(None, ("dp", "space")), rows,
            P(("dp", "space"), None, None), P("dp"), rows,
        ) + (P(),) * 17,
        out_specs=(
            rows, rows, component, P("space", None), P(None, "space"), P(None, "space"),
            P("space", None), P(), P(None, "space"), P("space"), P("space", None),
            P("space", None), P("space", None), P("space", None), P("space"), P("space", None),
            P("space", None), P("space"), P("space", None), P("space", None),
        ),
        check_vma=False,
    )
```

```python
import functools
import math

import jax
import jax.numpy as jnp
from jax import lax
from jax.experimental import pallas as pl
from jax.experimental.pallas import tpu as pltpu
from jax.sharding import PartitionSpec as P

D_S = 1024
D_V = 256
H_V = 513
H_P = 640
D_E = 32
NEIGH = 30
D_MODEL = 512
HEADS = 8
HEAD_DIM = 64
CAP = 16
GROUP = 5
VMEM_LIMIT = 60 * 1024 * 1024

MESH = pl.DeviceIdType.MESH
BF = jnp.bfloat16
F32 = jnp.float32


def layer_norm(values, gain_row):
    centred = values - jnp.mean(values, axis=-1, keepdims=True)
    spread = jnp.mean(centred * centred, axis=-1, keepdims=True)
    return centred * lax.rsqrt(spread + 1e-05) * gain_row


def vector_norm(vectors):
    mean_power = jnp.mean(jnp.sum(vectors * vectors, axis=0), axis=-1, keepdims=True)
    return vectors * lax.rsqrt(mean_power + 1e-05)[None]


def length_plus(vectors):
    return jnp.sqrt(jnp.sum(vectors * vectors, axis=0) + 1.0)


def vector_gate(vectors):
    return vectors * jax.nn.sigmoid(length_plus(vectors))[None]


def gelu_exact(values):
    return jax.nn.gelu(values, approximate=False)


def product(former, latter):
    return jnp.dot(former, latter, preferred_element_type=F32)


def product_lead(former, latter):
    leading = tuple(range(former.ndim - 1))
    return lax.dot_general(
        former, latter, ((leading, leading), ((), ())), preferred_element_type=F32
    )


def product_back(former, latter):
    return lax.dot_general(
        former, latter, (((former.ndim - 1,), (1,)), ((), ())), preferred_element_type=F32
    )


def pullback(function, at_point, cotangent_in):
    unused, puller = jax.vjp(function, at_point)
    return puller(cotangent_in)[0]


def sigmoid(values):
    return 0.5 * jnp.tanh(0.5 * values) + 0.5


LANE_BLOCKS = ((0, 256), (256, 256), (512, 128))
ROW_TILE = 64


def edge_forward_kernel(
    near_ref, es_ref, ev_ref, a_ref, b_ref, p_ref, q_ref, ve_ref, vo_ref,
    aggs_ref, aggv_ref, h_ref, lx_ref, ds_ref, z_ref, x_scr,
):
    nodes = b_ref.shape[0]
    table = p_ref.shape[1]
    rows = GROUP * nodes
    idx = near_ref[...].reshape(rows, 1)
    x_scr[:, :table] = (idx == lax.broadcasted_iota(jnp.int32, (rows, table), 1)).astype(BF)
    one_hot = x_scr[:, :table]
    for start, width in LANE_BLOCKS:
        cols = pl.ds(start, width)
        gathered = [product(one_hot, p_ref[c, :, cols]) for c in range(3)]
        for k in range(GROUP):
            for first in range(0, nodes, ROW_TILE):
                at = k * nodes + first
                evk = ev_ref[k, pl.ds(first, ROW_TILE), :]
                total = None
                for c in range(3):
                    h = (
                        gathered[c][at : at + ROW_TILE]
                        + q_ref[c, pl.ds(first, ROW_TILE), cols]
                        + evk[:, c : c + 1] * ve_ref[:, cols]
                    )
                    h_ref[k, c, pl.ds(first, ROW_TILE), cols] = h.astype(BF)
                    total = h * h + 1.0 if total is None else total + h * h
                length = total * lax.rsqrt(total)
                if start == 512:
                    lane = lax.broadcasted_iota(jnp.int32, (ROW_TILE, width), 1)
                    length = jnp.where(
                        lane == 0, length, es_ref[k, pl.ds(first, ROW_TILE), :].astype(F32)
                    )
                length = length.astype(BF)
                x_scr[pl.ds(at, ROW_TILE), pl.ds(table + start, width)] = length
                lx_ref[k, pl.ds(first, ROW_TILE), cols] = length

    @pl.when(pl.program_id(0) == 0)
    def _():
        aggs_ref[...] = jnp.zeros_like(aggs_ref)
        aggv_ref[...] = jnp.zeros_like(aggv_ref)

    full = x_scr[...]
    for start in range(0, D_S, 256):
        cols = pl.ds(start, 256)
        pre = product(full, a_ref[:, cols])
        for first in range(0, nodes, ROW_TILE):
            part = pl.ds(first, ROW_TILE)
            acc = None
            for k in range(GROUP):
                at = k * nodes + first
                x = pre[at : at + ROW_TILE] + b_ref[part, cols]
                s = sigmoid(x)
                y = x * s
                ds_ref[k, part, cols] = (s + y * (1.0 - s)).astype(BF)
                acc = y if acc is None else acc + y
            aggs_ref[part, cols] += acc * (1.0 / NEIGH)
    ups = [
        product(h_ref[:, c, :, :].reshape(rows, H_P), vo_ref[...]) for c in range(3)
    ]
    for first in range(0, nodes, ROW_TILE):
        part = pl.ds(first, ROW_TILE)
        acc = [None] * 3
        for k in range(GROUP):
            at = k * nodes + first
            z = [ups[c][at : at + ROW_TILE] for c in range(3)]
            power = z[0] * z[0] + z[1] * z[1] + z[2] * z[2] + 1.0
            s = sigmoid(power * lax.rsqrt(power))
            for c in range(3):
                z_ref[k, c, part, :] = z[c].astype(BF)
                gated = z[c] * s
                acc[c] = gated if acc[c] is None else acc[c] + gated
        for c in range(3):
            aggv_ref[c, part, :] += acc[c] * (1.0 / NEIGH)


def edge_forward(near_col, es_pad, ev_col, mix, b_target, p_source, q_target, ve_row, vout):
    nodes = b_target.shape[0]
    table = p_source.shape[1]
    whole = lambda shape: pl.BlockSpec(shape, lambda g: (0,) * len(shape))
    slots = lambda *shape: pl.BlockSpec((GROUP,) + shape, lambda g: (g,) + (0,) * len(shape))
    return pl.pallas_call(
        edge_forward_kernel,
        grid=(NEIGH // GROUP,),
        in_specs=[
            slots(nodes, 1),
            slots(nodes, 128),
            slots(nodes, 3),
            whole((table + H_P, D_S)),
            whole((nodes, D_S)),
            whole((3, table, H_P)),
            whole((3, nodes, H_P)),
            whole((1, H_P)),
            whole((H_P, D_V)),
        ],
        out_specs=[
            whole((nodes, D_S)),
            whole((3, nodes, D_V)),
            slots(3, nodes, H_P),
            slots(nodes, H_P),
            slots(nodes, D_S),
            slots(3, nodes, D_V),
        ],
        out_shape=[
            jax.ShapeDtypeStruct((nodes, D_S), F32),
            jax.ShapeDtypeStruct((3, nodes, D_V), F32),
            jax.ShapeDtypeStruct((NEIGH, 3, nodes, H_P), BF),
            jax.ShapeDtypeStruct((NEIGH, nodes, H_P), BF),
            jax.ShapeDtypeStruct((NEIGH, nodes, D_S), BF),
            jax.ShapeDtypeStruct((NEIGH, 3, nodes, D_V), BF),
        ],
        scratch_shapes=[pltpu.VMEM((GROUP * nodes, table + H_P), BF)],
        compiler_params=pltpu.CompilerParams(vmem_limit_bytes=VMEM_LIMIT),
        name="edge_forward",
    )(near_col, es_pad, ev_col, mix, b_target, p_source, q_target, ve_row, vout)


def message_kernel(
    near_ref, es_ref, ev_ref, ve_ref, ns_ref, nv_ref, sent_ref, vn_ref, we_ref, vout_ref, norms_ref,
    wnode_hbm,
    aggs_ref, aggv_ref, h_ref, lx_ref, ds_ref, z_ref, ts_hbm, tv_hbm, vs_hbm, vt_hbm, vo_hbm, wn_hbm,
    x_scr, turn_scr, b_ref, p_ref, q_ref, ts_ref, tv_ref, vs_ref, vt_ref, vo_ref, a_ref, wn_ref,
    pt_ref, wnode, row_scr, vt_scr, out_scr, in_scr, send_sem, recv_sem, load_sem, keep_sem,
):
    nodes = b_ref.shape[0]
    table = p_ref.shape[1]
    rows = GROUP * nodes
    keeps = [
        pltpu.make_async_copy(source, target, keep_sem.at[n])
        for n, (source, target) in enumerate(
            (
                (ts_ref, ts_hbm), (tv_ref, tv_hbm), (vs_ref, vs_hbm), (vt_ref, vt_hbm),
                (vo_ref, vo_hbm), (wn_ref, wn_hbm),
            )
        )
    ]

    @pl.when(pl.program_id(0) == 0)
    def _():
        prepare_kernel(
            ns_ref, nv_ref, sent_ref, vn_ref, we_ref, vout_ref, norms_ref, wnode_hbm,
            b_ref, p_ref, q_ref, ts_ref, tv_ref, vs_ref, vt_ref, vo_ref, a_ref, wn_ref, pt_ref,
            wnode, row_scr, vt_scr, out_scr, in_scr, send_sem, recv_sem, load_sem,
        )
        start_all(keeps)

    first_slot = pl.program_id(0) * GROUP

    @pl.when(pl.program_id(0) == 0)
    def _():
        for n in range(4):
            ref = near_ref if n == 3 else ev_ref.at[n]
            turn_scr[n, pl.ds(0, NEIGH), :] = ref[...].astype(F32)
            turn_scr[n] = jnp.transpose(turn_scr[n])

    back = lax.rem(128 - first_slot, 128)
    ev = [pltpu.roll(turn_scr[n], back, 1) for n in range(4)]
    slots = ev[3]
    places = lax.broadcasted_iota(jnp.int32, (nodes, table), 1).astype(F32)
    edges_in = []
    for k in range(GROUP):
        x_scr[pl.ds(k * nodes, nodes), :table] = (slots[:, k : k + 1] == places).astype(BF)
        rows_in = pl.ds(pl.multiple_of((first_slot + k) * D_E, D_E), D_E)
        edges_in.append(
            jnp.transpose(
                jnp.concatenate(
                    [
                        jnp.zeros((16, nodes), F32),
                        es_ref[rows_in, :].astype(F32),
                        jnp.zeros((112 - D_E, nodes), F32),
                    ],
                    0,
                )
            )
        )
    one_hot = x_scr[:, :table]
    for start, width in LANE_BLOCKS:
        cols = pl.ds(start, width)
        if start == 512:
            lane = lax.broadcasted_iota(jnp.int32, (rows, width), 1)
            three = product(one_hot, pt_ref[...])
            gathered = [
                jnp.where(lane == 0, three if c == 0 else pltpu.roll(three, width - c, 1), 0.0)
                for c in range(3)
            ]
        else:
            gathered = [product(one_hot, p_ref[c, :, cols]) for c in range(3)]
        for k in range(GROUP):
            for first in range(0, nodes, ROW_TILE):
                at = k * nodes + first
                total = None
                for c in range(3):
                    h = (
                        gathered[c][at : at + ROW_TILE]
                        + q_ref[c, pl.ds(first, ROW_TILE), cols]
                        + ev[c][first : first + ROW_TILE, k : k + 1]
                        * ve_ref[:, pl.ds(D_S + 2 * D_MODEL + start, width)]
                    )
                    h_ref[k, c, pl.ds(first, ROW_TILE), cols] = h.astype(BF)
                    total = h * h + 1.0 if total is None else total + h * h
                length = total * lax.rsqrt(total)
                if start == 512:
                    lane = lax.broadcasted_iota(jnp.int32, (ROW_TILE, width), 1)
                    length = jnp.where(
                        lane == 0, length, edges_in[k][first : first + ROW_TILE]
                    )
                length = length.astype(BF)
                x_scr[pl.ds(at, ROW_TILE), pl.ds(table + start, width)] = length
                lx_ref[k, pl.ds(first, ROW_TILE), cols] = length

    @pl.when(pl.program_id(0) == 0)
    def _():
        aggs_ref[...] = jnp.zeros_like(aggs_ref)
        aggv_ref[...] = jnp.zeros_like(aggv_ref)

    full = x_scr[...]
    for start in range(0, D_S, 256):
        cols = pl.ds(start, 256)
        pre = product(full, a_ref[:, cols])
        for first in range(0, nodes, ROW_TILE):
            part = pl.ds(first, ROW_TILE)
            acc = None
            for k in range(GROUP):
                at = k * nodes + first
                x = pre[at : at + ROW_TILE] + b_ref[part, cols]
                s = sigmoid(x)
                y = x * s
                ds_ref[k, part, cols] = (s + y * (1.0 - s)).astype(BF)
                acc = y if acc is None else acc + y
            aggs_ref[part, cols] += acc * (1.0 / NEIGH)
    ups = [
        product(h_ref[:, c, :, pl.ds(0, 512)].reshape(rows, 512), vo_ref[pl.ds(0, 512), :])
        for c in range(3)
    ]
    last_row = vo_ref[pl.ds(512, 16), :].astype(F32)[0:1, :]
    for first in range(0, nodes, ROW_TILE):
        part = pl.ds(first, ROW_TILE)
        acc = [None] * 3
        for k in range(GROUP):
            at = k * nodes + first
            z = [
                ups[c][at : at + ROW_TILE]
                + h_ref[k, c, part, pl.ds(512, 128)].astype(F32)[:, 0:1] * last_row
                for c in range(3)
            ]
            power = z[0] * z[0] + z[1] * z[1] + z[2] * z[2] + 1.0
            s = sigmoid(power * lax.rsqrt(power))
            for c in range(3):
                z_ref[k, c, part, :] = z[c].astype(BF)
                gated = z[c] * s
                acc[c] = gated if acc[c] is None else acc[c] + gated
        for c in range(3):
            aggv_ref[c, part, :] += acc[c] * (1.0 / NEIGH)

    @pl.when(pl.program_id(0) == pl.num_programs(0) - 1)
    def _():
        wait_all(keeps)


def message(operands, w_node):
    near, edge_scalar, ev, gain_row, node_scalar, node_vector, sent = operands[:7]
    nodes = node_scalar.shape[0]
    spaces = sent.shape[0]
    table = nodes + spaces * CAP
    rows = GROUP * nodes
    once = pl.Buffered(1)
    whole = lambda shape: pl.BlockSpec(shape, lambda g: (0,) * len(shape), pipeline_mode=once)
    slots = lambda *shape: pl.BlockSpec((GROUP,) + shape, lambda g: (g,) + (0,) * len(shape))
    hbm = pl.BlockSpec(memory_space=pl.ANY)
    bits = lambda *shape: pltpu.VMEM(shape, BF)
    wide = lambda *shape: pltpu.VMEM(shape, F32)
    kept = [(table, D_S), (3, table, D_V), (H_P, D_V), (H_P, D_V), (H_P, D_V), (H_P, D_S)]
    outs = [
        ((nodes, D_S), F32),
        ((3, nodes, D_V), F32),
        ((NEIGH, 3, nodes, H_P), BF),
        ((NEIGH, nodes, H_P), BF),
        ((NEIGH, nodes, D_S), BF),
        ((NEIGH, 3, nodes, D_V), BF),
    ] + [(shape, BF) for shape in kept]
    blocks = (spaces, CAP, D_S + 3 * D_V)
    return pl.pallas_call(
        message_kernel,
        grid=(NEIGH // GROUP,),
        in_specs=[whole(one.shape) for one in operands] + [hbm],
        out_specs=[
            whole((nodes, D_S)),
            whole((3, nodes, D_V)),
            slots(3, nodes, H_P),
            slots(nodes, H_P),
            slots(nodes, D_S),
            slots(3, nodes, D_V),
        ]
        + [hbm] * len(kept),
        out_shape=[jax.ShapeDtypeStruct(shape, kind) for shape, kind in outs],
        scratch_shapes=[
            bits(rows, table + H_P), wide(4, 128, nodes), wide(nodes, D_S), bits(3, table, H_P),
            wide(3, nodes, H_P), bits(*kept[0]), bits(*kept[1]), bits(*kept[2]), bits(*kept[3]),
            bits(*kept[4]), bits(table + H_P, D_S), bits(*kept[5]), bits(table, 128),
            bits(*w_node.shape), wide(8, 128), wide(H_P, D_V), bits(*blocks), bits(*blocks),
            pltpu.SemaphoreType.DMA((spaces - 1,)),
            pltpu.SemaphoreType.DMA((spaces - 1,)),
            pltpu.SemaphoreType.DMA,
            pltpu.SemaphoreType.DMA((len(kept),)),
        ],
        compiler_params=pltpu.CompilerParams(
            collective_id=3, has_side_effects=True, vmem_limit_bytes=VMEM_LIMIT
        ),
        name="message",
    )(*operands, w_node)


def edge_backward_kernel(
    near_ref, ev_ref, evr_ref, h_ref, lx_ref, ds_ref, z_ref, gs_ref, gv_ref, wn_ref, vo_ref,
    ga_ref, gw_ref, gb_ref, gp_ref, gq_ref, gvo_ref, pre_scr, up_scr, gh_scr,
):
    nodes = gs_ref.shape[0]
    table = ga_ref.shape[0]
    rows = GROUP * nodes

    @pl.when(pl.program_id(0) == 0)
    def _():
        for ref in (ga_ref, gw_ref, gb_ref, gp_ref, gq_ref, gvo_ref):
            ref[...] = jnp.zeros_like(ref)

    for start in range(0, D_S, 256):
        cols = pl.ds(start, 256)
        for first in range(0, nodes, ROW_TILE):
            part = pl.ds(first, ROW_TILE)
            share = gs_ref[part, cols]
            acc = None
            for k in range(GROUP):
                g = (ds_ref[k, part, cols].astype(F32) * share).astype(BF)
                pre_scr[pl.ds(k * nodes + first, ROW_TILE), cols] = g
                g = g.astype(F32)
                acc = g if acc is None else acc + g
            gb_ref[part, cols] += acc
    for first in range(0, nodes, ROW_TILE):
        part = pl.ds(first, ROW_TILE)
        share = [gv_ref[c, part, :] for c in range(3)]
        for k in range(GROUP):
            z = [z_ref[k, c, part, :].astype(F32) for c in range(3)]
            power = z[0] * z[0] + z[1] * z[1] + z[2] * z[2] + 1.0
            inverse = lax.rsqrt(power)
            s = sigmoid(power * inverse)
            dot = z[0] * share[0] + z[1] * share[1] + z[2] * share[2]
            factor = dot * inverse * (s * (1.0 - s))
            for c in range(3):
                up_scr[c, pl.ds(k * nodes + first, ROW_TILE), :] = (
                    share[c] * s + z[c] * factor
                ).astype(BF)

    near = near_ref[0]
    one_hot = (lax.broadcasted_iota(jnp.int32, (table, rows), 0) == near).astype(BF)
    grad_pre = pre_scr[...]
    ga_ref[...] += product(one_hot, grad_pre)
    lx = lx_ref[...].reshape(rows, H_P)
    gw_ref[...] += lax.dot_general(
        lx, grad_pre, (((0,), (0,)), ((), ())), preferred_element_type=F32
    )
    for start, width in LANE_BLOCKS:
        cols = pl.ds(start, width)
        grad_length = product_back(grad_pre, wn_ref[cols, :])
        grad_direct = [product_back(up_scr[c], vo_ref[cols, :]) for c in range(3)]
        for first in range(0, nodes, ROW_TILE):
            part = pl.ds(first, ROW_TILE)
            acc = [None] * 3
            for k in range(GROUP):
                at = k * nodes + first
                ratio = grad_length[at : at + ROW_TILE] * pl.reciprocal(
                    lx_ref[k, part, cols].astype(F32), approx=True
                )
                if start == 512:
                    lane = lax.broadcasted_iota(jnp.int32, (ROW_TILE, width), 1)
                    ratio = jnp.where(lane == 0, ratio, 0.0)
                for c in range(3):
                    g = grad_direct[c][at : at + ROW_TILE] + ratio * h_ref[
                        k, c, part, cols
                    ].astype(F32)
                    gh_scr[c, pl.ds(at, ROW_TILE), cols] = g.astype(BF)
                    acc[c] = g if acc[c] is None else acc[c] + g
            for c in range(3):
                gq_ref[c, part, cols] += acc[c]
    for c in range(3):
        evr = jnp.broadcast_to(evr_ref[0, c : c + 1, :], (16, rows))
        lead = jnp.concatenate([one_hot, evr.astype(BF)], axis=0)
        gp_ref[c] += product(lead, gh_scr[c])
        gvo_ref[...] += lax.dot_general(
            up_scr[c],
            h_ref[:, c, :, :].reshape(rows, H_P),
            (((0,), (0,)), ((), ())),
            preferred_element_type=F32,
        )


def edge_backward(near_row, ev_col, ev_row, hidden, lx, dsilu, update, gs, gv, wn, vout, table):
    nodes = gs.shape[0]
    rows = GROUP * nodes
    whole = lambda shape: pl.BlockSpec(shape, lambda g: (0,) * len(shape))
    slots = lambda *shape: pl.BlockSpec((GROUP,) + shape, lambda g: (g,) + (0,) * len(shape))
    steps = lambda *shape: pl.BlockSpec((1,) + shape, lambda g: (g,) + (0,) * len(shape))
    outs = [
        (table, D_S),
        (H_P, D_S),
        (nodes, D_S),
        (3, table + 16, H_P),
        (3, nodes, H_P),
        (D_V, H_P),
    ]
    return pl.pallas_call(
        edge_backward_kernel,
        grid=(NEIGH // GROUP,),
        in_specs=[
            steps(1, rows),
            slots(nodes, 3),
            steps(3, rows),
            slots(3, nodes, H_P),
            slots(nodes, H_P),
            slots(nodes, D_S),
            slots(3, nodes, D_V),
            whole((nodes, D_S)),
            whole((3, nodes, D_V)),
            whole((H_P, D_S)),
            whole((H_P, D_V)),
        ],
        out_specs=[whole(shape) for shape in outs],
        out_shape=[jax.ShapeDtypeStruct(shape, F32) for shape in outs],
        scratch_shapes=[
            pltpu.VMEM((rows, D_S), BF),
            pltpu.VMEM((3, rows, D_V), BF),
            pltpu.VMEM((3, rows, H_P), BF),
        ],
        compiler_params=pltpu.CompilerParams(vmem_limit_bytes=VMEM_LIMIT),
        name="edge_backward",
    )(near_row, ev_col, ev_row, hidden, lx, dsilu, update, gs, gv, wn, vout)


AT_AIN, AT_EMB, AT_FFIN, AT_FFH, AT_NV, FAC_NODE = 0, 512, 1792, 3072, 3840, 4608
AT_GELU, AT_GUP, AT_FIN, AT_COT, AT_ATT, AT_GBR, FAC_FEED = 0, 2048, 4096, 4608, 5120, 5632, 6144
AT_GQKV, AT_STREAM, AT_GPRE, AT_GFU, AT_GFH, FAC_BACK = 0, 1536, 2048, 3072, 3840, 4608
ROWS_F, ROWS_A, ROWS_N, ROWS_S, ROWS_B, ROWS_V = ALL_ROWS = (512, 256, 512, 256, 384, 128)
ROWS_E = ROWS_F // 4

def full_block(shape):
    return pl.BlockSpec(shape, lambda: (0,) * len(shape))


def lead_product(former, latter):
    return lax.dot_general(
        former, latter, (((0,), (0,)), ((), ())), preferred_element_type=F32
    )


def swap_halves(values):
    return pltpu.roll(values, 64, 1)


def lower_half(shape):
    return lax.broadcasted_iota(jnp.int32, shape, 1) < 64


def pack_tall(tile, odd):
    rows = tile.shape[0] // 2
    top, low = tile[:rows], tile[rows:]
    side = lower_half((rows, 128))
    if odd:
        return jnp.where(side, swap_halves(top), low)
    return jnp.where(side, top, swap_halves(low))


def unpack_tall(block):
    rows = block.shape[0]
    side = lower_half((rows, 128))
    return jnp.concatenate(
        [jnp.where(side, block, 0.0), jnp.where(side, swap_halves(block), 0.0)], 0
    )


def centre(values):
    centred = values - jnp.mean(values, axis=-1, keepdims=True)
    inverse = lax.rsqrt(jnp.mean(centred * centred, axis=-1, keepdims=True) + 1e-05)
    return centred * inverse, inverse


def centre_back(hat, inverse, grad):
    return inverse * (
        grad
        - jnp.mean(grad, axis=-1, keepdims=True)
        - hat * jnp.mean(grad * hat, axis=-1, keepdims=True)
    )


def power_of(parts):
    return parts[0] * parts[0] + parts[1] * parts[1] + parts[2] * parts[2]


def node_forward_kernel(
    ns_ref, nv_ref, as_ref, av_ref, ng_ref, fv_ref, fs_ref, fu_ref, we_ref, ag_ref, wq_ref,
    s1_ref, v1_ref, ffh_ref, ffp_ref, ffu_ref, v2_ref, sz_ref, fac_ref, out_ref, with_keys,
):
    nodes = ns_ref.shape[0]
    s1 = ns_ref[...].astype(F32) + as_ref[...]
    s1_ref[...] = s1
    hat, unused = centre(s1)
    normed_s = hat * ng_ref[...]
    v1 = [nv_ref[c].astype(F32) + av_ref[c] for c in range(3)]
    scale = lax.rsqrt(jnp.mean(power_of(v1), axis=-1, keepdims=True) + 1e-05)
    normed_v = [v * scale for v in v1]
    ffh = [product(v.astype(BF), fv_ref[...]) for v in normed_v]
    power = power_of(ffh) + 1.0
    fac_ref[:, pl.ds(AT_FFIN, D_S)] = normed_s.astype(BF)
    fac_ref[:, pl.ds(AT_FFIN + D_S, D_V)] = (power * lax.rsqrt(power)).astype(BF)
    ffp = product(fac_ref[:, pl.ds(AT_FFIN, D_S + D_V)], fs_ref[...])
    ffu = [product(h.astype(BF), fu_ref[...]) for h in ffh]
    for c in range(3):
        v1_ref[c] = v1[c]
        fac_ref[:, pl.ds(AT_FFH + c * D_V, D_V)] = ffh[c].astype(BF)
        fac_ref[:, pl.ds(AT_NV + c * D_V, D_V)] = normed_v[c].astype(BF)
        ffh_ref[c] = ffh[c]
        ffu_ref[c] = ffu[c]
    ffp_ref[...] = ffp
    s2 = normed_s + ffp * sigmoid(ffp)
    power = power_of(ffu) + 1.0
    gate = sigmoid(power * lax.rsqrt(power))
    v2 = [normed_v[c] + ffu[c] * gate for c in range(3)]
    for c in range(3):
        v2_ref[c] = v2[c]
    power = power_of(v2) + 1.0
    fac_ref[:, pl.ds(AT_EMB, D_S)] = s2.astype(BF)
    fac_ref[:, pl.ds(AT_EMB + D_S, D_V)] = (power * lax.rsqrt(power)).astype(BF)
    sz = product(fac_ref[:, pl.ds(AT_EMB, D_S + D_V)], we_ref[...])
    sz_ref[...] = sz
    hat, unused = centre(sz)
    attn_in = (hat * ag_ref[...]).astype(BF)
    fac_ref[:, pl.ds(AT_AIN, D_MODEL)] = attn_in
    q, k = [product(attn_in, wq_ref[:, pl.ds(n * D_MODEL, D_MODEL)]) for n in range(2)]
    side = lower_half((nodes, 128))
    for pair in range(HEADS // 2):
        cols = slice(pair * 128, pair * 128 + 128)
        qp, kp = q[:, cols], k[:, cols]
        even = jnp.where(side, qp, swap_halves(kp))
        odd = jnp.where(side, swap_halves(qp), kp)
        for n, block in enumerate((even, odd)):
            out_ref[2 * pair + n, pl.ds(0, nodes), :] = block.astype(BF)
    with_keys()
    v = product(attn_in, wq_ref[:, pl.ds(2 * D_MODEL, D_MODEL)])
    for head in range(HEADS):
        tile = v[:, head // 2 * 128 : head // 2 * 128 + 128]
        out_ref[head, pl.ds(nodes, nodes // 2), :] = pack_tall(tile, head % 2 == 1).astype(BF)


def split_heads(x_ref, nodes):
    spaces = x_ref.shape[0]
    both = x_ref[:, pl.ds(0, nodes), :].reshape(spaces * nodes, 128).astype(F32)
    queries = jnp.where(lower_half(both.shape), both, 0.0).astype(BF)
    keys = swap_halves(both).astype(BF)
    return queries, keys


def split_values(x_ref, nodes):
    spaces = x_ref.shape[0]
    return jnp.concatenate(
        [unpack_tall(x_ref[d, pl.ds(nodes, nodes // 2), :].astype(F32)) for d in range(spaces)], 0
    ).astype(BF)


def attend_kernel(x_ref, id_ref, probs_ref, att_ref, out_ref, with_probs):
    spaces = x_ref.shape[0]
    nodes = x_ref.shape[1] * 2 // 3
    count = spaces * nodes
    queries, keys = split_heads(x_ref, nodes)
    row_ids = id_ref[...]
    column_ids = jnp.transpose(jnp.broadcast_to(row_ids, (8, count)))[:, 0:1]
    block = 2 * nodes
    for first in range(0, count, block):
        scores = product_back(queries[first : first + block], keys) * HEAD_DIM ** (-0.5)
        same = column_ids[first : first + block] == row_ids
        scores = jnp.where(same, scores, -1000000000.0)
        shifted = jnp.exp(scores - jnp.max(scores, axis=-1, keepdims=True))
        probs = (shifted / jnp.sum(shifted, axis=-1, keepdims=True)).astype(BF)
        probs_ref[pl.ds(first, block), :] = probs
    with_probs()
    values = split_values(x_ref, nodes)
    for first in range(0, count, block):
        att = product(probs_ref[pl.ds(first, block), :], values)
        att_ref[pl.ds(first, block), :] = att
        for n in range(block // nodes):
            tile = att[n * nodes : (n + 1) * nodes]
            out_ref[first // nodes + n] = pack_tall(tile, False).astype(BF)


def attend_backward_kernel(x_ref, probs_ref, att_ref, g_ref, out_ref, gs_scr, with_values):
    spaces = x_ref.shape[0]
    nodes = x_ref.shape[1] * 2 // 3
    count = spaces * nodes
    queries, keys = split_heads(x_ref, nodes)
    values = split_values(x_ref, nodes)
    grad = jnp.concatenate(
        [unpack_tall(g_ref[d].astype(F32)) for d in range(spaces)], 0
    )
    dots = jnp.sum(grad * att_ref[...], axis=-1, keepdims=True)
    grad = grad.astype(BF)
    grad_values = jnp.transpose(lead_product(grad, probs_ref[...]))
    for d in range(spaces):
        tile = grad_values[d * nodes : (d + 1) * nodes]
        out_ref[d, pl.ds(nodes, nodes // 2), :] = pack_tall(tile, False).astype(BF)
    with_values()
    block = 2 * nodes
    scale = HEAD_DIM ** (-0.5)
    grad_queries = []
    for first in range(0, count, block):
        grad_probs = product_back(grad[first : first + block], values)
        part = probs_ref[pl.ds(first, block), :].astype(F32)
        grad_scores = (part * (grad_probs - dots[first : first + block])).astype(BF)
        gs_scr[pl.ds(first, block), :] = grad_scores
        grad_queries.append(product(grad_scores, keys))
    grad_queries = jnp.concatenate(grad_queries, 0) * scale
    grad_keys = jnp.transpose(lead_product(queries, gs_scr[...])) * scale
    side = lower_half((nodes, 128))
    for d in range(spaces):
        rows = slice(d * nodes, (d + 1) * nodes)
        out_ref[d, pl.ds(0, nodes), :] = jnp.where(
            side, grad_queries[rows], swap_halves(grad_keys[rows])
        ).astype(BF)


def merge_heads(block_ref, first, half):
    tiles = []
    for pair in range(HEADS // 2):
        even = unpack_tall(block_ref[2 * pair, pl.ds(first, half), :].astype(F32))
        odd = unpack_tall(block_ref[2 * pair + 1, pl.ds(first, half), :].astype(F32))
        tiles.append(even + swap_halves(odd))
    return jnp.concatenate(tiles, 1)


def feed_kernel(
    att_ref, sz_ref, wo_ref, fg_ref, wu_ref, wd_ref, cot_ref,
    out_ref, gatt_ref, gs1_ref, ggain_ref, fac_ref, with_up,
):
    nodes = sz_ref.shape[0]
    att = merge_heads(att_ref, 0, nodes // 2).astype(BF)
    fac_ref[:, pl.ds(AT_ATT, D_MODEL)] = att
    stream_one = sz_ref[...] + product(att, wo_ref[...])
    hat, inverse = centre(stream_one)
    ffn_in = (hat * fg_ref[...]).astype(BF)
    fac_ref[:, pl.ds(AT_FIN, D_MODEL)] = ffn_in
    ffn = wu_ref.shape[1]
    cot = cot_ref[...]
    fac_ref[:, pl.ds(AT_COT, D_MODEL)] = cot
    for start in range(0, ffn, 512):
        cols = pl.ds(start, 512)
        x = product(ffn_in, wu_ref[:, cols])
        cdf = 0.5 * (1.0 + lax.erf(x * (0.5**0.5)))
        fac_ref[:, pl.ds(AT_GELU + start, 512)] = (x * cdf).astype(BF)
        slope = cdf + x * jnp.exp(-0.5 * x * x) * ((0.5 / math.pi) ** 0.5)
        fac_ref[:, pl.ds(AT_GUP + start, 512)] = (
            product_back(cot, wd_ref[cols, :]) * slope
        ).astype(BF)
    with_up()
    out_ref[...] = (
        stream_one + product(fac_ref[:, pl.ds(AT_GELU, ffn)], wd_ref[...])
    ).astype(BF)
    grad_in = product_back(fac_ref[:, pl.ds(AT_GUP, ffn)], wu_ref[...])
    ggain_ref[...] = jnp.sum(grad_in * hat, axis=0, keepdims=True)
    grad_one = cot.astype(F32) + centre_back(hat, inverse, grad_in * fg_ref[...])
    gs1_ref[...] = grad_one
    branch = grad_one.astype(BF)
    fac_ref[:, pl.ds(AT_GBR, D_MODEL)] = branch
    grad_att = product_back(branch, wo_ref[...])
    for head in range(HEADS):
        tile = grad_att[:, head // 2 * 128 : head // 2 * 128 + 128]
        gatt_ref[head] = pack_tall(tile, head % 2 == 1).astype(BF)


def core_columns(values, core):
    values = values.astype(F32)
    side = lower_half((values.shape[0], 128))
    tiles = []
    for n in range(0, 512, 256):
        one, two = values[:, n : n + 128], values[:, n + 128 : n + 256]
        even = jnp.where(side, one, swap_halves(two))
        odd = jnp.where(side, swap_halves(one), two)
        tiles.append(jnp.where(core == 0, even, odd))
    return jnp.concatenate(tiles, 1).astype(BF)


def both_rows(own_ref, other_ref, start, width):
    return jnp.concatenate(
        [own_ref[:, pl.ds(start, width)], other_ref[:, pl.ds(start, width)]], 0
    )


def feed_grads_kernel(own_ref, other_ref, pack_ref):
    quads = pack_ref.shape[0]
    core = lax.rem(lax.axis_index("space"), 2)
    cot = both_rows(own_ref, other_ref, AT_COT, D_MODEL)
    for z in range(quads):
        start = pl.multiple_of(AT_GELU + (2 * z + core) * 256, 256)
        block = lead_product(both_rows(own_ref, other_ref, start, 256), cot)
        pack_ref[z, pl.ds(0, 256), :] = block.astype(BF)
    left = core_columns(both_rows(own_ref, other_ref, AT_FIN, D_MODEL), core)
    for n in range(4):
        block = lead_product(left, both_rows(own_ref, other_ref, AT_GUP + n * 512, 512)).astype(BF)
        for z in range(quads):
            pack_ref[z, pl.ds(256 + n * 64, 64), :] = block[z * 64 : (z + 1) * 64]


def attention_grads(node_ref, node_other, back_ref, back_other, feed_ref, feed_other, pack_ref):
    quads = pack_ref.shape[0]
    core = lax.rem(lax.axis_index("space"), 2)
    left = core_columns(both_rows(node_ref, node_other, AT_AIN, D_MODEL), core)
    pairs = [
        (left, both_rows(back_ref, back_other, AT_GQKV + n * D_MODEL, D_MODEL)) for n in range(3)
    ]
    pairs.append(
        (
            core_columns(both_rows(feed_ref, feed_other, AT_ATT, D_MODEL), core),
            both_rows(feed_ref, feed_other, AT_GBR, D_MODEL),
        )
    )
    for n, (one, two) in enumerate(pairs):
        block = lead_product(one, two).astype(BF)
        for z in range(quads):
            pack_ref[z, pl.ds(n * 64, 64), :] = block[z * 64 : (z + 1) * 64]


def node_grads(node_ref, node_other, back_ref, back_other, pack_ref, tall_scr, low_scr):
    quads = pack_ref.shape[0]
    core = lax.rem(lax.axis_index("space"), 2)
    emb = both_rows(node_ref, node_other, AT_EMB, D_S + D_V)
    ffin = both_rows(node_ref, node_other, AT_FFIN, D_S + D_V)
    rights = [(emb, back_ref, back_other, AT_STREAM)]
    rights += [(ffin, back_ref, back_other, AT_GPRE + n * 512) for n in range(2)]
    for n, (one, own, other, start) in enumerate(rights):
        tall_scr[...] = lead_product(one, both_rows(own, other, start, 512)).astype(BF)
        for z in range(quads):
            rows = pl.ds(pl.multiple_of((2 * z + core) * 160, 32), 160)
            pack_ref[z, pl.ds(n * 160, 160), :] = tall_scr[rows, :]
    vec = up = None
    for c in range(3):
        one = lead_product(
            both_rows(node_ref, node_other, AT_NV + c * D_V, D_V),
            both_rows(back_ref, back_other, AT_GFH + c * D_V, D_V),
        )
        vec = one if vec is None else vec + one
        one = lead_product(
            both_rows(node_ref, node_other, AT_FFH + c * D_V, D_V),
            both_rows(back_ref, back_other, AT_GFU + c * D_V, D_V),
        )
        up = one if up is None else up + one
    low_scr[...] = jnp.concatenate([vec, up], 1).astype(BF)
    for z in range(quads):
        rows = pl.ds(pl.multiple_of((2 * z + core) * 32, 32), 32)
        pack_ref[z, pl.ds(480, 32), :] = low_scr[rows, :]


def node_backward_kernel(
    gq_ref, gs1_ref, s1_ref, v1_ref, ffh_ref, ffp_ref, ffu_ref, v2_ref,
    sz_ref, ng_ref, fv_ref, fs_ref, fu_ref, we_ref, ag_ref, wq_ref, fgain_ref,
    gsone_ref, gvone_ref, gains_ref, back_ref, with_qkv,
):
    nodes = gs1_ref.shape[0]
    shards = gq_ref.shape[0]
    side = lower_half((nodes, 128))
    tiles = [[], []]
    for pair in range(HEADS // 2):
        even = gq_ref[2 * pair, pl.ds(0, nodes), :].astype(F32)
        odd = gq_ref[2 * pair + 1, pl.ds(0, nodes), :].astype(F32)
        tiles[0].append(jnp.where(side, even, swap_halves(odd)))
        tiles[1].append(jnp.where(side, swap_halves(even), odd))
    grads = [jnp.concatenate(tile, 1).astype(BF) for tile in tiles]
    grads.append(merge_heads(gq_ref, nodes, nodes // 2).astype(BF))
    for n in range(3):
        back_ref[:, pl.ds(AT_GQKV + n * D_MODEL, D_MODEL)] = grads[n]
    with_qkv()
    grad_in = product_back(back_ref[:, pl.ds(AT_GQKV, 3 * D_MODEL)], wq_ref[...])
    hat, inverse = centre(sz_ref[...])
    grad_attn_gain = jnp.sum(grad_in * hat, axis=0, keepdims=True)
    stream = gs1_ref[...] + centre_back(hat, inverse, grad_in * ag_ref[...])
    stream = stream.astype(BF)
    back_ref[:, pl.ds(AT_STREAM, D_MODEL)] = stream
    grad_emb = product_back(stream, we_ref[...])
    grad_s2, grad_len = grad_emb[:, :D_S], grad_emb[:, D_S:]
    v2 = [v2_ref[c] for c in range(3)]
    factor = grad_len * lax.rsqrt(power_of(v2) + 1.0)
    grad_v2 = [factor * v for v in v2]
    x = ffp_ref[...]
    s = sigmoid(x)
    grad_pre = (grad_s2 * (s + x * s * (1.0 - s))).astype(BF)
    back_ref[:, pl.ds(AT_GPRE, D_S)] = grad_pre
    grad_ffin = product_back(grad_pre, fs_ref[...])
    z = [ffu_ref[c] for c in range(3)]
    power = power_of(z) + 1.0
    inverse = lax.rsqrt(power)
    s = sigmoid(power * inverse)
    dot = z[0] * grad_v2[0] + z[1] * grad_v2[1] + z[2] * grad_v2[2]
    factor = dot * inverse * (s * (1.0 - s))
    grad_up = [(grad_v2[c] * s + z[c] * factor).astype(BF) for c in range(3)]
    h = [ffh_ref[c] for c in range(3)]
    factor = grad_ffin[:, D_S:] * lax.rsqrt(power_of(h) + 1.0)
    v1 = [v1_ref[c] for c in range(3)]
    scale = lax.rsqrt(jnp.mean(power_of(v1), axis=-1, keepdims=True) + 1e-05)
    grad_nv = []
    for c in range(3):
        back_ref[:, pl.ds(AT_GFU + c * D_V, D_V)] = grad_up[c]
        grad_h = (product_back(grad_up[c], fu_ref[...]) + factor * h[c]).astype(BF)
        back_ref[:, pl.ds(AT_GFH + c * D_V, D_V)] = grad_h
        grad_nv.append(grad_v2[c] + product_back(grad_h, fv_ref[...]))
    grad_ns = grad_s2 + grad_ffin[:, :D_S]
    hat, inverse = centre(s1_ref[...])
    grad_norm_gain = jnp.sum(grad_ns * hat, axis=0, keepdims=True)
    gsone_ref[...] = centre_back(hat, inverse, grad_ns * ng_ref[...])
    dot = grad_nv[0] * v1[0] + grad_nv[1] * v1[1] + grad_nv[2] * v1[2]
    dot = jnp.mean(dot, axis=-1, keepdims=True) * scale * scale
    for c in range(3):
        gvone_ref[c] = scale * (grad_nv[c] - v1[c] * dot)
    gains_ref[...] = jnp.zeros_like(gains_ref)
    gains_ref[0:1, :] = grad_norm_gain
    for p in range(shards):
        pair = slice(p // 2 * 128, p // 2 * 128 + 128)
        left = jnp.broadcast_to(grad_attn_gain[:, pair], (8, 128))
        right = jnp.broadcast_to(fgain_ref[:, pair], (8, 128))
        if p % 2 == 0:
            both = jnp.where(lower_half((8, 128)), left, swap_halves(right))
        else:
            both = jnp.where(lower_half((8, 128)), swap_halves(left), right)
        gains_ref[1:2, pl.ds(p * 128, 128)] = both[0:1]


BACKWARD_LIMIT = 62 * 1024 * 1024

def place():
    dp, space = lax.axis_index("dp"), lax.axis_index("space")
    return {"x": lax.rem(dp, 2), "y": dp // 2, "z": space // 2, "core": lax.rem(space, 2)}


def peer(way, shift=1):
    at = place()
    if way == "x":
        return {"dp": 2 * at["y"] + 1 - at["x"]}
    if way == "y":
        return {"dp": 2 * (1 - at["y"]) + at["x"]}
    if way == "diagonal":
        return {"dp": 2 * (1 - at["y"]) + 1 - at["x"]}
    if way == "core":
        return {"space": 2 * at["z"] + 1 - at["core"]}
    if way == "z":
        return {"space": 2 * lax.rem(at["z"] + shift, 4) + at["core"]}
    return {"space": lax.rem(lax.axis_index("space") + shift, lax.axis_size("space"))}


def greet(peers):
    barrier = pltpu.get_barrier_semaphore()
    for one in peers:
        pl.semaphore_signal(barrier, inc=1, device_id=one, device_id_type=MESH)
    pl.semaphore_wait(barrier, len(peers))


class Wires:
    def __init__(self, send_sem, recv_sem):
        self.send_sem, self.recv_sem, self.used = send_sem, recv_sem, 0

    def copy(self, source, target, to):
        n = self.used
        self.used += 1
        return pltpu.make_async_remote_copy(
            src_ref=source,
            dst_ref=target,
            send_sem=self.send_sem.at[n],
            recv_sem=self.recv_sem.at[n],
            device_id=to,
            device_id_type=MESH,
        )


def rows_at(ref, start, count):
    return ref.at[:, pl.ds(start, count), :]


def first_cut(wires, share_ref, got_ref):
    at = place()
    quarter = share_ref.shape[1] // 4
    return [
        wires.copy(rows_at(share_ref, (1 - at["x"]) * quarter, quarter), got_ref.at[0], peer("x")),
        wires.copy(
            rows_at(share_ref, (3 - at["y"]) * quarter, quarter), got_ref.at[1], peer("y")
        ),
    ]


def own_quarters(share_ref, own_ref, sems):
    at = place()
    quarter = share_ref.shape[1] // 4
    starts = (at["x"] * quarter, (2 + at["y"]) * quarter)
    return [
        pltpu.make_async_copy(rows_at(share_ref, start, quarter), own_ref.at[n], sems[n])
        for n, start in enumerate(starts)
    ]


def first_add(own_ref, got_ref, sum_ref):
    for n in range(2):
        sum_ref[n] = (own_ref[n].astype(F32) + got_ref[n].astype(F32)).astype(BF)


def first_add_whole(share_ref, got_ref, sum_ref):
    at = place()
    quarter = share_ref.shape[1] // 4
    for n, start in enumerate((at["x"] * quarter, (2 + at["y"]) * quarter)):
        own = share_ref[:, pl.ds(pl.multiple_of(start, 16), quarter), :]
        sum_ref[n] = (own.astype(F32) + got_ref[n].astype(F32)).astype(BF)


def second_cut(wires, sum_ref, got_ref):
    at = place()
    eighth = sum_ref.shape[2] // 2
    return [
        wires.copy(
            rows_at(sum_ref.at[0], (1 - at["y"]) * eighth, eighth), got_ref.at[0], peer("y")
        ),
        wires.copy(
            rows_at(sum_ref.at[1], (1 - at["x"]) * eighth, eighth), got_ref.at[1], peer("x")
        ),
    ]


def second_add(sum_ref, got_ref, out_ref, base=0):
    at = place()
    eighth = sum_ref.shape[2] // 2
    for n, start in enumerate((at["y"] * eighth, at["x"] * eighth)):
        own = sum_ref[n, :, pl.ds(pl.multiple_of(start, 16), eighth), :]
        out_ref[:, pl.ds(base + n * eighth, eighth), :] = (
            own.astype(F32) + got_ref[n].astype(F32)
        ).astype(BF)


def z_send(wires, part_ref, got_ref):
    at = place()
    return [
        wires.copy(
            part_ref.at[lax.rem(at["z"] + shift, 4)], got_ref.at[shift - 1], peer("z", shift)
        )
        for shift in (1, 2, 3)
    ]


def z_add(own, got_ref):
    total = own.astype(F32)
    for n in range(3):
        total = total + got_ref[n].astype(F32)
    return total.astype(BF)


class Share:
    def __init__(self, wires, packed, own, refs, loads=()):
        self.packed, self.own, self.loads = packed, own, list(loads)
        self.got, self.sum, self.got2, self.part, self.gotz = refs
        self.copies = first_cut(wires, packed, self.got)
        self.copies2 = second_cut(wires, self.sum, self.got2)
        self.copiesz = z_send(wires, self.part, self.gotz)

    def start(self):
        start_all(self.loads + self.copies)

    def cut(self):
        wait_all(self.loads + self.copies)
        if self.own is None:
            first_add_whole(self.packed, self.got, self.sum)
        else:
            first_add(self.own, self.got, self.sum)
        start_all(self.copies2)

    def spread(self):
        wait_all(self.copies2)
        second_add(self.sum, self.got2, self.part)
        start_all(self.copiesz)

    def total(self):
        wait_all(self.copiesz)
        return z_add(self.part[place()["z"]], self.gotz)


def start_all(copies):
    for copy in copies:
        copy.start()
    return copies


def wait_all(copies):
    for copy in copies:
        copy.wait()


def sent_row(sent_ref, scr):
    spaces = sent_ref.shape[0]
    scr[...] = jnp.zeros_like(scr)
    scr[pl.ds(0, spaces), pl.ds(0, CAP)] = sent_ref[...].astype(F32)
    row = scr[0:1, :]
    for d in range(1, spaces):
        row = row + pltpu.roll(scr[d : d + 1, :], d * CAP, 1)
    return row


def pick_matrix(row, nodes):
    places = lax.broadcasted_iota(jnp.int32, (nodes, row.shape[1]), 0).astype(F32)
    return (places == row).astype(BF)


def prepare_kernel(
    ns_ref, nv_ref, sent_ref, vn_ref, we_ref, vout_ref, norms_ref, wnode_hbm,
    b_ref, p_ref, q_ref, ts_ref, tv_ref, vs_ref, vt_ref, vo_ref, mix_ref, wn_ref, pt_ref,
    wnode, row_scr, vt_scr, out_scr, in_scr, send_sem, recv_sem, load_sem,
):
    nodes = ns_ref.shape[0]
    table = ts_ref.shape[0]
    spaces = lax.axis_size("space")
    me = lax.axis_index("space")
    wires = Wires(send_sem, recv_sem)
    ring = [peer("group", shift) for shift in range(1, spaces)]
    load = pltpu.make_async_copy(wnode_hbm, wnode, load_sem)
    load.start()
    pick = pick_matrix(sent_row(sent_ref, row_scr), nodes)
    rows = lead_product(pick, ns_ref[...]).astype(BF)
    for d in range(spaces):
        out_scr[d, :, pl.ds(0, D_S)] = rows[d * CAP : (d + 1) * CAP]
    for c in range(3):
        rows = lead_product(pick, nv_ref[c]).astype(BF)
        for d in range(spaces):
            out_scr[d, :, pl.ds(D_S + c * D_V, D_V)] = rows[d * CAP : (d + 1) * CAP]
    greet(ring)
    copies = start_all(
        [
            wires.copy(out_scr.at[lax.rem(me + n + 1, spaces)], in_scr.at[me], ring[n])
            for n in range(spaces - 1)
        ]
    )
    in_scr[me] = out_scr[me]
    vs_ref[pl.ds(0, 512), :] = vn_ref[pl.ds(0, 512), :]
    vt_scr[...] = jnp.zeros_like(vt_scr)
    vt_scr[pl.ds(0, H_V + 1), :] = vn_ref[pl.ds(512, H_V + 1), :].astype(F32)
    row = lax.broadcasted_iota(jnp.int32, (H_P, D_V), 0)
    vt_ref[...] = jnp.where(row < H_V, pltpu.roll(vt_scr[...], H_P - 1, 0), 0.0).astype(BF)
    low = row[: H_P - 512]
    first = jnp.broadcast_to(vt_scr[0:1, :], low.shape)
    vs_ref[pl.ds(512, H_P - 512), :] = jnp.where(low == 0, first, 0.0).astype(BF)
    vo_ref[pl.ds(0, 512), :] = vout_ref[pl.ds(0, 512), :]
    first = jnp.broadcast_to(vout_ref[pl.ds(512, 1), :].astype(F32), low.shape)
    vo_ref[pl.ds(512, H_P - 512), :] = jnp.where(low == 0, first, 0.0).astype(BF)

    def project(parts, start):
        last = None
        for c in range(3):
            whole = product_back(parts[c], vs_ref[...])
            p_ref[c, pl.ds(start, parts[c].shape[0]), :] = whole.astype(BF)
            tail = whole[:, 512:]
            last = tail if last is None else last + pltpu.roll(tail, c, 1)
        pt_ref[pl.ds(start, parts[0].shape[0]), :] = last.astype(BF)

    project([nv_ref[c] for c in range(3)], 0)
    for c in range(3):
        q_ref[c] = product_back(nv_ref[c], vt_ref[...])
        tv_ref[c, pl.ds(0, nodes), :] = nv_ref[c]
    ts_ref[pl.ds(0, nodes), :] = ns_ref[...]
    first = jnp.broadcast_to(norms_ref[pl.ds(512, 1), :].astype(F32), (16, D_S))
    row = lax.broadcasted_iota(jnp.int32, (16, D_S), 0)
    wn_ref[pl.ds(0, 512), :] = norms_ref[pl.ds(0, 512), :]
    wn_ref[pl.ds(512, 16), :] = jnp.where(row == 0, first, 0.0).astype(BF)
    wn_ref[pl.ds(528, D_E), :] = we_ref[...]
    wn_ref[pl.ds(528 + D_E, H_P - 528 - D_E), :] = jnp.zeros((H_P - 528 - D_E, D_S), BF)
    mix_ref[pl.ds(table, H_P), :] = wn_ref[...]
    load.wait()
    b_ref[...] = product(ns_ref[...], wnode[:, pl.ds(D_S, D_S)])
    mix_ref[pl.ds(0, nodes), :] = product(ns_ref[...], wnode[:, pl.ds(0, D_S)]).astype(BF)
    wait_all(copies)
    got = in_scr[...].reshape(spaces * CAP, D_S + 3 * D_V)
    ts_ref[pl.ds(nodes, table - nodes), :] = got[:, :D_S]
    mix_ref[pl.ds(nodes, table - nodes), :] = product(
        got[:, :D_S], wnode[:, pl.ds(0, D_S)]
    ).astype(BF)
    parts = [got[:, D_S + c * D_V : D_S + (c + 1) * D_V] for c in range(3)]
    project(parts, nodes)
    for c in range(3):
        tv_ref[c, pl.ds(nodes, table - nodes), :] = parts[c]


def middle_kernel(
    ns_ref, nv_ref, as_ref, av_ref, gains_in, fv_ref, fs_ref, fu_ref, we_ref, wq_ref, id_ref, cot_ref, wo_hbm, wu_hbm, wd_hbm, ts_hbm, ns_hbm,
    out_ref, gsone_ref, gvone_ref, gains_ref, a_ref, m_ref, e_ref, tso_hbm, nso_hbm,
    s1, v1, ffh, ffp, ffu, v2, sz, fac_node, fac_node_o, heads_out, heads_in,
    probs, att, att_out, att_in, wo_ref, wu_ref, wd_ref, gatt, gatt_in, gs1, fgain,
    fac_feed, fac_feed_o, gs_scr, ghead, ghead_in, fac_back, fac_back_o,
    first, first_got, first_sum, first_got2, tall_scr, low_scr,
    send_sem, recv_sem, load_sem,
):
    spaces = lax.axis_size("space")
    quads = spaces // 2
    me = lax.axis_index("space")
    ng_ref = gains_in.at[:, pl.ds(0, D_S)]
    ag_ref = gains_in.at[:, pl.ds(D_S, D_MODEL)]
    fg_ref = gains_in.at[:, pl.ds(D_S + D_MODEL, D_MODEL)]
    wires = Wires(send_sem, recv_sem)
    ring = [peer("group", shift) for shift in range(1, spaces)]

    def exchange(source, target, start=0, count=None):
        rows = pl.ds(start, source.shape[1] if count is None else count)
        return [
            wires.copy(source.at[lax.rem(me + n + 1, spaces), rows], target.at[me, rows], ring[n])
            for n in range(spaces - 1)
        ]

    def keep(source, target):
        target[me] = source[me]

    loads = [
        pltpu.make_async_copy(source, target, load_sem.at[n])
        for n, (source, target) in enumerate(
            ((wo_hbm, wo_ref), (wu_hbm, wu_ref), (wd_hbm, wd_ref))
        )
    ]
    start_all(loads)
    greet(ring + [peer("x"), peer("y")])
    swaps = start_all(
        [wires.copy(ts_hbm, tso_hbm, peer("core")), wires.copy(ns_hbm, nso_hbm, peer("core"))]
    )
    nodes = ns_ref.shape[0]
    key_copies = exchange(heads_out, heads_in, 0, nodes)
    value_copies = exchange(heads_out, heads_in, nodes, nodes // 2)
    grad_key_copies = exchange(ghead, ghead_in, 0, nodes)
    grad_value_copies = exchange(ghead, ghead_in, nodes, nodes // 2)
    start_later = lambda copies: functools.partial(start_all, copies)
    node_forward_kernel(
        ns_ref, nv_ref, as_ref, av_ref, ng_ref, fv_ref, fs_ref, fu_ref, we_ref, ag_ref, wq_ref,
        s1, v1, ffh, ffp, ffu, v2, sz, fac_node, heads_out, start_later(key_copies),
    )
    start_all(value_copies)
    swaps += start_all([wires.copy(fac_node, fac_node_o, peer("core"))])
    keep(heads_out, heads_in)
    wait_all(key_copies)
    attend_kernel(heads_in, id_ref, probs, att, att_out, functools.partial(wait_all, value_copies))
    copies = start_all(exchange(att_out, att_in))
    keep(att_out, att_in)
    wait_all(loads)
    wait_all(copies)
    up_cols, rest_cols = pl.ds(0, AT_ATT), pl.ds(AT_ATT, FAC_FEED - AT_ATT)
    feed_swap = wires.copy(fac_feed.at[:, up_cols], fac_feed_o.at[:, up_cols], peer("core"))
    feed_kernel(
        att_in, sz, wo_ref, fg_ref, wu_ref, wd_ref, cot_ref, out_ref, gatt, gs1, fgain, fac_feed,
        feed_swap.start,
    )
    copies = start_all(exchange(gatt, gatt_in))
    swaps += start_all(
        [wires.copy(fac_feed.at[:, rest_cols], fac_feed_o.at[:, rest_cols], peer("core"))]
    )
    keep(gatt, gatt_in)
    feed_swap.wait()
    feed_grads_kernel(fac_feed, fac_feed_o, first)
    cuts = start_all(first_cut(wires, first, first_got))
    wait_all(copies)
    attend_backward_kernel(
        heads_in, probs, att, gatt_in, ghead, gs_scr, start_later(grad_value_copies)
    )
    copies = start_all(grad_key_copies) + grad_value_copies
    keep(ghead, ghead_in)
    wait_all(cuts)
    first_add_whole(first, first_got, first_sum)
    cuts = start_all(second_cut(wires, first_sum, first_got2))
    wait_all(copies)
    qkv_cols, other_cols = pl.ds(0, AT_STREAM), pl.ds(AT_STREAM, FAC_BACK - AT_STREAM)
    qkv_swap = wires.copy(fac_back.at[:, qkv_cols], fac_back_o.at[:, qkv_cols], peer("core"))

    node_backward_kernel(
        ghead_in, gs1, s1, v1, ffh, ffp, ffu, v2, sz,
        ng_ref, fv_ref, fs_ref, fu_ref, we_ref, ag_ref, wq_ref, fgain,
        gsone_ref, gvone_ref, gains_ref, fac_back, qkv_swap.start,
    )
    swap = start_all(
        [wires.copy(fac_back.at[:, other_cols], fac_back_o.at[:, other_cols], peer("core"))]
    )
    qkv_swap.wait()
    wait_all(swaps)
    attention_grads(fac_node, fac_node_o, fac_back, fac_back_o, fac_feed, fac_feed_o, a_ref)
    wait_all(cuts)
    second_add(first_sum, first_got2, e_ref)
    wait_all(swap)
    node_grads(fac_node, fac_node_o, fac_back, fac_back_o, m_ref, tall_scr, low_scr)


def middle(vmem_operands, hbm_operands, table_s, node_scalar, quads):
    nodes = node_scalar.shape[0]
    spaces = 2 * quads
    count = spaces * nodes
    hbm = pl.BlockSpec(memory_space=pl.ANY)
    vmem = pl.BlockSpec(memory_space=pltpu.VMEM)
    operands = tuple(vmem_operands) + tuple(hbm_operands) + (table_s, node_scalar)
    bits = lambda *shape: pltpu.VMEM(shape, BF)
    wide = lambda *shape: pltpu.VMEM(shape, F32)
    packed = (spaces, nodes + nodes // 2, 128)
    small = (spaces, nodes // 2, 128)
    outs = [
        ((nodes, D_MODEL), BF),
        ((nodes, D_S), F32),
        ((3, nodes, D_V), F32),
        ((8, D_S), F32),
        ((quads, ROWS_A, 512), BF),
        ((quads, ROWS_N, 512), BF),
        ((quads, ROWS_E, 512), BF),
        (table_s.shape, BF),
        (node_scalar.shape, BF),
    ]
    wires = 6 * (spaces - 1) + 12
    return pl.pallas_call(
        middle_kernel,
        out_shape=[jax.ShapeDtypeStruct(shape, kind) for shape, kind in outs],
        in_specs=[vmem] * len(vmem_operands) + [hbm] * (len(hbm_operands) + 2),
        out_specs=[vmem] * 7 + [hbm] * 2,
        scratch_shapes=[
            wide(nodes, D_S), wide(3, nodes, D_V), wide(3, nodes, D_V), wide(nodes, D_S),
            wide(3, nodes, D_V), wide(3, nodes, D_V), wide(nodes, D_MODEL),
            bits(nodes, FAC_NODE), bits(nodes, FAC_NODE), bits(*packed), bits(*packed),
            bits(count, count), wide(count, 128), bits(*small), bits(*small),
        ]
        + [bits(*one.shape) for one in hbm_operands]
        + [
            bits(*small), bits(*small), wide(nodes, D_MODEL), wide(1, D_MODEL),
            bits(nodes, FAC_FEED), bits(nodes, FAC_FEED), bits(count, count),
            bits(*packed), bits(*packed), bits(nodes, FAC_BACK), bits(nodes, FAC_BACK),
            bits(quads, ROWS_F, 512), bits(2, quads, ROWS_F // 4, 512),
            bits(2, quads, ROWS_F // 4, 512), bits(2, quads, ROWS_F // 8, 512),
            bits(D_S + D_V, 512), bits(D_V, 512),
            pltpu.SemaphoreType.DMA((wires,)),
            pltpu.SemaphoreType.DMA((wires,)),
            pltpu.SemaphoreType.DMA((len(hbm_operands),)),
        ],
        compiler_params=pltpu.CompilerParams(
            collective_id=0, has_side_effects=True, vmem_limit_bytes=VMEM_LIMIT
        ),
        name="middle",
    )(*operands)


def slot_rows(rows_scr, first_slot, nodes):
    return jnp.concatenate([rows_scr[pl.ds(first_slot + k, 1), :] for k in range(GROUP)], 1)


def one_hot_rows(rows_scr, first_slot, table, nodes):
    row = slot_rows(rows_scr, first_slot, nodes)
    return (lax.broadcasted_iota(jnp.int32, (table, row.shape[1]), 0).astype(F32) == row).astype(BF)


def keep_rows(ref, rows_scr):
    rows_scr[pl.ds(0, ref.shape[0]), :] = ref[...].astype(F32)


def backward_kernel(
    near_ref, ev_ref, lx_ref, ds_ref, h_ref, z_ref, gsone_ref, wn_ref, gvone_ref, vo_ref, tv_ref,
    nv_ref, vs_ref, vt_ref, gains_ref,
    ts_hbm, ns_hbm, wnode_hbm, tso_hbm, nso_hbm, e_hbm, a_hbm, n_hbm,
    gscal_ref, gvec_ref, plane_hbm, got_hbm,
    near_scr, ev_scr, ga_ref, gw_ref, gb_ref, pre_scr, gp_ref, gq_ref, gvo_ref, up_scr,
    gh_scr, ts_ref, ns_ref, wnode_ref, tso_ref, nso_ref,
    grads_scr, grads_got, mix_scr, mix_got, rest_scr, rest_got, e_own, e_got, a_own, n_own,
    s_scr, b_scr, v_got, backs_scr, backv_scr, fin_scr,
    send_sem, recv_sem, load_sem, *share_refs,
):
    nodes = gsone_ref.shape[0]
    table = ts_ref.shape[0]
    rows = GROUP * nodes
    spaces = lax.axis_size("space")
    quads = spaces // 2
    step = pl.program_id(0)
    half = NEIGH // GROUP
    last = 2 * half - 1
    first_slot = lax.rem(step, half) * GROUP
    at = place()
    core = at["core"]
    me = lax.axis_index("space")
    mine = 2 * at["x"] + at["y"]
    ring = [peer("group", shift) for shift in range(1, spaces)]
    plane = [peer("x"), peer("y"), peer("diagonal")]

    wires = Wires(send_sem, recv_sem)
    own_copy = lambda n, source, target: pltpu.make_async_copy(source, target, load_sem.at[n])
    quarters = lambda share_ref, own_ref, n: own_quarters(
        share_ref, own_ref, [load_sem.at[n], load_sem.at[n + 1]]
    )
    refs = [share_refs[n : n + 5] for n in range(0, len(share_refs), 5)]
    e_copiesz = z_send(wires, e_hbm, e_got)
    share_a = Share(wires, a_hbm, a_own, refs[0], quarters(a_hbm, a_own, 9))
    share_n = Share(wires, n_hbm, n_own, refs[1], quarters(n_hbm, n_own, 11))
    share_s = Share(wires, s_scr, None, refs[2])
    share_b = Share(wires, b_scr, None, refs[3])
    v_scr = s_scr.at[:, pl.ds(0, ROWS_V), :]
    share_v = Share(wires, v_scr, None, refs[4])
    pair_copies = [
        wires.copy(source, target, peer("core"))
        for source, target in ((grads_scr, grads_got), (mix_scr, mix_got), (rest_scr, rest_got))
    ]
    v_pair = n_own
    v_copies = [wires.copy(v_pair.at[1 - core], v_got, peer("core"))]
    bounds = [0]
    for count in ALL_ROWS:
        bounds.append(bounds[-1] + count // 4)
    rows_e, rows_a, rows_n, rows_s, rows_b, rows_v = [
        pl.ds(lo, hi - lo) for lo, hi in zip(bounds, bounds[1:])
    ]
    batches = [(bounds[0], bounds[3]), (bounds[3], bounds[4]), (bounds[4], bounds[5])]
    rounds = [
        [
            wires.copy(fin_scr.at[pl.ds(lo, hi - lo), :], plane_hbm.at[mine, pl.ds(lo, hi - lo), :], to)
            for to in plane[:2]
        ]
        for lo, hi in batches
    ]
    relays = []
    over_x, over_y = 2 * (1 - at["x"]) + at["y"], 2 * at["x"] + 1 - at["y"]
    for lo, hi in batches:
        middle_row = (lo + hi) // 2
        upper, lower = pl.ds(lo, middle_row - lo), pl.ds(middle_row, hi - middle_row)
        relays.append(
            [
                wires.copy(plane_hbm.at[over_x, upper, :], plane_hbm.at[over_x, upper, :], plane[1]),
                wires.copy(plane_hbm.at[over_y, lower, :], plane_hbm.at[over_y, lower, :], plane[0]),
            ]
        )
    last_round = [
        wires.copy(fin_scr.at[rows_v, :], plane_hbm.at[mine, rows_v, :], to) for to in plane
    ]
    back_scalar, back_vector = pl.ds(0, D_S), pl.ds(D_S, 3 * D_V)
    scalar_copies = [
        wires.copy(
            backs_scr.at[lax.rem(me + n + 1, spaces)], got_hbm.at[me, :, back_scalar], ring[n]
        )
        for n in range(spaces - 1)
    ]
    vector_copies = [
        wires.copy(
            backv_scr.at[lax.rem(me + n + 1, spaces)], got_hbm.at[me, :, back_vector], ring[n]
        )
        for n in range(spaces - 1)
    ]
    e_load = own_copy(0, e_hbm.at[at["z"]], e_own)
    loads = [
        own_copy(1 + n, source, target)
        for n, (source, target) in enumerate(
            (
                (ts_hbm, ts_ref), (ns_hbm, ns_ref), (wnode_hbm.at[:, pl.ds(0, D_S)], wnode_ref),
                (tso_hbm, tso_ref),
                (nso_hbm, nso_ref),
            )
        )
    ]
    own_scalar = own_copy(6, backs_scr.at[me], got_hbm.at[me, :, back_scalar])
    own_vector = own_copy(7, backv_scr.at[me], got_hbm.at[me, :, back_vector])
    own_plane = own_copy(8, fin_scr, plane_hbm.at[mine])
    target_load = own_copy(13, wnode_hbm.at[:, pl.ds(D_S, D_S)], wnode_ref)

    def early_total():
        e_load.wait()
        wait_all(e_copiesz)
        fin_scr[rows_e, :] = z_add(e_own[...], e_got)

    def middle_total():
        fin_scr[rows_a, :] = share_a.total()
        fin_scr[rows_n, :] = share_n.total()
        start_all(rounds[0])

    def source_total():
        fin_scr[rows_s, :] = share_s.total()
        start_all(rounds[1])

    def relay(n):
        wait_all(rounds[n])
        start_all(relays[n])

    schedule = {
        (4, 0): [share_a.cut],
        (7, 0): [share_a.spread],
        (7, 1): [share_n.spread],
        (9, 0): [share_s.cut],
        (9, 1): [early_total],
        (10, 0): [share_b.cut],
        (10, 1): [share_s.spread, middle_total],
        (11, 1): [share_b.spread, source_total],
    }

    def carry_on(part):
        for (at_step, at_part), actions in schedule.items():
            if at_part == part:

                @pl.when(step == at_step)
                def _():
                    for action in actions:
                        action()

    @pl.when(step == 0)
    def _():
        greet(ring + plane)
        share_a.start()
        share_n.start()
        start_all(e_copiesz)
        start_all([e_load] + loads)
        keep_rows(near_ref, near_scr)
        for c in range(3):
            keep_rows(ev_ref.at[c], ev_scr.at[c])
        for ref in (ga_ref, gw_ref, gb_ref, gp_ref, gq_ref, gvo_ref):
            ref[...] = jnp.zeros_like(ref)

    carry_on(0)

    @pl.when(step < half)
    def _():
        for start in range(0, D_S, 256):
            cols = pl.ds(start, 256)
            for first in range(0, nodes, ROW_TILE):
                part = pl.ds(first, ROW_TILE)
                share = gsone_ref[part, cols] * (1.0 / NEIGH)
                acc = None
                for k in range(GROUP):
                    g = (ds_ref[k, part, cols].astype(F32) * share).astype(BF)
                    pre_scr[step, pl.ds(k * nodes + first, ROW_TILE), cols] = g
                    g = g.astype(F32)
                    acc = g if acc is None else acc + g
                gb_ref[part, cols] += acc
        one_hot = one_hot_rows(near_scr, first_slot, table, nodes)
        grad_pre = pre_scr[step]
        ga_ref[...] += product(one_hot, grad_pre)
        lx = lx_ref[...].reshape(rows, H_P)
        gw_ref[...] += lead_product(lx, grad_pre)
    @pl.when(step == half - 1)
    def _():
        grads_scr[pl.ds(0, table), :] = ga_ref[...].astype(BF)
        grads_scr[pl.ds(table, nodes), :] = gb_ref[...].astype(BF)
        for z in range(quads):
            away = pl.ds(pl.multiple_of((2 * z + 1 - core) * 128, 128), 128)
            for r in range(4):
                mix_scr[z, :, pl.ds(r * 128, 128)] = gw_ref[pl.ds(r * 128, 128), away].astype(BF)
            rest_scr[z] = gw_ref[pl.ds(512, 64), away].astype(BF)
        start_all(pair_copies)
        wait_all(loads)
        ga = grads_scr[pl.ds(0, table), :]
        projected = product_back(ga, wnode_ref[...])
        target_load.start()
        gscal_ref[...] = gsone_ref[...] + projected[:nodes]
        for d in range(spaces):
            backs_scr[d] = projected[nodes + d * CAP : nodes + (d + 1) * CAP].astype(BF)
        start_all(scalar_copies)
        own_scalar.start()

    @pl.when(step == half)
    def _():
        share_n.cut()

    @pl.when(step == half + 1)
    def _():
        wait_all(pair_copies)
        grad_rows = pl.ds(0, table), pl.ds(table, nodes)
        for side, (left, lefto, pack) in enumerate(
            ((ts_ref, tso_ref, s_scr), (ns_ref, nso_ref, b_scr))
        ):
            right, righto = grads_scr[grad_rows[side], :], grads_got[grad_rows[side], :]
            for z in range(quads):
                own = pl.ds(pl.multiple_of((2 * z + core) * 128, 128), 128)
                block = lead_product(left[:, own], right) + lead_product(lefto[:, own], righto)
                block = block.astype(BF)
                for n in range(2):
                    pack[z, pl.ds(n * 128, 128), :] = block[:, n * 512 : (n + 1) * 512]
            if side == 0:
                share_s.start()
        for z in range(quads):
            own = pl.ds(pl.multiple_of((2 * z + core) * 128, 128), 128)
            for r in range(4):
                lanes = pl.ds(r * 128, 128)
                b_scr[z, pl.ds(256, 128), lanes] = (
                    gw_ref[pl.ds(r * 128, 128), own] + mix_got[z, :, lanes].astype(F32)
                ).astype(BF)
        share_b.start()
        target_load.wait()
        gscal_ref[...] += product_back(grads_scr[pl.ds(table, nodes), :], wnode_ref[...])

    @pl.when(step >= half)
    def _():
        for first in range(0, nodes, ROW_TILE):
            part = pl.ds(first, ROW_TILE)
            share = [gvone_ref[c, part, :] * (1.0 / NEIGH) for c in range(3)]
            for k in range(GROUP):
                z = [z_ref[k, c, part, :].astype(F32) for c in range(3)]
                power = power_of(z) + 1.0
                inverse = lax.rsqrt(power)
                s = sigmoid(power * inverse)
                dot = z[0] * share[0] + z[1] * share[1] + z[2] * share[2]
                factor = dot * inverse * (s * (1.0 - s))
                for c in range(3):
                    up_scr[c, pl.ds(k * nodes + first, ROW_TILE), :] = (
                        share[c] * s + z[c] * factor
                    ).astype(BF)
        for start, width in LANE_BLOCKS:
            cols = pl.ds(start, width)
            grad_length = product_back(pre_scr[step - half], wn_ref[cols, :])
            grad_direct = [product_back(up_scr[c], vo_ref[cols, :]) for c in range(3)]
            for first in range(0, nodes, ROW_TILE):
                part = pl.ds(first, ROW_TILE)
                acc = [None] * 3
                for k in range(GROUP):
                    row = k * nodes + first
                    ratio = grad_length[row : row + ROW_TILE] * pl.reciprocal(
                        lx_ref[k, part, cols].astype(F32), approx=True
                    )
                    if start == 512:
                        lane = lax.broadcasted_iota(jnp.int32, (ROW_TILE, width), 1)
                        ratio = jnp.where(lane == 0, ratio, 0.0)
                    for c in range(3):
                        g = grad_direct[c][row : row + ROW_TILE] + ratio * h_ref[
                            k, c, part, cols
                        ].astype(F32)
                        gh_scr[c, pl.ds(row, ROW_TILE), cols] = g.astype(BF)
                        acc[c] = g if acc[c] is None else acc[c] + g
                for c in range(3):
                    gq_ref[c, part, cols] += acc[c]
    carry_on(1)

    @pl.when(step >= half)
    def _():
        one_hot = one_hot_rows(near_scr, first_slot, table, nodes)
        for c in range(3):
            evr = jnp.broadcast_to(slot_rows(ev_scr.at[c], first_slot, nodes), (16, rows))
            lead = jnp.concatenate([one_hot, evr.astype(BF)], axis=0)
            gp_ref[c] += product(lead, gh_scr[c])
            gvo_ref[...] += lead_product(up_scr[c], h_ref[:, c, :, :].reshape(rows, H_P))

    @pl.when(step == last)
    def _():
        tall = D_V // spaces
        gp = [gp_ref[c, pl.ds(0, table), :].astype(BF) for c in range(3)]
        gq = [gq_ref[c].astype(BF) for c in range(3)]
        grads = []
        for lead_ref, right in ((tv_ref, gp), (nv_ref, gq)):
            total = None
            for c in range(3):
                one = lead_product(lead_ref[c], right[c])
                total = one if total is None else total + one
            grads.append(total)
        grads.append(gvo_ref[...])
        lane = lax.broadcasted_iota(jnp.int32, (D_V, 128), 1)
        tails = jnp.zeros((D_V, 128), F32)
        for n, grad in enumerate(grads):
            for p in range(spaces):
                v_pair[p % 2, p // 2, pl.ds(n * tall, tall), :] = grad[
                    p * tall : (p + 1) * tall, :512
                ].astype(BF)
            tails = tails + jnp.where(
                lane == n, jnp.broadcast_to(grad[:, 512:513], (D_V, 128)), 0.0
            )
        tails = tails.astype(BF)
        vedge = gp_ref[0, pl.ds(table, 8), :] + gp_ref[1, pl.ds(table, 8), :]
        vedge = vedge + gp_ref[2, pl.ds(table, 8), :]
        row = lax.broadcasted_iota(jnp.int32, (tall, 128), 0)
        below = pl.ds(3 * tall, tall)
        for p in range(spaces):
            own = pl.ds(p * 128, 128)
            rest = gw_ref[pl.ds(512, 64), own] + rest_got[p // 2].astype(F32)
            rest = jnp.where(core == p % 2, rest, 0.0)
            v_pair[p % 2, p // 2, below, pl.ds(0, 128)] = tails[p * tall : (p + 1) * tall]
            v_pair[p % 2, p // 2, below, pl.ds(128, 128)] = rest[16 : 16 + tall].astype(BF)
            extra = jnp.where(row == 0, jnp.broadcast_to(rest[0:1], (tall, 128)), 0.0)
            for n in range(5):
                piece = jnp.broadcast_to(vedge[0:1, n * 128 : (n + 1) * 128], (tall, 128))
                extra = jnp.where(row == 1 + n, piece, extra)
            for n in range(2):
                piece = jnp.broadcast_to(
                    gains_ref[n : n + 1, p * 128 : (p + 1) * 128], (tall, 128)
                )
                extra = jnp.where(row == 6 + n, piece, extra)
            v_pair[p % 2, p // 2, below, pl.ds(256, 128)] = extra.astype(BF)
            v_pair[p % 2, p // 2, below, pl.ds(384, 128)] = jnp.zeros((tall, 128), BF)
        start_all(v_copies)
        for c in range(3):
            projected = product(gp[c], vs_ref[...])
            gvec_ref[c] = gvone_ref[c] + product(gq[c], vt_ref[...]) + projected[:nodes]
            for d in range(spaces):
                backv_scr[d, :, pl.ds(c * D_V, D_V)] = projected[
                    nodes + d * CAP : nodes + (d + 1) * CAP
                ].astype(BF)
        relay(0)
        start_all(vector_copies)
        own_vector.start()
        wait_all(v_copies)
        v_scr[...] = (v_pair[core].astype(F32) + v_got[...].astype(F32)).astype(BF)
        share_v.start()
        share_v.cut()
        fin_scr[rows_b, :] = share_b.total()
        start_all(rounds[2])
        share_v.spread()
        relay(1)
        relay(2)
        fin_scr[rows_v, :] = share_v.total()
        start_all(last_round)
        own_plane.start()
        for copies in relays:
            wait_all(copies)
        wait_all(scalar_copies)
        wait_all(vector_copies)
        own_scalar.wait()
        own_vector.wait()
        own_plane.wait()
        wait_all(last_round)


def backward(blocked, whole_operands, hbm_operands):
    near, ev, lx, dsilu, hidden, update = blocked
    ts, ns, w_node = hbm_operands[:3]
    nodes = ns.shape[0]
    table = ts.shape[0]
    quads = hbm_operands[-1].shape[0]
    spaces = 2 * quads
    rows = GROUP * nodes
    half = NEIGH // GROUP
    once = pl.Buffered(1)
    whole = lambda shape: pl.BlockSpec(shape, lambda g: (0,) * len(shape), pipeline_mode=once)
    early = lambda *shape: pl.BlockSpec(
        (GROUP,) + shape, lambda g: (jnp.minimum(g, half - 1),) + (0,) * len(shape)
    )
    late = lambda *shape: pl.BlockSpec(
        (GROUP,) + shape, lambda g: (jnp.maximum(g - half, 0),) + (0,) * len(shape)
    )
    both = lambda *shape: pl.BlockSpec(
        (GROUP,) + shape, lambda g: (lax.rem(g, half),) + (0,) * len(shape)
    )
    hbm = pl.BlockSpec(memory_space=pl.ANY)
    outs = [
        ((nodes, D_S), F32),
        ((3, nodes, D_V), F32),
        ((4, sum(ALL_ROWS) // 4, 512), BF),
        ((spaces, CAP, D_S + 3 * D_V), BF),
    ]
    bits = lambda *shape: pltpu.VMEM(shape, BF)
    wide = lambda *shape: pltpu.VMEM(shape, F32)
    grads = (table + nodes, D_S)
    pieces = lambda count: [
        bits(2, quads, count // 4, 512), bits(2, quads, count // 4, 512),
        bits(2, quads, count // 8, 512), bits(quads, count // 4, 512), bits(3, count // 4, 512),
    ]
    wires = 57 + 2 * (spaces - 1)
    return pl.pallas_call(
        backward_kernel,
        grid=(2 * half,),
        in_specs=[
            whole(near.shape),
            whole(ev.shape),
            both(nodes, H_P),
            early(nodes, D_S),
            late(3, nodes, H_P),
            late(3, nodes, D_V),
        ]
        + [whole(one.shape) for one in whole_operands]
        + [hbm] * len(hbm_operands),
        out_specs=[whole(outs[0][0]), whole(outs[1][0]), hbm, hbm],
        out_shape=[jax.ShapeDtypeStruct(shape, kind) for shape, kind in outs],
        scratch_shapes=[
            wide(32, 128), wide(3, 32, 128),
            wide(table, D_S), wide(H_P, D_S), wide(nodes, D_S), bits(half, rows, D_S),
            wide(3, table + 16, H_P), wide(3, nodes, H_P), wide(D_V, H_P), bits(3, rows, D_V),
            bits(3, rows, H_P),
        ]
        + [
            bits(*(one.shape if one is not w_node else (D_S, D_S))) for one in hbm_operands[:5]
        ]
        + [
            bits(*grads), bits(*grads), bits(quads, 128, 512), bits(quads, 128, 512),
            bits(quads, 64, 128), bits(quads, 64, 128), bits(ROWS_E, 512), bits(3, ROWS_E, 512),
            bits(2, quads, ROWS_A // 4, 512), bits(2, quads, ROWS_N // 4, 512),
            bits(quads, ROWS_S, 512), bits(quads, ROWS_B, 512),
            bits(quads, ROWS_V, 512),
            bits(spaces, CAP, D_S), bits(spaces, CAP, 3 * D_V), bits(sum(ALL_ROWS) // 4, 512),
            pltpu.SemaphoreType.DMA((wires,)),
            pltpu.SemaphoreType.DMA((wires,)),
            pltpu.SemaphoreType.DMA((14,)),
        ]
        + sum([pieces(count) for count in ALL_ROWS[1:]], []),
        compiler_params=pltpu.CompilerParams(
            collective_id=1, has_side_effects=True, vmem_limit_bytes=BACKWARD_LIMIT
        ),
        name="backward",
    )(*blocked, *whole_operands, *hbm_operands)


def finish_kernel(
    plane_ref, got_ref, sent_ref, gscal_ref, gvec_ref, stream_ref,
    gs_ref, gv_ref, node_ref, edge_ref, norms_ref, vnode_ref, vedge_ref, vout_ref, ffv_ref, ffs_ref,
    ffu_ref, embed_ref, qkv_ref, out_ref, up_ref, down_ref, ngain_ref, again_ref, fgain_ref,
    stream_out_ref, row_scr, sent_scr,
):
    base = 0
    for rows in ALL_ROWS:
        eighth = rows // 8
        for half, order in enumerate(((0, 1, 2, 3), (0, 2, 1, 3))):
            for n, q in enumerate(order):
                row_scr[pl.ds(4 * base + (4 * half + n) * eighth, eighth), :] = plane_ref[
                    q, pl.ds(base + half * eighth, eighth), :
                ]
        base += rows // 4

    def take(start, rows, lane=0, width=512):
        return row_scr[pl.ds(start, rows), pl.ds(lane, width)].astype(F32)

    at = 0
    down_ref[...] = take(at, 256)
    for n in range(4):
        up_ref[:, pl.ds(n * 512, 512)] = take(at + 256 + n * 64, 64)
    at += ROWS_F
    for n in range(3):
        qkv_ref[:, pl.ds(n * 512, 512)] = take(at + n * 64, 64)
    out_ref[...] = take(at + 192, 64)
    at += ROWS_A
    embed_ref[...] = take(at, 160)
    for n in range(2):
        ffs_ref[:, pl.ds(n * 512, 512)] = take(at + 160 + n * 160, 160)
    ffv_ref[...] = take(at + 480, 32, 0, 256)
    ffu_ref[...] = take(at + 480, 32, 256, 256)
    at += ROWS_N
    for n in range(4):
        node_ref[:, pl.ds(n * 512, 512)] = take(at + n * 128, 128)
        norms_ref[pl.ds(n * 128, 128), :] = take(at + 512, 128, n * 128, 128)
    at += ROWS_S + ROWS_B
    tails = take(at + 96, 32, 0, 128)
    edge_ref[...] = take(at + 96, 32, 128, 128)
    extra = take(at + 96, 32, 256, 128)
    norms_ref[pl.ds(512, 1), :] = extra[0:1]
    for n in range(5):
        width = min(128, H_V - n * 128)
        vedge_ref[:, pl.ds(n * 128, width)] = extra[1 + n : 2 + n, :width]
    ngain_ref[...] = extra[6]
    again_ref[...] = extra[7, :64]
    fgain_ref[...] = extra[7, 64:]
    vnode_ref[:, pl.ds(0, 512)] = take(at, 32)
    wide = jnp.concatenate([take(at + 32, 32), jnp.zeros((32, 128), F32)], 1)
    lane = lax.broadcasted_iota(jnp.int32, (32, 640), 1)
    wide = pltpu.roll(wide, 1, 1)
    wide = jnp.where(lane == 0, tails[:, 0:1], wide)
    wide = jnp.where(lane == 513, tails[:, 1:2], wide)
    vnode_ref[:, pl.ds(512, 514)] = wide[:, :514]
    vout_ref[:, pl.ds(0, 512)] = take(at + 64, 32)
    vout_ref[:, pl.ds(512, 1)] = tails[:, 2:3]
    stream_out_ref[...] = stream_ref[...]
    nodes = gscal_ref.shape[0]
    slots = got_ref.shape[0] * got_ref.shape[1]
    got = got_ref[...].reshape(slots, D_S + 3 * D_V)
    pick = pick_matrix(sent_row(sent_ref, sent_scr), nodes)
    added = product(pick, got)
    gs_ref[...] = (gscal_ref[...] + added[:, :D_S]).astype(BF)
    for c in range(3):
        gv_ref[c] = (
            gvec_ref[c] + added[:, D_S + c * D_V : D_S + (c + 1) * D_V]
        ).astype(BF)


def finish(plane, got, sent, gscal, gvec, stream):
    nodes = gscal.shape[0]
    outs = [
        ((nodes, D_S), BF),
        ((3, nodes, D_V), BF),
        ((128, 2048), F32),
        ((32, 128), F32),
        ((513, 128), F32),
        ((32, 1026), F32),
        ((1, 513), F32),
        ((32, 513), F32),
        ((32, 256), F32),
        ((160, 1024), F32),
        ((32, 256), F32),
        ((160, 512), F32),
        ((64, 1536), F32),
        ((64, 512), F32),
        ((64, 2048), F32),
        ((256, 512), F32),
        ((128,), F32),
        ((64,), F32),
        ((64,), F32),
        (stream.shape, BF),
    ]
    return pl.pallas_call(
        finish_kernel,
        out_shape=[jax.ShapeDtypeStruct(shape, kind) for shape, kind in outs],
        scratch_shapes=[
            pltpu.VMEM((sum(ALL_ROWS), 512), BF),
            pltpu.VMEM((8, 128), F32),
        ],
        compiler_params=pltpu.CompilerParams(vmem_limit_bytes=VMEM_LIMIT),
        name="finish",
    )(plane, got, sent, gscal, gvec, stream)


def pad_to(values, size, axis):
    pads = [(0, 0)] * values.ndim
    pads[axis] = (0, size - values.shape[axis])
    return jnp.pad(values, pads)


def fold(blocks, width=512):
    shards, rows, columns = blocks.shape
    parts = columns // width
    return jnp.moveaxis(blocks.reshape(shards, rows, parts, width), 2, 1).reshape(
        shards, parts * rows, width
    )


def unfold(rows_in, rows, columns, width=512):
    parts = columns // width
    return jnp.moveaxis(rows_in.reshape(parts, rows, width), 0, 1).reshape(rows, columns)


def body(
    node_scalar, node_vector, edge_scalar, edge_vector, neighbours, send_rows, complex_id, cotangent,
    w_node, w_edge, w_norms, vec_node, vec_edge, vec_out, norm_gain, ff_vec, ff_scalar, ff_up,
    w_embed, attn_gain, w_qkv, w_out, ffn_gain, w_up, w_down,
):
    local_rows = node_scalar.shape[0]
    spaces = lax.axis_size("space")
    extra_rows = spaces * CAP
    table_count = local_rows + extra_rows
    all_nodes = complex_id.shape[0]
    steps = NEIGH // GROUP

    if spaces == HEADS and lax.axis_size("dp") == 4 and local_rows == 128:
        quads = spaces // 2
        sent = send_rows[0]
        near = neighbours.T
        ev = edge_vector.reshape(3, local_rows, NEIGH).transpose(0, 2, 1).astype(F32)
        gain_row, at = 0.0, 0
        for gain in (norm_gain, attn_gain, ffn_gain, vec_edge[0]):
            after = D_S + 2 * D_MODEL + H_P - at - gain.shape[0]
            gain_row = gain_row + jnp.pad(gain.astype(F32), (at, after))
            at += gain.shape[0]
        gain_row = gain_row[None]
        (
            agg_s, agg_v, hidden, lx, dsilu, update, table_s, table_v, vec_source, vec_target, vout,
            wn_mix,
        ) = message(
            (
                near, edge_scalar.T, ev, gain_row, node_scalar, node_vector, sent, vec_node.T, w_edge,
                vec_out, w_norms,
            ),
            w_node,
        )
        (
            stream_out, gsone, gvone, gains, attention_share, node_share, early_share, table_o, node_o,
        ) = middle(
            (
                node_scalar, node_vector, agg_s, agg_v, gain_row, ff_vec, ff_scalar, ff_up,
                w_embed, w_qkv, complex_id[None], cotangent,
            ),
            (w_out, w_up, w_down), table_s, node_scalar, quads,
        )
        gscal, gvec, plane, got = backward(
            (near, ev, lx, dsilu, hidden, update),
            (
                gsone, wn_mix, gvone, vout, table_v, node_vector, vec_source, vec_target, gains,
            ),
            (table_s, node_scalar, w_node, table_o, node_o, early_share, attention_share, node_share),
        )
        (
            grad_scalar, grad_vector, out_node, out_edge, out_norms, out_vnode, out_vedge, out_vout,
            out_ffv, out_ffs, out_ffu, out_embed, out_qkv, out_out, out_up, out_down, out_ng, out_ag,
            out_fg, stream_out,
        ) = finish(plane, got, sent, gscal, gvec, stream_out)
        return (
            stream_out, grad_scalar, grad_vector, out_node, out_edge, out_norms, out_vnode,
            out_vedge, out_vout.T, out_ng, out_ffv, out_ffs, out_ffu, out_embed, out_ag,
            out_qkv, out_out, out_fg, out_up, out_down,
        )

    sent_index = send_rows[0].reshape(-1)
    sent_live = sent_index >= 0
    pick = sent_index[:, None] == jnp.arange(local_rows, dtype=jnp.int32)[None, :]
    pick = pick.astype(BF)
    flat_nodes = jnp.concatenate([node_scalar] + [node_vector[c] for c in range(3)], 1)
    outgoing = product(pick, flat_nodes).astype(BF).reshape(spaces, CAP, D_S + 3 * D_V)
    incoming = lax.all_to_all(outgoing, "space", split_axis=0, concat_axis=0, tiled=True)
    incoming = incoming.reshape(extra_rows, D_S + 3 * D_V)
    table_s = jnp.concatenate([node_scalar, incoming[:, :D_S]], 0)
    table_v = jnp.stack(
        [
            jnp.concatenate(
                [node_vector[c], incoming[:, D_S + c * D_V : D_S + (c + 1) * D_V]], 0
            )
            for c in range(3)
        ]
    )
    vec_source = pad_to(vec_node[:, :H_V], H_P, 1)
    vec_target = pad_to(vec_node[:, H_V:], H_P, 1)
    a_source = product(table_s, w_node[:, :D_S]).astype(BF)
    b_target = product(node_scalar, w_node[:, D_S:])
    p_source = product(table_v, vec_source).astype(BF)
    q_target = product(node_vector, vec_target)
    ve_row = pad_to(vec_edge.astype(F32), H_P, 1)
    vout = pad_to(vec_out, H_P, 0)
    wn_mix = pad_to(jnp.concatenate([w_norms, w_edge], 0), H_P, 0)
    mix = jnp.concatenate([a_source, wn_mix], 0)

    near = neighbours.T
    near_col = near[:, :, None]
    near_row = near.reshape(steps, 1, GROUP * local_rows)
    es_k = edge_scalar.reshape(local_rows, NEIGH, D_E).transpose(1, 0, 2)
    es_pad = jnp.pad(es_k, ((0, 0), (0, 0), (1, 128 - 1 - D_E)))
    ev_k = edge_vector.reshape(3, local_rows, NEIGH)
    ev_col = ev_k.transpose(2, 1, 0).astype(F32)
    ev_row = ev_k.transpose(2, 0, 1).reshape(steps, GROUP, 3, local_rows)
    ev_row = ev_row.transpose(0, 2, 1, 3).reshape(steps, 3, GROUP * local_rows)

    agg_s, agg_v, hidden, lx, dsilu, update = edge_forward(
        near_col, es_pad, ev_col, mix, b_target, p_source, q_target, ve_row, vout
    )

    scalar_one = node_scalar.astype(F32) + agg_s
    vector_one = node_vector.astype(F32) + agg_v
    gain_norm = norm_gain.astype(F32)
    normed_s = layer_norm(scalar_one, gain_norm)
    normed_v = vector_norm(vector_one)
    normed_vr = normed_v.astype(BF)
    ff_hidden = product(normed_vr, ff_vec)
    ff_hidden_r = ff_hidden.astype(BF)
    ff_length = length_plus(ff_hidden)
    ff_input = jnp.concatenate([normed_s.astype(BF), ff_length.astype(BF)], -1)
    ff_preact = product(ff_input, ff_scalar)
    ff_update = product(ff_hidden_r, ff_up)
    scalar_two = normed_s + jax.nn.silu(ff_preact)
    vector_two = normed_v + vector_gate(ff_update)
    embed_input = jnp.concatenate([scalar_two.astype(BF), length_plus(vector_two).astype(BF)], -1)
    stream_zero = product(embed_input, w_embed)
    gain_attn = attn_gain.astype(F32)
    attn_in = layer_norm(stream_zero, gain_attn).astype(BF)
    qkv = product(attn_in, w_qkv).astype(BF)
    queries = qkv[:, :D_MODEL]
    keys_own = qkv[:, D_MODEL : 2 * D_MODEL]
    values_own = qkv[:, 2 * D_MODEL :]
    full_qkv = lax.all_gather(qkv, "space", axis=0, tiled=True)
    heads = lambda values: values.reshape(values.shape[0], HEADS, HEAD_DIM)
    full_queries = heads(full_qkv[:, :D_MODEL])
    full_keys = heads(full_qkv[:, D_MODEL : 2 * D_MODEL])
    full_values = heads(full_qkv[:, 2 * D_MODEL :])
    position = lax.axis_index("space")
    own_ids = lax.dynamic_slice_in_dim(complex_id, position * local_rows, local_rows, 0)
    same = own_ids[:, None] == complex_id[None, :]
    score_scale = HEAD_DIM ** (-0.5)
    scores = jnp.einsum("qhd,khd->hqk", heads(queries), full_keys, preferred_element_type=F32)
    scores = jnp.where(same[None], scores * score_scale, -1000000000.0)
    row_peak = jnp.max(scores, axis=-1, keepdims=True)
    shifted = jnp.exp(scores - row_peak)
    totals = jnp.sum(shifted, axis=-1, keepdims=True)
    probs = shifted / totals
    log_total = row_peak + jnp.log(totals)
    attended = jnp.einsum(
        "hqk,khd->qhd", probs.astype(BF), full_values, preferred_element_type=F32
    ).reshape(local_rows, D_MODEL)
    attended_r = attended.astype(BF)
    stream_one = stream_zero + product(attended_r, w_out)
    gain_ffn = ffn_gain.astype(F32)
    ffn_in = layer_norm(stream_one, gain_ffn).astype(BF)
    hidden_up = product(ffn_in, w_up)
    gelu_r = gelu_exact(hidden_up).astype(BF)
    stream_out = (stream_one + product(gelu_r, w_down)).astype(BF)
    grad_w_down = product_lead(gelu_r, cotangent)
    grad_gelu = product_back(cotangent, w_down)
    grad_up_r = pullback(gelu_exact, hidden_up, grad_gelu).astype(BF)
    grad_w_up = product_lead(ffn_in, grad_up_r)
    grad_ffn_in = product_back(grad_up_r, w_up)
    unused, ffn_pull = jax.vjp(layer_norm, stream_one, gain_ffn)
    grad_stream_ln, grad_ffn_gain = ffn_pull(grad_ffn_in)
    grad_stream_one = cotangent.astype(F32) + grad_stream_ln
    grad_branch = grad_stream_one.astype(BF)
    grad_w_out = product_lead(attended_r, grad_branch)
    grad_attended = product_back(grad_branch, w_out).astype(BF)
    row_dots = jnp.sum(heads(grad_attended).astype(F32) * heads(attended), axis=-1).T

    def halves(values):
        high = lax.reduce_precision(values, exponent_bits=8, mantissa_bits=7)
        return [high.astype(BF), (values - high).astype(BF)]

    numbers = jnp.concatenate(halves(log_total[:, :, 0]) + halves(row_dots), 0)
    packed = jnp.concatenate([grad_attended, pad_to(numbers.T, 128, 1)], 1)
    full_packed = lax.all_gather(packed, "space", axis=0, tiled=True)
    full_grad = heads(full_packed[:, :D_MODEL])
    numbers = full_packed[:, D_MODEL : D_MODEL + 4 * HEADS].astype(F32).T
    full_log = numbers[:HEADS] + numbers[HEADS : 2 * HEADS]
    full_dots = numbers[2 * HEADS : 3 * HEADS] + numbers[3 * HEADS :]

    grad_probs = jnp.einsum(
        "qhd,khd->hqk", heads(grad_attended), full_values, preferred_element_type=F32
    )
    grad_scores = (probs * (grad_probs - row_dots[:, :, None])).astype(BF)
    grad_query = jnp.einsum("hqk,khd->qhd", grad_scores, full_keys, preferred_element_type=F32)
    own_scores = jnp.einsum(
        "khd,qhd->hkq", heads(keys_own), full_queries, preferred_element_type=F32
    )
    own_scores = jnp.where(same[None], own_scores * score_scale, -1000000000.0)
    own_probs = jnp.exp(own_scores - full_log[:, None, :])
    own_grad_probs = jnp.einsum(
        "khd,qhd->hkq", heads(values_own), full_grad, preferred_element_type=F32
    )
    own_grad_scores = (own_probs * (own_grad_probs - full_dots[:, None, :])).astype(BF)
    grad_keys = jnp.einsum(
        "hkq,qhd->khd", own_grad_scores, full_queries, preferred_element_type=F32
    )
    grad_values = jnp.einsum(
        "hkq,qhd->khd", own_probs.astype(BF), full_grad, preferred_element_type=F32
    )
    flat = lambda values: values.reshape(local_rows, D_MODEL)
    grad_qkv = jnp.concatenate(
        [flat(grad_query) * score_scale, flat(grad_keys) * score_scale, flat(grad_values)], -1
    ).astype(BF)
    grad_w_qkv = product_lead(attn_in, grad_qkv)
    grad_attn_in = product_back(grad_qkv, w_qkv)
    unused, attn_pull = jax.vjp(layer_norm, stream_zero, gain_attn)
    grad_zero_ln, grad_attn_gain = attn_pull(grad_attn_in)
    grad_stream_r = (grad_stream_one + grad_zero_ln).astype(BF)
    grad_w_embed = product_lead(embed_input, grad_stream_r)
    grad_embed_in = product_back(grad_stream_r, w_embed)
    grad_vector_two = pullback(length_plus, vector_two, grad_embed_in[:, D_S:])
    grad_ff_pre = pullback(jax.nn.silu, ff_preact, grad_embed_in[:, :D_S]).astype(BF)
    grad_ff_scalar = product_lead(ff_input, grad_ff_pre)
    grad_ff_input = product_back(grad_ff_pre, ff_scalar)
    grad_ff_update = pullback(vector_gate, ff_update, grad_vector_two).astype(BF)
    grad_ff_up = product_lead(ff_hidden_r, grad_ff_update)
    grad_ff_hidden = (
        product_back(grad_ff_update, ff_up)
        + pullback(length_plus, ff_hidden, grad_ff_input[:, D_S:])
    ).astype(BF)
    grad_ff_vec = product_lead(normed_vr, grad_ff_hidden)
    grad_normed_v = grad_vector_two + product_back(grad_ff_hidden, ff_vec)
    grad_normed_s = grad_embed_in[:, :D_S] + grad_ff_input[:, :D_S]
    unused, norm_pull = jax.vjp(layer_norm, scalar_one, gain_norm)
    grad_scalar_one, grad_norm_gain = norm_pull(grad_normed_s)
    grad_vector_one = pullback(vector_norm, vector_one, grad_normed_v)

    shard = lambda grad: grad.astype(BF).reshape((spaces, grad.shape[0] // spaces) + grad.shape[1:])
    gains = jnp.concatenate(
        [shard(grad_norm_gain), shard(grad_attn_gain), shard(grad_ffn_gain)], 1
    )
    gains = pad_to(pad_to(gains, 512, 1)[:, None, :], 16, 1)
    first_share = jnp.concatenate(
        [
            shard(grad_w_down),
            fold(shard(grad_w_up)),
            fold(shard(grad_w_qkv)),
            shard(grad_w_out),
            shard(grad_w_embed),
            fold(shard(grad_ff_scalar)),
            jnp.concatenate([shard(grad_ff_vec), shard(grad_ff_up)], 2),
            gains,
        ],
        1,
    )
    first_sum = lax.psum_scatter(first_share, "space", scatter_dimension=0, tiled=False)
    first_sum = lax.psum(first_sum, "dp").astype(F32)

    grad_a, grad_mix, grad_b, grad_p, grad_q, grad_vout = edge_backward(
        near_row, ev_col, ev_row, hidden, lx, dsilu, update,
        grad_scalar_one * (1.0 / NEIGH), grad_vector_one * (1.0 / NEIGH), wn_mix, vout, table_count,
    )
    grad_vedge = jnp.sum(grad_p[:, table_count], 0)[:H_V]
    grad_vec_edge = lax.psum(grad_vedge[None, :], ("dp", "space"))
    grad_a_r = grad_a.astype(BF)
    grad_p_r = grad_p[:, :table_count].astype(BF)
    grad_b_r = grad_b.astype(BF)
    grad_q_r = grad_q.astype(BF)
    grad_node_a = product_lead(table_s, grad_a_r)
    grad_node_b = product_lead(node_scalar, grad_b_r)
    grad_vec_a = product_lead(table_v, grad_p_r)
    grad_vec_b = product_lead(node_vector, grad_q_r)
    grad_table_scalar = product_back(grad_a_r, w_node[:, :D_S])
    grad_table_vector = product_back(grad_p_r, vec_source)
    grad_scalar = (
        grad_scalar_one + product_back(grad_b_r, w_node[:, D_S:]) + grad_table_scalar[:local_rows]
    )
    grad_vector = (
        grad_vector_one + product_back(grad_q_r, vec_target) + grad_table_vector[:, :local_rows]
    )
    back = jnp.concatenate(
        [grad_table_scalar[local_rows:]] + [grad_table_vector[c, local_rows:] for c in range(3)], 1
    )
    back = back.astype(BF).reshape(spaces, CAP, D_S + 3 * D_V)
    got = lax.all_to_all(back, "space", split_axis=0, concat_axis=0, tiled=True)
    got = got.reshape(extra_rows, D_S + 3 * D_V)
    got = jnp.where(sent_live[:, None], got, 0)
    added = lax.dot_general(pick, got, (((0,), (0,)), ((), ())), preferred_element_type=F32)
    grad_scalar = grad_scalar + added[:, :D_S]
    grad_vector = grad_vector + jnp.moveaxis(
        added[:, D_S:].reshape(local_rows, 3, D_V), 1, 0
    )

    columns = lambda grad: jnp.moveaxis(
        grad.reshape(grad.shape[0], spaces, grad.shape[1] // spaces), 1, 0
    )
    mix_block = columns(grad_mix.astype(BF))
    mix_width = D_S // spaces
    mix_rows = H_P * mix_width // 512
    second_share = jnp.concatenate(
        [
            fold(shard(grad_node_a)),
            fold(shard(grad_node_b)),
            mix_block.reshape(spaces, mix_rows, 512),
            shard(grad_vec_a)[:, :, :512],
            shard(grad_vec_b)[:, :, :512],
            shard(grad_vout)[:, :, :512],
            jnp.concatenate(
                [
                    shard(grad_vec_a)[:, :, 512:],
                    shard(grad_vec_b)[:, :, 512:],
                    shard(grad_vout)[:, :, 512:],
                    jnp.zeros((spaces, D_V // spaces, 128), BF),
                ],
                2,
            ),
        ],
        1,
    )
    second_sum = lax.psum_scatter(second_share, "space", scatter_dimension=0, tiled=False)
    second_sum = lax.psum(second_sum, "dp").astype(F32)

    def taker(rows_in):
        at = [0]

        def take(rows, cols, blocks=1):
            part = rows_in[at[0] : at[0] + rows * blocks]
            at[0] += rows * blocks
            return unfold(part, rows, cols) if blocks > 1 else part

        return take

    take = taker(first_sum)
    out_down = take(grad_w_down.shape[0] // spaces, 512)
    out_up = take(D_MODEL // spaces, 2048, 4)
    out_qkv = take(D_MODEL // spaces, 1536, 3)
    out_out = take(D_MODEL // spaces, 512)
    out_embed = take((D_S + D_V) // spaces, 512)
    out_ffs = take((D_S + D_V) // spaces, 1024, 2)
    both = take(D_V // spaces, 512)
    out_ffv, out_ffu = both[:, :D_V], both[:, D_V:]
    gain_row = take(16, 512)[0]
    cuts = [D_S // spaces, D_MODEL // spaces, D_MODEL // spaces]
    out_gn = gain_row[: cuts[0]]
    out_ga = gain_row[cuts[0] : cuts[0] + cuts[1]]
    out_gf = gain_row[cuts[0] + cuts[1] : sum(cuts)]
    take = taker(second_sum)
    node_a = take(D_S // spaces, 1024, 2)
    node_b = take(D_S // spaces, 1024, 2)
    mixed = take(mix_rows, 512).reshape(H_P, mix_width)
    vec_a = take(D_V // spaces, 512)
    vec_b = take(D_V // spaces, 512)
    vout_t = take(D_V // spaces, 512)
    tails = take(D_V // spaces, 512)
    out_vec_node = jnp.concatenate([vec_a, tails[:, :1], vec_b, tails[:, 128:129]], 1)
    out_vec_out = jnp.concatenate([vout_t, tails[:, 256:257]], 1).T
    return (
        stream_out,
        grad_scalar.astype(BF),
        grad_vector.astype(BF),
        jnp.concatenate([node_a, node_b], 1),
        mixed[H_V : H_V + D_E],
        mixed[:H_V],
        out_vec_node,
        grad_vec_edge,
        out_vec_out,
        out_gn,
        out_ffv,
        out_ffs,
        out_ffu,
        out_embed,
        out_ga,
        out_qkv,
        out_out,
        out_gf,
        out_up,
        out_down,
    )


def solution(mesh):
    rows = P(("dp", "space"), None)
    component = P(None, ("dp", "space"), None)
    return jax.shard_map(
        body,
        mesh=mesh,
        in_specs=(
            rows, component, rows, P(None, ("dp", "space")), rows,
            P(("dp", "space"), None, None), P("dp"), rows,
        ) + (P(),) * 17,
        out_specs=(
            rows, rows, component, P("space", None), P(None, "space"), P(None, "space"),
            P("space", None), P(), P(None, "space"), P("space"), P("space", None),
            P("space", None), P("space", None), P("space", None), P("space"), P("space", None),
            P("space", None), P("space"), P("space", None), P("space", None),
        ),
        check_vma=False,
    )
```

```python
import functools
import math

import jax
import jax.numpy as jnp
from jax import lax
from jax.experimental import pallas as pl
from jax.experimental.pallas import tpu as pltpu
from jax.sharding import PartitionSpec as P

D_S = 1024
D_V = 256
H_V = 513
H_P = 640
D_E = 32
NEIGH = 30
D_MODEL = 512
HEADS = 8
HEAD_DIM = 64
CAP = 16
GROUP = 5
VMEM_LIMIT = 60 * 1024 * 1024

MESH = pl.DeviceIdType.MESH
BF = jnp.bfloat16
F32 = jnp.float32


def layer_norm(values, gain_row):
    centred = values - jnp.mean(values, axis=-1, keepdims=True)
    spread = jnp.mean(centred * centred, axis=-1, keepdims=True)
    return centred * lax.rsqrt(spread + 1e-05) * gain_row


def vector_norm(vectors):
    mean_power = jnp.mean(jnp.sum(vectors * vectors, axis=0), axis=-1, keepdims=True)
    return vectors * lax.rsqrt(mean_power + 1e-05)[None]


def length_plus(vectors):
    return jnp.sqrt(jnp.sum(vectors * vectors, axis=0) + 1.0)


def vector_gate(vectors):
    return vectors * jax.nn.sigmoid(length_plus(vectors))[None]


def gelu_exact(values):
    return jax.nn.gelu(values, approximate=False)


def product(former, latter):
    return jnp.dot(former, latter, preferred_element_type=F32)


def product_lead(former, latter):
    leading = tuple(range(former.ndim - 1))
    return lax.dot_general(
        former, latter, ((leading, leading), ((), ())), preferred_element_type=F32
    )


def product_back(former, latter):
    return lax.dot_general(
        former, latter, (((former.ndim - 1,), (1,)), ((), ())), preferred_element_type=F32
    )


def pullback(function, at_point, cotangent_in):
    unused, puller = jax.vjp(function, at_point)
    return puller(cotangent_in)[0]


def sigmoid(values):
    return 0.5 * jnp.tanh(0.5 * values) + 0.5


LANE_BLOCKS = ((0, 256), (256, 256), (512, 128))
ROW_TILE = 64


def edge_forward_kernel(
    near_ref, es_ref, ev_ref, a_ref, b_ref, p_ref, q_ref, ve_ref, vo_ref,
    aggs_ref, aggv_ref, h_ref, lx_ref, ds_ref, z_ref, x_scr,
):
    nodes = b_ref.shape[0]
    table = p_ref.shape[1]
    rows = GROUP * nodes
    idx = near_ref[...].reshape(rows, 1)
    x_scr[:, :table] = (idx == lax.broadcasted_iota(jnp.int32, (rows, table), 1)).astype(BF)
    one_hot = x_scr[:, :table]
    for start, width in LANE_BLOCKS:
        cols = pl.ds(start, width)
        gathered = [product(one_hot, p_ref[c, :, cols]) for c in range(3)]
        for k in range(GROUP):
            for first in range(0, nodes, ROW_TILE):
                at = k * nodes + first
                evk = ev_ref[k, pl.ds(first, ROW_TILE), :]
                total = None
                for c in range(3):
                    h = (
                        gathered[c][at : at + ROW_TILE]
                        + q_ref[c, pl.ds(first, ROW_TILE), cols]
                        + evk[:, c : c + 1] * ve_ref[:, cols]
                    )
                    h_ref[k, c, pl.ds(first, ROW_TILE), cols] = h.astype(BF)
                    total = h * h + 1.0 if total is None else total + h * h
                length = total * lax.rsqrt(total)
                if start == 512:
                    lane = lax.broadcasted_iota(jnp.int32, (ROW_TILE, width), 1)
                    length = jnp.where(
                        lane == 0, length, es_ref[k, pl.ds(first, ROW_TILE), :].astype(F32)
                    )
                length = length.astype(BF)
                x_scr[pl.ds(at, ROW_TILE), pl.ds(table + start, width)] = length
                lx_ref[k, pl.ds(first, ROW_TILE), cols] = length

    @pl.when(pl.program_id(0) == 0)
    def _():
        aggs_ref[...] = jnp.zeros_like(aggs_ref)
        aggv_ref[...] = jnp.zeros_like(aggv_ref)

    full = x_scr[...]
    for start in range(0, D_S, 256):
        cols = pl.ds(start, 256)
        pre = product(full, a_ref[:, cols])
        for first in range(0, nodes, ROW_TILE):
            part = pl.ds(first, ROW_TILE)
            acc = None
            for k in range(GROUP):
                at = k * nodes + first
                x = pre[at : at + ROW_TILE] + b_ref[part, cols]
                s = sigmoid(x)
                y = x * s
                ds_ref[k, part, cols] = (s + y * (1.0 - s)).astype(BF)
                acc = y if acc is None else acc + y
            aggs_ref[part, cols] += acc * (1.0 / NEIGH)
    ups = [
        product(h_ref[:, c, :, :].reshape(rows, H_P), vo_ref[...]) for c in range(3)
    ]
    for first in range(0, nodes, ROW_TILE):
        part = pl.ds(first, ROW_TILE)
        acc = [None] * 3
        for k in range(GROUP):
            at = k * nodes + first
            z = [ups[c][at : at + ROW_TILE] for c in range(3)]
            power = z[0] * z[0] + z[1] * z[1] + z[2] * z[2] + 1.0
            s = sigmoid(power * lax.rsqrt(power))
            for c in range(3):
                z_ref[k, c, part, :] = z[c].astype(BF)
                gated = z[c] * s
                acc[c] = gated if acc[c] is None else acc[c] + gated
        for c in range(3):
            aggv_ref[c, part, :] += acc[c] * (1.0 / NEIGH)


def edge_forward(near_col, es_pad, ev_col, mix, b_target, p_source, q_target, ve_row, vout):
    nodes = b_target.shape[0]
    table = p_source.shape[1]
    whole = lambda shape: pl.BlockSpec(shape, lambda g: (0,) * len(shape))
    slots = lambda *shape: pl.BlockSpec((GROUP,) + shape, lambda g: (g,) + (0,) * len(shape))
    return pl.pallas_call(
        edge_forward_kernel,
        grid=(NEIGH // GROUP,),
        in_specs=[
            slots(nodes, 1),
            slots(nodes, 128),
            slots(nodes, 3),
            whole((table + H_P, D_S)),
            whole((nodes, D_S)),
            whole((3, table, H_P)),
            whole((3, nodes, H_P)),
            whole((1, H_P)),
            whole((H_P, D_V)),
        ],
        out_specs=[
            whole((nodes, D_S)),
            whole((3, nodes, D_V)),
            slots(3, nodes, H_P),
            slots(nodes, H_P),
            slots(nodes, D_S),
            slots(3, nodes, D_V),
        ],
        out_shape=[
            jax.ShapeDtypeStruct((nodes, D_S), F32),
            jax.ShapeDtypeStruct((3, nodes, D_V), F32),
            jax.ShapeDtypeStruct((NEIGH, 3, nodes, H_P), BF),
            jax.ShapeDtypeStruct((NEIGH, nodes, H_P), BF),
            jax.ShapeDtypeStruct((NEIGH, nodes, D_S), BF),
            jax.ShapeDtypeStruct((NEIGH, 3, nodes, D_V), BF),
        ],
        scratch_shapes=[pltpu.VMEM((GROUP * nodes, table + H_P), BF)],
        compiler_params=pltpu.CompilerParams(vmem_limit_bytes=VMEM_LIMIT),
        name="edge_forward",
    )(near_col, es_pad, ev_col, mix, b_target, p_source, q_target, ve_row, vout)


def message_kernel(
    near_ref, es_ref, ev_ref, ve_ref, ns_ref, nv_ref, sent_ref, vn_ref, we_ref, vout_ref, norms_ref,
    wnode_hbm,
    aggs_ref, aggv_ref, h_ref, lx_ref, ds_ref, z_ref, ts_hbm, tv_hbm, vs_hbm, vt_hbm, vo_hbm, wn_hbm,
    x_scr, turn_scr, b_ref, p_ref, q_ref, ts_ref, tv_ref, vs_ref, vt_ref, vo_ref, a_ref, wn_ref,
    pt_ref, wnode, row_scr, vt_scr, out_scr, in_scr, send_sem, recv_sem, load_sem, keep_sem,
):
    nodes = b_ref.shape[0]
    table = p_ref.shape[1]
    rows = GROUP * nodes
    keeps = [
        pltpu.make_async_copy(source, target, keep_sem.at[n])
        for n, (source, target) in enumerate(
            (
                (ts_ref, ts_hbm), (tv_ref, tv_hbm), (vs_ref, vs_hbm), (vt_ref, vt_hbm),
                (vo_ref, vo_hbm), (wn_ref, wn_hbm),
            )
        )
    ]

    @pl.when(pl.program_id(0) == 0)
    def _():
        prepare_kernel(
            ns_ref, nv_ref, sent_ref, vn_ref, we_ref, vout_ref, norms_ref, wnode_hbm,
            b_ref, p_ref, q_ref, ts_ref, tv_ref, vs_ref, vt_ref, vo_ref, a_ref, wn_ref, pt_ref,
            wnode, row_scr, vt_scr, out_scr, in_scr, send_sem, recv_sem, load_sem,
        )
        start_all(keeps)

    first_slot = pl.program_id(0) * GROUP

    @pl.when(pl.program_id(0) == 0)
    def _():
        for n in range(4):
            ref = near_ref if n == 3 else ev_ref.at[n]
            turn_scr[n, pl.ds(0, NEIGH), :] = ref[...].astype(F32)
            turn_scr[n] = jnp.transpose(turn_scr[n])

    back = lax.rem(128 - first_slot, 128)
    ev = [pltpu.roll(turn_scr[n], back, 1) for n in range(4)]
    slots = ev[3]
    places = lax.broadcasted_iota(jnp.int32, (nodes, table), 1).astype(F32)
    edges_in = []
    for k in range(GROUP):
        x_scr[pl.ds(k * nodes, nodes), :table] = (slots[:, k : k + 1] == places).astype(BF)
        rows_in = pl.ds(pl.multiple_of((first_slot + k) * D_E, D_E), D_E)
        edges_in.append(
            jnp.transpose(
                jnp.concatenate(
                    [
                        jnp.zeros((16, nodes), F32),
                        es_ref[rows_in, :].astype(F32),
                        jnp.zeros((112 - D_E, nodes), F32),
                    ],
                    0,
                )
            )
        )
    one_hot = x_scr[:, :table]
    for start, width in LANE_BLOCKS:
        cols = pl.ds(start, width)
        if start == 512:
            lane = lax.broadcasted_iota(jnp.int32, (rows, width), 1)
            three = product(one_hot, pt_ref[...])
            gathered = [
                jnp.where(lane == 0, three if c == 0 else pltpu.roll(three, width - c, 1), 0.0)
                for c in range(3)
            ]
        else:
            gathered = [product(one_hot, p_ref[c, :, cols]) for c in range(3)]
        for k in range(GROUP):
            for first in range(0, nodes, ROW_TILE):
                at = k * nodes + first
                total = None
                for c in range(3):
                    h = (
                        gathered[c][at : at + ROW_TILE]
                        + q_ref[c, pl.ds(first, ROW_TILE), cols]
                        + ev[c][first : first + ROW_TILE, k : k + 1]
                        * ve_ref[:, pl.ds(D_S + 2 * D_MODEL + start, width)]
                    )
                    h_ref[k, c, pl.ds(first, ROW_TILE), cols] = h.astype(BF)
                    total = h * h + 1.0 if total is None else total + h * h
                length = total * lax.rsqrt(total)
                if start == 512:
                    lane = lax.broadcasted_iota(jnp.int32, (ROW_TILE, width), 1)
                    length = jnp.where(
                        lane == 0, length, edges_in[k][first : first + ROW_TILE]
                    )
                length = length.astype(BF)
                x_scr[pl.ds(at, ROW_TILE), pl.ds(table + start, width)] = length
                lx_ref[k, pl.ds(first, ROW_TILE), cols] = length

    @pl.when(pl.program_id(0) == 0)
    def _():
        aggs_ref[...] = jnp.zeros_like(aggs_ref)
        aggv_ref[...] = jnp.zeros_like(aggv_ref)

    full = x_scr[...]
    for start in range(0, D_S, 256):
        cols = pl.ds(start, 256)
        pre = product(full, a_ref[:, cols])
        for first in range(0, nodes, ROW_TILE):
            part = pl.ds(first, ROW_TILE)
            acc = None
            for k in range(GROUP):
                at = k * nodes + first
                x = pre[at : at + ROW_TILE] + b_ref[part, cols]
                s = sigmoid(x)
                y = x * s
                ds_ref[k, part, cols] = (s + y * (1.0 - s)).astype(BF)
                acc = y if acc is None else acc + y
            aggs_ref[part, cols] += acc * (1.0 / NEIGH)
    ups = [
        product(h_ref[:, c, :, pl.ds(0, 512)].reshape(rows, 512), vo_ref[pl.ds(0, 512), :])
        for c in range(3)
    ]
    last_row = vo_ref[pl.ds(512, 16), :].astype(F32)[0:1, :]
    for first in range(0, nodes, ROW_TILE):
        part = pl.ds(first, ROW_TILE)
        acc = [None] * 3
        for k in range(GROUP):
            at = k * nodes + first
            z = [
                ups[c][at : at + ROW_TILE]
                + h_ref[k, c, part, pl.ds(512, 128)].astype(F32)[:, 0:1] * last_row
                for c in range(3)
            ]
            power = z[0] * z[0] + z[1] * z[1] + z[2] * z[2] + 1.0
            s = sigmoid(power * lax.rsqrt(power))
            for c in range(3):
                z_ref[k, c, part, :] = z[c].astype(BF)
                gated = z[c] * s
                acc[c] = gated if acc[c] is None else acc[c] + gated
        for c in range(3):
            aggv_ref[c, part, :] += acc[c] * (1.0 / NEIGH)

    @pl.when(pl.program_id(0) == pl.num_programs(0) - 1)
    def _():
        wait_all(keeps)


def message(operands, w_node):
    near, edge_scalar, ev, gain_row, node_scalar, node_vector, sent = operands[:7]
    nodes = node_scalar.shape[0]
    spaces = sent.shape[0]
    table = nodes + spaces * CAP
    rows = GROUP * nodes
    once = pl.Buffered(1)
    whole = lambda shape: pl.BlockSpec(shape, lambda g: (0,) * len(shape), pipeline_mode=once)
    slots = lambda *shape: pl.BlockSpec((GROUP,) + shape, lambda g: (g,) + (0,) * len(shape))
    hbm = pl.BlockSpec(memory_space=pl.ANY)
    bits = lambda *shape: pltpu.VMEM(shape, BF)
    wide = lambda *shape: pltpu.VMEM(shape, F32)
    kept = [(table, D_S), (3, table, D_V), (H_P, D_V), (H_P, D_V), (H_P, D_V), (H_P, D_S)]
    outs = [
        ((nodes, D_S), F32),
        ((3, nodes, D_V), F32),
        ((NEIGH, 3, nodes, H_P), BF),
        ((NEIGH, nodes, H_P), BF),
        ((NEIGH, nodes, D_S), BF),
        ((NEIGH, 3, nodes, D_V), BF),
    ] + [(shape, BF) for shape in kept]
    blocks = (spaces, CAP, D_S + 3 * D_V)
    return pl.pallas_call(
        message_kernel,
        grid=(NEIGH // GROUP,),
        in_specs=[whole(one.shape) for one in operands] + [hbm],
        out_specs=[
            whole((nodes, D_S)),
            whole((3, nodes, D_V)),
            slots(3, nodes, H_P),
            slots(nodes, H_P),
            slots(nodes, D_S),
            slots(3, nodes, D_V),
        ]
        + [hbm] * len(kept),
        out_shape=[jax.ShapeDtypeStruct(shape, kind) for shape, kind in outs],
        scratch_shapes=[
            bits(rows, table + H_P), wide(4, 128, nodes), wide(nodes, D_S), bits(3, table, H_P),
            wide(3, nodes, H_P), bits(*kept[0]), bits(*kept[1]), bits(*kept[2]), bits(*kept[3]),
            bits(*kept[4]), bits(table + H_P, D_S), bits(*kept[5]), bits(table, 128),
            bits(*w_node.shape), wide(8, 128), wide(H_P, D_V), bits(*blocks), bits(*blocks),
            pltpu.SemaphoreType.DMA((spaces - 1,)),
            pltpu.SemaphoreType.DMA((spaces - 1,)),
            pltpu.SemaphoreType.DMA,
            pltpu.SemaphoreType.DMA((len(kept),)),
        ],
        compiler_params=pltpu.CompilerParams(
            collective_id=3, has_side_effects=True, vmem_limit_bytes=VMEM_LIMIT
        ),
        name="message",
    )(*operands, w_node)


def edge_backward_kernel(
    near_ref, ev_ref, evr_ref, h_ref, lx_ref, ds_ref, z_ref, gs_ref, gv_ref, wn_ref, vo_ref,
    ga_ref, gw_ref, gb_ref, gp_ref, gq_ref, gvo_ref, pre_scr, up_scr, gh_scr,
):
    nodes = gs_ref.shape[0]
    table = ga_ref.shape[0]
    rows = GROUP * nodes

    @pl.when(pl.program_id(0) == 0)
    def _():
        for ref in (ga_ref, gw_ref, gb_ref, gp_ref, gq_ref, gvo_ref):
            ref[...] = jnp.zeros_like(ref)

    for start in range(0, D_S, 256):
        cols = pl.ds(start, 256)
        for first in range(0, nodes, ROW_TILE):
            part = pl.ds(first, ROW_TILE)
            share = gs_ref[part, cols]
            acc = None
            for k in range(GROUP):
                g = (ds_ref[k, part, cols].astype(F32) * share).astype(BF)
                pre_scr[pl.ds(k * nodes + first, ROW_TILE), cols] = g
                g = g.astype(F32)
                acc = g if acc is None else acc + g
            gb_ref[part, cols] += acc
    for first in range(0, nodes, ROW_TILE):
        part = pl.ds(first, ROW_TILE)
        share = [gv_ref[c, part, :] for c in range(3)]
        for k in range(GROUP):
            z = [z_ref[k, c, part, :].astype(F32) for c in range(3)]
            power = z[0] * z[0] + z[1] * z[1] + z[2] * z[2] + 1.0
            inverse = lax.rsqrt(power)
            s = sigmoid(power * inverse)
            dot = z[0] * share[0] + z[1] * share[1] + z[2] * share[2]
            factor = dot * inverse * (s * (1.0 - s))
            for c in range(3):
                up_scr[c, pl.ds(k * nodes + first, ROW_TILE), :] = (
                    share[c] * s + z[c] * factor
                ).astype(BF)

    near = near_ref[0]
    one_hot = (lax.broadcasted_iota(jnp.int32, (table, rows), 0) == near).astype(BF)
    grad_pre = pre_scr[...]
    ga_ref[...] += product(one_hot, grad_pre)
    lx = lx_ref[...].reshape(rows, H_P)
    gw_ref[...] += lax.dot_general(
        lx, grad_pre, (((0,), (0,)), ((), ())), preferred_element_type=F32
    )
    for start, width in LANE_BLOCKS:
        cols = pl.ds(start, width)
        grad_length = product_back(grad_pre, wn_ref[cols, :])
        grad_direct = [product_back(up_scr[c], vo_ref[cols, :]) for c in range(3)]
        for first in range(0, nodes, ROW_TILE):
            part = pl.ds(first, ROW_TILE)
            acc = [None] * 3
            for k in range(GROUP):
                at = k * nodes + first
                ratio = grad_length[at : at + ROW_TILE] * pl.reciprocal(
                    lx_ref[k, part, cols].astype(F32), approx=True
                )
                if start == 512:
                    lane = lax.broadcasted_iota(jnp.int32, (ROW_TILE, width), 1)
                    ratio = jnp.where(lane == 0, ratio, 0.0)
                for c in range(3):
                    g = grad_direct[c][at : at + ROW_TILE] + ratio * h_ref[
                        k, c, part, cols
                    ].astype(F32)
                    gh_scr[c, pl.ds(at, ROW_TILE), cols] = g.astype(BF)
                    acc[c] = g if acc[c] is None else acc[c] + g
            for c in range(3):
                gq_ref[c, part, cols] += acc[c]
    for c in range(3):
        evr = jnp.broadcast_to(evr_ref[0, c : c + 1, :], (16, rows))
        lead = jnp.concatenate([one_hot, evr.astype(BF)], axis=0)
        gp_ref[c] += product(lead, gh_scr[c])
        gvo_ref[...] += lax.dot_general(
            up_scr[c],
            h_ref[:, c, :, :].reshape(rows, H_P),
            (((0,), (0,)), ((), ())),
            preferred_element_type=F32,
        )


def edge_backward(near_row, ev_col, ev_row, hidden, lx, dsilu, update, gs, gv, wn, vout, table):
    nodes = gs.shape[0]
    rows = GROUP * nodes
    whole = lambda shape: pl.BlockSpec(shape, lambda g: (0,) * len(shape))
    slots = lambda *shape: pl.BlockSpec((GROUP,) + shape, lambda g: (g,) + (0,) * len(shape))
    steps = lambda *shape: pl.BlockSpec((1,) + shape, lambda g: (g,) + (0,) * len(shape))
    outs = [
        (table, D_S),
        (H_P, D_S),
        (nodes, D_S),
        (3, table + 16, H_P),
        (3, nodes, H_P),
        (D_V, H_P),
    ]
    return pl.pallas_call(
        edge_backward_kernel,
        grid=(NEIGH // GROUP,),
        in_specs=[
            steps(1, rows),
            slots(nodes, 3),
            steps(3, rows),
            slots(3, nodes, H_P),
            slots(nodes, H_P),
            slots(nodes, D_S),
            slots(3, nodes, D_V),
            whole((nodes, D_S)),
            whole((3, nodes, D_V)),
            whole((H_P, D_S)),
            whole((H_P, D_V)),
        ],
        out_specs=[whole(shape) for shape in outs],
        out_shape=[jax.ShapeDtypeStruct(shape, F32) for shape in outs],
        scratch_shapes=[
            pltpu.VMEM((rows, D_S), BF),
            pltpu.VMEM((3, rows, D_V), BF),
            pltpu.VMEM((3, rows, H_P), BF),
        ],
        compiler_params=pltpu.CompilerParams(vmem_limit_bytes=VMEM_LIMIT),
        name="edge_backward",
    )(near_row, ev_col, ev_row, hidden, lx, dsilu, update, gs, gv, wn, vout)


AT_AIN, AT_EMB, AT_FFIN, AT_FFH, AT_NV, FAC_NODE = 0, 512, 1792, 3072, 3840, 4608
AT_GELU, AT_GUP, AT_FIN, AT_COT, AT_ATT, AT_GBR, FAC_FEED = 0, 2048, 4096, 4608, 5120, 5632, 6144
AT_GQKV, AT_STREAM, AT_GPRE, AT_GFU, AT_GFH, FAC_BACK = 0, 1536, 2048, 3072, 3840, 4608
ROWS_F, ROWS_A, ROWS_N, ROWS_S, ROWS_B, ROWS_V = ALL_ROWS = (512, 256, 512, 256, 384, 128)
ROWS_E = ROWS_F // 4

def full_block(shape):
    return pl.BlockSpec(shape, lambda: (0,) * len(shape))


def lead_product(former, latter):
    return lax.dot_general(
        former, latter, (((0,), (0,)), ((), ())), preferred_element_type=F32
    )


def swap_halves(values):
    return pltpu.roll(values, 64, 1)


def lower_half(shape):
    return lax.broadcasted_iota(jnp.int32, shape, 1) < 64


def pack_tall(tile, odd):
    rows = tile.shape[0] // 2
    top, low = tile[:rows], tile[rows:]
    side = lower_half((rows, 128))
    if odd:
        return jnp.where(side, swap_halves(top), low)
    return jnp.where(side, top, swap_halves(low))


def unpack_tall(block):
    rows = block.shape[0]
    side = lower_half((rows, 128))
    return jnp.concatenate(
        [jnp.where(side, block, 0.0), jnp.where(side, swap_halves(block), 0.0)], 0
    )


def centre(values):
    centred = values - jnp.mean(values, axis=-1, keepdims=True)
    inverse = lax.rsqrt(jnp.mean(centred * centred, axis=-1, keepdims=True) + 1e-05)
    return centred * inverse, inverse


def centre_back(hat, inverse, grad):
    return inverse * (
        grad
        - jnp.mean(grad, axis=-1, keepdims=True)
        - hat * jnp.mean(grad * hat, axis=-1, keepdims=True)
    )


def power_of(parts):
    return parts[0] * parts[0] + parts[1] * parts[1] + parts[2] * parts[2]


def node_forward_kernel(
    ns_ref, nv_ref, as_ref, av_ref, ng_ref, fv_ref, fs_ref, fu_ref, we_ref, ag_ref, wq_ref,
    s1_ref, v1_ref, ffh_ref, ffp_ref, ffu_ref, v2_ref, sz_ref, fac_ref, out_ref, with_keys,
):
    nodes = ns_ref.shape[0]
    s1 = ns_ref[...].astype(F32) + as_ref[...]
    s1_ref[...] = s1
    hat, unused = centre(s1)
    normed_s = hat * ng_ref[...]
    v1 = [nv_ref[c].astype(F32) + av_ref[c] for c in range(3)]
    scale = lax.rsqrt(jnp.mean(power_of(v1), axis=-1, keepdims=True) + 1e-05)
    normed_v = [v * scale for v in v1]
    ffh = [product(v.astype(BF), fv_ref[...]) for v in normed_v]
    power = power_of(ffh) + 1.0
    fac_ref[:, pl.ds(AT_FFIN, D_S)] = normed_s.astype(BF)
    fac_ref[:, pl.ds(AT_FFIN + D_S, D_V)] = (power * lax.rsqrt(power)).astype(BF)
    ffp = product(fac_ref[:, pl.ds(AT_FFIN, D_S + D_V)], fs_ref[...])
    ffu = [product(h.astype(BF), fu_ref[...]) for h in ffh]
    for c in range(3):
        v1_ref[c] = v1[c]
        fac_ref[:, pl.ds(AT_FFH + c * D_V, D_V)] = ffh[c].astype(BF)
        fac_ref[:, pl.ds(AT_NV + c * D_V, D_V)] = normed_v[c].astype(BF)
        ffh_ref[c] = ffh[c]
        ffu_ref[c] = ffu[c]
    ffp_ref[...] = ffp
    s2 = normed_s + ffp * sigmoid(ffp)
    power = power_of(ffu) + 1.0
    gate = sigmoid(power * lax.rsqrt(power))
    v2 = [normed_v[c] + ffu[c] * gate for c in range(3)]
    for c in range(3):
        v2_ref[c] = v2[c]
    power = power_of(v2) + 1.0
    fac_ref[:, pl.ds(AT_EMB, D_S)] = s2.astype(BF)
    fac_ref[:, pl.ds(AT_EMB + D_S, D_V)] = (power * lax.rsqrt(power)).astype(BF)
    sz = product(fac_ref[:, pl.ds(AT_EMB, D_S + D_V)], we_ref[...])
    sz_ref[...] = sz
    hat, unused = centre(sz)
    attn_in = (hat * ag_ref[...]).astype(BF)
    fac_ref[:, pl.ds(AT_AIN, D_MODEL)] = attn_in
    q, k = [product(attn_in, wq_ref[:, pl.ds(n * D_MODEL, D_MODEL)]) for n in range(2)]
    side = lower_half((nodes, 128))
    for pair in range(HEADS // 2):
        cols = slice(pair * 128, pair * 128 + 128)
        qp, kp = q[:, cols], k[:, cols]
        even = jnp.where(side, qp, swap_halves(kp))
        odd = jnp.where(side, swap_halves(qp), kp)
        for n, block in enumerate((even, odd)):
            out_ref[2 * pair + n, pl.ds(0, nodes), :] = block.astype(BF)
    with_keys()
    v = product(attn_in, wq_ref[:, pl.ds(2 * D_MODEL, D_MODEL)])
    for head in range(HEADS):
        tile = v[:, head // 2 * 128 : head // 2 * 128 + 128]
        out_ref[head, pl.ds(nodes, nodes // 2), :] = pack_tall(tile, head % 2 == 1).astype(BF)


def split_heads(x_ref, nodes):
    spaces = x_ref.shape[0]
    both = x_ref[:, pl.ds(0, nodes), :].reshape(spaces * nodes, 128).astype(F32)
    queries = jnp.where(lower_half(both.shape), both, 0.0).astype(BF)
    keys = swap_halves(both).astype(BF)
    return queries, keys


def split_values(x_ref, nodes):
    spaces = x_ref.shape[0]
    return jnp.concatenate(
        [unpack_tall(x_ref[d, pl.ds(nodes, nodes // 2), :].astype(F32)) for d in range(spaces)], 0
    ).astype(BF)


def attend_kernel(x_ref, id_ref, probs_ref, att_ref, out_ref, with_probs):
    spaces = x_ref.shape[0]
    nodes = x_ref.shape[1] * 2 // 3
    count = spaces * nodes
    queries, keys = split_heads(x_ref, nodes)
    row_ids = id_ref[...]
    column_ids = jnp.transpose(jnp.broadcast_to(row_ids, (8, count)))[:, 0:1]
    block = 2 * nodes
    for first in range(0, count, block):
        scores = product_back(queries[first : first + block], keys) * HEAD_DIM ** (-0.5)
        same = column_ids[first : first + block] == row_ids
        scores = jnp.where(same, scores, -1000000000.0)
        shifted = jnp.exp(scores - jnp.max(scores, axis=-1, keepdims=True))
        probs = (shifted / jnp.sum(shifted, axis=-1, keepdims=True)).astype(BF)
        probs_ref[pl.ds(first, block), :] = probs
    with_probs()
    values = split_values(x_ref, nodes)
    for first in range(0, count, block):
        att = product(probs_ref[pl.ds(first, block), :], values)
        att_ref[pl.ds(first, block), :] = att
        for n in range(block // nodes):
            tile = att[n * nodes : (n + 1) * nodes]
            out_ref[first // nodes + n] = pack_tall(tile, False).astype(BF)


def attend_backward_kernel(x_ref, probs_ref, att_ref, g_ref, out_ref, gs_scr, with_values):
    spaces = x_ref.shape[0]
    nodes = x_ref.shape[1] * 2 // 3
    count = spaces * nodes
    queries, keys = split_heads(x_ref, nodes)
    values = split_values(x_ref, nodes)
    grad = jnp.concatenate(
        [unpack_tall(g_ref[d].astype(F32)) for d in range(spaces)], 0
    )
    dots = jnp.sum(grad * att_ref[...], axis=-1, keepdims=True)
    grad = grad.astype(BF)
    grad_values = jnp.transpose(lead_product(grad, probs_ref[...]))
    for d in range(spaces):
        tile = grad_values[d * nodes : (d + 1) * nodes]
        out_ref[d, pl.ds(nodes, nodes // 2), :] = pack_tall(tile, False).astype(BF)
    with_values()
    block = 2 * nodes
    scale = HEAD_DIM ** (-0.5)
    grad_queries = []
    for first in range(0, count, block):
        grad_probs = product_back(grad[first : first + block], values)
        part = probs_ref[pl.ds(first, block), :].astype(F32)
        grad_scores = (part * (grad_probs - dots[first : first + block])).astype(BF)
        gs_scr[pl.ds(first, block), :] = grad_scores
        grad_queries.append(product(grad_scores, keys))
    grad_queries = jnp.concatenate(grad_queries, 0) * scale
    grad_keys = jnp.transpose(lead_product(queries, gs_scr[...])) * scale
    side = lower_half((nodes, 128))
    for d in range(spaces):
        rows = slice(d * nodes, (d + 1) * nodes)
        out_ref[d, pl.ds(0, nodes), :] = jnp.where(
            side, grad_queries[rows], swap_halves(grad_keys[rows])
        ).astype(BF)


def merge_heads(block_ref, first, half):
    tiles = []
    for pair in range(HEADS // 2):
        even = unpack_tall(block_ref[2 * pair, pl.ds(first, half), :].astype(F32))
        odd = unpack_tall(block_ref[2 * pair + 1, pl.ds(first, half), :].astype(F32))
        tiles.append(even + swap_halves(odd))
    return jnp.concatenate(tiles, 1)


def feed_kernel(
    att_ref, sz_ref, wo_ref, fg_ref, wu_ref, wd_ref, cot_ref,
    out_ref, gatt_ref, gs1_ref, ggain_ref, fac_ref, with_up,
):
    nodes = sz_ref.shape[0]
    att = merge_heads(att_ref, 0, nodes // 2).astype(BF)
    fac_ref[:, pl.ds(AT_ATT, D_MODEL)] = att
    stream_one = sz_ref[...] + product(att, wo_ref[...])
    hat, inverse = centre(stream_one)
    ffn_in = (hat * fg_ref[...]).astype(BF)
    fac_ref[:, pl.ds(AT_FIN, D_MODEL)] = ffn_in
    ffn = wu_ref.shape[1]
    cot = cot_ref[...]
    fac_ref[:, pl.ds(AT_COT, D_MODEL)] = cot
    for start in range(0, ffn, 512):
        cols = pl.ds(start, 512)
        x = product(ffn_in, wu_ref[:, cols])
        cdf = 0.5 * (1.0 + lax.erf(x * (0.5**0.5)))
        fac_ref[:, pl.ds(AT_GELU + start, 512)] = (x * cdf).astype(BF)
        slope = cdf + x * jnp.exp(-0.5 * x * x) * ((0.5 / math.pi) ** 0.5)
        fac_ref[:, pl.ds(AT_GUP + start, 512)] = (
            product_back(cot, wd_ref[cols, :]) * slope
        ).astype(BF)
    with_up()
    out_ref[...] = (
        stream_one + product(fac_ref[:, pl.ds(AT_GELU, ffn)], wd_ref[...])
    ).astype(BF)
    grad_in = product_back(fac_ref[:, pl.ds(AT_GUP, ffn)], wu_ref[...])
    ggain_ref[...] = jnp.sum(grad_in * hat, axis=0, keepdims=True)
    grad_one = cot.astype(F32) + centre_back(hat, inverse, grad_in * fg_ref[...])
    gs1_ref[...] = grad_one
    branch = grad_one.astype(BF)
    fac_ref[:, pl.ds(AT_GBR, D_MODEL)] = branch
    grad_att = product_back(branch, wo_ref[...])
    for head in range(HEADS):
        tile = grad_att[:, head // 2 * 128 : head // 2 * 128 + 128]
        gatt_ref[head] = pack_tall(tile, head % 2 == 1).astype(BF)


def core_columns(values, core):
    values = values.astype(F32)
    side = lower_half((values.shape[0], 128))
    tiles = []
    for n in range(0, 512, 256):
        one, two = values[:, n : n + 128], values[:, n + 128 : n + 256]
        even = jnp.where(side, one, swap_halves(two))
        odd = jnp.where(side, swap_halves(one), two)
        tiles.append(jnp.where(core == 0, even, odd))
    return jnp.concatenate(tiles, 1).astype(BF)


def both_rows(own_ref, other_ref, start, width):
    return jnp.concatenate(
        [own_ref[:, pl.ds(start, width)], other_ref[:, pl.ds(start, width)]], 0
    )


def feed_grads_kernel(own_ref, other_ref, pack_ref):
    quads = pack_ref.shape[0]
    core = lax.rem(lax.axis_index("space"), 2)
    cot = both_rows(own_ref, other_ref, AT_COT, D_MODEL)
    for z in range(quads):
        start = pl.multiple_of(AT_GELU + (2 * z + core) * 256, 256)
        block = lead_product(both_rows(own_ref, other_ref, start, 256), cot)
        pack_ref[z, pl.ds(0, 256), :] = block.astype(BF)
    left = core_columns(both_rows(own_ref, other_ref, AT_FIN, D_MODEL), core)
    for n in range(4):
        block = lead_product(left, both_rows(own_ref, other_ref, AT_GUP + n * 512, 512)).astype(BF)
        for z in range(quads):
            pack_ref[z, pl.ds(256 + n * 64, 64), :] = block[z * 64 : (z + 1) * 64]


def attention_grads(node_ref, node_other, back_ref, back_other, feed_ref, feed_other, pack_ref):
    quads = pack_ref.shape[0]
    core = lax.rem(lax.axis_index("space"), 2)
    left = core_columns(both_rows(node_ref, node_other, AT_AIN, D_MODEL), core)
    pairs = [
        (left, both_rows(back_ref, back_other, AT_GQKV + n * D_MODEL, D_MODEL)) for n in range(3)
    ]
    pairs.append(
        (
            core_columns(both_rows(feed_ref, feed_other, AT_ATT, D_MODEL), core),
            both_rows(feed_ref, feed_other, AT_GBR, D_MODEL),
        )
    )
    for n, (one, two) in enumerate(pairs):
        block = lead_product(one, two).astype(BF)
        for z in range(quads):
            pack_ref[z, pl.ds(n * 64, 64), :] = block[z * 64 : (z + 1) * 64]


def node_grads(node_ref, node_other, back_ref, back_other, pack_ref, tall_scr, low_scr):
    quads = pack_ref.shape[0]
    core = lax.rem(lax.axis_index("space"), 2)
    emb = both_rows(node_ref, node_other, AT_EMB, D_S + D_V)
    ffin = both_rows(node_ref, node_other, AT_FFIN, D_S + D_V)
    rights = [(emb, back_ref, back_other, AT_STREAM)]
    rights += [(ffin, back_ref, back_other, AT_GPRE + n * 512) for n in range(2)]
    for n, (one, own, other, start) in enumerate(rights):
        tall_scr[...] = lead_product(one, both_rows(own, other, start, 512)).astype(BF)
        for z in range(quads):
            rows = pl.ds(pl.multiple_of((2 * z + core) * 160, 32), 160)
            pack_ref[z, pl.ds(n * 160, 160), :] = tall_scr[rows, :]
    vec = up = None
    for c in range(3):
        one = lead_product(
            both_rows(node_ref, node_other, AT_NV + c * D_V, D_V),
            both_rows(back_ref, back_other, AT_GFH + c * D_V, D_V),
        )
        vec = one if vec is None else vec + one
        one = lead_product(
            both_rows(node_ref, node_other, AT_FFH + c * D_V, D_V),
            both_rows(back_ref, back_other, AT_GFU + c * D_V, D_V),
        )
        up = one if up is None else up + one
    low_scr[...] = jnp.concatenate([vec, up], 1).astype(BF)
    for z in range(quads):
        rows = pl.ds(pl.multiple_of((2 * z + core) * 32, 32), 32)
        pack_ref[z, pl.ds(480, 32), :] = low_scr[rows, :]


def node_backward_kernel(
    gq_ref, gs1_ref, s1_ref, v1_ref, ffh_ref, ffp_ref, ffu_ref, v2_ref,
    sz_ref, ng_ref, fv_ref, fs_ref, fu_ref, we_ref, ag_ref, wq_ref, fgain_ref,
    gsone_ref, gvone_ref, gains_ref, back_ref, with_qkv,
):
    nodes = gs1_ref.shape[0]
    shards = gq_ref.shape[0]
    side = lower_half((nodes, 128))
    tiles = [[], []]
    for pair in range(HEADS // 2):
        even = gq_ref[2 * pair, pl.ds(0, nodes), :].astype(F32)
        odd = gq_ref[2 * pair + 1, pl.ds(0, nodes), :].astype(F32)
        tiles[0].append(jnp.where(side, even, swap_halves(odd)))
        tiles[1].append(jnp.where(side, swap_halves(even), odd))
    grads = [jnp.concatenate(tile, 1).astype(BF) for tile in tiles]
    grads.append(merge_heads(gq_ref, nodes, nodes // 2).astype(BF))
    for n in range(3):
        back_ref[:, pl.ds(AT_GQKV + n * D_MODEL, D_MODEL)] = grads[n]
    with_qkv()
    grad_in = product_back(back_ref[:, pl.ds(AT_GQKV, 3 * D_MODEL)], wq_ref[...])
    hat, inverse = centre(sz_ref[...])
    grad_attn_gain = jnp.sum(grad_in * hat, axis=0, keepdims=True)
    stream = gs1_ref[...] + centre_back(hat, inverse, grad_in * ag_ref[...])
    stream = stream.astype(BF)
    back_ref[:, pl.ds(AT_STREAM, D_MODEL)] = stream
    grad_emb = product_back(stream, we_ref[...])
    grad_s2, grad_len = grad_emb[:, :D_S], grad_emb[:, D_S:]
    v2 = [v2_ref[c] for c in range(3)]
    factor = grad_len * lax.rsqrt(power_of(v2) + 1.0)
    grad_v2 = [factor * v for v in v2]
    x = ffp_ref[...]
    s = sigmoid(x)
    grad_pre = (grad_s2 * (s + x * s * (1.0 - s))).astype(BF)
    back_ref[:, pl.ds(AT_GPRE, D_S)] = grad_pre
    grad_ffin = product_back(grad_pre, fs_ref[...])
    z = [ffu_ref[c] for c in range(3)]
    power = power_of(z) + 1.0
    inverse = lax.rsqrt(power)
    s = sigmoid(power * inverse)
    dot = z[0] * grad_v2[0] + z[1] * grad_v2[1] + z[2] * grad_v2[2]
    factor = dot * inverse * (s * (1.0 - s))
    grad_up = [(grad_v2[c] * s + z[c] * factor).astype(BF) for c in range(3)]
    h = [ffh_ref[c] for c in range(3)]
    factor = grad_ffin[:, D_S:] * lax.rsqrt(power_of(h) + 1.0)
    v1 = [v1_ref[c] for c in range(3)]
    scale = lax.rsqrt(jnp.mean(power_of(v1), axis=-1, keepdims=True) + 1e-05)
    grad_nv = []
    for c in range(3):
        back_ref[:, pl.ds(AT_GFU + c * D_V, D_V)] = grad_up[c]
        grad_h = (product_back(grad_up[c], fu_ref[...]) + factor * h[c]).astype(BF)
        back_ref[:, pl.ds(AT_GFH + c * D_V, D_V)] = grad_h
        grad_nv.append(grad_v2[c] + product_back(grad_h, fv_ref[...]))
    grad_ns = grad_s2 + grad_ffin[:, :D_S]
    hat, inverse = centre(s1_ref[...])
    grad_norm_gain = jnp.sum(grad_ns * hat, axis=0, keepdims=True)
    gsone_ref[...] = centre_back(hat, inverse, grad_ns * ng_ref[...])
    dot = grad_nv[0] * v1[0] + grad_nv[1] * v1[1] + grad_nv[2] * v1[2]
    dot = jnp.mean(dot, axis=-1, keepdims=True) * scale * scale
    for c in range(3):
        gvone_ref[c] = scale * (grad_nv[c] - v1[c] * dot)
    gains_ref[...] = jnp.zeros_like(gains_ref)
    gains_ref[0:1, :] = grad_norm_gain
    for p in range(shards):
        pair = slice(p // 2 * 128, p // 2 * 128 + 128)
        left = jnp.broadcast_to(grad_attn_gain[:, pair], (8, 128))
        right = jnp.broadcast_to(fgain_ref[:, pair], (8, 128))
        if p % 2 == 0:
            both = jnp.where(lower_half((8, 128)), left, swap_halves(right))
        else:
            both = jnp.where(lower_half((8, 128)), swap_halves(left), right)
        gains_ref[1:2, pl.ds(p * 128, 128)] = both[0:1]


BACKWARD_LIMIT = 62 * 1024 * 1024

def place():
    dp, space = lax.axis_index("dp"), lax.axis_index("space")
    return {"x": lax.rem(dp, 2), "y": dp // 2, "z": space // 2, "core": lax.rem(space, 2)}


def peer(way, shift=1):
    at = place()
    if way == "x":
        return {"dp": 2 * at["y"] + 1 - at["x"]}
    if way == "y":
        return {"dp": 2 * (1 - at["y"]) + at["x"]}
    if way == "diagonal":
        return {"dp": 2 * (1 - at["y"]) + 1 - at["x"]}
    if way == "core":
        return {"space": 2 * at["z"] + 1 - at["core"]}
    if way == "z":
        return {"space": 2 * lax.rem(at["z"] + shift, 4) + at["core"]}
    return {"space": lax.rem(lax.axis_index("space") + shift, lax.axis_size("space"))}


def greet(peers):
    barrier = pltpu.get_barrier_semaphore()
    for one in peers:
        pl.semaphore_signal(barrier, inc=1, device_id=one, device_id_type=MESH)
    pl.semaphore_wait(barrier, len(peers))


class Wires:
    def __init__(self, send_sem, recv_sem):
        self.send_sem, self.recv_sem, self.used = send_sem, recv_sem, 0

    def copy(self, source, target, to):
        n = self.used
        self.used += 1
        return pltpu.make_async_remote_copy(
            src_ref=source,
            dst_ref=target,
            send_sem=self.send_sem.at[n],
            recv_sem=self.recv_sem.at[n],
            device_id=to,
            device_id_type=MESH,
        )


def rows_at(ref, start, count):
    return ref.at[:, pl.ds(start, count), :]


def first_cut(wires, share_ref, got_ref):
    at = place()
    quarter = share_ref.shape[1] // 4
    return [
        wires.copy(rows_at(share_ref, (1 - at["x"]) * quarter, quarter), got_ref.at[0], peer("x")),
        wires.copy(
            rows_at(share_ref, (3 - at["y"]) * quarter, quarter), got_ref.at[1], peer("y")
        ),
    ]


def own_quarters(share_ref, own_ref, sems):
    at = place()
    quarter = share_ref.shape[1] // 4
    starts = (at["x"] * quarter, (2 + at["y"]) * quarter)
    return [
        pltpu.make_async_copy(rows_at(share_ref, start, quarter), own_ref.at[n], sems[n])
        for n, start in enumerate(starts)
    ]


def first_add(own_ref, got_ref, sum_ref):
    for n in range(2):
        sum_ref[n] = (own_ref[n].astype(F32) + got_ref[n].astype(F32)).astype(BF)


def first_add_whole(share_ref, got_ref, sum_ref):
    at = place()
    quarter = share_ref.shape[1] // 4
    for n, start in enumerate((at["x"] * quarter, (2 + at["y"]) * quarter)):
        own = share_ref[:, pl.ds(pl.multiple_of(start, 16), quarter), :]
        sum_ref[n] = (own.astype(F32) + got_ref[n].astype(F32)).astype(BF)


def second_cut(wires, sum_ref, got_ref):
    at = place()
    eighth = sum_ref.shape[2] // 2
    return [
        wires.copy(
            rows_at(sum_ref.at[0], (1 - at["y"]) * eighth, eighth), got_ref.at[0], peer("y")
        ),
        wires.copy(
            rows_at(sum_ref.at[1], (1 - at["x"]) * eighth, eighth), got_ref.at[1], peer("x")
        ),
    ]


def second_add(sum_ref, got_ref, out_ref, base=0):
    at = place()
    eighth = sum_ref.shape[2] // 2
    for n, start in enumerate((at["y"] * eighth, at["x"] * eighth)):
        own = sum_ref[n, :, pl.ds(pl.multiple_of(start, 16), eighth), :]
        out_ref[:, pl.ds(base + n * eighth, eighth), :] = (
            own.astype(F32) + got_ref[n].astype(F32)
        ).astype(BF)


def z_send(wires, part_ref, got_ref):
    at = place()
    return [
        wires.copy(
            part_ref.at[lax.rem(at["z"] + shift, 4)], got_ref.at[shift - 1], peer("z", shift)
        )
        for shift in (1, 2, 3)
    ]


def z_add(own, got_ref):
    total = own.astype(F32)
    for n in range(3):
        total = total + got_ref[n].astype(F32)
    return total.astype(BF)


class Share:
    def __init__(self, wires, packed, own, refs, loads=()):
        self.packed, self.own, self.loads = packed, own, list(loads)
        self.got, self.sum, self.got2, self.part, self.gotz = refs
        self.copies = first_cut(wires, packed, self.got)
        self.copies2 = second_cut(wires, self.sum, self.got2)
        self.copiesz = z_send(wires, self.part, self.gotz)

    def start(self):
        start_all(self.loads + self.copies)

    def cut(self):
        wait_all(self.loads + self.copies)
        if self.own is None:
            first_add_whole(self.packed, self.got, self.sum)
        else:
            first_add(self.own, self.got, self.sum)
        start_all(self.copies2)

    def spread(self):
        wait_all(self.copies2)
        second_add(self.sum, self.got2, self.part)
        start_all(self.copiesz)

    def total(self):
        wait_all(self.copiesz)
        return z_add(self.part[place()["z"]], self.gotz)


def start_all(copies):
    for copy in copies:
        copy.start()
    return copies


def wait_all(copies):
    for copy in copies:
        copy.wait()


def sent_row(sent_ref, scr):
    spaces = sent_ref.shape[0]
    scr[...] = jnp.zeros_like(scr)
    scr[pl.ds(0, spaces), pl.ds(0, CAP)] = sent_ref[...].astype(F32)
    row = scr[0:1, :]
    for d in range(1, spaces):
        row = row + pltpu.roll(scr[d : d + 1, :], d * CAP, 1)
    return row


def pick_matrix(row, nodes):
    places = lax.broadcasted_iota(jnp.int32, (nodes, row.shape[1]), 0).astype(F32)
    return (places == row).astype(BF)


def prepare_kernel(
    ns_ref, nv_ref, sent_ref, vn_ref, we_ref, vout_ref, norms_ref, wnode_hbm,
    b_ref, p_ref, q_ref, ts_ref, tv_ref, vs_ref, vt_ref, vo_ref, mix_ref, wn_ref, pt_ref,
    wnode, row_scr, vt_scr, out_scr, in_scr, send_sem, recv_sem, load_sem,
):
    nodes = ns_ref.shape[0]
    table = ts_ref.shape[0]
    spaces = lax.axis_size("space")
    me = lax.axis_index("space")
    wires = Wires(send_sem, recv_sem)
    ring = [peer("group", shift) for shift in range(1, spaces)]
    load = pltpu.make_async_copy(wnode_hbm, wnode, load_sem)
    load.start()
    pick = pick_matrix(sent_row(sent_ref, row_scr), nodes)
    rows = lead_product(pick, ns_ref[...]).astype(BF)
    for d in range(spaces):
        out_scr[d, :, pl.ds(0, D_S)] = rows[d * CAP : (d + 1) * CAP]
    for c in range(3):
        rows = lead_product(pick, nv_ref[c]).astype(BF)
        for d in range(spaces):
            out_scr[d, :, pl.ds(D_S + c * D_V, D_V)] = rows[d * CAP : (d + 1) * CAP]
    greet(ring)
    copies = start_all(
        [
            wires.copy(out_scr.at[lax.rem(me + n + 1, spaces)], in_scr.at[me], ring[n])
            for n in range(spaces - 1)
        ]
    )
    in_scr[me] = out_scr[me]
    vs_ref[pl.ds(0, 512), :] = vn_ref[pl.ds(0, 512), :]
    vt_scr[...] = jnp.zeros_like(vt_scr)
    vt_scr[pl.ds(0, H_V + 1), :] = vn_ref[pl.ds(512, H_V + 1), :].astype(F32)
    row = lax.broadcasted_iota(jnp.int32, (H_P, D_V), 0)
    vt_ref[...] = jnp.where(row < H_V, pltpu.roll(vt_scr[...], H_P - 1, 0), 0.0).astype(BF)
    low = row[: H_P - 512]
    first = jnp.broadcast_to(vt_scr[0:1, :], low.shape)
    vs_ref[pl.ds(512, H_P - 512), :] = jnp.where(low == 0, first, 0.0).astype(BF)
    vo_ref[pl.ds(0, 512), :] = vout_ref[pl.ds(0, 512), :]
    first = jnp.broadcast_to(vout_ref[pl.ds(512, 1), :].astype(F32), low.shape)
    vo_ref[pl.ds(512, H_P - 512), :] = jnp.where(low == 0, first, 0.0).astype(BF)

    def project(parts, start):
        last = None
        for c in range(3):
            whole = product_back(parts[c], vs_ref[...])
            p_ref[c, pl.ds(start, parts[c].shape[0]), :] = whole.astype(BF)
            tail = whole[:, 512:]
            last = tail if last is None else last + pltpu.roll(tail, c, 1)
        pt_ref[pl.ds(start, parts[0].shape[0]), :] = last.astype(BF)

    project([nv_ref[c] for c in range(3)], 0)
    for c in range(3):
        q_ref[c] = product_back(nv_ref[c], vt_ref[...])
        tv_ref[c, pl.ds(0, nodes), :] = nv_ref[c]
    ts_ref[pl.ds(0, nodes), :] = ns_ref[...]
    first = jnp.broadcast_to(norms_ref[pl.ds(512, 1), :].astype(F32), (16, D_S))
    row = lax.broadcasted_iota(jnp.int32, (16, D_S), 0)
    wn_ref[pl.ds(0, 512), :] = norms_ref[pl.ds(0, 512), :]
    wn_ref[pl.ds(512, 16), :] = jnp.where(row == 0, first, 0.0).astype(BF)
    wn_ref[pl.ds(528, D_E), :] = we_ref[...]
    wn_ref[pl.ds(528 + D_E, H_P - 528 - D_E), :] = jnp.zeros((H_P - 528 - D_E, D_S), BF)
    mix_ref[pl.ds(table, H_P), :] = wn_ref[...]
    load.wait()
    b_ref[...] = product(ns_ref[...], wnode[:, pl.ds(D_S, D_S)])
    mix_ref[pl.ds(0, nodes), :] = product(ns_ref[...], wnode[:, pl.ds(0, D_S)]).astype(BF)
    wait_all(copies)
    got = in_scr[...].reshape(spaces * CAP, D_S + 3 * D_V)
    ts_ref[pl.ds(nodes, table - nodes), :] = got[:, :D_S]
    mix_ref[pl.ds(nodes, table - nodes), :] = product(
        got[:, :D_S], wnode[:, pl.ds(0, D_S)]
    ).astype(BF)
    parts = [got[:, D_S + c * D_V : D_S + (c + 1) * D_V] for c in range(3)]
    project(parts, nodes)
    for c in range(3):
        tv_ref[c, pl.ds(nodes, table - nodes), :] = parts[c]


def middle_kernel(
    ns_ref, nv_ref, as_ref, av_ref, gains_in, fv_ref, fs_ref, fu_ref, we_ref, wq_ref, id_ref, cot_ref, wo_hbm, wu_hbm, wd_hbm, ts_hbm, ns_hbm,
    out_ref, gsone_ref, gvone_ref, gains_ref, a_ref, m_ref, e_ref, tso_hbm, nso_hbm,
    s1, v1, ffh, ffp, ffu, v2, sz, fac_node, fac_node_o, heads_out, heads_in,
    probs, att, att_out, att_in, wo_ref, wu_ref, wd_ref, gatt, gatt_in, gs1, fgain,
    fac_feed, fac_feed_o, gs_scr, ghead, ghead_in, fac_back, fac_back_o,
    first, first_got, first_sum, first_got2, tall_scr, low_scr,
    send_sem, recv_sem, load_sem,
):
    spaces = lax.axis_size("space")
    quads = spaces // 2
    me = lax.axis_index("space")
    ng_ref = gains_in.at[:, pl.ds(0, D_S)]
    ag_ref = gains_in.at[:, pl.ds(D_S, D_MODEL)]
    fg_ref = gains_in.at[:, pl.ds(D_S + D_MODEL, D_MODEL)]
    wires = Wires(send_sem, recv_sem)
    ring = [peer("group", shift) for shift in range(1, spaces)]

    def exchange(source, target, start=0, count=None):
        rows = pl.ds(start, source.shape[1] if count is None else count)
        return [
            wires.copy(source.at[lax.rem(me + n + 1, spaces), rows], target.at[me, rows], ring[n])
            for n in range(spaces - 1)
        ]

    def keep(source, target):
        target[me] = source[me]

    loads = [
        pltpu.make_async_copy(source, target, load_sem.at[n])
        for n, (source, target) in enumerate(
            ((wo_hbm, wo_ref), (wu_hbm, wu_ref), (wd_hbm, wd_ref))
        )
    ]
    start_all(loads)
    greet(ring + [peer("x"), peer("y")])
    swaps = start_all(
        [wires.copy(ts_hbm, tso_hbm, peer("core")), wires.copy(ns_hbm, nso_hbm, peer("core"))]
    )
    nodes = ns_ref.shape[0]
    key_copies = exchange(heads_out, heads_in, 0, nodes)
    value_copies = exchange(heads_out, heads_in, nodes, nodes // 2)
    grad_key_copies = exchange(ghead, ghead_in, 0, nodes)
    grad_value_copies = exchange(ghead, ghead_in, nodes, nodes // 2)
    start_later = lambda copies: functools.partial(start_all, copies)
    node_forward_kernel(
        ns_ref, nv_ref, as_ref, av_ref, ng_ref, fv_ref, fs_ref, fu_ref, we_ref, ag_ref, wq_ref,
        s1, v1, ffh, ffp, ffu, v2, sz, fac_node, heads_out, start_later(key_copies),
    )
    start_all(value_copies)
    swaps += start_all([wires.copy(fac_node, fac_node_o, peer("core"))])
    keep(heads_out, heads_in)
    wait_all(key_copies)
    attend_kernel(heads_in, id_ref, probs, att, att_out, functools.partial(wait_all, value_copies))
    copies = start_all(exchange(att_out, att_in))
    keep(att_out, att_in)
    wait_all(loads)
    wait_all(copies)
    up_cols, rest_cols = pl.ds(0, AT_ATT), pl.ds(AT_ATT, FAC_FEED - AT_ATT)
    feed_swap = wires.copy(fac_feed.at[:, up_cols], fac_feed_o.at[:, up_cols], peer("core"))
    feed_kernel(
        att_in, sz, wo_ref, fg_ref, wu_ref, wd_ref, cot_ref, out_ref, gatt, gs1, fgain, fac_feed,
        feed_swap.start,
    )
    copies = start_all(exchange(gatt, gatt_in))
    swaps += start_all(
        [wires.copy(fac_feed.at[:, rest_cols], fac_feed_o.at[:, rest_cols], peer("core"))]
    )
    keep(gatt, gatt_in)
    feed_swap.wait()
    feed_grads_kernel(fac_feed, fac_feed_o, first)
    cuts = start_all(first_cut(wires, first, first_got))
    wait_all(copies)
    attend_backward_kernel(
        heads_in, probs, att, gatt_in, ghead, gs_scr, start_later(grad_value_copies)
    )
    copies = start_all(grad_key_copies) + grad_value_copies
    keep(ghead, ghead_in)
    wait_all(cuts)
    first_add_whole(first, first_got, first_sum)
    cuts = start_all(second_cut(wires, first_sum, first_got2))
    wait_all(copies)
    qkv_cols, other_cols = pl.ds(0, AT_STREAM), pl.ds(AT_STREAM, FAC_BACK - AT_STREAM)
    qkv_swap = wires.copy(fac_back.at[:, qkv_cols], fac_back_o.at[:, qkv_cols], peer("core"))

    node_backward_kernel(
        ghead_in, gs1, s1, v1, ffh, ffp, ffu, v2, sz,
        ng_ref, fv_ref, fs_ref, fu_ref, we_ref, ag_ref, wq_ref, fgain,
        gsone_ref, gvone_ref, gains_ref, fac_back, qkv_swap.start,
    )
    swap = start_all(
        [wires.copy(fac_back.at[:, other_cols], fac_back_o.at[:, other_cols], peer("core"))]
    )
    qkv_swap.wait()
    wait_all(swaps)
    attention_grads(fac_node, fac_node_o, fac_back, fac_back_o, fac_feed, fac_feed_o, a_ref)
    wait_all(cuts)
    second_add(first_sum, first_got2, e_ref)
    wait_all(swap)
    node_grads(fac_node, fac_node_o, fac_back, fac_back_o, m_ref, tall_scr, low_scr)


def middle(vmem_operands, hbm_operands, table_s, node_scalar, quads):
    nodes = node_scalar.shape[0]
    spaces = 2 * quads
    count = spaces * nodes
    hbm = pl.BlockSpec(memory_space=pl.ANY)
    vmem = pl.BlockSpec(memory_space=pltpu.VMEM)
    operands = tuple(vmem_operands) + tuple(hbm_operands) + (table_s, node_scalar)
    bits = lambda *shape: pltpu.VMEM(shape, BF)
    wide = lambda *shape: pltpu.VMEM(shape, F32)
    packed = (spaces, nodes + nodes // 2, 128)
    small = (spaces, nodes // 2, 128)
    outs = [
        ((nodes, D_MODEL), BF),
        ((nodes, D_S), F32),
        ((3, nodes, D_V), F32),
        ((8, D_S), F32),
        ((quads, ROWS_A, 512), BF),
        ((quads, ROWS_N, 512), BF),
        ((quads, ROWS_E, 512), BF),
        (table_s.shape, BF),
        (node_scalar.shape, BF),
    ]
    wires = 6 * (spaces - 1) + 12
    return pl.pallas_call(
        middle_kernel,
        out_shape=[jax.ShapeDtypeStruct(shape, kind) for shape, kind in outs],
        in_specs=[vmem] * len(vmem_operands) + [hbm] * (len(hbm_operands) + 2),
        out_specs=[vmem] * 7 + [hbm] * 2,
        scratch_shapes=[
            wide(nodes, D_S), wide(3, nodes, D_V), wide(3, nodes, D_V), wide(nodes, D_S),
            wide(3, nodes, D_V), wide(3, nodes, D_V), wide(nodes, D_MODEL),
            bits(nodes, FAC_NODE), bits(nodes, FAC_NODE), bits(*packed), bits(*packed),
            bits(count, count), wide(count, 128), bits(*small), bits(*small),
        ]
        + [bits(*one.shape) for one in hbm_operands]
        + [
            bits(*small), bits(*small), wide(nodes, D_MODEL), wide(1, D_MODEL),
            bits(nodes, FAC_FEED), bits(nodes, FAC_FEED), bits(count, count),
            bits(*packed), bits(*packed), bits(nodes, FAC_BACK), bits(nodes, FAC_BACK),
            bits(quads, ROWS_F, 512), bits(2, quads, ROWS_F // 4, 512),
            bits(2, quads, ROWS_F // 4, 512), bits(2, quads, ROWS_F // 8, 512),
            bits(D_S + D_V, 512), bits(D_V, 512),
            pltpu.SemaphoreType.DMA((wires,)),
            pltpu.SemaphoreType.DMA((wires,)),
            pltpu.SemaphoreType.DMA((len(hbm_operands),)),
        ],
        compiler_params=pltpu.CompilerParams(
            collective_id=0, has_side_effects=True, vmem_limit_bytes=VMEM_LIMIT
        ),
        name="middle",
    )(*operands)


def slot_rows(rows_scr, first_slot, nodes):
    return jnp.concatenate([rows_scr[pl.ds(first_slot + k, 1), :] for k in range(GROUP)], 1)


def one_hot_rows(rows_scr, first_slot, table, nodes):
    row = slot_rows(rows_scr, first_slot, nodes)
    return (lax.broadcasted_iota(jnp.int32, (table, row.shape[1]), 0).astype(F32) == row).astype(BF)


def keep_rows(ref, rows_scr):
    rows_scr[pl.ds(0, ref.shape[0]), :] = ref[...].astype(F32)


def backward_kernel(
    near_ref, ev_ref, lx_ref, ds_ref, h_ref, z_ref, gsone_ref, wn_ref, gvone_ref, vo_ref, tv_ref,
    nv_ref, vs_ref, vt_ref, gains_ref,
    ts_hbm, ns_hbm, wnode_hbm, tso_hbm, nso_hbm, e_hbm, a_hbm, n_hbm,
    gscal_ref, gvec_ref, plane_hbm, got_hbm,
    near_scr, ev_scr, ga_ref, gw_ref, gb_ref, pre_scr, gp_ref, gq_ref, gvo_ref, up_scr,
    gh_scr, ts_ref, ns_ref, wnode_ref, tso_ref, nso_ref,
    grads_scr, grads_got, mix_scr, mix_got, rest_scr, rest_got, e_own, e_got, a_own, n_own,
    s_scr, b_scr, v_got, backs_scr, backv_scr, fin_scr,
    send_sem, recv_sem, load_sem, *share_refs,
):
    nodes = gsone_ref.shape[0]
    table = ts_ref.shape[0]
    rows = GROUP * nodes
    spaces = lax.axis_size("space")
    quads = spaces // 2
    step = pl.program_id(0)
    half = NEIGH // GROUP
    last = 2 * half - 1
    first_slot = lax.rem(step, half) * GROUP
    at = place()
    core = at["core"]
    me = lax.axis_index("space")
    mine = 2 * at["x"] + at["y"]
    ring = [peer("group", shift) for shift in range(1, spaces)]
    plane = [peer("x"), peer("y"), peer("diagonal")]

    wires = Wires(send_sem, recv_sem)
    own_copy = lambda n, source, target: pltpu.make_async_copy(source, target, load_sem.at[n])
    quarters = lambda share_ref, own_ref, n: own_quarters(
        share_ref, own_ref, [load_sem.at[n], load_sem.at[n + 1]]
    )
    refs = [share_refs[n : n + 5] for n in range(0, len(share_refs), 5)]
    e_copiesz = z_send(wires, e_hbm, e_got)
    share_a = Share(wires, a_hbm, a_own, refs[0], quarters(a_hbm, a_own, 9))
    share_n = Share(wires, n_hbm, n_own, refs[1], quarters(n_hbm, n_own, 11))
    share_s = Share(wires, s_scr, None, refs[2])
    share_b = Share(wires, b_scr, None, refs[3])
    v_scr = s_scr.at[:, pl.ds(0, ROWS_V), :]
    share_v = Share(wires, v_scr, None, refs[4])
    pair_copies = [
        wires.copy(source, target, peer("core"))
        for source, target in ((grads_scr, grads_got), (mix_scr, mix_got), (rest_scr, rest_got))
    ]
    v_pair = n_own
    v_copies = [wires.copy(v_pair.at[1 - core], v_got, peer("core"))]
    bounds = [0]
    for count in ALL_ROWS:
        bounds.append(bounds[-1] + count // 4)
    rows_e, rows_a, rows_n, rows_s, rows_b, rows_v = [
        pl.ds(lo, hi - lo) for lo, hi in zip(bounds, bounds[1:])
    ]
    batches = [(bounds[0], bounds[3]), (bounds[3], bounds[4]), (bounds[4], bounds[5])]
    rounds = [
        [
            wires.copy(fin_scr.at[pl.ds(lo, hi - lo), :], plane_hbm.at[mine, pl.ds(lo, hi - lo), :], to)
            for to in plane[:2]
        ]
        for lo, hi in batches
    ]
    relays = []
    over_x, over_y = 2 * (1 - at["x"]) + at["y"], 2 * at["x"] + 1 - at["y"]
    for lo, hi in batches:
        middle_row = (lo + hi) // 2
        upper, lower = pl.ds(lo, middle_row - lo), pl.ds(middle_row, hi - middle_row)
        relays.append(
            [
                wires.copy(plane_hbm.at[over_x, upper, :], plane_hbm.at[over_x, upper, :], plane[1]),
                wires.copy(plane_hbm.at[over_y, lower, :], plane_hbm.at[over_y, lower, :], plane[0]),
            ]
        )
    last_round = [
        wires.copy(fin_scr.at[rows_v, :], plane_hbm.at[mine, rows_v, :], to) for to in plane
    ]
    back_scalar, back_vector = pl.ds(0, D_S), pl.ds(D_S, 3 * D_V)
    scalar_copies = [
        wires.copy(
            backs_scr.at[lax.rem(me + n + 1, spaces)], got_hbm.at[me, :, back_scalar], ring[n]
        )
        for n in range(spaces - 1)
    ]
    vector_copies = [
        wires.copy(
            backv_scr.at[lax.rem(me + n + 1, spaces)], got_hbm.at[me, :, back_vector], ring[n]
        )
        for n in range(spaces - 1)
    ]
    e_load = own_copy(0, e_hbm.at[at["z"]], e_own)
    loads = [
        own_copy(1 + n, source, target)
        for n, (source, target) in enumerate(
            (
                (ts_hbm, ts_ref), (ns_hbm, ns_ref), (wnode_hbm.at[:, pl.ds(0, D_S)], wnode_ref),
                (tso_hbm, tso_ref),
                (nso_hbm, nso_ref),
            )
        )
    ]
    own_scalar = own_copy(6, backs_scr.at[me], got_hbm.at[me, :, back_scalar])
    own_vector = own_copy(7, backv_scr.at[me], got_hbm.at[me, :, back_vector])
    own_plane = own_copy(8, fin_scr, plane_hbm.at[mine])
    target_load = own_copy(13, wnode_hbm.at[:, pl.ds(D_S, D_S)], wnode_ref)

    def early_total():
        e_load.wait()
        wait_all(e_copiesz)
        fin_scr[rows_e, :] = z_add(e_own[...], e_got)

    def middle_total():
        fin_scr[rows_a, :] = share_a.total()
        fin_scr[rows_n, :] = share_n.total()
        start_all(rounds[0])

    def source_total():
        fin_scr[rows_s, :] = share_s.total()
        start_all(rounds[1])

    def relay(n):
        wait_all(rounds[n])
        start_all(relays[n])

    schedule = {
        (4, 0): [share_a.cut],
        (7, 0): [share_a.spread],
        (7, 1): [share_n.spread],
        (9, 0): [share_s.cut],
        (9, 1): [early_total],
        (10, 0): [share_b.cut],
        (10, 1): [share_s.spread, middle_total],
        (11, 1): [share_b.spread, source_total],
    }

    def carry_on(part):
        for (at_step, at_part), actions in schedule.items():
            if at_part == part:

                @pl.when(step == at_step)
                def _():
                    for action in actions:
                        action()

    @pl.when(step == 0)
    def _():
        greet(ring + plane)
        share_a.start()
        share_n.start()
        start_all(e_copiesz)
        start_all([e_load] + loads)
        keep_rows(near_ref, near_scr)
        for c in range(3):
            keep_rows(ev_ref.at[c], ev_scr.at[c])
        for ref in (ga_ref, gw_ref, gb_ref, gp_ref, gq_ref, gvo_ref):
            ref[...] = jnp.zeros_like(ref)

    carry_on(0)

    @pl.when(step < half)
    def _():
        for start in range(0, D_S, 256):
            cols = pl.ds(start, 256)
            for first in range(0, nodes, ROW_TILE):
                part = pl.ds(first, ROW_TILE)
                share = gsone_ref[part, cols] * (1.0 / NEIGH)
                acc = None
                for k in range(GROUP):
                    g = (ds_ref[k, part, cols].astype(F32) * share).astype(BF)
                    pre_scr[step, pl.ds(k * nodes + first, ROW_TILE), cols] = g
                    g = g.astype(F32)
                    acc = g if acc is None else acc + g
                gb_ref[part, cols] += acc
        one_hot = one_hot_rows(near_scr, first_slot, table, nodes)
        grad_pre = pre_scr[step]
        ga_ref[...] += product(one_hot, grad_pre)
        lx = lx_ref[...].reshape(rows, H_P)
        gw_ref[...] += lead_product(lx, grad_pre)
    @pl.when(step == half - 1)
    def _():
        grads_scr[pl.ds(0, table), :] = ga_ref[...].astype(BF)
        grads_scr[pl.ds(table, nodes), :] = gb_ref[...].astype(BF)
        for z in range(quads):
            away = pl.ds(pl.multiple_of((2 * z + 1 - core) * 128, 128), 128)
            for r in range(4):
                mix_scr[z, :, pl.ds(r * 128, 128)] = gw_ref[pl.ds(r * 128, 128), away].astype(BF)
            rest_scr[z] = gw_ref[pl.ds(512, 64), away].astype(BF)
        start_all(pair_copies)
        wait_all(loads)
        ga = grads_scr[pl.ds(0, table), :]
        projected = product_back(ga, wnode_ref[...])
        target_load.start()
        gscal_ref[...] = gsone_ref[...] + projected[:nodes]
        for d in range(spaces):
            backs_scr[d] = projected[nodes + d * CAP : nodes + (d + 1) * CAP].astype(BF)
        start_all(scalar_copies)
        own_scalar.start()

    @pl.when(step == half)
    def _():
        share_n.cut()

    @pl.when(step == half + 1)
    def _():
        wait_all(pair_copies)
        grad_rows = pl.ds(0, table), pl.ds(table, nodes)
        for side, (left, lefto, pack) in enumerate(
            ((ts_ref, tso_ref, s_scr), (ns_ref, nso_ref, b_scr))
        ):
            right, righto = grads_scr[grad_rows[side], :], grads_got[grad_rows[side], :]
            for z in range(quads):
                own = pl.ds(pl.multiple_of((2 * z + core) * 128, 128), 128)
                block = lead_product(left[:, own], right) + lead_product(lefto[:, own], righto)
                block = block.astype(BF)
                for n in range(2):
                    pack[z, pl.ds(n * 128, 128), :] = block[:, n * 512 : (n + 1) * 512]
            if side == 0:
                share_s.start()
        for z in range(quads):
            own = pl.ds(pl.multiple_of((2 * z + core) * 128, 128), 128)
            for r in range(4):
                lanes = pl.ds(r * 128, 128)
                b_scr[z, pl.ds(256, 128), lanes] = (
                    gw_ref[pl.ds(r * 128, 128), own] + mix_got[z, :, lanes].astype(F32)
                ).astype(BF)
        share_b.start()
        target_load.wait()
        gscal_ref[...] += product_back(grads_scr[pl.ds(table, nodes), :], wnode_ref[...])

    @pl.when(step >= half)
    def _():
        for first in range(0, nodes, ROW_TILE):
            part = pl.ds(first, ROW_TILE)
            share = [gvone_ref[c, part, :] * (1.0 / NEIGH) for c in range(3)]
            for k in range(GROUP):
                z = [z_ref[k, c, part, :].astype(F32) for c in range(3)]
                power = power_of(z) + 1.0
                inverse = lax.rsqrt(power)
                s = sigmoid(power * inverse)
                dot = z[0] * share[0] + z[1] * share[1] + z[2] * share[2]
                factor = dot * inverse * (s * (1.0 - s))
                for c in range(3):
                    up_scr[c, pl.ds(k * nodes + first, ROW_TILE), :] = (
                        share[c] * s + z[c] * factor
                    ).astype(BF)
        for start, width in LANE_BLOCKS:
            cols = pl.ds(start, width)
            grad_length = product_back(pre_scr[step - half], wn_ref[cols, :])
            grad_direct = [product_back(up_scr[c], vo_ref[cols, :]) for c in range(3)]
            for first in range(0, nodes, ROW_TILE):
                part = pl.ds(first, ROW_TILE)
                acc = [None] * 3
                for k in range(GROUP):
                    row = k * nodes + first
                    ratio = grad_length[row : row + ROW_TILE] * pl.reciprocal(
                        lx_ref[k, part, cols].astype(F32), approx=True
                    )
                    if start == 512:
                        lane = lax.broadcasted_iota(jnp.int32, (ROW_TILE, width), 1)
                        ratio = jnp.where(lane == 0, ratio, 0.0)
                    for c in range(3):
                        g = grad_direct[c][row : row + ROW_TILE] + ratio * h_ref[
                            k, c, part, cols
                        ].astype(F32)
                        gh_scr[c, pl.ds(row, ROW_TILE), cols] = g.astype(BF)
                        acc[c] = g if acc[c] is None else acc[c] + g
                for c in range(3):
                    gq_ref[c, part, cols] += acc[c]
    carry_on(1)

    @pl.when(step >= half)
    def _():
        one_hot = one_hot_rows(near_scr, first_slot, table, nodes)
        for c in range(3):
            evr = jnp.broadcast_to(slot_rows(ev_scr.at[c], first_slot, nodes), (16, rows))
            lead = jnp.concatenate([one_hot, evr.astype(BF)], axis=0)
            gp_ref[c] += product(lead, gh_scr[c])
            gvo_ref[...] += lead_product(up_scr[c], h_ref[:, c, :, :].reshape(rows, H_P))

    @pl.when(step == last)
    def _():
        tall = D_V // spaces
        gp = [gp_ref[c, pl.ds(0, table), :].astype(BF) for c in range(3)]
        gq = [gq_ref[c].astype(BF) for c in range(3)]
        grads = []
        for lead_ref, right in ((tv_ref, gp), (nv_ref, gq)):
            total = None
            for c in range(3):
                one = lead_product(lead_ref[c], right[c])
                total = one if total is None else total + one
            grads.append(total)
        grads.append(gvo_ref[...])
        lane = lax.broadcasted_iota(jnp.int32, (D_V, 128), 1)
        tails = jnp.zeros((D_V, 128), F32)
        for n, grad in enumerate(grads):
            for p in range(spaces):
                v_pair[p % 2, p // 2, pl.ds(n * tall, tall), :] = grad[
                    p * tall : (p + 1) * tall, :512
                ].astype(BF)
            tails = tails + jnp.where(
                lane == n, jnp.broadcast_to(grad[:, 512:513], (D_V, 128)), 0.0
            )
        tails = tails.astype(BF)
        vedge = gp_ref[0, pl.ds(table, 8), :] + gp_ref[1, pl.ds(table, 8), :]
        vedge = vedge + gp_ref[2, pl.ds(table, 8), :]
        row = lax.broadcasted_iota(jnp.int32, (tall, 128), 0)
        below = pl.ds(3 * tall, tall)
        for p in range(spaces):
            own = pl.ds(p * 128, 128)
            rest = gw_ref[pl.ds(512, 64), own] + rest_got[p // 2].astype(F32)
            rest = jnp.where(core == p % 2, rest, 0.0)
            v_pair[p % 2, p // 2, below, pl.ds(0, 128)] = tails[p * tall : (p + 1) * tall]
            v_pair[p % 2, p // 2, below, pl.ds(128, 128)] = rest[16 : 16 + tall].astype(BF)
            extra = jnp.where(row == 0, jnp.broadcast_to(rest[0:1], (tall, 128)), 0.0)
            for n in range(5):
                piece = jnp.broadcast_to(vedge[0:1, n * 128 : (n + 1) * 128], (tall, 128))
                extra = jnp.where(row == 1 + n, piece, extra)
            for n in range(2):
                piece = jnp.broadcast_to(
                    gains_ref[n : n + 1, p * 128 : (p + 1) * 128], (tall, 128)
                )
                extra = jnp.where(row == 6 + n, piece, extra)
            v_pair[p % 2, p // 2, below, pl.ds(256, 128)] = extra.astype(BF)
            v_pair[p % 2, p // 2, below, pl.ds(384, 128)] = jnp.zeros((tall, 128), BF)
        start_all(v_copies)
        relay(0)
        wait_all(v_copies)
        v_scr[...] = (v_pair[core].astype(F32) + v_got[...].astype(F32)).astype(BF)
        share_v.start()
        for c in range(3):
            projected = product(gp[c], vs_ref[...])
            gvec_ref[c] = gvone_ref[c] + product(gq[c], vt_ref[...]) + projected[:nodes]
            for d in range(spaces):
                backv_scr[d, :, pl.ds(c * D_V, D_V)] = projected[
                    nodes + d * CAP : nodes + (d + 1) * CAP
                ].astype(BF)
        start_all(vector_copies)
        own_vector.start()
        share_v.cut()
        fin_scr[rows_b, :] = share_b.total()
        start_all(rounds[2])
        share_v.spread()
        relay(1)
        relay(2)
        fin_scr[rows_v, :] = share_v.total()
        start_all(last_round)
        own_plane.start()
        for copies in relays:
            wait_all(copies)
        wait_all(scalar_copies)
        wait_all(vector_copies)
        own_scalar.wait()
        own_vector.wait()
        own_plane.wait()
        wait_all(last_round)


def backward(blocked, whole_operands, hbm_operands):
    near, ev, lx, dsilu, hidden, update = blocked
    ts, ns, w_node = hbm_operands[:3]
    nodes = ns.shape[0]
    table = ts.shape[0]
    quads = hbm_operands[-1].shape[0]
    spaces = 2 * quads
    rows = GROUP * nodes
    half = NEIGH // GROUP
    once = pl.Buffered(1)
    whole = lambda shape: pl.BlockSpec(shape, lambda g: (0,) * len(shape), pipeline_mode=once)
    early = lambda *shape: pl.BlockSpec(
        (GROUP,) + shape, lambda g: (jnp.minimum(g, half - 1),) + (0,) * len(shape)
    )
    late = lambda *shape: pl.BlockSpec(
        (GROUP,) + shape, lambda g: (jnp.maximum(g - half, 0),) + (0,) * len(shape)
    )
    both = lambda *shape: pl.BlockSpec(
        (GROUP,) + shape, lambda g: (lax.rem(g, half),) + (0,) * len(shape)
    )
    hbm = pl.BlockSpec(memory_space=pl.ANY)
    outs = [
        ((nodes, D_S), F32),
        ((3, nodes, D_V), F32),
        ((4, sum(ALL_ROWS) // 4, 512), BF),
        ((spaces, CAP, D_S + 3 * D_V), BF),
    ]
    bits = lambda *shape: pltpu.VMEM(shape, BF)
    wide = lambda *shape: pltpu.VMEM(shape, F32)
    grads = (table + nodes, D_S)
    pieces = lambda count: [
        bits(2, quads, count // 4, 512), bits(2, quads, count // 4, 512),
        bits(2, quads, count // 8, 512), bits(quads, count // 4, 512), bits(3, count // 4, 512),
    ]
    wires = 57 + 2 * (spaces - 1)
    return pl.pallas_call(
        backward_kernel,
        grid=(2 * half,),
        in_specs=[
            whole(near.shape),
            whole(ev.shape),
            both(nodes, H_P),
            early(nodes, D_S),
            late(3, nodes, H_P),
            late(3, nodes, D_V),
        ]
        + [whole(one.shape) for one in whole_operands]
        + [hbm] * len(hbm_operands),
        out_specs=[whole(outs[0][0]), whole(outs[1][0]), hbm, hbm],
        out_shape=[jax.ShapeDtypeStruct(shape, kind) for shape, kind in outs],
        scratch_shapes=[
            wide(32, 128), wide(3, 32, 128),
            wide(table, D_S), wide(H_P, D_S), wide(nodes, D_S), bits(half, rows, D_S),
            wide(3, table + 16, H_P), wide(3, nodes, H_P), wide(D_V, H_P), bits(3, rows, D_V),
            bits(3, rows, H_P),
        ]
        + [
            bits(*(one.shape if one is not w_node else (D_S, D_S))) for one in hbm_operands[:5]
        ]
        + [
            bits(*grads), bits(*grads), bits(quads, 128, 512), bits(quads, 128, 512),
            bits(quads, 64, 128), bits(quads, 64, 128), bits(ROWS_E, 512), bits(3, ROWS_E, 512),
            bits(2, quads, ROWS_A // 4, 512), bits(2, quads, ROWS_N // 4, 512),
            bits(quads, ROWS_S, 512), bits(quads, ROWS_B, 512),
            bits(quads, ROWS_V, 512),
            bits(spaces, CAP, D_S), bits(spaces, CAP, 3 * D_V), bits(sum(ALL_ROWS) // 4, 512),
            pltpu.SemaphoreType.DMA((wires,)),
            pltpu.SemaphoreType.DMA((wires,)),
            pltpu.SemaphoreType.DMA((14,)),
        ]
        + sum([pieces(count) for count in ALL_ROWS[1:]], []),
        compiler_params=pltpu.CompilerParams(
            collective_id=1, has_side_effects=True, vmem_limit_bytes=BACKWARD_LIMIT
        ),
        name="backward",
    )(*blocked, *whole_operands, *hbm_operands)


def finish_kernel(
    plane_ref, got_ref, sent_ref, gscal_ref, gvec_ref, stream_ref,
    gs_ref, gv_ref, node_ref, edge_ref, norms_ref, vnode_ref, vedge_ref, vout_ref, ffv_ref, ffs_ref,
    ffu_ref, embed_ref, qkv_ref, out_ref, up_ref, down_ref, ngain_ref, again_ref, fgain_ref,
    stream_out_ref, row_scr, sent_scr,
):
    base = 0
    for rows in ALL_ROWS:
        eighth = rows // 8
        for half, order in enumerate(((0, 1, 2, 3), (0, 2, 1, 3))):
            for n, q in enumerate(order):
                row_scr[pl.ds(4 * base + (4 * half + n) * eighth, eighth), :] = plane_ref[
                    q, pl.ds(base + half * eighth, eighth), :
                ]
        base += rows // 4

    def take(start, rows, lane=0, width=512):
        return row_scr[pl.ds(start, rows), pl.ds(lane, width)].astype(F32)

    at = 0
    down_ref[...] = take(at, 256)
    for n in range(4):
        up_ref[:, pl.ds(n * 512, 512)] = take(at + 256 + n * 64, 64)
    at += ROWS_F
    for n in range(3):
        qkv_ref[:, pl.ds(n * 512, 512)] = take(at + n * 64, 64)
    out_ref[...] = take(at + 192, 64)
    at += ROWS_A
    embed_ref[...] = take(at, 160)
    for n in range(2):
        ffs_ref[:, pl.ds(n * 512, 512)] = take(at + 160 + n * 160, 160)
    ffv_ref[...] = take(at + 480, 32, 0, 256)
    ffu_ref[...] = take(at + 480, 32, 256, 256)
    at += ROWS_N
    for n in range(4):
        node_ref[:, pl.ds(n * 512, 512)] = take(at + n * 128, 128)
        norms_ref[pl.ds(n * 128, 128), :] = take(at + 512, 128, n * 128, 128)
    at += ROWS_S + ROWS_B
    tails = take(at + 96, 32, 0, 128)
    edge_ref[...] = take(at + 96, 32, 128, 128)
    extra = take(at + 96, 32, 256, 128)
    norms_ref[pl.ds(512, 1), :] = extra[0:1]
    for n in range(5):
        width = min(128, H_V - n * 128)
        vedge_ref[:, pl.ds(n * 128, width)] = extra[1 + n : 2 + n, :width]
    ngain_ref[...] = extra[6]
    again_ref[...] = extra[7, :64]
    fgain_ref[...] = extra[7, 64:]
    vnode_ref[:, pl.ds(0, 512)] = take(at, 32)
    wide = jnp.concatenate([take(at + 32, 32), jnp.zeros((32, 128), F32)], 1)
    lane = lax.broadcasted_iota(jnp.int32, (32, 640), 1)
    wide = pltpu.roll(wide, 1, 1)
    wide = jnp.where(lane == 0, tails[:, 0:1], wide)
    wide = jnp.where(lane == 513, tails[:, 1:2], wide)
    vnode_ref[:, pl.ds(512, 514)] = wide[:, :514]
    vout_ref[:, pl.ds(0, 512)] = take(at + 64, 32)
    vout_ref[:, pl.ds(512, 1)] = tails[:, 2:3]
    stream_out_ref[...] = stream_ref[...]
    nodes = gscal_ref.shape[0]
    slots = got_ref.shape[0] * got_ref.shape[1]
    got = got_ref[...].reshape(slots, D_S + 3 * D_V)
    pick = pick_matrix(sent_row(sent_ref, sent_scr), nodes)
    added = product(pick, got)
    gs_ref[...] = (gscal_ref[...] + added[:, :D_S]).astype(BF)
    for c in range(3):
        gv_ref[c] = (
            gvec_ref[c] + added[:, D_S + c * D_V : D_S + (c + 1) * D_V]
        ).astype(BF)


def finish(plane, got, sent, gscal, gvec, stream):
    nodes = gscal.shape[0]
    outs = [
        ((nodes, D_S), BF),
        ((3, nodes, D_V), BF),
        ((128, 2048), F32),
        ((32, 128), F32),
        ((513, 128), F32),
        ((32, 1026), F32),
        ((1, 513), F32),
        ((32, 513), F32),
        ((32, 256), F32),
        ((160, 1024), F32),
        ((32, 256), F32),
        ((160, 512), F32),
        ((64, 1536), F32),
        ((64, 512), F32),
        ((64, 2048), F32),
        ((256, 512), F32),
        ((128,), F32),
        ((64,), F32),
        ((64,), F32),
        (stream.shape, BF),
    ]
    return pl.pallas_call(
        finish_kernel,
        out_shape=[jax.ShapeDtypeStruct(shape, kind) for shape, kind in outs],
        scratch_shapes=[
            pltpu.VMEM((sum(ALL_ROWS), 512), BF),
            pltpu.VMEM((8, 128), F32),
        ],
        compiler_params=pltpu.CompilerParams(vmem_limit_bytes=VMEM_LIMIT),
        name="finish",
    )(plane, got, sent, gscal, gvec, stream)


def pad_to(values, size, axis):
    pads = [(0, 0)] * values.ndim
    pads[axis] = (0, size - values.shape[axis])
    return jnp.pad(values, pads)


def fold(blocks, width=512):
    shards, rows, columns = blocks.shape
    parts = columns // width
    return jnp.moveaxis(blocks.reshape(shards, rows, parts, width), 2, 1).reshape(
        shards, parts * rows, width
    )


def unfold(rows_in, rows, columns, width=512):
    parts = columns // width
    return jnp.moveaxis(rows_in.reshape(parts, rows, width), 0, 1).reshape(rows, columns)


def body(
    node_scalar, node_vector, edge_scalar, edge_vector, neighbours, send_rows, complex_id, cotangent,
    w_node, w_edge, w_norms, vec_node, vec_edge, vec_out, norm_gain, ff_vec, ff_scalar, ff_up,
    w_embed, attn_gain, w_qkv, w_out, ffn_gain, w_up, w_down,
):
    local_rows = node_scalar.shape[0]
    spaces = lax.axis_size("space")
    extra_rows = spaces * CAP
    table_count = local_rows + extra_rows
    all_nodes = complex_id.shape[0]
    steps = NEIGH // GROUP

    if spaces == HEADS and lax.axis_size("dp") == 4 and local_rows == 128:
        quads = spaces // 2
        sent = send_rows[0]
        near = neighbours.T
        ev = edge_vector.reshape(3, local_rows, NEIGH).transpose(0, 2, 1).astype(F32)
        gain_row, at = 0.0, 0
        for gain in (norm_gain, attn_gain, ffn_gain, vec_edge[0]):
            after = D_S + 2 * D_MODEL + H_P - at - gain.shape[0]
            gain_row = gain_row + jnp.pad(gain.astype(F32), (at, after))
            at += gain.shape[0]
        gain_row = gain_row[None]
        (
            agg_s, agg_v, hidden, lx, dsilu, update, table_s, table_v, vec_source, vec_target, vout,
            wn_mix,
        ) = message(
            (
                near, edge_scalar.T, ev, gain_row, node_scalar, node_vector, sent, vec_node.T, w_edge,
                vec_out, w_norms,
            ),
            w_node,
        )
        (
            stream_out, gsone, gvone, gains, attention_share, node_share, early_share, table_o, node_o,
        ) = middle(
            (
                node_scalar, node_vector, agg_s, agg_v, gain_row, ff_vec, ff_scalar, ff_up,
                w_embed, w_qkv, complex_id[None], cotangent,
            ),
            (w_out, w_up, w_down), table_s, node_scalar, quads,
        )
        gscal, gvec, plane, got = backward(
            (near, ev, lx, dsilu, hidden, update),
            (
                gsone, wn_mix, gvone, vout, table_v, node_vector, vec_source, vec_target, gains,
            ),
            (table_s, node_scalar, w_node, table_o, node_o, early_share, attention_share, node_share),
        )
        (
            grad_scalar, grad_vector, out_node, out_edge, out_norms, out_vnode, out_vedge, out_vout,
            out_ffv, out_ffs, out_ffu, out_embed, out_qkv, out_out, out_up, out_down, out_ng, out_ag,
            out_fg, stream_out,
        ) = finish(plane, got, sent, gscal, gvec, stream_out)
        return (
            stream_out, grad_scalar, grad_vector, out_node, out_edge, out_norms, out_vnode,
            out_vedge, out_vout.T, out_ng, out_ffv, out_ffs, out_ffu, out_embed, out_ag,
            out_qkv, out_out, out_fg, out_up, out_down,
        )

    sent_index = send_rows[0].reshape(-1)
    sent_live = sent_index >= 0
    pick = sent_index[:, None] == jnp.arange(local_rows, dtype=jnp.int32)[None, :]
    pick = pick.astype(BF)
    flat_nodes = jnp.concatenate([node_scalar] + [node_vector[c] for c in range(3)], 1)
    outgoing = product(pick, flat_nodes).astype(BF).reshape(spaces, CAP, D_S + 3 * D_V)
    incoming = lax.all_to_all(outgoing, "space", split_axis=0, concat_axis=0, tiled=True)
    incoming = incoming.reshape(extra_rows, D_S + 3 * D_V)
    table_s = jnp.concatenate([node_scalar, incoming[:, :D_S]], 0)
    table_v = jnp.stack(
        [
            jnp.concatenate(
                [node_vector[c], incoming[:, D_S + c * D_V : D_S + (c + 1) * D_V]], 0
            )
            for c in range(3)
        ]
    )
    vec_source = pad_to(vec_node[:, :H_V], H_P, 1)
    vec_target = pad_to(vec_node[:, H_V:], H_P, 1)
    a_source = product(table_s, w_node[:, :D_S]).astype(BF)
    b_target = product(node_scalar, w_node[:, D_S:])
    p_source = product(table_v, vec_source).astype(BF)
    q_target = product(node_vector, vec_target)
    ve_row = pad_to(vec_edge.astype(F32), H_P, 1)
    vout = pad_to(vec_out, H_P, 0)
    wn_mix = pad_to(jnp.concatenate([w_norms, w_edge], 0), H_P, 0)
    mix = jnp.concatenate([a_source, wn_mix], 0)

    near = neighbours.T
    near_col = near[:, :, None]
    near_row = near.reshape(steps, 1, GROUP * local_rows)
    es_k = edge_scalar.reshape(local_rows, NEIGH, D_E).transpose(1, 0, 2)
    es_pad = jnp.pad(es_k, ((0, 0), (0, 0), (1, 128 - 1 - D_E)))
    ev_k = edge_vector.reshape(3, local_rows, NEIGH)
    ev_col = ev_k.transpose(2, 1, 0).astype(F32)
    ev_row = ev_k.transpose(2, 0, 1).reshape(steps, GROUP, 3, local_rows)
    ev_row = ev_row.transpose(0, 2, 1, 3).reshape(steps, 3, GROUP * local_rows)

    agg_s, agg_v, hidden, lx, dsilu, update = edge_forward(
        near_col, es_pad, ev_col, mix, b_target, p_source, q_target, ve_row, vout
    )

    scalar_one = node_scalar.astype(F32) + agg_s
    vector_one = node_vector.astype(F32) + agg_v
    gain_norm = norm_gain.astype(F32)
    normed_s = layer_norm(scalar_one, gain_norm)
    normed_v = vector_norm(vector_one)
    normed_vr = normed_v.astype(BF)
    ff_hidden = product(normed_vr, ff_vec)
    ff_hidden_r = ff_hidden.astype(BF)
    ff_length = length_plus(ff_hidden)
    ff_input = jnp.concatenate([normed_s.astype(BF), ff_length.astype(BF)], -1)
    ff_preact = product(ff_input, ff_scalar)
    ff_update = product(ff_hidden_r, ff_up)
    scalar_two = normed_s + jax.nn.silu(ff_preact)
    vector_two = normed_v + vector_gate(ff_update)
    embed_input = jnp.concatenate([scalar_two.astype(BF), length_plus(vector_two).astype(BF)], -1)
    stream_zero = product(embed_input, w_embed)
    gain_attn = attn_gain.astype(F32)
    attn_in = layer_norm(stream_zero, gain_attn).astype(BF)
    qkv = product(attn_in, w_qkv).astype(BF)
    queries = qkv[:, :D_MODEL]
    keys_own = qkv[:, D_MODEL : 2 * D_MODEL]
    values_own = qkv[:, 2 * D_MODEL :]
    full_qkv = lax.all_gather(qkv, "space", axis=0, tiled=True)
    heads = lambda values: values.reshape(values.shape[0], HEADS, HEAD_DIM)
    full_queries = heads(full_qkv[:, :D_MODEL])
    full_keys = heads(full_qkv[:, D_MODEL : 2 * D_MODEL])
    full_values = heads(full_qkv[:, 2 * D_MODEL :])
    position = lax.axis_index("space")
    own_ids = lax.dynamic_slice_in_dim(complex_id, position * local_rows, local_rows, 0)
    same = own_ids[:, None] == complex_id[None, :]
    score_scale = HEAD_DIM ** (-0.5)
    scores = jnp.einsum("qhd,khd->hqk", heads(queries), full_keys, preferred_element_type=F32)
    scores = jnp.where(same[None], scores * score_scale, -1000000000.0)
    row_peak = jnp.max(scores, axis=-1, keepdims=True)
    shifted = jnp.exp(scores - row_peak)
    totals = jnp.sum(shifted, axis=-1, keepdims=True)
    probs = shifted / totals
    log_total = row_peak + jnp.log(totals)
    attended = jnp.einsum(
        "hqk,khd->qhd", probs.astype(BF), full_values, preferred_element_type=F32
    ).reshape(local_rows, D_MODEL)
    attended_r = attended.astype(BF)
    stream_one = stream_zero + product(attended_r, w_out)
    gain_ffn = ffn_gain.astype(F32)
    ffn_in = layer_norm(stream_one, gain_ffn).astype(BF)
    hidden_up = product(ffn_in, w_up)
    gelu_r = gelu_exact(hidden_up).astype(BF)
    stream_out = (stream_one + product(gelu_r, w_down)).astype(BF)
    grad_w_down = product_lead(gelu_r, cotangent)
    grad_gelu = product_back(cotangent, w_down)
    grad_up_r = pullback(gelu_exact, hidden_up, grad_gelu).astype(BF)
    grad_w_up = product_lead(ffn_in, grad_up_r)
    grad_ffn_in = product_back(grad_up_r, w_up)
    unused, ffn_pull = jax.vjp(layer_norm, stream_one, gain_ffn)
    grad_stream_ln, grad_ffn_gain = ffn_pull(grad_ffn_in)
    grad_stream_one = cotangent.astype(F32) + grad_stream_ln
    grad_branch = grad_stream_one.astype(BF)
    grad_w_out = product_lead(attended_r, grad_branch)
    grad_attended = product_back(grad_branch, w_out).astype(BF)
    row_dots = jnp.sum(heads(grad_attended).astype(F32) * heads(attended), axis=-1).T

    def halves(values):
        high = lax.reduce_precision(values, exponent_bits=8, mantissa_bits=7)
        return [high.astype(BF), (values - high).astype(BF)]

    numbers = jnp.concatenate(halves(log_total[:, :, 0]) + halves(row_dots), 0)
    packed = jnp.concatenate([grad_attended, pad_to(numbers.T, 128, 1)], 1)
    full_packed = lax.all_gather(packed, "space", axis=0, tiled=True)
    full_grad = heads(full_packed[:, :D_MODEL])
    numbers = full_packed[:, D_MODEL : D_MODEL + 4 * HEADS].astype(F32).T
    full_log = numbers[:HEADS] + numbers[HEADS : 2 * HEADS]
    full_dots = numbers[2 * HEADS : 3 * HEADS] + numbers[3 * HEADS :]

    grad_probs = jnp.einsum(
        "qhd,khd->hqk", heads(grad_attended), full_values, preferred_element_type=F32
    )
    grad_scores = (probs * (grad_probs - row_dots[:, :, None])).astype(BF)
    grad_query = jnp.einsum("hqk,khd->qhd", grad_scores, full_keys, preferred_element_type=F32)
    own_scores = jnp.einsum(
        "khd,qhd->hkq", heads(keys_own), full_queries, preferred_element_type=F32
    )
    own_scores = jnp.where(same[None], own_scores * score_scale, -1000000000.0)
    own_probs = jnp.exp(own_scores - full_log[:, None, :])
    own_grad_probs = jnp.einsum(
        "khd,qhd->hkq", heads(values_own), full_grad, preferred_element_type=F32
    )
    own_grad_scores = (own_probs * (own_grad_probs - full_dots[:, None, :])).astype(BF)
    grad_keys = jnp.einsum(
        "hkq,qhd->khd", own_grad_scores, full_queries, preferred_element_type=F32
    )
    grad_values = jnp.einsum(
        "hkq,qhd->khd", own_probs.astype(BF), full_grad, preferred_element_type=F32
    )
    flat = lambda values: values.reshape(local_rows, D_MODEL)
    grad_qkv = jnp.concatenate(
        [flat(grad_query) * score_scale, flat(grad_keys) * score_scale, flat(grad_values)], -1
    ).astype(BF)
    grad_w_qkv = product_lead(attn_in, grad_qkv)
    grad_attn_in = product_back(grad_qkv, w_qkv)
    unused, attn_pull = jax.vjp(layer_norm, stream_zero, gain_attn)
    grad_zero_ln, grad_attn_gain = attn_pull(grad_attn_in)
    grad_stream_r = (grad_stream_one + grad_zero_ln).astype(BF)
    grad_w_embed = product_lead(embed_input, grad_stream_r)
    grad_embed_in = product_back(grad_stream_r, w_embed)
    grad_vector_two = pullback(length_plus, vector_two, grad_embed_in[:, D_S:])
    grad_ff_pre = pullback(jax.nn.silu, ff_preact, grad_embed_in[:, :D_S]).astype(BF)
    grad_ff_scalar = product_lead(ff_input, grad_ff_pre)
    grad_ff_input = product_back(grad_ff_pre, ff_scalar)
    grad_ff_update = pullback(vector_gate, ff_update, grad_vector_two).astype(BF)
    grad_ff_up = product_lead(ff_hidden_r, grad_ff_update)
    grad_ff_hidden = (
        product_back(grad_ff_update, ff_up)
        + pullback(length_plus, ff_hidden, grad_ff_input[:, D_S:])
    ).astype(BF)
    grad_ff_vec = product_lead(normed_vr, grad_ff_hidden)
    grad_normed_v = grad_vector_two + product_back(grad_ff_hidden, ff_vec)
    grad_normed_s = grad_embed_in[:, :D_S] + grad_ff_input[:, :D_S]
    unused, norm_pull = jax.vjp(layer_norm, scalar_one, gain_norm)
    grad_scalar_one, grad_norm_gain = norm_pull(grad_normed_s)
    grad_vector_one = pullback(vector_norm, vector_one, grad_normed_v)

    shard = lambda grad: grad.astype(BF).reshape((spaces, grad.shape[0] // spaces) + grad.shape[1:])
    gains = jnp.concatenate(
        [shard(grad_norm_gain), shard(grad_attn_gain), shard(grad_ffn_gain)], 1
    )
    gains = pad_to(pad_to(gains, 512, 1)[:, None, :], 16, 1)
    first_share = jnp.concatenate(
        [
            shard(grad_w_down),
            fold(shard(grad_w_up)),
            fold(shard(grad_w_qkv)),
            shard(grad_w_out),
            shard(grad_w_embed),
            fold(shard(grad_ff_scalar)),
            jnp.concatenate([shard(grad_ff_vec), shard(grad_ff_up)], 2),
            gains,
        ],
        1,
    )
    first_sum = lax.psum_scatter(first_share, "space", scatter_dimension=0, tiled=False)
    first_sum = lax.psum(first_sum, "dp").astype(F32)

    grad_a, grad_mix, grad_b, grad_p, grad_q, grad_vout = edge_backward(
        near_row, ev_col, ev_row, hidden, lx, dsilu, update,
        grad_scalar_one * (1.0 / NEIGH), grad_vector_one * (1.0 / NEIGH), wn_mix, vout, table_count,
    )
    grad_vedge = jnp.sum(grad_p[:, table_count], 0)[:H_V]
    grad_vec_edge = lax.psum(grad_vedge[None, :], ("dp", "space"))
    grad_a_r = grad_a.astype(BF)
    grad_p_r = grad_p[:, :table_count].astype(BF)
    grad_b_r = grad_b.astype(BF)
    grad_q_r = grad_q.astype(BF)
    grad_node_a = product_lead(table_s, grad_a_r)
    grad_node_b = product_lead(node_scalar, grad_b_r)
    grad_vec_a = product_lead(table_v, grad_p_r)
    grad_vec_b = product_lead(node_vector, grad_q_r)
    grad_table_scalar = product_back(grad_a_r, w_node[:, :D_S])
    grad_table_vector = product_back(grad_p_r, vec_source)
    grad_scalar = (
        grad_scalar_one + product_back(grad_b_r, w_node[:, D_S:]) + grad_table_scalar[:local_rows]
    )
    grad_vector = (
        grad_vector_one + product_back(grad_q_r, vec_target) + grad_table_vector[:, :local_rows]
    )
    back = jnp.concatenate(
        [grad_table_scalar[local_rows:]] + [grad_table_vector[c, local_rows:] for c in range(3)], 1
    )
    back = back.astype(BF).reshape(spaces, CAP, D_S + 3 * D_V)
    got = lax.all_to_all(back, "space", split_axis=0, concat_axis=0, tiled=True)
    got = got.reshape(extra_rows, D_S + 3 * D_V)
    got = jnp.where(sent_live[:, None], got, 0)
    added = lax.dot_general(pick, got, (((0,), (0,)), ((), ())), preferred_element_type=F32)
    grad_scalar = grad_scalar + added[:, :D_S]
    grad_vector = grad_vector + jnp.moveaxis(
        added[:, D_S:].reshape(local_rows, 3, D_V), 1, 0
    )

    columns = lambda grad: jnp.moveaxis(
        grad.reshape(grad.shape[0], spaces, grad.shape[1] // spaces), 1, 0
    )
    mix_block = columns(grad_mix.astype(BF))
    mix_width = D_S // spaces
    mix_rows = H_P * mix_width // 512
    second_share = jnp.concatenate(
        [
            fold(shard(grad_node_a)),
            fold(shard(grad_node_b)),
            mix_block.reshape(spaces, mix_rows, 512),
            shard(grad_vec_a)[:, :, :512],
            shard(grad_vec_b)[:, :, :512],
            shard(grad_vout)[:, :, :512],
            jnp.concatenate(
                [
                    shard(grad_vec_a)[:, :, 512:],
                    shard(grad_vec_b)[:, :, 512:],
                    shard(grad_vout)[:, :, 512:],
                    jnp.zeros((spaces, D_V // spaces, 128), BF),
                ],
                2,
            ),
        ],
        1,
    )
    second_sum = lax.psum_scatter(second_share, "space", scatter_dimension=0, tiled=False)
    second_sum = lax.psum(second_sum, "dp").astype(F32)

    def taker(rows_in):
        at = [0]

        def take(rows, cols, blocks=1):
            part = rows_in[at[0] : at[0] + rows * blocks]
            at[0] += rows * blocks
            return unfold(part, rows, cols) if blocks > 1 else part

        return take

    take = taker(first_sum)
    out_down = take(grad_w_down.shape[0] // spaces, 512)
    out_up = take(D_MODEL // spaces, 2048, 4)
    out_qkv = take(D_MODEL // spaces, 1536, 3)
    out_out = take(D_MODEL // spaces, 512)
    out_embed = take((D_S + D_V) // spaces, 512)
    out_ffs = take((D_S + D_V) // spaces, 1024, 2)
    both = take(D_V // spaces, 512)
    out_ffv, out_ffu = both[:, :D_V], both[:, D_V:]
    gain_row = take(16, 512)[0]
    cuts = [D_S // spaces, D_MODEL // spaces, D_MODEL // spaces]
    out_gn = gain_row[: cuts[0]]
    out_ga = gain_row[cuts[0] : cuts[0] + cuts[1]]
    out_gf = gain_row[cuts[0] + cuts[1] : sum(cuts)]
    take = taker(second_sum)
    node_a = take(D_S // spaces, 1024, 2)
    node_b = take(D_S // spaces, 1024, 2)
    mixed = take(mix_rows, 512).reshape(H_P, mix_width)
    vec_a = take(D_V // spaces, 512)
    vec_b = take(D_V // spaces, 512)
    vout_t = take(D_V // spaces, 512)
    tails = take(D_V // spaces, 512)
    out_vec_node = jnp.concatenate([vec_a, tails[:, :1], vec_b, tails[:, 128:129]], 1)
    out_vec_out = jnp.concatenate([vout_t, tails[:, 256:257]], 1).T
    return (
        stream_out,
        grad_scalar.astype(BF),
        grad_vector.astype(BF),
        jnp.concatenate([node_a, node_b], 1),
        mixed[H_V : H_V + D_E],
        mixed[:H_V],
        out_vec_node,
        grad_vec_edge,
        out_vec_out,
        out_gn,
        out_ffv,
        out_ffs,
        out_ffu,
        out_embed,
        out_ga,
        out_qkv,
        out_out,
        out_gf,
        out_up,
        out_down,
    )


def solution(mesh):
    rows = P(("dp", "space"), None)
    component = P(None, ("dp", "space"), None)
    return jax.shard_map(
        body,
        mesh=mesh,
        in_specs=(
            rows, component, rows, P(None, ("dp", "space")), rows,
            P(("dp", "space"), None, None), P("dp"), rows,
        ) + (P(),) * 17,
        out_specs=(
            rows, rows, component, P("space", None), P(None, "space"), P(None, "space"),
            P("space", None), P(), P(None, "space"), P("space"), P("space", None),
            P("space", None), P("space", None), P("space", None), P("space"), P("space", None),
            P("space", None), P("space"), P("space", None), P("space", None),
        ),
        check_vma=False,
    )
```
